32 devices in a mesh: blk: 8 (over z, y), narrow: 4 (over x, core).
Axes of the slice: x: 2, y: 2, z: 4, core: 2. Of those that a mesh axis runs over, the one named last changes fastest.
Arguments:
- factors_a: bfloat16 [2, 2048, 512], replicated, may hold values from -0.25 to 0.25
- factors_b: bfloat16 [128, 2048, 512], P('blk', 'narrow'), may hold values from -0.0078125 to 0.0078125
- amplitudes: bfloat16 [64, 2048, 2048], P('blk', 'narrow'), may hold values from -6 to 6
- screen: int32 [8, 16], replicated, may hold values from 0 to 1, as said below
Outputs:
- residual: float32 [3, 8, 256], P(None, 'blk', 'narrow')
The draws below stay inside these ranges and needn't reach their ends.
Inputs may be any that keep to these rules, and one draw needn't show every extreme that they name: `screen`: entry [i, s] is 1 where c sub-tile s is kept for pair tile i. Every row keeps 1 to 8 sub-tiles and some row keeps exactly 8.
All inputs are finite; a program needn't handle non-finite values.
Results may differ from the reference program's by a relative error of at most 0.0029.
Values may be sent and summed in bfloat16 or wider, within the bound.
No kernel may reach another device: no remote copies, remote signals or barrier semaphores. Data moves between devices by JAX's collectives and lax.ppermute only.
A program may use at most 128 MiB of HBM per device.

```python
import jax
import jax.numpy as jnp
from jax import lax

V = 2048
NAUX = 512
CS = 128
AROWS = 2
BT = 16
P_SLAB = 8
STEPS = 3
PAIRS = 64
BW = 128
NSUB = 16
MOST = 8
N_BLK = 8


def draw_screen(key, part):
    key_count = jax.random.fold_in(key, 11)
    key_busy = jax.random.fold_in(key, 12)
    key_order = jax.random.fold_in(key, 13)
    counts = 1 + jax.random.randint(key_count, (N_BLK,), 0, 3)
    counts = jnp.minimum(counts, MOST)
    busiest = jax.random.randint(key_busy, (), 0, N_BLK)
    counts = jnp.where(jnp.arange(N_BLK) == busiest, MOST, counts)
    scores = jax.random.randint(key_order, (N_BLK, NSUB), 0, 1 << 20) * NSUB + jnp.arange(NSUB)[None, :]
    order = jnp.argsort(scores, axis=1)
    ranks = jnp.argsort(order, axis=1)
    return (ranks < counts[:, None]).astype(jnp.int32)


def levels(stream_key, extent, split, smallest, largest):
    def one(dim, parts):
        heights = jax.random.uniform(jax.random.fold_in(jax.random.fold_in(stream_key, 6), dim), (parts,), jnp.float32, smallest / len(split), largest / len(split))
        return jnp.repeat(jnp.exp(heights), extent[dim] // parts).reshape((-1,) + (1,) * (len(extent) - dim - 1))

    factor_of = one(*split[0])
    for cut in split[1:]:
        factor_of = factor_of * one(*cut)
    return factor_of


def normal_values(stream_key, dims, deviation, limit, pieces=(), kind=jnp.bfloat16):
    drawn = jax.random.normal(stream_key, dims, jnp.float32) * deviation
    if len(pieces) > 0:
        drawn = levels(stream_key, dims, pieces, -0.22, 0.18) * drawn
    return jnp.clip(drawn, min=-limit, max=limit).astype(kind)


def setup_inputs(seed: int = 0) -> dict:
    seeds = jax.random.split(jax.random.key(seed), 5)
    return {
        "factors_a": normal_values(seeds[0], (AROWS, V, NAUX), NAUX ** -0.5, 0.25),
        "factors_b": normal_values(seeds[1], (BW, V, NAUX), (2 * CS * V) ** -0.5, 0.0078125, ((0, 8), (1, 4))),
        "amplitudes": normal_values(seeds[2], (PAIRS, V, V), 1.0, 6.0, ((0, 8), (1, 4))),
        "screen": draw_screen(jax.random.fold_in(seeds[4], 71), 0),
    }


def reference(factors_a, factors_b, amplitudes, screen):
    tile_count = N_BLK

    def per_tile(tile_at):
        b_panel = lax.dynamic_slice_in_dim(factors_b, (tile_at * BT).astype(jnp.int32), BT, 0).reshape(BT * V, NAUX)
        slab_stack = jnp.stack([lax.dynamic_slice_in_dim(amplitudes, (((tile_at - offset) % tile_count) * P_SLAB).astype(jnp.int32), P_SLAB, 0) for offset in range(STEPS)])

        def add_tile(sub_at, running):
            sub_at = sub_at.astype(jnp.int32)

            def compute(running):
                factor_block = lax.dynamic_slice_in_dim(factors_a, sub_at * CS, CS, 1).reshape(AROWS * CS, NAUX)
                integral = jnp.dot(factor_block, b_panel.T, preferred_element_type=jnp.float32)
                integral = integral.astype(jnp.bfloat16).reshape(AROWS, CS, BT, V)
                amp_block = lax.dynamic_slice_in_dim(slab_stack, sub_at * CS, CS, 3)
                return running + jnp.einsum("xpdc,acbd->xpab", amp_block.astype(jnp.float32), integral.astype(jnp.float32))

            return lax.cond(screen[tile_at, sub_at] != 0, compute, lambda kept: kept, running)

        running = lax.fori_loop(0, V // CS, add_tile, jnp.zeros((STEPS, P_SLAB, AROWS, BT), jnp.float32))
        return running.reshape(STEPS, P_SLAB * AROWS * BT)

    results = lax.map(per_tile, jnp.arange(tile_count, dtype=jnp.int32))
    return jnp.transpose(results, (1, 0, 2))
```

```python
import functools

import jax
import jax.numpy as jnp
from jax import lax
from jax.experimental import pallas as pl
from jax.experimental.pallas import tpu as pltpu
from jax.sharding import PartitionSpec as P

STEPS = 3
MOST = 8
ROUNDS = 3
GROUP = 16
LANES = 128


def rotated(value, by):
    size = lax.axis_size("blk")
    return lax.ppermute(value, "blk", [(i, (i + by) % size) for i in range(size)])


def swapped(value):
    size = lax.axis_size("blk")
    return lax.ppermute(value, "blk", [(i, i ^ 1) for i in range(size)])


def take_kernel(list_ref, source_ref, out_ref):
    out_ref[0] = source_ref[...]


def take_columns(amplitudes, sub_list, width, start, extent):
    pairs = amplitudes.shape[0]
    slots = sub_list.shape[0]
    return pl.pallas_call(
        take_kernel,
        grid_spec=pltpu.PrefetchScalarGridSpec(
            num_scalar_prefetch=1,
            grid=(slots,),
            in_specs=[
                pl.BlockSpec(
                    (pairs, extent, width), lambda s, sub: (0, start // extent, sub[s])
                )
            ],
            out_specs=pl.BlockSpec((1, pairs, extent, width), lambda s, sub: (s, 0, 0, 0)),
        ),
        out_shape=jax.ShapeDtypeStruct((slots, pairs, extent, width), amplitudes.dtype),
        compiler_params=pltpu.CompilerParams(vmem_limit_bytes=32 * 1024 * 1024),
        cost_estimate=pl.CostEstimate(
            flops=0,
            bytes_accessed=4 * slots * pairs * extent * width,
            transcendentals=0,
        ),
        name="take_columns",
    )(sub_list, amplitudes)


def terms_kernel(slots, list_ref, *refs):
    amp_refs = refs[:slots]
    factor_refs = refs[slots : 2 * slots]
    panel_ref, out_ref, total, mixed = refs[2 * slots :]
    count = list_ref[slots]
    pairs, d_rows, width = amp_refs[0].shape[-3:]
    a_rows, _, aux = factor_refs[0].shape
    b_rows = panel_ref.shape[0]
    groups = d_rows // GROUP

    @pl.when(pl.program_id(0) == 0)
    def _():
        total[...] = jnp.zeros_like(total)

    def amp_of(k):
        return amp_refs[k][...].reshape(pairs * d_rows, width)

    @pl.when(count > 0)
    def _():
        for k in range(0, slots, 2):

            @pl.when(k < count)
            def _():
                lhs = amp_of(k)
                if k + 1 < slots:
                    lhs = jnp.concatenate([lhs, amp_of(k + 1)], axis=1)
                for a in range(a_rows):
                    rhs = factor_refs[k][a]
                    if k + 1 < slots:
                        second = factor_refs[k + 1][a]
                        second = jnp.where(k + 1 < count, second, jnp.zeros_like(second))
                        rhs = jnp.concatenate([rhs, second], axis=0)
                    product = jnp.dot(lhs, rhs, preferred_element_type=jnp.float32)
                    if k == 0:
                        mixed[a] = product
                    else:
                        mixed[a] += product

        rounded = [
            mixed[a].astype(jnp.bfloat16).reshape(pairs, d_rows, aux) for a in range(a_rows)
        ]
        panel = panel_ref[...]

        def cut(value, g):
            part = value[:, g * GROUP : (g + 1) * GROUP, :]
            return part.reshape(value.shape[0] * GROUP, aux)

        lhs = jnp.concatenate(
            [
                jnp.concatenate([cut(value, g) for value in rounded], axis=0)
                for g in range(groups)
            ],
            axis=1,
        )
        rhs = jnp.concatenate([cut(panel, g) for g in range(groups)], axis=1)
        total[...] += lax.dot_general(
            lhs, rhs, (((1,), (1,)), ((), ())), preferred_element_type=jnp.float32
        )

    @pl.when(pl.program_id(0) == pl.num_programs(0) - 1)
    def _():
        rows, columns = total.shape
        row_d = lax.broadcasted_iota(jnp.int32, (rows, columns), 0) % GROUP
        column_d = lax.broadcasted_iota(jnp.int32, (rows, columns), 1) % GROUP
        kept = jnp.where(row_d == column_d, total[...], 0.0)
        kept = kept.reshape(rows // GROUP, GROUP, columns).sum(axis=1)
        from_b = lax.broadcasted_iota(jnp.int32, (columns, LANES), 0) // GROUP
        to_b = lax.broadcasted_iota(jnp.int32, (columns, LANES), 1)
        gather = jnp.where(from_b == to_b, 1.0, 0.0)
        out_ref[...] = jnp.dot(
            kept, gather, precision=lax.Precision.HIGHEST, preferred_element_type=jnp.float32
        )


def pair_terms(factors_a, panel, amps, sub_list, count, width, extent, amp_at=0, panel_at=0):
    slots = sub_list.shape[0]
    a_rows, _, aux = factors_a.shape
    pairs = amps.shape[-3]
    b_rows = panel.shape[0]
    d_rows = min(64, extent)
    steps = extent // d_rows
    amp_block, panel_block = amp_at // d_rows, panel_at // d_rows

    def step_of(d, ref, k):
        return jnp.where(k < ref[slots], d, 0)

    if amps.ndim == 3:
        amp_specs = [
            pl.BlockSpec(
                (pairs, d_rows, width),
                lambda d, ref, k=k: (0, amp_block + step_of(d, ref, k), ref[k]),
            )
            for k in range(slots)
        ]
    else:
        amp_specs = [
            pl.BlockSpec(
                (1, pairs, d_rows, width),
                lambda d, ref, k=k: (k, 0, amp_block + step_of(d, ref, k), 0),
            )
            for k in range(slots)
        ]
    factor_specs = [
        pl.BlockSpec((a_rows, width, aux), lambda d, ref, k=k: (0, ref[k], 0))
        for k in range(slots)
    ]
    panel_spec = pl.BlockSpec(
        (b_rows, d_rows, aux), lambda d, ref: (0, panel_block + step_of(d, ref, 0), 0)
    )
    rows = a_rows * pairs * GROUP
    columns = b_rows * GROUP
    out = pl.pallas_call(
        functools.partial(terms_kernel, slots),
        grid_spec=pltpu.PrefetchScalarGridSpec(
            num_scalar_prefetch=1,
            grid=(steps,),
            in_specs=amp_specs + factor_specs + [panel_spec],
            out_specs=pl.BlockSpec((a_rows * pairs, LANES), lambda d, ref: (0, 0)),
            scratch_shapes=[
                pltpu.VMEM((rows, columns), jnp.float32),
                pltpu.VMEM((a_rows, pairs * d_rows, aux), jnp.float32),
            ],
        ),
        out_shape=jax.ShapeDtypeStruct((a_rows * pairs, LANES), jnp.float32),
        compiler_params=pltpu.CompilerParams(vmem_limit_bytes=48 * 1024 * 1024),
        cost_estimate=pl.CostEstimate(
            flops=2 * pairs * extent * a_rows * aux * (slots * width + GROUP * b_rows),
            bytes_accessed=2 * extent * (pairs * slots * width + b_rows * aux),
            transcendentals=0,
        ),
        name="pair_terms",
    )(
        jnp.concatenate([sub_list, count.reshape(1)]).astype(jnp.int32),
        *([amps] * slots),
        *([factors_a] * slots),
        panel,
    )
    return out[:, :b_rows]


def kept_lists(screen):
    subs = screen.shape[1]
    keep = screen != 0
    at = jnp.arange(subs, dtype=jnp.int32)
    earlier = (at[:, None] > at[None, :])[None] & keep[:, None, :]
    rank = jnp.sum(earlier.astype(jnp.int32), axis=2)
    hit = keep[:, None, :] & (rank[:, None, :] == jnp.arange(MOST, dtype=jnp.int32)[None, :, None])
    lists = jnp.sum(jnp.where(hit, at[None, None, :], 0), axis=2)
    return lists, jnp.sum(keep.astype(jnp.int32), axis=1)


def local(factors_a, factors_b, amplitudes, screen):
    pairs, d_extent, virtuals = amplitudes.shape
    width = virtuals // screen.shape[1]
    tiles = lax.axis_size("blk")
    position = lax.axis_index("blk")
    half = d_extent // 2
    quarter = half // 2

    lists, counts = kept_lists(screen)
    fullest = jnp.argmax(counts).astype(jnp.int32)
    others = jnp.max(jnp.where(jnp.arange(tiles) == fullest, 0, counts))

    def row(tile):
        return (
            lax.dynamic_index_in_dim(lists, tile, 0, keepdims=False),
            lax.dynamic_index_in_dim(counts, tile, 0, keepdims=False),
        )

    own_list, own_count = row(position)
    next_list, _ = row((position + 1) % tiles)
    after_list, _ = row((position + 2) % tiles)
    full_list, full_count = row(fullest)
    extra_list = full_list[ROUNDS:]
    extra_count = jnp.maximum(full_count - ROUNDS, 0)
    is_first = position % 2 == 0
    is_full = position == fullest
    feeds_one = (position + 1) % tiles == fullest
    feeds_two = (position + 2) % tiles == fullest

    def run(wrapped, odd, operands):
        factors_a, factors_b, amplitudes = operands
        terms = functools.partial(pair_terms, factors_a, width=width)
        take = functools.partial(take_columns, amplitudes, width=width)
        straight = [(i, i + 2) for i in range(tiles - 2)]
        around = [(i, (i + 2) % tiles) for i in range(tiles - 2, tiles)]
        ahead = around if wrapped else straight
        back = [(to, at) for at, to in ahead]

        def forward(value):
            return lax.ppermute(value, "blk", ahead)

        def backward(value):
            return lax.ppermute(value, "blk", back)

        first_half = take(next_list[:ROUNDS], start=0, extent=half)
        second_half = take(next_list[:ROUNDS], start=half, extent=half)
        after = take(after_list[:ROUNDS], start=0, extent=d_extent)
        near_a = swapped(first_half)
        hop_a = rotated(jnp.where(is_first, near_a, second_half), 2)
        got_after = rotated(after, 2)
        near_b = swapped(jnp.where(is_first, second_half, hop_a))
        low = jnp.where(is_first, hop_a, near_a)
        high = near_b

        extra = take(extra_list, start=0, extent=half)
        extra_two = forward(extra)
        extra_one = swapped(extra if odd else extra_two)
        panel_0 = factors_b[:, half : half + quarter]
        panel_1 = factors_b[:, half + quarter :]
        if odd:
            side_0 = swapped(panel_0)
            side_1 = swapped(panel_1)
            far_0 = backward(panel_0)
            far_1 = swapped(backward(side_1))
            out_0 = jnp.where(feeds_one, side_0, far_0)
            out_1 = jnp.where(feeds_one, side_1, far_1)
        else:
            far_0 = backward(panel_0)
            far_1 = backward(swapped(panel_1))
            out_0 = jnp.where(feeds_two, far_0, swapped(far_0))
            out_1 = jnp.where(feeds_two, swapped(far_1), far_1)

        here = terms(factors_b, amplitudes, own_list, own_count, extent=d_extent)
        light = jnp.minimum(own_count, ROUNDS)
        one = terms(factors_b, low, own_list[:ROUNDS], light, extent=half)
        one += terms(factors_b, high, own_list[:ROUNDS], light, extent=half, panel_at=half)
        two = terms(factors_b, got_after, own_list[:ROUNDS], light, extent=d_extent)
        mine = jnp.where(is_full, extra_count, 0)
        one += terms(factors_b, extra_one, extra_list, mine, extent=half)
        two += terms(factors_b, extra_two, extra_list, mine, extent=half)
        fed = jnp.where(feeds_one | feeds_two, extra_count, 0)
        sent = terms(out_0, amplitudes, extra_list, fed, extent=quarter, amp_at=half)
        sent += terms(out_1, amplitudes, extra_list, fed, extent=quarter, amp_at=half + quarter)
        one += rotated(jnp.where(feeds_one, sent, 0.0), 1)
        two += rotated(jnp.where(feeds_two, sent, 0.0), 2)

        def add_round(r, running):
            one, two = running
            own_sub = lax.dynamic_slice_in_dim(own_list, r, 1)
            count = jnp.where((r < own_count) & ~is_full, 1, 0)
            next_sub = lax.dynamic_slice_in_dim(next_list, r, 1)
            after_sub = lax.dynamic_slice_in_dim(after_list, r, 1)
            from_one = rotated(take(next_sub, start=0, extent=d_extent), 1)
            from_two = rotated(take(after_sub, start=0, extent=d_extent), 2)
            return (
                one + terms(factors_b, from_one, own_sub, count, extent=d_extent),
                two + terms(factors_b, from_two, own_sub, count, extent=d_extent),
            )

        one, two = lax.fori_loop(ROUNDS, jnp.maximum(others, ROUNDS), add_round, (one, two))
        return jnp.stack([here, one, two])

    case = jnp.where(fullest < 2, 2, 0) + fullest % 2
    branches = [
        functools.partial(run, wrapped, odd) for wrapped in (False, True) for odd in (False, True)
    ]
    terms = lax.switch(case, branches, (factors_a, factors_b, amplitudes))
    a_rows = factors_a.shape[0]
    terms = terms.reshape(STEPS, a_rows, pairs, -1).swapaxes(1, 2).reshape(STEPS, 1, -1)
    return lax.psum_scatter(terms, "narrow", scatter_dimension=2, tiled=True)


def solution(mesh):
    return jax.shard_map(
        local,
        mesh=mesh,
        in_specs=(P(), P("blk", "narrow", None), P("blk", "narrow", None), P()),
        out_specs=P(None, "blk", "narrow"),
        check_vma=False,
    )
```

```python
import functools

import jax
import jax.numpy as jnp
from jax import lax
from jax.experimental import pallas as pl
from jax.experimental.pallas import tpu as pltpu
from jax.sharding import PartitionSpec as P

STEPS = 3
MOST = 8
ROUNDS = 3
GROUP = 16
LANES = 128
DBLK = 128
ROW = MOST + 1

OWN, LIGHT, NEXT, AFTER, LEAD, REST, MINE, FED, MISC = range(9)


def send(value, pairs):
    return lax.ppermute(value, "blk", pairs)


def rotated(value, by):
    size = lax.axis_size("blk")
    return send(value, [(i, (i + by) % size) for i in range(size)])


def lists_kernel(position_ref, screen_ref, out_ref):
    tiles, subs = screen_ref.shape
    position = position_ref[0]

    def count_of(tile):
        return sum(jnp.where(screen_ref[tile, s] != 0, 1, 0) for s in range(subs))

    def look(tile, found):
        best, fullest, others = found
        count = count_of(tile)
        larger = count > best
        others = jnp.where(larger, best, jnp.maximum(others, count))
        return jnp.where(larger, count, best), jnp.where(larger, tile, fullest), others

    zero = jnp.int32(0)
    best, fullest, others = lax.fori_loop(0, tiles, look, (zero, zero, zero))

    def fill(row, tile, skip, count):
        for k in range(MOST):
            out_ref[row * ROW + k] = 0
        seen = jnp.int32(0)
        for s in range(subs):
            kept = screen_ref[tile, s] != 0

            @pl.when(kept & (seen >= skip))
            def _():
                out_ref[row * ROW + seen - skip] = s

            seen += jnp.where(kept, 1, 0)
        out_ref[row * ROW + MOST] = seen if count is None else count

    following = lax.rem(position + 1, tiles)
    second = lax.rem(position + 2, tiles)
    is_first = lax.rem(position, 2) == 0
    own_count = count_of(position)
    extra = jnp.maximum(best - ROUNDS, 0)
    feeds = (following == fullest) | (second == fullest)
    fill(OWN, position, 0, own_count)
    fill(LIGHT, position, 0, jnp.minimum(own_count, ROUNDS))
    fill(NEXT, following, 0, None)
    fill(AFTER, second, 0, None)
    fill(LEAD, jnp.where(is_first, second, following), 0, None)
    fill(REST, jnp.where(is_first, following, second), 0, None)
    fill(MINE, fullest, ROUNDS, jnp.where(position == fullest, extra, 0))
    fill(FED, fullest, ROUNDS, jnp.where(feeds, extra, 0))
    out_ref[MISC * ROW] = jnp.where(fullest < 2, 2, 0) + lax.rem(fullest, 2)
    out_ref[MISC * ROW + 1] = fullest
    out_ref[MISC * ROW + 2] = others
    for k in range(3, ROW):
        out_ref[MISC * ROW + k] = 0


def kept_lists(position, screen):
    return pl.pallas_call(
        lists_kernel,
        in_specs=[pl.BlockSpec(memory_space=pltpu.SMEM)] * 2,
        out_specs=pl.BlockSpec(memory_space=pltpu.SMEM),
        out_shape=jax.ShapeDtypeStruct(((MISC + 1) * ROW,), jnp.int32),
        name="kept_lists",
    )(position.reshape(1), screen)


def take_kernel(lists_ref, source_ref, out_ref):
    out_ref[0] = source_ref[...]


def take_columns(lists, amplitudes, row, slots, width, start, extent):
    pairs = amplitudes.shape[0]
    return pl.pallas_call(
        take_kernel,
        grid_spec=pltpu.PrefetchScalarGridSpec(
            num_scalar_prefetch=1,
            grid=(slots,),
            in_specs=[
                pl.BlockSpec(
                    (pairs, extent, width),
                    lambda s, ref: (0, start // extent, ref[row * ROW + s]),
                )
            ],
            out_specs=pl.BlockSpec((1, pairs, extent, width), lambda s, ref: (s, 0, 0, 0)),
        ),
        out_shape=jax.ShapeDtypeStruct((slots, pairs, extent, width), amplitudes.dtype),
        compiler_params=pltpu.CompilerParams(vmem_limit_bytes=16 * 1024 * 1024),
        cost_estimate=pl.CostEstimate(
            flops=0,
            bytes_accessed=4 * slots * pairs * extent * width,
            transcendentals=0,
        ),
        name="take_columns",
    )(lists, amplitudes)


def terms_kernel(slots, row, lists_ref, *refs):
    amp_refs = refs[:slots]
    factor_refs = refs[slots : 2 * slots]
    panel_ref, out_ref, total, mixed = refs[2 * slots :]
    count = lists_ref[row * ROW + MOST]
    pairs, d_rows, width = amp_refs[0].shape[-3:]
    a_rows, _, aux = factor_refs[0].shape
    groups = d_rows // GROUP

    @pl.when(pl.program_id(0) == 0)
    def _():
        total[...] = jnp.zeros_like(total)

    def amp_of(k):
        return amp_refs[k][...].reshape(pairs * d_rows, width)

    def mix(top):
        lhs = jnp.concatenate([amp_of(k) for k in range(top)], axis=1)
        for a in range(a_rows):
            rows = [factor_refs[k][a] for k in range(top)]
            rows[-1] = jnp.where(top - 1 < count, rows[-1], jnp.zeros_like(rows[-1]))
            product = jnp.dot(
                lhs, jnp.concatenate(rows, axis=0), preferred_element_type=jnp.float32
            )
            mixed[a] = product.astype(mixed.dtype).reshape(pairs, d_rows, aux)

    for low in range(0, slots, 2):
        pl.when((count > low) & (count <= low + 2))(functools.partial(mix, min(low + 2, slots)))

    @pl.when(count > 0)
    def _():
        def cut(value, g):
            part = value[:, g * GROUP : (g + 1) * GROUP, :]
            return part.reshape(value.shape[0] * GROUP, aux)

        values = [mixed[a] for a in range(a_rows)]
        panel = panel_ref[...]
        lhs = jnp.concatenate(
            [
                jnp.concatenate([cut(value, g) for value in values], axis=0)
                for g in range(groups)
            ],
            axis=1,
        )
        rhs = jnp.concatenate([cut(panel, g) for g in range(groups)], axis=1)
        total[...] += lax.dot_general(
            lhs, rhs, (((1,), (1,)), ((), ())), preferred_element_type=jnp.float32
        )

    @pl.when(pl.program_id(0) == pl.num_programs(0) - 1)
    def _():
        rows, columns = total.shape
        row_d = lax.broadcasted_iota(jnp.int32, (rows, columns), 0) % GROUP
        column_d = lax.broadcasted_iota(jnp.int32, (rows, columns), 1) % GROUP
        kept = jnp.where(row_d == column_d, total[...], 0.0)
        kept = kept.reshape(rows // GROUP, GROUP, columns).sum(axis=1)
        from_b = lax.broadcasted_iota(jnp.int32, (columns, LANES), 0) // GROUP
        to_b = lax.broadcasted_iota(jnp.int32, (columns, LANES), 1)
        gather = jnp.where(from_b == to_b, 1.0, 0.0)
        out_ref[...] = jnp.dot(
            kept, gather, precision=lax.Precision.HIGHEST, preferred_element_type=jnp.float32
        )


def pair_terms(lists, factors_a, panel, amps, row, slots, width, extent, amp_at=0, panel_at=0):
    a_rows, _, aux = factors_a.shape
    pairs = amps.shape[-3]
    b_rows = panel.shape[0]
    d_rows = min(DBLK, extent)
    steps = extent // d_rows
    amp_block, panel_block = amp_at // d_rows, panel_at // d_rows
    base = row * ROW

    def step_of(d, ref, k):
        return jnp.where(k < ref[base + MOST], d, 0)

    if amps.ndim == 3:
        amp_specs = [
            pl.BlockSpec(
                (pairs, d_rows, width),
                lambda d, ref, k=k: (0, amp_block + step_of(d, ref, k), ref[base + k]),
            )
            for k in range(slots)
        ]
    else:
        amp_specs = [
            pl.BlockSpec(
                (1, pairs, d_rows, width),
                lambda d, ref, k=k: (k, 0, amp_block + step_of(d, ref, k), 0),
            )
            for k in range(slots)
        ]
    factor_specs = [
        pl.BlockSpec((a_rows, width, aux), lambda d, ref, k=k: (0, ref[base + k], 0))
        for k in range(slots)
    ]
    panel_spec = pl.BlockSpec(
        (b_rows, d_rows, aux), lambda d, ref: (0, panel_block + step_of(d, ref, 0), 0)
    )
    rows = a_rows * pairs * GROUP
    columns = b_rows * GROUP
    out = pl.pallas_call(
        functools.partial(terms_kernel, slots, row),
        grid_spec=pltpu.PrefetchScalarGridSpec(
            num_scalar_prefetch=1,
            grid=(steps,),
            in_specs=amp_specs + factor_specs + [panel_spec],
            out_specs=pl.BlockSpec((a_rows * pairs, LANES), lambda d, ref: (0, 0)),
            scratch_shapes=[
                pltpu.VMEM((rows, columns), jnp.float32),
                pltpu.VMEM((a_rows, pairs, d_rows, aux), jnp.bfloat16),
            ],
        ),
        out_shape=jax.ShapeDtypeStruct((a_rows * pairs, LANES), jnp.float32),
        compiler_params=pltpu.CompilerParams(vmem_limit_bytes=40 * 1024 * 1024),
        cost_estimate=pl.CostEstimate(
            flops=2 * pairs * extent * a_rows * aux * (slots * width + GROUP * b_rows),
            bytes_accessed=2 * extent * (pairs * slots * width + b_rows * aux),
            transcendentals=0,
        ),
        name="pair_terms",
    )(lists, *([amps] * slots), *([factors_a] * slots), panel)
    return out[:, :b_rows]


def summed_over_narrow(value):
    size = lax.axis_size("narrow")
    me = lax.axis_index("narrow")
    share = value.shape[2] // size

    def part(owner):
        return lax.dynamic_slice_in_dim(value, owner * share, share, 2)

    parts = [part(me)]
    for k in range(1, size):
        to = [(i, (i + k) % size) for i in range(size)]
        parts.append(lax.ppermute(part((me + k) % size), "narrow", to))
    return sum(parts[1:], parts[0])


def local(factors_a, factors_b, amplitudes, screen):
    pairs, d_extent, virtuals = amplitudes.shape
    width = virtuals // screen.shape[1]
    tiles = lax.axis_size("blk")
    position = lax.axis_index("blk")
    half = d_extent // 2
    quarter = half // 2
    extras = MOST - ROUNDS

    lists = kept_lists(position, screen)
    fullest = lists[MISC * ROW + 1]
    others = lists[MISC * ROW + 2]
    is_first = position % 2 == 0
    is_full = position == fullest
    feeds_one = (position + 1) % tiles == fullest
    feeds_two = (position + 2) % tiles == fullest

    evens, odds = range(0, tiles, 2), range(1, tiles, 2)
    up = [(i, i + 1) for i in evens]
    down = [(i + 1, i) for i in evens]
    around = [(i, (i + 2) % tiles) for i in range(tiles)]

    def run(wrapped, odd, operands):
        lists, factors_a, factors_b, amplitudes = operands
        terms = functools.partial(pair_terms, lists, factors_a, width=width)
        take = functools.partial(take_columns, lists, amplitudes, width=width)

        def ahead(at):
            return (at >= tiles - 2) == wrapped

        def hops(keep):
            return [(at, to) for at, to in around if keep(at)]

        panel_0 = factors_b[:, half : half + quarter]
        panel_1 = factors_b[:, half + quarter :]
        if odd:
            near_l = take(row=NEXT, slots=ROUNDS, start=0, extent=half)
            side_l = send(near_l, up + down)
            after_l = take(row=AFTER, slots=ROUNDS, start=0, extent=half)
            two_l = send(after_l, around)
            near_h = take(row=NEXT, slots=ROUNDS, start=half, extent=half)
            side_h = send(near_h, up + down)
            extra = take(row=MINE, slots=extras, start=0, extent=half)
            second = [at for at in odds if ahead(at)]
            far_0 = send(panel_0, [(to, at) for at, to in around if at in second])
            side_0 = send(panel_0, down)
            extra_two = send(extra, hops(lambda at: at in second))
            extra_one = send(extra, up)
            after_h = take(row=AFTER, slots=ROUNDS, start=half, extent=half)
            two_h = send(after_h, around)
            far_1 = send(panel_1, [(to, at) for at, to in around if at in second])
            side_1 = send(panel_1, down)
            on_l = send(side_l, hops(lambda at: at in evens))
            on_h = send(side_h, hops(lambda at: at in evens))
            one_l = jnp.where(is_first, on_l, side_l)
            one_h = jnp.where(is_first, on_h, side_h)
            out_0 = jnp.where(feeds_one, side_0, far_0)
            out_1 = jnp.where(feeds_one, side_1, far_1)
            extra_ones = [extra_one]
            extra_twos = [extra_two]
        else:
            lead_l = take(row=LEAD, slots=ROUNDS, start=0, extent=half)
            early = hops(lambda at: at in odds or ahead(at))
            late = hops(lambda at: not (at in odds or ahead(at)))
            first = [at for at in evens if ahead(at)]
            second = [at for at in odds if ahead(at)]
            hop_l = send(lead_l, early)
            rest_l = take(row=REST, slots=ROUNDS, start=0, extent=half)
            side_l = send(rest_l, up)
            far_0 = send(panel_0, [(to, at) for at, to in around if at in first])
            extra_0 = take(row=MINE, slots=extras, start=0, extent=quarter)
            cross_0 = send(extra_0, down)
            lead_h = take(row=LEAD, slots=ROUNDS, start=half, extent=half)
            hop_h = send(lead_h, early)
            rest_h = take(row=REST, slots=ROUNDS, start=half, extent=half)
            side_h = send(rest_h, up)
            far_1 = send(panel_1, [(to, at) for at, to in around if at in first])
            extra_1 = take(row=MINE, slots=extras, start=quarter, extent=quarter)
            extra_two_0 = send(extra_0, hops(lambda at: at in first))
            extra_two_1 = send(extra_1, hops(lambda at: at in first or at in second))
            cross_l = send(hop_l, down)
            last_l = send(lead_l, late)
            last_h = send(lead_h, late)
            tail_l = send(rest_l, hops(lambda at: at in odds))
            tail_h = send(rest_h, hops(lambda at: at in odds))
            cross_h = send(hop_h, down)
            extra_one_1 = send(extra_two_1, down)
            extra_one_0 = send(cross_0, hops(lambda at: at in first))
            out_0 = jnp.where(feeds_two, far_0, send(far_0, up))
            out_1 = jnp.where(feeds_two, far_1, send(far_1, up))
            late_first = is_first & ((position < 2) != wrapped)
            two_l = jnp.where(is_first, jnp.where(late_first, last_l, hop_l), tail_l)
            two_h = jnp.where(is_first, jnp.where(late_first, last_h, hop_h), tail_h)
            one_l = jnp.where(is_first, cross_l, side_l)
            one_h = jnp.where(is_first, cross_h, side_h)
            extra_ones = [extra_one_0, extra_one_1]
            extra_twos = [extra_two_0, extra_two_1]

        here = terms(factors_b, amplitudes, row=OWN, slots=MOST, extent=d_extent)
        light = functools.partial(terms, factors_b, row=LIGHT, slots=ROUNDS, extent=half)
        one = light(one_l) + light(one_h, panel_at=half)
        two = light(two_l) + light(two_h, panel_at=half)
        share = half // len(extra_ones)
        mine = functools.partial(terms, factors_b, row=MINE, slots=extras, extent=share)
        for k, moved in enumerate(extra_ones):
            one += mine(moved, panel_at=k * share)
        for k, moved in enumerate(extra_twos):
            two += mine(moved, panel_at=k * share)
        fed = functools.partial(
            terms, amps=amplitudes, row=FED, slots=extras, extent=quarter
        )
        sent = fed(out_0, amp_at=half) + fed(out_1, amp_at=half + quarter)
        one += rotated(jnp.where(feeds_one, sent, 0.0), 1)
        two += rotated(jnp.where(feeds_two, sent, 0.0), 2)

        def add_round(r, running):
            one, two = running

            def only(row, count):
                sub = lax.dynamic_slice_in_dim(lists, row * ROW + r, 1)
                return jnp.concatenate([sub, jnp.zeros(MOST - 1, jnp.int32), count.reshape(1)])

            has = jnp.where((r < lists[OWN * ROW + MOST]) & ~is_full, 1, 0).astype(jnp.int32)
            own = only(OWN, has)
            moved = [
                rotated(
                    take_columns(only(row, has), amplitudes, 0, 1, width, 0, d_extent), by
                )
                for row, by in ((NEXT, 1), (AFTER, 2))
            ]
            one_more, two_more = [
                pair_terms(own, factors_a, factors_b, columns, 0, 1, width, d_extent)
                for columns in moved
            ]
            return one + one_more, two + two_more

        one, two = lax.fori_loop(ROUNDS, jnp.maximum(others, ROUNDS), add_round, (one, two))
        return jnp.stack([here, one, two])

    branches = [
        functools.partial(run, wrapped, odd) for wrapped in (False, True) for odd in (False, True)
    ]
    operands = (lists, factors_a, factors_b, amplitudes)
    terms = lax.switch(lists[MISC * ROW], branches, operands)
    a_rows = factors_a.shape[0]
    terms = terms.reshape(STEPS, a_rows, pairs, -1).swapaxes(1, 2).reshape(STEPS, 1, -1)
    return summed_over_narrow(terms)


def solution(mesh):
    return jax.shard_map(
        local,
        mesh=mesh,
        in_specs=(P(), P("blk", "narrow", None), P("blk", "narrow", None), P()),
        out_specs=P(None, "blk", "narrow"),
        check_vma=False,
    )
```

```python
import functools

import jax
import jax.numpy as jnp
from jax import lax
from jax.experimental import pallas as pl
from jax.experimental.pallas import tpu as pltpu
from jax.sharding import PartitionSpec as P

STEPS = 3
MOST = 8
ROUNDS = 3
GROUP = 16
LANES = 128
ROW = MOST + 1

OWN, LIGHT, LIGHT_0, LIGHT_1, NEXT, AFTER, LEAD, MIXED, MINE, MINE_0, MINE_1, FED, MISC = range(13)
SPLIT = 3


def send(value, pairs):
    return lax.ppermute(value, "blk", pairs)


def rotated(value, by):
    size = lax.axis_size("blk")
    return send(value, [(i, (i + by) % size) for i in range(size)])


def lists_kernel(position_ref, screen_ref, out_ref):
    tiles, subs = screen_ref.shape
    position = position_ref[0]

    def count_of(tile):
        return sum(jnp.where(screen_ref[tile, s] != 0, 1, 0) for s in range(subs))

    def look(tile, found):
        best, fullest, others = found
        count = count_of(tile)
        larger = count > best
        others = jnp.where(larger, best, jnp.maximum(others, count))
        return jnp.where(larger, count, best), jnp.where(larger, tile, fullest), others

    zero = jnp.int32(0)
    best, fullest, others = lax.fori_loop(0, tiles, look, (zero, zero, zero))

    def fill(row, tile, skip, count):
        for k in range(MOST):
            out_ref[row * ROW + k] = 0
        seen = jnp.int32(0)
        for s in range(subs):
            kept = screen_ref[tile, s] != 0

            @pl.when(kept & (seen >= skip))
            def _():
                out_ref[row * ROW + seen - skip] = s

            seen += jnp.where(kept, 1, 0)
        out_ref[row * ROW + MOST] = seen if count is None else count

    following = lax.rem(position + 1, tiles)
    second = lax.rem(position + 2, tiles)
    is_first = lax.rem(position, 2) == 0
    own_count = count_of(position)
    extra = jnp.maximum(best - ROUNDS, 0)
    feeds = (following == fullest) | (second == fullest)
    light = jnp.minimum(own_count, ROUNDS)
    mine = jnp.where(position == fullest, extra, 0)
    fill(OWN, position, 0, own_count)
    fill(LIGHT, position, 0, light)
    fill(LIGHT_0, position, 0, jnp.where(is_first, light, 0))
    fill(LIGHT_1, position, 0, jnp.where(is_first, 0, light))
    fill(NEXT, following, 0, None)
    fill(AFTER, second, 0, None)
    fill(LEAD, jnp.where(is_first, second, following), 0, None)
    fill(MINE, fullest, ROUNDS, mine)
    fill(MINE_0, fullest, ROUNDS, jnp.minimum(mine, SPLIT))
    fill(MINE_1, fullest, ROUNDS + SPLIT, jnp.maximum(mine - SPLIT, 0))
    fill(FED, fullest, ROUNDS, jnp.where(feeds, extra, 0))
    tail = MOST - ROUNDS - SPLIT
    for k in range(ROW):
        other = out_ref[MINE_1 * ROW + k] if k < tail else 0
        if tail <= k < tail + ROUNDS:
            other = out_ref[AFTER * ROW + k - tail]
        out_ref[MIXED * ROW + k] = jnp.where(is_first, out_ref[MINE * ROW + k], other)
    out_ref[MISC * ROW] = jnp.where(fullest < 2, 2, 0) + lax.rem(fullest, 2)
    out_ref[MISC * ROW + 1] = fullest
    out_ref[MISC * ROW + 2] = others
    for k in range(3, ROW):
        out_ref[MISC * ROW + k] = 0


def kept_lists(position, screen):
    return pl.pallas_call(
        lists_kernel,
        in_specs=[pl.BlockSpec(memory_space=pltpu.SMEM)] * 2,
        out_specs=pl.BlockSpec(memory_space=pltpu.SMEM),
        out_shape=jax.ShapeDtypeStruct(((MISC + 1) * ROW,), jnp.int32),
        name="kept_lists",
    )(position.reshape(1), screen)


def take_kernel(lists_ref, source_ref, *refs):
    refs[-1][0] = source_ref[...]


def take_columns(lists, amplitudes, row, slots, width, start, extent, behind=()):
    pairs = amplitudes.shape[0]
    return pl.pallas_call(
        take_kernel,
        grid_spec=pltpu.PrefetchScalarGridSpec(
            num_scalar_prefetch=1,
            grid=(slots,),
            in_specs=[
                pl.BlockSpec(
                    (pairs, extent, width),
                    lambda s, ref: (0, start // extent, ref[row * ROW + s]),
                )
            ]
            + [pl.BlockSpec(memory_space=pl.ANY)] * len(behind),
            out_specs=pl.BlockSpec((1, pairs, extent, width), lambda s, ref: (s, 0, 0, 0)),
        ),
        out_shape=jax.ShapeDtypeStruct((slots, pairs, extent, width), amplitudes.dtype),
        compiler_params=pltpu.CompilerParams(vmem_limit_bytes=16 * 1024 * 1024),
        cost_estimate=pl.CostEstimate(
            flops=0,
            bytes_accessed=4 * slots * pairs * extent * width,
            transcendentals=0,
        ),
        name="take_columns",
    )(lists, amplitudes, *behind)


def tie_kernel(*refs):
    pass


def tied(value, *behind):
    return pl.pallas_call(
        tie_kernel,
        in_specs=[pl.BlockSpec(memory_space=pl.ANY)] * (1 + len(behind)),
        out_specs=pl.BlockSpec(memory_space=pl.ANY),
        out_shape=jax.ShapeDtypeStruct(value.shape, value.dtype),
        input_output_aliases={0: 0},
        name="tied",
    )(value, *behind)


def panel_kernel(source_ref, *refs):
    refs[-1][...] = source_ref[...]


def take_panel(panel, start, extent, rows, behind=()):
    b_rows, _, aux = panel.shape
    return pl.pallas_call(
        panel_kernel,
        grid=(extent // rows,),
        in_specs=[pl.BlockSpec((b_rows, rows, aux), lambda d: (0, start // rows + d, 0))]
        + [pl.BlockSpec(memory_space=pl.ANY)] * len(behind),
        out_specs=pl.BlockSpec((b_rows, rows, aux), lambda d: (0, d, 0)),
        out_shape=jax.ShapeDtypeStruct((b_rows, extent, aux), panel.dtype),
        compiler_params=pltpu.CompilerParams(vmem_limit_bytes=16 * 1024 * 1024),
        cost_estimate=pl.CostEstimate(
            flops=0, bytes_accessed=4 * b_rows * extent * aux, transcendentals=0
        ),
        name="take_panel",
    )(panel, *behind)


def terms_kernel(slots, row, lists_ref, *refs):
    amp_refs = refs[:slots]
    factor_refs = refs[slots : 2 * slots]
    panel_ref, out_ref, total, mixed = refs[2 * slots :]
    count = lists_ref[row * ROW + MOST]
    pairs, d_rows, width = amp_refs[0].shape[-3:]
    a_rows, _, aux = factor_refs[0].shape
    b_rows = panel_ref.shape[0]

    @pl.when(pl.program_id(0) == 0)
    def _():
        total[...] = jnp.zeros_like(total)

    def amp_of(k):
        return amp_refs[k][...].reshape(pairs * d_rows, width)

    for k in range(0, slots, 2):

        @pl.when(k < count)
        def _():
            lhs = amp_of(k)
            if k + 1 < slots:
                lhs = jnp.concatenate([lhs, amp_of(k + 1)], axis=1)
            for a in range(a_rows):
                rhs = factor_refs[k][a]
                if k + 1 < slots:
                    second = factor_refs[k + 1][a]
                    second = jnp.where(k + 1 < count, second, jnp.zeros_like(second))
                    rhs = jnp.concatenate([rhs, second], axis=0)
                product = jnp.dot(lhs, rhs, preferred_element_type=jnp.float32)
                product = product.reshape(pairs, d_rows, aux)
                mixed[a] = product if k == 0 else mixed[a] + product

    @pl.when(count > 0)
    def _():
        partial = total[...]
        for at in range(0, d_rows, GROUP):
            lhs = jnp.concatenate(
                [
                    mixed[a, :, at : at + GROUP, :].astype(jnp.bfloat16).reshape(-1, aux)
                    for a in range(a_rows)
                ],
                axis=0,
            )
            rhs = panel_ref[:, at : at + GROUP, :].reshape(b_rows * GROUP, aux)
            partial += lax.dot_general(
                lhs, rhs, (((1,), (1,)), ((), ())), preferred_element_type=jnp.float32
            )
        total[...] = partial

    @pl.when(pl.program_id(0) == pl.num_programs(0) - 1)
    def _():
        rows, columns = total.shape
        row_d = lax.broadcasted_iota(jnp.int32, (rows, columns), 0) % GROUP
        column_d = lax.broadcasted_iota(jnp.int32, (rows, columns), 1) % GROUP
        kept = jnp.where(row_d == column_d, total[...], 0.0)
        kept = kept.reshape(rows // GROUP, GROUP, columns).sum(axis=1)
        from_b = lax.broadcasted_iota(jnp.int32, (columns, LANES), 0) // GROUP
        to_b = lax.broadcasted_iota(jnp.int32, (columns, LANES), 1)
        gather = jnp.where(from_b == to_b, 1.0, 0.0)
        out_ref[...] = jnp.dot(
            kept, gather, precision=lax.Precision.HIGHEST, preferred_element_type=jnp.float32
        )


def pair_terms(
    lists, factors_a, panel, amps, row, slots, width, extent, amp_at=0, panel_at=0, slot_at=0, d_rows=0
):
    a_rows, _, aux = factors_a.shape
    pairs = amps.shape[-3]
    b_rows = panel.shape[0]
    d_rows = d_rows or extent
    steps = extent // d_rows
    amp_block, panel_block = amp_at // d_rows, panel_at // d_rows
    base = row * ROW

    def step_of(d, ref, k):
        return jnp.where(k < ref[base + MOST], d, 0)

    if amps.ndim == 3:
        amp_specs = [
            pl.BlockSpec(
                (pairs, d_rows, width),
                lambda d, ref, k=k: (0, amp_block + step_of(d, ref, k), ref[base + k]),
            )
            for k in range(slots)
        ]
    else:
        amp_specs = [
            pl.BlockSpec(
                (1, pairs, d_rows, width),
                lambda d, ref, k=k: (slot_at + k, 0, amp_block + step_of(d, ref, k), 0),
            )
            for k in range(slots)
        ]
    factor_specs = [
        pl.BlockSpec((a_rows, width, aux), lambda d, ref, k=k: (0, ref[base + k], 0))
        for k in range(slots)
    ]
    panel_spec = pl.BlockSpec(
        (b_rows, d_rows, aux), lambda d, ref: (0, panel_block + step_of(d, ref, 0), 0)
    )
    rows = a_rows * pairs * GROUP
    columns = b_rows * GROUP
    out = pl.pallas_call(
        functools.partial(terms_kernel, slots, row),
        grid_spec=pltpu.PrefetchScalarGridSpec(
            num_scalar_prefetch=1,
            grid=(steps,),
            in_specs=amp_specs + factor_specs + [panel_spec],
            out_specs=pl.BlockSpec((a_rows * pairs, LANES), lambda d, ref: (0, 0)),
            scratch_shapes=[
                pltpu.VMEM((rows, columns), jnp.float32),
                pltpu.VMEM((a_rows, pairs, d_rows, aux), jnp.float32),
            ],
        ),
        out_shape=jax.ShapeDtypeStruct((a_rows * pairs, LANES), jnp.float32),
        compiler_params=pltpu.CompilerParams(vmem_limit_bytes=40 * 1024 * 1024),
        cost_estimate=pl.CostEstimate(
            flops=2 * pairs * extent * a_rows * aux * (slots * width + GROUP * b_rows),
            bytes_accessed=2 * extent * (pairs * slots * width + b_rows * aux),
            transcendentals=0,
        ),
        name="pair_terms",
    )(lists, *([amps] * slots), *([factors_a] * slots), panel)
    return out[:, :b_rows]


def summed_over_narrow(value):
    size = lax.axis_size("narrow")
    me = lax.axis_index("narrow")
    share = value.shape[2] // size

    def part(owner):
        return lax.dynamic_slice_in_dim(value, owner * share, share, 2)

    parts = [part(me)]
    for k in range(1, size):
        to = [(i, (i + k) % size) for i in range(size)]
        parts.append(lax.ppermute(part((me + k) % size), "narrow", to))
    return sum(parts[1:], parts[0])


def local(factors_a, factors_b, amplitudes, screen):
    pairs, d_extent, virtuals = amplitudes.shape
    width = virtuals // screen.shape[1]
    tiles = lax.axis_size("blk")
    position = lax.axis_index("blk")
    extras = MOST - ROUNDS
    d_rows = min(64, d_extent // 4)

    lists = kept_lists(position, screen)
    fullest = lists[MISC * ROW + 1]
    others = lists[MISC * ROW + 2]
    is_first = position % 2 == 0
    is_full = position == fullest
    feeds_one = (position + 1) % tiles == fullest
    feeds_two = (position + 2) % tiles == fullest

    evens, odds = range(0, tiles, 2), range(1, tiles, 2)
    up = [(i, i + 1) for i in evens]
    down = [(i + 1, i) for i in evens]
    around = [(i, (i + 2) % tiles) for i in range(tiles)]

    def run(wrapped, odd, operands):
        lists, factors_a, factors_b, amplitudes = operands
        terms = functools.partial(pair_terms, lists, factors_a, width=width, d_rows=d_rows)
        take = functools.partial(take_columns, lists, amplitudes, width=width)
        cut = functools.partial(take_panel, factors_b, rows=d_rows)

        def ahead(at):
            return (at >= tiles - 2) == wrapped

        def hops(keep):
            return [(at, to) for at, to in around if keep(at)]

        def backs(keep):
            return [(to, at) for at, to in around if keep(at)]

        def rounds_of(amps, panel_at, row=LIGHT, extent=d_extent, **more):
            return terms(
                factors_b, amps, row=row, slots=ROUNDS, extent=extent, panel_at=panel_at, **more
            )

        here = terms(factors_b, amplitudes, row=OWN, slots=MOST, extent=d_extent)
        if odd:
            given = max(3 * d_extent // 8 // d_rows, 1) * d_rows
            moved = d_extent - given

            def seconds(at):
                return at in odds and ahead(at)

            near = take(row=NEXT, slots=ROUNDS, start=0, extent=d_extent)
            side = send(near, up + down)
            after = take(row=AFTER, slots=ROUNDS, start=0, extent=d_extent)
            got_two = send(after, around)
            far = send(cut(start=moved, extent=given), backs(seconds))
            extra = take(row=MINE, slots=extras, start=0, extent=moved)
            extra_two = send(extra, hops(seconds))
            extra_one = send(extra, up)
            side = tied(side, here)
            on = send(side, hops(lambda at: at in evens))
            beside = send(cut(start=moved, extent=given, behind=[side, got_two]), down)
            got_one = jnp.where(is_first, on, side)
            out = jnp.where(feeds_one, beside, far)

            two = rounds_of(got_two, 0)
            mine = functools.partial(terms, factors_b, row=MINE, slots=extras, extent=moved)
            one = mine(extra_one)
            two += mine(extra_two)
            one += rounds_of(got_one, 0)
            sent = terms(out, amplitudes, row=FED, slots=extras, extent=given, amp_at=moved)
        else:
            half, quarter = d_extent // 2, d_extent // 4

            def firsts(at):
                return at in evens and ahead(at)

            def early(at):
                return at in odds or ahead(at)

            lead = take(row=LEAD, slots=ROUNDS, start=0, extent=d_extent)
            hop = send(lead, hops(early))
            far_0 = send(cut(start=half, extent=quarter), backs(firsts))
            extra = take(row=MINE, slots=SPLIT, start=0, extent=half)
            cross = send(extra, down)
            near = take(row=NEXT, slots=ROUNDS, start=0, extent=d_extent)
            side = send(near, up)
            far_1 = send(cut(start=half + quarter, extent=quarter), backs(firsts))

            far_0 = tied(far_0, here, cross)
            up_0 = send(far_0, up)
            mixed = take(row=MIXED, slots=extras, start=0, extent=half, behind=[far_0])
            got_mixed = send(mixed, hops(early))

            hop = tied(hop, mixed)
            hop_down = send(hop, down)
            late = take(row=LEAD, slots=ROUNDS, start=0, extent=d_extent, behind=[hop, side])
            hop_late = send(late, hops(lambda at: not early(at)))

            far_1 = tied(far_1, late)
            up_1 = send(far_1, up)
            after = take(
                row=AFTER, slots=ROUNDS, start=half, extent=half, behind=[up_0, far_1]
            )
            got_last = send(jnp.where(is_first, cross, after), hops(early))
            extra_down = send(tied(got_mixed[: extras - SPLIT], after, hop_down), down)

            got_one = jnp.where(is_first, hop_down, side)
            came_late = (position < 2) != wrapped
            got_two = jnp.where(came_late, hop_late, hop)
            mine = functools.partial(terms, factors_b, extent=half)
            one = rounds_of(got_one, 0)
            two = rounds_of(got_two, 0, row=LIGHT_0)
            two += mine(got_mixed, row=MINE, slots=extras)
            two += rounds_of(got_mixed, 0, row=LIGHT_1, extent=half, slot_at=extras - SPLIT)
            fed = functools.partial(
                terms, amps=amplitudes, row=FED, slots=extras, extent=quarter
            )
            sent = fed(jnp.where(feeds_two, far_0, up_0), amp_at=half)
            sent += fed(jnp.where(feeds_two, far_1, up_1), amp_at=half + quarter)
            one += mine(got_last, row=MINE_0, slots=SPLIT)
            two += rounds_of(got_last, half, row=LIGHT_1, extent=half)
            one += mine(extra_down, row=MINE_1, slots=extras - SPLIT)
        one += rotated(jnp.where(feeds_one, sent, 0.0), 1)
        two += rotated(jnp.where(feeds_two, sent, 0.0), 2)

        def add_round(r, running):
            one, two = running

            def only(row, count):
                sub = lax.dynamic_slice_in_dim(lists, row * ROW + r, 1)
                return jnp.concatenate([sub, jnp.zeros(MOST - 1, jnp.int32), count.reshape(1)])

            has = jnp.where((r < lists[OWN * ROW + MOST]) & ~is_full, 1, 0).astype(jnp.int32)
            own = only(OWN, has)
            moved = [
                rotated(
                    take_columns(only(row, has), amplitudes, 0, 1, width, 0, d_extent), by
                )
                for row, by in ((NEXT, 1), (AFTER, 2))
            ]
            one_more, two_more = [
                pair_terms(own, factors_a, factors_b, columns, 0, 1, width, d_extent)
                for columns in moved
            ]
            return one + one_more, two + two_more

        one, two = lax.fori_loop(ROUNDS, jnp.maximum(others, ROUNDS), add_round, (one, two))
        return jnp.stack([here, one, two])

    branches = [
        functools.partial(run, wrapped, odd) for wrapped in (False, True) for odd in (False, True)
    ]
    operands = (lists, factors_a, factors_b, amplitudes)
    terms = lax.switch(lists[MISC * ROW], branches, operands)
    a_rows = factors_a.shape[0]
    terms = terms.reshape(STEPS, a_rows, pairs, -1).swapaxes(1, 2).reshape(STEPS, 1, -1)
    return summed_over_narrow(terms)


def solution(mesh):
    return jax.shard_map(
        local,
        mesh=mesh,
        in_specs=(P(), P("blk", "narrow", None), P("blk", "narrow", None), P()),
        out_specs=P(None, "blk", "narrow"),
        check_vma=False,
    )
```

```python
import functools

import jax
import jax.numpy as jnp
from jax import lax
from jax.experimental import pallas as pl
from jax.experimental.pallas import tpu as pltpu
from jax.sharding import PartitionSpec as P

STEPS = 3
MOST = 8
ROUNDS = 3
GROUP = 16
LANES = 128
ROW = MOST + 1

(
    OWN,
    LIGHT,
    LIGHT_0,
    LIGHT_1,
    EARLY,
    LATE,
    NEXT,
    AFTER,
    LEAD,
    MIXED,
    MINE,
    MINE_0,
    MINE_1,
    FED_1,
    FED_2,
    MISC,
) = range(16)
SPLIT = 3


def send(value, pairs):
    return lax.ppermute(value, "blk", pairs)


def rotated(value, by):
    size = lax.axis_size("blk")
    return send(value, [(i, (i + by) % size) for i in range(size)])


def lists_kernel(position_ref, screen_ref, out_ref):
    tiles, subs = screen_ref.shape
    position = position_ref[0]

    def count_of(tile):
        return sum(jnp.where(screen_ref[tile, s] != 0, 1, 0) for s in range(subs))

    def look(tile, found):
        best, fullest, others = found
        count = count_of(tile)
        larger = count > best
        others = jnp.where(larger, best, jnp.maximum(others, count))
        return jnp.where(larger, count, best), jnp.where(larger, tile, fullest), others

    zero = jnp.int32(0)
    best, fullest, others = lax.fori_loop(0, tiles, look, (zero, zero, zero))

    def fill(row, tile, skip, count):
        for k in range(MOST):
            out_ref[row * ROW + k] = 0
        seen = jnp.int32(0)
        for s in range(subs):
            kept = screen_ref[tile, s] != 0

            @pl.when(kept & (seen >= skip))
            def _():
                out_ref[row * ROW + seen - skip] = s

            seen += jnp.where(kept, 1, 0)
        out_ref[row * ROW + MOST] = seen if count is None else count

    following = lax.rem(position + 1, tiles)
    second = lax.rem(position + 2, tiles)
    is_first = lax.rem(position, 2) == 0
    own_count = count_of(position)
    extra = jnp.maximum(best - ROUNDS, 0)
    came_late = (position < 2) != (fullest < 2)
    light = jnp.minimum(own_count, ROUNDS)
    mine = jnp.where(position == fullest, extra, 0)
    fill(OWN, position, 0, own_count)
    fill(LIGHT, position, 0, light)
    fill(LIGHT_0, position, 0, jnp.where(is_first, light, 0))
    fill(LIGHT_1, position, 0, jnp.where(is_first, 0, light))
    fill(EARLY, position, 0, jnp.where(is_first & ~came_late, light, 0))
    fill(LATE, position, 0, jnp.where(is_first & came_late, light, 0))
    fill(NEXT, following, 0, None)
    fill(AFTER, second, 0, None)
    fill(LEAD, jnp.where(is_first, second, following), 0, None)
    fill(MINE, fullest, ROUNDS, mine)
    fill(MINE_0, fullest, ROUNDS, jnp.minimum(mine, SPLIT))
    fill(MINE_1, fullest, ROUNDS + SPLIT, jnp.maximum(mine - SPLIT, 0))
    fill(FED_1, fullest, ROUNDS, jnp.where(following == fullest, extra, 0))
    fill(FED_2, fullest, ROUNDS, jnp.where(second == fullest, extra, 0))
    tail = MOST - ROUNDS - SPLIT
    for k in range(ROW):
        other = out_ref[MINE_1 * ROW + k] if k < tail else 0
        if tail <= k < tail + ROUNDS:
            other = out_ref[AFTER * ROW + k - tail]
        out_ref[MIXED * ROW + k] = jnp.where(is_first, out_ref[MINE * ROW + k], other)
    out_ref[MISC * ROW] = jnp.where(fullest < 2, 2, 0) + lax.rem(fullest, 2)
    out_ref[MISC * ROW + 1] = fullest
    out_ref[MISC * ROW + 2] = others
    for k in range(3, ROW):
        out_ref[MISC * ROW + k] = 0


def kept_lists(position, screen):
    return pl.pallas_call(
        lists_kernel,
        in_specs=[pl.BlockSpec(memory_space=pltpu.SMEM)] * 2,
        out_specs=pl.BlockSpec(memory_space=pltpu.SMEM),
        out_shape=jax.ShapeDtypeStruct(((MISC + 1) * ROW,), jnp.int32),
        name="kept_lists",
    )(position.reshape(1), screen)


def take_kernel(lists_ref, source_ref, *refs):
    refs[-1][0] = source_ref[...]


def take_columns(lists, amplitudes, row, slots, width, start, extent, behind=()):
    pairs = amplitudes.shape[0]
    return pl.pallas_call(
        take_kernel,
        grid_spec=pltpu.PrefetchScalarGridSpec(
            num_scalar_prefetch=1,
            grid=(slots,),
            in_specs=[
                pl.BlockSpec(
                    (pairs, extent, width),
                    lambda s, ref: (0, start // extent, ref[row * ROW + s]),
                )
            ]
            + [pl.BlockSpec(memory_space=pl.ANY)] * len(behind),
            out_specs=pl.BlockSpec((1, pairs, extent, width), lambda s, ref: (s, 0, 0, 0)),
        ),
        out_shape=jax.ShapeDtypeStruct((slots, pairs, extent, width), amplitudes.dtype),
        compiler_params=pltpu.CompilerParams(vmem_limit_bytes=16 * 1024 * 1024),
        cost_estimate=pl.CostEstimate(
            flops=0,
            bytes_accessed=4 * slots * pairs * extent * width,
            transcendentals=0,
        ),
        name="take_columns",
    )(lists, amplitudes, *behind)


def tie_kernel(*refs):
    pass


def tied(value, *behind):
    return pl.pallas_call(
        tie_kernel,
        in_specs=[pl.BlockSpec(memory_space=pl.ANY)] * (1 + len(behind)),
        out_specs=pl.BlockSpec(memory_space=pl.ANY),
        out_shape=jax.ShapeDtypeStruct(value.shape, value.dtype),
        input_output_aliases={0: 0},
        name="tied",
    )(value, *behind)


def panel_kernel(source_ref, *refs):
    refs[-1][...] = source_ref[...]


def take_panel(panel, start, extent, rows, behind=()):
    b_rows, _, aux = panel.shape
    return pl.pallas_call(
        panel_kernel,
        grid=(extent // rows,),
        in_specs=[pl.BlockSpec((b_rows, rows, aux), lambda d: (0, start // rows + d, 0))]
        + [pl.BlockSpec(memory_space=pl.ANY)] * len(behind),
        out_specs=pl.BlockSpec((b_rows, rows, aux), lambda d: (0, d, 0)),
        out_shape=jax.ShapeDtypeStruct((b_rows, extent, aux), panel.dtype),
        compiler_params=pltpu.CompilerParams(vmem_limit_bytes=16 * 1024 * 1024),
        cost_estimate=pl.CostEstimate(
            flops=0, bytes_accessed=4 * b_rows * extent * aux, transcendentals=0
        ),
        name="take_panel",
    )(panel, *behind)


class Segment:
    def __init__(self, into, row, slots, amps, panel, extent, amp_at=0, panel_at=0, slot_at=0):
        self.into, self.row, self.slots = into, row, slots
        self.amps, self.panel, self.extent = amps, panel, extent
        self.amp_at, self.panel_at, self.slot_at = amp_at, panel_at, slot_at


def terms_kernel(segments, places, d_rows, lists_ref, *refs):
    arrays = refs[: -8]
    out_ref, amp_buf, panel_buf, factor_buf, mixed, total, sems, factor_sems = refs[-8:]
    factors = arrays[0]
    outs = out_ref.shape[0]
    _, most, pairs, _, width = amp_buf.shape
    b_rows = panel_buf.shape[1]
    _, _, a_rows, _, aux = factor_buf.shape

    counts = [lists_ref[seg.row * ROW + MOST] for seg in segments]
    starts, orders = [], []
    begin = order = jnp.int32(0)
    for seg, count in zip(segments, counts):
        starts.append(begin)
        orders.append(order)
        begin = begin + jnp.where(count > 0, seg.extent // d_rows, 0)
        order = order + jnp.where(count > 0, 1, 0)
    items = begin

    def pick(at, values):
        found = values[0]
        for s in range(1, len(segments)):
            found = jnp.where(at == s, values[s], found)
        return found

    def locate(t):
        at = jnp.int32(0)
        for s in range(len(segments)):
            at = jnp.where((counts[s] > 0) & (t >= starts[s]), s, at)
        return at, t - pick(at, starts), lax.rem(pick(at, orders), 2)

    def copies(t, act):
        at, block, turn = locate(t)
        slot = lax.rem(t, 2)
        for s, seg in enumerate(segments):
            amps, panel = arrays[places[s][0]], arrays[places[s][1]]

            @pl.when(at == s)
            def _():
                amp_d = pl.ds(pl.multiple_of(seg.amp_at + block * d_rows, d_rows), d_rows)
                panel_d = pl.ds(pl.multiple_of(seg.panel_at + block * d_rows, d_rows), d_rows)
                act(pltpu.make_async_copy(
                    panel.at[:, panel_d, :], panel_buf.at[slot], sems.at[slot, most]
                ))
                for k in range(seg.slots):

                    @pl.when(k < counts[s])
                    def _():
                        sub = pl.multiple_of(lists_ref[seg.row * ROW + k] * width, width)
                        columns = pl.ds(sub, width)
                        if len(amps.shape) == 3:
                            source = amps.at[:, amp_d, columns]
                        else:
                            source = amps.at[seg.slot_at + k, :, amp_d, :]
                        act(pltpu.make_async_copy(source, amp_buf.at[slot, k], sems.at[slot, k]))

                        @pl.when(block == 0)
                        def _():
                            act(pltpu.make_async_copy(
                                factors.at[:, columns, :],
                                factor_buf.at[turn, k],
                                factor_sems.at[turn, k],
                            ))

    total[...] = jnp.zeros_like(total)

    @pl.when(items > 0)
    def _():
        copies(0, lambda copy: copy.start())

    def step(t, carry):
        @pl.when(t + 1 < items)
        def _():
            copies(t + 1, lambda copy: copy.start())

        copies(t, lambda copy: copy.wait())
        at, _, turn = locate(t)
        slot = lax.rem(t, 2)
        count = pick(at, counts)
        into = pick(at, [seg.into for seg in segments])

        def couple(c, carry):
            k = 2 * c
            other = jnp.minimum(k + 1, most - 1)
            whole = k + 1 < count
            second = amp_buf[slot, other]
            second = jnp.where(whole, second, jnp.zeros_like(second))
            lhs = jnp.concatenate(
                [
                    amp_buf[slot, k].reshape(pairs * d_rows, width),
                    second.reshape(pairs * d_rows, width),
                ],
                axis=1,
            )
            for a in range(a_rows):
                lower = factor_buf[turn, other, a]
                lower = jnp.where(whole, lower, jnp.zeros_like(lower))
                rhs = jnp.concatenate([factor_buf[turn, k, a], lower], axis=0)
                product = jnp.dot(lhs, rhs, preferred_element_type=jnp.float32)
                product = product.reshape(pairs, d_rows, aux)
                mixed[a] = product + jnp.where(c > 0, mixed[a], 0.0)
            return carry

        lax.fori_loop(0, (count + 1) // 2, couple, 0)

        partial = total[into]
        for g in range(0, d_rows, GROUP):
            lhs = jnp.concatenate(
                [
                    mixed[a, :, g : g + GROUP, :].astype(jnp.bfloat16).reshape(-1, aux)
                    for a in range(a_rows)
                ],
                axis=0,
            )
            rhs = panel_buf[slot, :, g : g + GROUP, :].reshape(b_rows * GROUP, aux)
            partial += lax.dot_general(
                lhs, rhs, (((1,), (1,)), ((), ())), preferred_element_type=jnp.float32
            )
        total[into] = partial
        return carry

    lax.fori_loop(0, items, step, 0)

    def finish(o, carry):
        _, rows, columns = total.shape
        row_d = lax.broadcasted_iota(jnp.int32, (rows, columns), 0) % GROUP
        column_d = lax.broadcasted_iota(jnp.int32, (rows, columns), 1) % GROUP
        kept = jnp.where(row_d == column_d, total[o], 0.0)
        kept = kept.reshape(rows // GROUP, GROUP, columns).sum(axis=1)
        from_b = lax.broadcasted_iota(jnp.int32, (columns, LANES), 0) // GROUP
        to_b = lax.broadcasted_iota(jnp.int32, (columns, LANES), 1)
        gather = jnp.where(from_b == to_b, 1.0, 0.0)
        out_ref[o] = jnp.dot(
            kept, gather, precision=lax.Precision.HIGHEST, preferred_element_type=jnp.float32
        )
        return carry

    lax.fori_loop(0, outs, finish, 0)


def pair_terms(lists, factors_a, segments, outs, width, d_rows):
    arrays, places = [factors_a], []
    for seg in segments:
        place = []
        for array in (seg.amps, seg.panel):
            known = [n for n, other in enumerate(arrays) if other is array]
            place.append(known[0] if known else len(arrays))
            if not known:
                arrays.append(array)
        places.append(place)
    a_rows, _, aux = factors_a.shape
    pairs = segments[0].amps.shape[-3]
    b_rows = segments[0].panel.shape[0]
    most = max(2, *(seg.slots for seg in segments))
    flops = sum(
        2 * pairs * seg.extent * a_rows * aux * (seg.slots * width + GROUP * b_rows)
        for seg in segments
    )
    out = pl.pallas_call(
        functools.partial(terms_kernel, segments, places, d_rows),
        in_specs=[pl.BlockSpec(memory_space=pltpu.SMEM)]
        + [pl.BlockSpec(memory_space=pl.ANY)] * len(arrays),
        out_specs=pl.BlockSpec(memory_space=pltpu.VMEM),
        scratch_shapes=[
            pltpu.VMEM((2, most, pairs, d_rows, width), jnp.bfloat16),
            pltpu.VMEM((2, b_rows, d_rows, aux), jnp.bfloat16),
            pltpu.VMEM((2, most, a_rows, width, aux), jnp.bfloat16),
            pltpu.VMEM((a_rows, pairs, d_rows, aux), jnp.float32),
            pltpu.VMEM((outs, a_rows * pairs * GROUP, b_rows * GROUP), jnp.float32),
            pltpu.SemaphoreType.DMA((2, most + 1)),
            pltpu.SemaphoreType.DMA((2, most)),
        ],
        out_shape=jax.ShapeDtypeStruct((outs, a_rows * pairs, LANES), jnp.float32),
        compiler_params=pltpu.CompilerParams(vmem_limit_bytes=32 * 1024 * 1024),
        cost_estimate=pl.CostEstimate(
            flops=flops, bytes_accessed=flops // 512, transcendentals=0
        ),
        name="pair_terms",
    )(lists, *arrays)
    return out[:, :, :b_rows]


def summed_over_narrow(value):
    size = lax.axis_size("narrow")
    me = lax.axis_index("narrow")
    share = value.shape[2] // size

    def part(owner):
        return lax.dynamic_slice_in_dim(value, owner * share, share, 2)

    parts = [part(me)]
    for k in range(1, size):
        to = [(i, (i + k) % size) for i in range(size)]
        parts.append(lax.ppermute(part((me + k) % size), "narrow", to))
    return sum(parts[1:], parts[0])


def local(factors_a, factors_b, amplitudes, screen):
    pairs, d_extent, virtuals = amplitudes.shape
    width = virtuals // screen.shape[1]
    tiles = lax.axis_size("blk")
    position = lax.axis_index("blk")
    extras = MOST - ROUNDS
    d_rows = min(64, d_extent // 4)

    lists = kept_lists(position, screen)
    fullest = lists[MISC * ROW + 1]
    others = lists[MISC * ROW + 2]
    is_first = position % 2 == 0
    is_full = position == fullest
    feeds_one = (position + 1) % tiles == fullest
    feeds_two = (position + 2) % tiles == fullest

    evens, odds = range(0, tiles, 2), range(1, tiles, 2)
    up = [(i, i + 1) for i in evens]
    down = [(i + 1, i) for i in evens]
    around = [(i, (i + 2) % tiles) for i in range(tiles)]

    def run(wrapped, odd, operands):
        lists, factors_a, factors_b, amplitudes = operands
        terms = functools.partial(pair_terms, lists, factors_a, width=width, d_rows=d_rows)
        columns_of = functools.partial(Segment, panel=factors_b)
        given_to = functools.partial(Segment, amps=amplitudes, slots=extras)
        take = functools.partial(take_columns, lists, amplitudes, width=width)
        cut = functools.partial(take_panel, factors_b, rows=d_rows)

        def ahead(at):
            return (at >= tiles - 2) == wrapped

        def hops(keep):
            return [(at, to) for at, to in around if keep(at)]

        def backs(keep):
            return [(to, at) for at, to in around if keep(at)]

        here = terms(
            [columns_of(0, row=OWN, slots=MOST, amps=amplitudes, extent=d_extent)], 1
        )
        if odd:
            given = max(3 * d_extent // 8 // d_rows, 1) * d_rows
            moved = d_extent - given

            def seconds(at):
                return at in odds and ahead(at)

            near = take(row=NEXT, slots=ROUNDS, start=0, extent=d_extent)
            side = send(near, up + down)
            after = take(row=AFTER, slots=ROUNDS, start=0, extent=d_extent)
            got_two = send(after, around)
            far = send(cut(start=moved, extent=given), backs(seconds))
            extra = take(row=MINE, slots=extras, start=0, extent=moved)
            extra_two = send(extra, hops(seconds))
            extra_one = send(extra, up)
            side = tied(side, here)
            on = send(side, hops(lambda at: at in evens))
            beside = send(cut(start=moved, extent=given, behind=[side, got_two]), down)

            first = terms(
                [
                    columns_of(1, row=LIGHT, slots=ROUNDS, amps=got_two, extent=d_extent),
                    columns_of(0, row=LIGHT_1, slots=ROUNDS, amps=side, extent=d_extent),
                ],
                2,
            )
            then = terms(
                [
                    columns_of(0, row=MINE, slots=extras, amps=extra_one, extent=moved),
                    columns_of(1, row=MINE, slots=extras, amps=extra_two, extent=moved),
                ],
                2,
            )
            sent = terms(
                [
                    given_to(0, row=FED_1, panel=beside, extent=given, amp_at=moved),
                    given_to(0, row=FED_2, panel=far, extent=given, amp_at=moved),
                ],
                1,
            )[0]
            last = terms(
                [columns_of(0, row=LIGHT_0, slots=ROUNDS, amps=on, extent=d_extent)], 1
            )
            one = first[0] + then[0] + last[0]
            two = first[1] + then[1]
        else:
            half, quarter = d_extent // 2, d_extent // 4

            def firsts(at):
                return at in evens and ahead(at)

            def early(at):
                return at in odds or ahead(at)

            lead = take(row=LEAD, slots=ROUNDS, start=0, extent=d_extent)
            hop = send(lead, hops(early))
            far_0 = send(cut(start=half, extent=quarter), backs(firsts))
            extra = take(row=MINE, slots=SPLIT, start=0, extent=half)
            cross = send(extra, down)
            near = take(row=NEXT, slots=ROUNDS, start=0, extent=d_extent)
            side = send(near, up)
            far_1 = send(cut(start=half + quarter, extent=quarter), backs(firsts))

            far_0 = tied(far_0, here, cross)
            up_0 = send(far_0, up)
            mixed = take(row=MIXED, slots=extras, start=0, extent=half, behind=[far_0])
            got_mixed = send(mixed, hops(early))

            hop = tied(hop, mixed)
            hop_down = send(hop, down)
            late = take(row=LEAD, slots=ROUNDS, start=0, extent=d_extent, behind=[hop, side])
            hop_late = send(late, hops(lambda at: not early(at)))

            far_1 = tied(far_1, late)
            up_1 = send(far_1, up)
            after = take(
                row=AFTER, slots=ROUNDS, start=half, extent=half, behind=[up_0, far_1]
            )
            got_last = send(jnp.where(is_first, cross, after), hops(early))
            extra_down = send(tied(got_mixed[: extras - SPLIT], after, hop_down), down)

            first = terms(
                [
                    columns_of(0, row=LIGHT_1, slots=ROUNDS, amps=side, extent=d_extent),
                    columns_of(1, row=EARLY, slots=ROUNDS, amps=hop, extent=d_extent),
                ],
                2,
            )
            then = terms(
                [
                    given_to(0, row=FED_1, panel=up_0, extent=quarter, amp_at=half),
                    given_to(0, row=FED_2, panel=far_0, extent=quarter, amp_at=half),
                    given_to(
                        0, row=FED_2, panel=far_1, extent=quarter, amp_at=half + quarter
                    ),
                    columns_of(1, row=MINE, slots=extras, amps=got_mixed, extent=half),
                    columns_of(
                        1,
                        row=LIGHT_1,
                        slots=ROUNDS,
                        amps=got_mixed,
                        extent=half,
                        slot_at=extras - SPLIT,
                    ),
                ],
                2,
            )
            sent = terms(
                [given_to(0, row=FED_1, panel=up_1, extent=quarter, amp_at=half + quarter)], 1
            )[0]
            sent += then[0]
            low = terms(
                [columns_of(0, row=LIGHT_0, slots=ROUNDS, amps=hop_down, extent=d_extent)], 1
            )
            last = terms(
                [
                    columns_of(0, row=MINE_0, slots=SPLIT, amps=got_last, extent=half),
                    columns_of(
                        0, row=MINE_1, slots=extras - SPLIT, amps=extra_down, extent=half
                    ),
                    columns_of(
                        1, row=LIGHT_1, slots=ROUNDS, amps=got_last, extent=half, panel_at=half
                    ),
                    columns_of(1, row=LATE, slots=ROUNDS, amps=hop_late, extent=d_extent),
                ],
                2,
            )
            one = first[0] + low[0] + last[0]
            two = first[1] + then[1] + last[1]
        one += rotated(jnp.where(feeds_one, sent, 0.0), 1)
        two += rotated(jnp.where(feeds_two, sent, 0.0), 2)

        def add_round(r, running):
            one, two = running

            def only(row, count):
                sub = lax.dynamic_slice_in_dim(lists, row * ROW + r, 1)
                return jnp.concatenate([sub, jnp.zeros(MOST - 1, jnp.int32), count.reshape(1)])

            has = jnp.where((r < lists[OWN * ROW + MOST]) & ~is_full, 1, 0).astype(jnp.int32)
            own = only(OWN, has)
            moved = [
                rotated(
                    take_columns(only(row, has), amplitudes, 0, 1, width, 0, d_extent), by
                )
                for row, by in ((NEXT, 1), (AFTER, 2))
            ]
            more = pair_terms(
                own,
                factors_a,
                [
                    columns_of(into, row=0, slots=1, amps=columns, extent=d_extent)
                    for into, columns in enumerate(moved)
                ],
                2,
                width,
                d_rows,
            )
            return one + more[0], two + more[1]

        one, two = lax.fori_loop(ROUNDS, jnp.maximum(others, ROUNDS), add_round, (one, two))
        return jnp.stack([here[0], one, two])

    branches = [
        functools.partial(run, wrapped, odd) for wrapped in (False, True) for odd in (False, True)
    ]
    operands = (lists, factors_a, factors_b, amplitudes)
    terms = lax.switch(lists[MISC * ROW], branches, operands)
    a_rows = factors_a.shape[0]
    terms = terms.reshape(STEPS, a_rows, pairs, -1).swapaxes(1, 2).reshape(STEPS, 1, -1)
    return summed_over_narrow(terms)


def solution(mesh):
    return jax.shard_map(
        local,
        mesh=mesh,
        in_specs=(P(), P("blk", "narrow", None), P("blk", "narrow", None), P()),
        out_specs=P(None, "blk", "narrow"),
        check_vma=False,
    )
```

```python
import functools

import jax
import jax.numpy as jnp
from jax import lax
from jax.experimental import pallas as pl
from jax.experimental.pallas import tpu as pltpu
from jax.sharding import PartitionSpec as P

STEPS = 3
MOST = 8
ROUNDS = 3
GROUP = 16
LANES = 128
ROW = MOST + 1

(
    OWN,
    LIGHT,
    LIGHT_0,
    LIGHT_1,
    EARLY,
    LATE,
    NEXT,
    AFTER,
    LEAD,
    MIXED,
    MINE,
    MINE_0,
    MINE_1,
    FED_1,
    FED_2,
    MISC,
) = range(16)
SPLIT = 3


def send(value, pairs):
    return lax.ppermute(value, "blk", pairs)


def rotated(value, by):
    size = lax.axis_size("blk")
    return send(value, [(i, (i + by) % size) for i in range(size)])


def lists_kernel(position_ref, screen_ref, out_ref):
    tiles, subs = screen_ref.shape
    position = position_ref[0]

    def count_of(tile):
        return sum(jnp.where(screen_ref[tile, s] != 0, 1, 0) for s in range(subs))

    def look(tile, found):
        best, fullest, others = found
        count = count_of(tile)
        larger = count > best
        others = jnp.where(larger, best, jnp.maximum(others, count))
        return jnp.where(larger, count, best), jnp.where(larger, tile, fullest), others

    zero = jnp.int32(0)
    best, fullest, others = lax.fori_loop(0, tiles, look, (zero, zero, zero))

    def fill(row, tile, skip, count):
        for k in range(MOST):
            out_ref[row * ROW + k] = 0
        seen = jnp.int32(0)
        for s in range(subs):
            kept = screen_ref[tile, s] != 0

            @pl.when(kept & (seen >= skip))
            def _():
                out_ref[row * ROW + seen - skip] = s

            seen += jnp.where(kept, 1, 0)
        out_ref[row * ROW + MOST] = seen if count is None else count

    following = lax.rem(position + 1, tiles)
    second = lax.rem(position + 2, tiles)
    is_first = lax.rem(position, 2) == 0
    own_count = count_of(position)
    extra = jnp.maximum(best - ROUNDS, 0)
    came_late = (position < 2) != (fullest < 2)
    light = jnp.minimum(own_count, ROUNDS)
    mine = jnp.where(position == fullest, extra, 0)
    fill(OWN, position, 0, own_count)
    fill(LIGHT, position, 0, light)
    fill(LIGHT_0, position, 0, jnp.where(is_first, light, 0))
    fill(LIGHT_1, position, 0, jnp.where(is_first, 0, light))
    fill(EARLY, position, 0, jnp.where(is_first & ~came_late, light, 0))
    fill(LATE, position, 0, jnp.where(is_first & came_late, light, 0))
    fill(NEXT, following, 0, None)
    fill(AFTER, second, 0, None)
    fill(LEAD, jnp.where(is_first, second, following), 0, None)
    fill(MINE, fullest, ROUNDS, mine)
    fill(MINE_0, fullest, ROUNDS, jnp.minimum(mine, SPLIT))
    fill(MINE_1, fullest, ROUNDS + SPLIT, jnp.maximum(mine - SPLIT, 0))
    fill(FED_1, fullest, ROUNDS, jnp.where(following == fullest, extra, 0))
    fill(FED_2, fullest, ROUNDS, jnp.where(second == fullest, extra, 0))
    tail = MOST - ROUNDS - SPLIT
    for k in range(ROW):
        other = out_ref[MINE_1 * ROW + k] if k < tail else 0
        if tail <= k < tail + ROUNDS:
            other = out_ref[AFTER * ROW + k - tail]
        out_ref[MIXED * ROW + k] = jnp.where(is_first, out_ref[MINE * ROW + k], other)
    out_ref[MISC * ROW] = jnp.where(fullest < 2, 2, 0) + lax.rem(fullest, 2)
    out_ref[MISC * ROW + 1] = fullest
    out_ref[MISC * ROW + 2] = others
    for k in range(3, ROW):
        out_ref[MISC * ROW + k] = 0


def kept_lists(position, screen):
    return pl.pallas_call(
        lists_kernel,
        in_specs=[pl.BlockSpec(memory_space=pltpu.SMEM)] * 2,
        out_specs=pl.BlockSpec(memory_space=pltpu.SMEM),
        out_shape=jax.ShapeDtypeStruct(((MISC + 1) * ROW,), jnp.int32),
        name="kept_lists",
    )(position.reshape(1), screen)


def take_kernel(lists_ref, source_ref, *refs):
    refs[-1][0] = source_ref[...]


def take_columns(lists, amplitudes, row, slots, width, start, extent, behind=()):
    pairs = amplitudes.shape[0]
    return pl.pallas_call(
        take_kernel,
        grid_spec=pltpu.PrefetchScalarGridSpec(
            num_scalar_prefetch=1,
            grid=(slots,),
            in_specs=[
                pl.BlockSpec(
                    (pairs, extent, width),
                    lambda s, ref: (0, start // extent, ref[row * ROW + s]),
                )
            ]
            + [pl.BlockSpec(memory_space=pl.ANY)] * len(behind),
            out_specs=pl.BlockSpec((1, pairs, extent, width), lambda s, ref: (s, 0, 0, 0)),
        ),
        out_shape=jax.ShapeDtypeStruct((slots, pairs, extent, width), amplitudes.dtype),
        compiler_params=pltpu.CompilerParams(vmem_limit_bytes=16 * 1024 * 1024),
        cost_estimate=pl.CostEstimate(
            flops=0,
            bytes_accessed=4 * slots * pairs * extent * width,
            transcendentals=0,
        ),
        name="take_columns",
    )(lists, amplitudes, *behind)


def tie_kernel(*refs):
    pass


def tied(value, *behind):
    return pl.pallas_call(
        tie_kernel,
        in_specs=[pl.BlockSpec(memory_space=pl.ANY)] * (1 + len(behind)),
        out_specs=pl.BlockSpec(memory_space=pl.ANY),
        out_shape=jax.ShapeDtypeStruct(value.shape, value.dtype),
        input_output_aliases={0: 0},
        name="tied",
    )(value, *behind)


def panel_kernel(source_ref, *refs):
    refs[-1][...] = source_ref[...]


def take_panel(panel, start, extent, rows, behind=()):
    b_rows, _, aux = panel.shape
    return pl.pallas_call(
        panel_kernel,
        grid=(extent // rows,),
        in_specs=[pl.BlockSpec((b_rows, rows, aux), lambda d: (0, start // rows + d, 0))]
        + [pl.BlockSpec(memory_space=pl.ANY)] * len(behind),
        out_specs=pl.BlockSpec((b_rows, rows, aux), lambda d: (0, d, 0)),
        out_shape=jax.ShapeDtypeStruct((b_rows, extent, aux), panel.dtype),
        compiler_params=pltpu.CompilerParams(vmem_limit_bytes=16 * 1024 * 1024),
        cost_estimate=pl.CostEstimate(
            flops=0, bytes_accessed=4 * b_rows * extent * aux, transcendentals=0
        ),
        name="take_panel",
    )(panel, *behind)


class Segment:
    def __init__(self, into, row, slots, amps, panel, extent, amp_at=0, panel_at=0, slot_at=0):
        self.into, self.row, self.slots = into, row, slots
        self.amps, self.panel, self.extent = amps, panel, extent
        self.amp_at, self.panel_at, self.slot_at = amp_at, panel_at, slot_at


def terms_kernel(segments, places, d_rows, lists_ref, *refs):
    arrays = refs[: -8]
    out_ref, amp_buf, panel_buf, factor_buf, mixed, total, sems, factor_sems = refs[-8:]
    factors = arrays[0]
    outs = out_ref.shape[0]
    _, most, pairs, _, width = amp_buf.shape
    b_rows = panel_buf.shape[1]
    _, _, a_rows, _, aux = factor_buf.shape

    counts = [lists_ref[seg.row * ROW + MOST] for seg in segments]
    starts, orders = [], []
    begin = order = jnp.int32(0)
    for seg, count in zip(segments, counts):
        starts.append(begin)
        orders.append(order)
        begin = begin + jnp.where(count > 0, seg.extent // d_rows, 0)
        order = order + jnp.where(count > 0, 1, 0)
    items = begin

    def pick(at, values):
        found = values[0]
        for s in range(1, len(segments)):
            found = jnp.where(at == s, values[s], found)
        return found

    def locate(t):
        at = jnp.int32(0)
        for s in range(len(segments)):
            at = jnp.where((counts[s] > 0) & (t >= starts[s]), s, at)
        return at, t - pick(at, starts), lax.rem(pick(at, orders), 2)

    def fetch(t):
        at, block, turn = locate(t)
        slot = lax.rem(t, 2)
        for s, seg in enumerate(segments):
            amps, panel = arrays[places[s][0]], arrays[places[s][1]]

            @pl.when(at == s)
            def _():
                amp_d = pl.ds(pl.multiple_of(seg.amp_at + block * d_rows, d_rows), d_rows)
                panel_d = pl.ds(pl.multiple_of(seg.panel_at + block * d_rows, d_rows), d_rows)
                pltpu.make_async_copy(
                    panel.at[:, panel_d, :], panel_buf.at[slot], sems.at[slot, most]
                ).start()

                def one(k, carry):
                    sub = pl.multiple_of(lists_ref[seg.row * ROW + k] * width, width)
                    columns = pl.ds(sub, width)
                    if len(amps.shape) == 3:
                        source = amps.at[:, amp_d, columns]
                    else:
                        source = amps.at[seg.slot_at + k, :, amp_d, :]
                    pltpu.make_async_copy(
                        source, amp_buf.at[slot, k], sems.at[slot, k]
                    ).start()

                    @pl.when(block == 0)
                    def _():
                        pltpu.make_async_copy(
                            factors.at[:, columns, :],
                            factor_buf.at[turn, k],
                            factor_sems.at[turn, k],
                        ).start()

                    return carry

                lax.fori_loop(0, counts[s], one, 0)

    def arrive(slot, block, turn, count):
        pltpu.make_async_copy(
            panel_buf.at[slot], panel_buf.at[slot], sems.at[slot, most]
        ).wait()

        def one(k, carry):
            pltpu.make_async_copy(
                amp_buf.at[slot, k], amp_buf.at[slot, k], sems.at[slot, k]
            ).wait()

            @pl.when(block == 0)
            def _():
                pltpu.make_async_copy(
                    factor_buf.at[turn, k], factor_buf.at[turn, k], factor_sems.at[turn, k]
                ).wait()

            return carry

        lax.fori_loop(0, count, one, 0)

    total[...] = jnp.zeros_like(total)

    def mix(couples, slot, turn, count):
        slots = min(2 * couples, most)
        whole = slots - 1 < count
        columns = [amp_buf[slot, k].reshape(pairs * d_rows, width) for k in range(slots)]
        columns[-1] = jnp.where(whole, columns[-1], jnp.zeros_like(columns[-1]))
        lhs = jnp.concatenate(columns, axis=1)
        for a in range(a_rows):
            rows = [factor_buf[turn, k, a] for k in range(slots)]
            rows[-1] = jnp.where(whole, rows[-1], jnp.zeros_like(rows[-1]))
            product = jnp.dot(
                lhs, jnp.concatenate(rows, axis=0), preferred_element_type=jnp.float32
            )
            mixed[a] = product.astype(mixed.dtype).reshape(pairs, d_rows, aux)

    def step(n, carry):
        @pl.when(n < items)
        def _():
            fetch(n)

        @pl.when(n > 0)
        def _():
            t = n - 1
            at, block, turn = locate(t)
            slot = lax.rem(t, 2)
            count = pick(at, counts)
            into = pick(at, [seg.into for seg in segments])
            arrive(slot, block, turn, count)
            for couples in range(1, (most + 1) // 2 + 1):

                @pl.when((count + 1) // 2 == couples)
                def _():
                    mix(couples, slot, turn, count)

            partial = total[into]
            for g in range(0, d_rows, GROUP):
                lhs = jnp.concatenate(
                    [mixed[a, :, g : g + GROUP, :].reshape(-1, aux) for a in range(a_rows)],
                    axis=0,
                )
                rhs = panel_buf[slot, :, g : g + GROUP, :].reshape(b_rows * GROUP, aux)
                partial += lax.dot_general(
                    lhs, rhs, (((1,), (1,)), ((), ())), preferred_element_type=jnp.float32
                )
            total[into] = partial

        return carry

    lax.fori_loop(0, jnp.where(items > 0, items + 1, 0), step, 0)

    def finish(o, carry):
        _, rows, columns = total.shape
        row_d = lax.broadcasted_iota(jnp.int32, (rows, columns), 0) % GROUP
        column_d = lax.broadcasted_iota(jnp.int32, (rows, columns), 1) % GROUP
        kept = jnp.where(row_d == column_d, total[o], 0.0)
        kept = kept.reshape(rows // GROUP, GROUP, columns).sum(axis=1)
        from_b = lax.broadcasted_iota(jnp.int32, (columns, LANES), 0) // GROUP
        to_b = lax.broadcasted_iota(jnp.int32, (columns, LANES), 1)
        gather = jnp.where(from_b == to_b, 1.0, 0.0)
        out_ref[o] = jnp.dot(
            kept, gather, precision=lax.Precision.HIGHEST, preferred_element_type=jnp.float32
        )
        return carry

    lax.fori_loop(0, outs, finish, 0)


def pair_terms(lists, factors_a, segments, outs, width, d_rows):
    arrays, places = [factors_a], []
    for seg in segments:
        place = []
        for array in (seg.amps, seg.panel):
            known = [n for n, other in enumerate(arrays) if other is array]
            place.append(known[0] if known else len(arrays))
            if not known:
                arrays.append(array)
        places.append(place)
    a_rows, _, aux = factors_a.shape
    pairs = segments[0].amps.shape[-3]
    b_rows = segments[0].panel.shape[0]
    most = max(2, *(seg.slots for seg in segments))
    flops = sum(
        2 * pairs * seg.extent * a_rows * aux * (seg.slots * width + GROUP * b_rows)
        for seg in segments
    )
    out = pl.pallas_call(
        functools.partial(terms_kernel, segments, places, d_rows),
        in_specs=[pl.BlockSpec(memory_space=pltpu.SMEM)]
        + [pl.BlockSpec(memory_space=pl.ANY)] * len(arrays),
        out_specs=pl.BlockSpec(memory_space=pltpu.VMEM),
        scratch_shapes=[
            pltpu.VMEM((2, most, pairs, d_rows, width), jnp.bfloat16),
            pltpu.VMEM((2, b_rows, d_rows, aux), jnp.bfloat16),
            pltpu.VMEM((2, most, a_rows, width, aux), jnp.bfloat16),
            pltpu.VMEM((a_rows, pairs, d_rows, aux), jnp.bfloat16),
            pltpu.VMEM((outs, a_rows * pairs * GROUP, b_rows * GROUP), jnp.float32),
            pltpu.SemaphoreType.DMA((2, most + 1)),
            pltpu.SemaphoreType.DMA((2, most)),
        ],
        out_shape=jax.ShapeDtypeStruct((outs, a_rows * pairs, LANES), jnp.float32),
        compiler_params=pltpu.CompilerParams(vmem_limit_bytes=32 * 1024 * 1024),
        cost_estimate=pl.CostEstimate(
            flops=flops, bytes_accessed=flops // 512, transcendentals=0
        ),
        name="pair_terms",
    )(lists, *arrays)
    return out[:, :, :b_rows]


def summed_over_narrow(value):
    size = lax.axis_size("narrow")
    me = lax.axis_index("narrow")
    share = value.shape[2] // size

    def part(owner):
        return lax.dynamic_slice_in_dim(value, owner * share, share, 2)

    parts = [part(me)]
    for k in range(1, size):
        to = [(i, (i + k) % size) for i in range(size)]
        parts.append(lax.ppermute(part((me + k) % size), "narrow", to))
    return sum(parts[1:], parts[0])


def local(factors_a, factors_b, amplitudes, screen):
    pairs, d_extent, virtuals = amplitudes.shape
    width = virtuals // screen.shape[1]
    tiles = lax.axis_size("blk")
    position = lax.axis_index("blk")
    extras = MOST - ROUNDS
    d_rows = min(64, d_extent // 4)

    lists = kept_lists(position, screen)
    fullest = lists[MISC * ROW + 1]
    others = lists[MISC * ROW + 2]
    is_first = position % 2 == 0
    is_full = position == fullest
    feeds_one = (position + 1) % tiles == fullest
    feeds_two = (position + 2) % tiles == fullest

    evens, odds = range(0, tiles, 2), range(1, tiles, 2)
    up = [(i, i + 1) for i in evens]
    down = [(i + 1, i) for i in evens]
    around = [(i, (i + 2) % tiles) for i in range(tiles)]

    def run(wrapped, odd, operands):
        lists, factors_a, factors_b, amplitudes = operands
        terms = functools.partial(pair_terms, lists, factors_a, width=width, d_rows=d_rows)
        columns_of = functools.partial(Segment, panel=factors_b)
        given_to = functools.partial(Segment, amps=amplitudes, slots=extras)
        take = functools.partial(take_columns, lists, amplitudes, width=width)
        cut = functools.partial(take_panel, factors_b, rows=d_rows)

        def ahead(at):
            return (at >= tiles - 2) == wrapped

        def hops(keep):
            return [(at, to) for at, to in around if keep(at)]

        def backs(keep):
            return [(to, at) for at, to in around if keep(at)]

        here = terms(
            [columns_of(0, row=OWN, slots=MOST, amps=amplitudes, extent=d_extent)], 1
        )
        if odd:
            given = max(3 * d_extent // 8 // d_rows, 1) * d_rows
            moved = d_extent - given

            def seconds(at):
                return at in odds and ahead(at)

            half = d_extent // 2
            near_l = take(row=NEXT, slots=ROUNDS, start=0, extent=half)
            side_l = send(near_l, up + down)
            near_h = take(row=NEXT, slots=ROUNDS, start=half, extent=half)
            side_h = send(near_h, up + down)
            after = take(row=AFTER, slots=ROUNDS, start=0, extent=d_extent)
            got_two = send(after, around)
            far = send(cut(start=moved, extent=given), backs(seconds))

            side_l = tied(side_l, here)
            on_l = send(side_l, hops(lambda at: at in evens))
            beside = send(cut(start=moved, extent=given, behind=[side_l]), down)
            extra = take(
                row=MINE, slots=extras, start=0, extent=moved, behind=[side_h, got_two]
            )
            extra_two = send(extra, hops(seconds))
            extra_one = send(extra, up)
            side_h = tied(side_h, on_l)
            on_h = send(side_h, hops(lambda at: at in evens))

            first = terms(
                [
                    columns_of(1, row=LIGHT, slots=ROUNDS, amps=got_two, extent=d_extent),
                    columns_of(0, row=LIGHT_1, slots=ROUNDS, amps=side_l, extent=half),
                    columns_of(
                        0, row=LIGHT_1, slots=ROUNDS, amps=side_h, extent=half, panel_at=half
                    ),
                ],
                2,
            )
            early = terms(
                [columns_of(0, row=LIGHT_0, slots=ROUNDS, amps=on_l, extent=half)], 1
            )
            sent = terms(
                [
                    given_to(0, row=FED_1, panel=beside, extent=given, amp_at=moved),
                    given_to(0, row=FED_2, panel=far, extent=given, amp_at=moved),
                ],
                1,
            )[0]
            last = terms(
                [
                    columns_of(
                        0, row=LIGHT_0, slots=ROUNDS, amps=on_h, extent=half, panel_at=half
                    ),
                    columns_of(0, row=MINE, slots=extras, amps=extra_one, extent=moved),
                    columns_of(1, row=MINE, slots=extras, amps=extra_two, extent=moved),
                ],
                2,
            )
            one = first[0] + early[0] + last[0]
            two = first[1] + last[1]
        else:
            half, quarter = d_extent // 2, d_extent // 4

            def firsts(at):
                return at in evens and ahead(at)

            def early(at):
                return at in odds or ahead(at)

            lead = take(row=LEAD, slots=ROUNDS, start=0, extent=d_extent)
            hop = send(lead, hops(early))
            far_0 = send(cut(start=half, extent=quarter), backs(firsts))
            extra = take(row=MINE, slots=SPLIT, start=0, extent=half)
            cross = send(extra, down)
            near = take(row=NEXT, slots=ROUNDS, start=0, extent=d_extent)
            side = send(near, up)
            far_1 = send(cut(start=half + quarter, extent=quarter), backs(firsts))

            far_0 = tied(far_0, here, cross)
            up_0 = send(far_0, up)
            mixed = take(row=MIXED, slots=extras, start=0, extent=half, behind=[far_0])
            got_mixed = send(mixed, hops(early))

            hop = tied(hop, mixed)
            hop_down = send(hop, down)
            late = take(row=LEAD, slots=ROUNDS, start=0, extent=d_extent, behind=[hop, side])
            hop_late = send(late, hops(lambda at: not early(at)))

            far_1 = tied(far_1, late)
            up_1 = send(far_1, up)
            after = take(
                row=AFTER, slots=ROUNDS, start=half, extent=half, behind=[up_0, far_1]
            )
            got_last = send(jnp.where(is_first, cross, after), hops(early))
            extra_down = send(tied(got_mixed[: extras - SPLIT], after, hop_down), down)

            first = terms(
                [
                    columns_of(0, row=LIGHT_1, slots=ROUNDS, amps=side, extent=d_extent),
                    columns_of(1, row=EARLY, slots=ROUNDS, amps=hop, extent=d_extent),
                ],
                2,
            )
            then = terms(
                [
                    given_to(0, row=FED_1, panel=up_0, extent=quarter, amp_at=half),
                    given_to(0, row=FED_2, panel=far_0, extent=quarter, amp_at=half),
                    given_to(
                        0, row=FED_2, panel=far_1, extent=quarter, amp_at=half + quarter
                    ),
                    columns_of(1, row=MINE, slots=extras, amps=got_mixed, extent=half),
                    columns_of(
                        1,
                        row=LIGHT_1,
                        slots=ROUNDS,
                        amps=got_mixed,
                        extent=half,
                        slot_at=extras - SPLIT,
                    ),
                ],
                2,
            )
            sent = terms(
                [given_to(0, row=FED_1, panel=up_1, extent=quarter, amp_at=half + quarter)], 1
            )[0]
            sent += then[0]
            low = terms(
                [columns_of(0, row=LIGHT_0, slots=ROUNDS, amps=hop_down, extent=d_extent)], 1
            )
            last = terms(
                [
                    columns_of(0, row=MINE_0, slots=SPLIT, amps=got_last, extent=half),
                    columns_of(
                        0, row=MINE_1, slots=extras - SPLIT, amps=extra_down, extent=half
                    ),
                    columns_of(
                        1, row=LIGHT_1, slots=ROUNDS, amps=got_last, extent=half, panel_at=half
                    ),
                    columns_of(1, row=LATE, slots=ROUNDS, amps=hop_late, extent=d_extent),
                ],
                2,
            )
            one = first[0] + low[0] + last[0]
            two = first[1] + then[1] + last[1]
        one += rotated(jnp.where(feeds_one, sent, 0.0), 1)
        two += rotated(jnp.where(feeds_two, sent, 0.0), 2)

        def add_round(r, running):
            one, two = running

            def only(row, count):
                sub = lax.dynamic_slice_in_dim(lists, row * ROW + r, 1)
                return jnp.concatenate([sub, jnp.zeros(MOST - 1, jnp.int32), count.reshape(1)])

            has = jnp.where((r < lists[OWN * ROW + MOST]) & ~is_full, 1, 0).astype(jnp.int32)
            own = only(OWN, has)
            moved = [
                rotated(
                    take_columns(only(row, has), amplitudes, 0, 1, width, 0, d_extent), by
                )
                for row, by in ((NEXT, 1), (AFTER, 2))
            ]
            more = pair_terms(
                own,
                factors_a,
                [
                    columns_of(into, row=0, slots=1, amps=columns, extent=d_extent)
                    for into, columns in enumerate(moved)
                ],
                2,
                width,
                d_rows,
            )
            return one + more[0], two + more[1]

        one, two = lax.fori_loop(ROUNDS, jnp.maximum(others, ROUNDS), add_round, (one, two))
        return jnp.stack([here[0], one, two])

    branches = [
        functools.partial(run, wrapped, odd) for wrapped in (False, True) for odd in (False, True)
    ]
    operands = (lists, factors_a, factors_b, amplitudes)
    terms = lax.switch(lists[MISC * ROW], branches, operands)
    a_rows = factors_a.shape[0]
    terms = terms.reshape(STEPS, a_rows, pairs, -1).swapaxes(1, 2).reshape(STEPS, 1, -1)
    return summed_over_narrow(terms)


def solution(mesh):
    return jax.shard_map(
        local,
        mesh=mesh,
        in_specs=(P(), P("blk", "narrow", None), P("blk", "narrow", None), P()),
        out_specs=P(None, "blk", "narrow"),
        check_vma=False,
    )
```

```python
import functools

import jax
import jax.numpy as jnp
from jax import lax
from jax.experimental import pallas as pl
from jax.experimental.pallas import tpu as pltpu
from jax.sharding import PartitionSpec as P

STEPS = 3
MOST = 8
ROUNDS = 3
GROUP = 16
LANES = 128
ROW = MOST + 1

(
    OWN,
    LIGHT,
    LIGHT_0,
    LIGHT_1,
    NEXT,
    AFTER,
    LEAD,
    PART,
    MINE,
    FED_1,
    FED_2,
    MISC,
) = range(12)
AHEAD = 4


def send(value, pairs):
    return lax.ppermute(value, "blk", pairs)


def rotated(value, by):
    size = lax.axis_size("blk")
    return send(value, [(i, (i + by) % size) for i in range(size)])


def lists_kernel(position_ref, screen_ref, out_ref):
    tiles, subs = screen_ref.shape
    position = position_ref[0]

    def count_of(tile):
        return sum(jnp.where(screen_ref[tile, s] != 0, 1, 0) for s in range(subs))

    def look(tile, found):
        best, fullest, others = found
        count = count_of(tile)
        larger = count > best
        others = jnp.where(larger, best, jnp.maximum(others, count))
        return jnp.where(larger, count, best), jnp.where(larger, tile, fullest), others

    zero = jnp.int32(0)
    best, fullest, others = lax.fori_loop(0, tiles, look, (zero, zero, zero))

    def fill(row, tile, skip, count):
        for k in range(MOST):
            out_ref[row * ROW + k] = 0
        seen = jnp.int32(0)
        for s in range(subs):
            kept = screen_ref[tile, s] != 0

            @pl.when(kept & (seen >= skip))
            def _():
                out_ref[row * ROW + seen - skip] = s

            seen += jnp.where(kept, 1, 0)
        out_ref[row * ROW + MOST] = seen if count is None else count

    following = lax.rem(position + 1, tiles)
    second = lax.rem(position + 2, tiles)
    is_first = lax.rem(position, 2) == 0
    own_count = count_of(position)
    extra = jnp.maximum(best - ROUNDS, 0)
    light = jnp.minimum(own_count, ROUNDS)
    fill(OWN, position, 0, own_count)
    fill(LIGHT, position, 0, light)
    fill(LIGHT_0, position, 0, jnp.where(is_first, light, 0))
    fill(LIGHT_1, position, 0, jnp.where(is_first, 0, light))
    fill(NEXT, following, 0, None)
    fill(AFTER, second, 0, None)
    fill(MINE, fullest, ROUNDS, jnp.where(position == fullest, extra, 0))
    fill(FED_1, fullest, ROUNDS, jnp.where(following == fullest, extra, 0))
    fill(FED_2, fullest, ROUNDS, jnp.where(second == fullest, extra, 0))
    for k in range(ROW):
        other = out_ref[NEXT * ROW + k % ROUNDS] if k < 2 * ROUNDS else 0
        out_ref[LEAD * ROW + k] = jnp.where(is_first, out_ref[MINE * ROW + k], other)
        out_ref[PART * ROW + k] = jnp.where(is_first, 0, k // ROUNDS)
    out_ref[MISC * ROW] = jnp.where(fullest < 2, 2, 0) + lax.rem(fullest, 2)
    out_ref[MISC * ROW + 1] = fullest
    out_ref[MISC * ROW + 2] = others
    for k in range(3, ROW):
        out_ref[MISC * ROW + k] = 0


def kept_lists(position, screen):
    return pl.pallas_call(
        lists_kernel,
        in_specs=[pl.BlockSpec(memory_space=pltpu.SMEM)] * 2,
        out_specs=pl.BlockSpec(memory_space=pltpu.SMEM),
        out_shape=jax.ShapeDtypeStruct(((MISC + 1) * ROW,), jnp.int32),
        name="kept_lists",
    )(position.reshape(1), screen)


def take_kernel(lists_ref, source_ref, *refs):
    refs[-1][0] = source_ref[...]


def take_columns(lists, amplitudes, row, slots, width, start, extent, behind=(), part=None):
    pairs = amplitudes.shape[0]

    def block_of(s, ref):
        first = start // extent + (0 if part is None else ref[part * ROW + s])
        return 0, first, ref[row * ROW + s]

    return pl.pallas_call(
        take_kernel,
        grid_spec=pltpu.PrefetchScalarGridSpec(
            num_scalar_prefetch=1,
            grid=(slots,),
            in_specs=[pl.BlockSpec((pairs, extent, width), block_of)]
            + [pl.BlockSpec(memory_space=pl.ANY)] * len(behind),
            out_specs=pl.BlockSpec((1, pairs, extent, width), lambda s, ref: (s, 0, 0, 0)),
        ),
        out_shape=jax.ShapeDtypeStruct((slots, pairs, extent, width), amplitudes.dtype),
        compiler_params=pltpu.CompilerParams(vmem_limit_bytes=16 * 1024 * 1024),
        cost_estimate=pl.CostEstimate(
            flops=0,
            bytes_accessed=4 * slots * pairs * extent * width,
            transcendentals=0,
        ),
        name="take_columns",
    )(lists, amplitudes, *behind)


def tie_kernel(*refs):
    pass


def tied(value, *behind):
    return pl.pallas_call(
        tie_kernel,
        in_specs=[pl.BlockSpec(memory_space=pl.ANY)] * (1 + len(behind)),
        out_specs=pl.BlockSpec(memory_space=pl.ANY),
        out_shape=jax.ShapeDtypeStruct(value.shape, value.dtype),
        input_output_aliases={0: 0},
        name="tied",
    )(value, *behind)


def panel_kernel(source_ref, *refs):
    refs[-1][...] = source_ref[...]


def take_panel(panel, start, extent, rows, behind=()):
    b_rows, _, aux = panel.shape
    return pl.pallas_call(
        panel_kernel,
        grid=(extent // rows,),
        in_specs=[pl.BlockSpec((b_rows, rows, aux), lambda d: (0, start // rows + d, 0))]
        + [pl.BlockSpec(memory_space=pl.ANY)] * len(behind),
        out_specs=pl.BlockSpec((b_rows, rows, aux), lambda d: (0, d, 0)),
        out_shape=jax.ShapeDtypeStruct((b_rows, extent, aux), panel.dtype),
        compiler_params=pltpu.CompilerParams(vmem_limit_bytes=16 * 1024 * 1024),
        cost_estimate=pl.CostEstimate(
            flops=0, bytes_accessed=4 * b_rows * extent * aux, transcendentals=0
        ),
        name="take_panel",
    )(panel, *behind)


class Segment:
    def __init__(self, into, row, slots, amps, panel, extent, amp_at=0, panel_at=0, slot_at=0):
        self.into, self.row, self.slots = into, row, slots
        self.amps, self.panel, self.extent = amps, panel, extent
        self.amp_at, self.panel_at, self.slot_at = amp_at, panel_at, slot_at


def terms_kernel(segments, places, d_rows, lists_ref, *refs):
    arrays = refs[: -8]
    out_ref, amp_buf, panel_buf, factor_buf, mixed, total, sems, factor_sems = refs[-8:]
    factors = arrays[0]
    outs = out_ref.shape[0]
    _, most, pairs, _, width = amp_buf.shape
    b_rows = panel_buf.shape[1]
    _, _, a_rows, _, aux = factor_buf.shape

    counts = [lists_ref[seg.row * ROW + MOST] for seg in segments]
    starts, orders = [], []
    begin = order = jnp.int32(0)
    for seg, count in zip(segments, counts):
        starts.append(begin)
        orders.append(order)
        begin = begin + jnp.where(count > 0, seg.extent // d_rows, 0)
        order = order + jnp.where(count > 0, 1, 0)
    items = begin

    def pick(at, values):
        found = values[0]
        for s in range(1, len(segments)):
            found = jnp.where(at == s, values[s], found)
        return found

    def locate(t):
        at = jnp.int32(0)
        for s in range(len(segments)):
            at = jnp.where((counts[s] > 0) & (t >= starts[s]), s, at)
        return at, t - pick(at, starts), lax.rem(pick(at, orders), AHEAD)

    def fetch(t):
        at, block, turn = locate(t)
        slot = lax.rem(t, AHEAD)
        for s, seg in enumerate(segments):
            amps, panel = arrays[places[s][0]], arrays[places[s][1]]

            @pl.when(at == s)
            def _():
                amp_d = pl.ds(pl.multiple_of(seg.amp_at + block * d_rows, d_rows), d_rows)
                panel_d = pl.ds(pl.multiple_of(seg.panel_at + block * d_rows, d_rows), d_rows)
                pltpu.make_async_copy(
                    panel.at[:, panel_d, :], panel_buf.at[slot], sems.at[slot, most]
                ).start()

                def one(k, carry):
                    sub = pl.multiple_of(lists_ref[seg.row * ROW + k] * width, width)
                    columns = pl.ds(sub, width)
                    if len(amps.shape) == 3:
                        source = amps.at[:, amp_d, columns]
                    else:
                        source = amps.at[seg.slot_at + k, :, amp_d, :]
                    pltpu.make_async_copy(
                        source, amp_buf.at[slot, k], sems.at[slot, k]
                    ).start()

                    @pl.when(block == 0)
                    def _():
                        pltpu.make_async_copy(
                            factors.at[:, columns, :],
                            factor_buf.at[turn, k],
                            factor_sems.at[turn, k],
                        ).start()

                    return carry

                lax.fori_loop(0, counts[s], one, 0)

    def arrive(slot, block, turn, count):
        pltpu.make_async_copy(
            panel_buf.at[slot], panel_buf.at[slot], sems.at[slot, most]
        ).wait()

        def one(k, carry):
            pltpu.make_async_copy(
                amp_buf.at[slot, k], amp_buf.at[slot, k], sems.at[slot, k]
            ).wait()

            @pl.when(block == 0)
            def _():
                pltpu.make_async_copy(
                    factor_buf.at[turn, k], factor_buf.at[turn, k], factor_sems.at[turn, k]
                ).wait()

            return carry

        lax.fori_loop(0, count, one, 0)

    total[...] = jnp.zeros_like(total)

    def mix(couples, slot, turn, count):
        slots = min(2 * couples, most)
        whole = slots - 1 < count
        columns = [amp_buf[slot, k].reshape(pairs * d_rows, width) for k in range(slots)]
        columns[-1] = jnp.where(whole, columns[-1], jnp.zeros_like(columns[-1]))
        lhs = jnp.concatenate(columns, axis=1)
        for a in range(a_rows):
            rows = [factor_buf[turn, k, a] for k in range(slots)]
            rows[-1] = jnp.where(whole, rows[-1], jnp.zeros_like(rows[-1]))
            product = jnp.dot(
                lhs, jnp.concatenate(rows, axis=0), preferred_element_type=jnp.float32
            )
            mixed[a] = product.astype(mixed.dtype).reshape(pairs, d_rows, aux)

    def step(n, carry):
        @pl.when(n < items)
        def _():
            fetch(n)

        @pl.when(n >= AHEAD - 1)
        def _():
            t = n - (AHEAD - 1)
            at, block, turn = locate(t)
            slot = lax.rem(t, AHEAD)
            count = pick(at, counts)
            into = pick(at, [seg.into for seg in segments])
            arrive(slot, block, turn, count)
            for couples in range(1, (most + 1) // 2 + 1):

                @pl.when((count + 1) // 2 == couples)
                def _():
                    mix(couples, slot, turn, count)

            partial = total[into]
            for g in range(0, d_rows, GROUP):
                lhs = jnp.concatenate(
                    [mixed[a, :, g : g + GROUP, :].reshape(-1, aux) for a in range(a_rows)],
                    axis=0,
                )
                rhs = panel_buf[slot, :, g : g + GROUP, :].reshape(b_rows * GROUP, aux)
                partial += lax.dot_general(
                    lhs, rhs, (((1,), (1,)), ((), ())), preferred_element_type=jnp.float32
                )
            total[into] = partial

        return carry

    lax.fori_loop(0, jnp.where(items > 0, items + AHEAD - 1, 0), step, 0)

    def finish(o, carry):
        _, rows, columns = total.shape
        row_d = lax.broadcasted_iota(jnp.int32, (rows, columns), 0) % GROUP
        column_d = lax.broadcasted_iota(jnp.int32, (rows, columns), 1) % GROUP
        kept = jnp.where(row_d == column_d, total[o], 0.0)
        kept = kept.reshape(rows // GROUP, GROUP, columns).sum(axis=1)
        from_b = lax.broadcasted_iota(jnp.int32, (columns, LANES), 0) // GROUP
        to_b = lax.broadcasted_iota(jnp.int32, (columns, LANES), 1)
        gather = jnp.where(from_b == to_b, 1.0, 0.0)
        out_ref[o] = jnp.dot(
            kept, gather, precision=lax.Precision.HIGHEST, preferred_element_type=jnp.float32
        )
        return carry

    lax.fori_loop(0, outs, finish, 0)


def pair_terms(lists, factors_a, segments, outs, width, d_rows):
    arrays, places = [factors_a], []
    for seg in segments:
        place = []
        for array in (seg.amps, seg.panel):
            known = [n for n, other in enumerate(arrays) if other is array]
            place.append(known[0] if known else len(arrays))
            if not known:
                arrays.append(array)
        places.append(place)
    a_rows, _, aux = factors_a.shape
    pairs = segments[0].amps.shape[-3]
    b_rows = segments[0].panel.shape[0]
    most = max(2, *(seg.slots for seg in segments))
    flops = sum(
        2 * pairs * seg.extent * a_rows * aux * (seg.slots * width + GROUP * b_rows)
        for seg in segments
    )
    out = pl.pallas_call(
        functools.partial(terms_kernel, segments, places, d_rows),
        in_specs=[pl.BlockSpec(memory_space=pltpu.SMEM)]
        + [pl.BlockSpec(memory_space=pl.ANY)] * len(arrays),
        out_specs=pl.BlockSpec(memory_space=pltpu.VMEM),
        scratch_shapes=[
            pltpu.VMEM((AHEAD, most, pairs, d_rows, width), jnp.bfloat16),
            pltpu.VMEM((AHEAD, b_rows, d_rows, aux), jnp.bfloat16),
            pltpu.VMEM((AHEAD, most, a_rows, width, aux), jnp.bfloat16),
            pltpu.VMEM((a_rows, pairs, d_rows, aux), jnp.bfloat16),
            pltpu.VMEM((outs, a_rows * pairs * GROUP, b_rows * GROUP), jnp.float32),
            pltpu.SemaphoreType.DMA((AHEAD, most + 1)),
            pltpu.SemaphoreType.DMA((AHEAD, most)),
        ],
        out_shape=jax.ShapeDtypeStruct((outs, a_rows * pairs, LANES), jnp.float32),
        compiler_params=pltpu.CompilerParams(vmem_limit_bytes=32 * 1024 * 1024),
        cost_estimate=pl.CostEstimate(
            flops=flops, bytes_accessed=flops // 512, transcendentals=0
        ),
        name="pair_terms",
    )(lists, *arrays)
    return out[:, :, :b_rows]


def summed_over_narrow(value):
    size = lax.axis_size("narrow")
    me = lax.axis_index("narrow")
    share = value.shape[2] // size

    def part(owner):
        return lax.dynamic_slice_in_dim(value, owner * share, share, 2)

    parts = [part(me)]
    for k in range(1, size):
        to = [(i, (i + k) % size) for i in range(size)]
        parts.append(lax.ppermute(part((me + k) % size), "narrow", to))
    return sum(parts[1:], parts[0])


def local(factors_a, factors_b, amplitudes, screen):
    pairs, d_extent, virtuals = amplitudes.shape
    width = virtuals // screen.shape[1]
    tiles = lax.axis_size("blk")
    position = lax.axis_index("blk")
    extras = MOST - ROUNDS
    d_rows = min(64, d_extent // 4)

    lists = kept_lists(position, screen)
    fullest = lists[MISC * ROW + 1]
    others = lists[MISC * ROW + 2]
    is_first = position % 2 == 0
    is_full = position == fullest
    feeds_one = (position + 1) % tiles == fullest
    feeds_two = (position + 2) % tiles == fullest

    evens, odds = range(0, tiles, 2), range(1, tiles, 2)
    up = [(i, i + 1) for i in evens]
    down = [(i + 1, i) for i in evens]
    around = [(i, (i + 2) % tiles) for i in range(tiles)]

    def run(wrapped, odd, operands):
        lists, factors_a, factors_b, amplitudes = operands
        terms = functools.partial(pair_terms, lists, factors_a, width=width, d_rows=d_rows)
        columns_of = functools.partial(Segment, panel=factors_b)
        given_to = functools.partial(Segment, amps=amplitudes, slots=extras)
        take = functools.partial(take_columns, lists, amplitudes, width=width)
        cut = functools.partial(take_panel, factors_b, rows=d_rows)

        def ahead(at):
            return (at >= tiles - 2) == wrapped

        def hops(keep):
            return [(at, to) for at, to in around if keep(at)]

        def backs(keep):
            return [(to, at) for at, to in around if keep(at)]

        here = terms(
            [columns_of(0, row=OWN, slots=MOST, amps=amplitudes, extent=d_extent)], 1
        )
        half, quarter = d_extent // 2, d_extent // 4
        after = functools.partial(take, row=AFTER, slots=ROUNDS, extent=half)
        if odd:
            given = max(3 * d_extent // 8 // d_rows, 1) * d_rows
            moved = d_extent - given

            def seconds(at):
                return at in odds and ahead(at)

            near_l = take(row=NEXT, slots=ROUNDS, start=0, extent=half)
            side_l = send(near_l, up + down)
            near_h = take(row=NEXT, slots=ROUNDS, start=half, extent=half)
            side_h = send(near_h, up + down)
            direct = take(row=AFTER, slots=ROUNDS, start=0, extent=d_extent)
            got_direct = send(direct, hops(lambda at: at in evens))
            extra = take(row=MINE, slots=extras, start=0, extent=moved)
            extra_two = send(extra, hops(seconds))
            far = send(cut(start=moved, extent=given), backs(seconds))

            side_l = tied(side_l, here)
            on_l = send(jnp.where(is_first, side_l, after(start=0)), around)
            beside = send(cut(start=moved, extent=given, behind=[side_l]), down)
            extra = take(row=MINE, slots=extras, start=0, extent=moved, behind=[side_l])
            extra = tied(extra, got_direct, extra_two, far, side_h)
            extra_one = send(extra, up)
            on_h = send(jnp.where(is_first, side_h, after(start=half)), around)

            first = terms(
                [
                    columns_of(1, row=LIGHT_0, slots=ROUNDS, amps=got_direct, extent=d_extent),
                    columns_of(0, row=LIGHT_1, slots=ROUNDS, amps=side_l, extent=half),
                    columns_of(
                        0, row=LIGHT_1, slots=ROUNDS, amps=side_h, extent=half, panel_at=half
                    ),
                    columns_of(1, row=MINE, slots=extras, amps=extra_two, extent=moved),
                ],
                2,
            )
            then = terms(
                [
                    columns_of(0, row=LIGHT_0, slots=ROUNDS, amps=on_l, extent=half),
                    columns_of(1, row=LIGHT_1, slots=ROUNDS, amps=on_l, extent=half),
                ],
                2,
            )
            sent = terms(
                [
                    given_to(0, row=FED_1, panel=beside, extent=given, amp_at=moved),
                    given_to(0, row=FED_2, panel=far, extent=given, amp_at=moved),
                ],
                1,
            )[0]
            last = terms(
                [
                    columns_of(
                        0, row=LIGHT_0, slots=ROUNDS, amps=on_h, extent=half, panel_at=half
                    ),
                    columns_of(
                        1, row=LIGHT_1, slots=ROUNDS, amps=on_h, extent=half, panel_at=half
                    ),
                    columns_of(0, row=MINE, slots=extras, amps=extra_one, extent=moved),
                ],
                2,
            )
            one = first[0] + then[0] + last[0]
            two = first[1] + then[1] + last[1]
        else:
            def firsts(at):
                return at in evens and ahead(at)

            lead = take(row=LEAD, part=PART, slots=2 * ROUNDS, start=0, extent=half)
            got_lead = send(lead, hops(lambda at: at in odds or ahead(at)))
            far_0 = send(cut(start=half, extent=quarter), backs(firsts))
            extra_0 = take(row=MINE, slots=extras, start=0, extent=quarter)
            cross = send(extra_0, down)
            near = take(row=NEXT, slots=ROUNDS, start=0, extent=d_extent)
            side = send(near, up)
            far_1 = send(cut(start=half + quarter, extent=quarter), backs(firsts))

            extra_1 = take(row=MINE, slots=extras, start=quarter, extent=quarter)
            cross = tied(cross, here)
            got_extra = send(jnp.where(is_first, cross, extra_1), hops(ahead))
            far_0 = tied(far_0, here, cross)
            up_0 = send(far_0, up)
            lead_down = send(got_lead, down)
            after_l = after(start=0, behind=[got_lead, side])
            got_l = send(after_l, around)
            far_1 = tied(far_1, after_l)
            up_1 = send(far_1, up)
            after_h = after(start=half, behind=[far_1, got_extra])
            got_h = send(after_h, around)
            extra_down = send(tied(got_extra, after_h), down)

            first = terms(
                [
                    columns_of(0, row=LIGHT_1, slots=ROUNDS, amps=side, extent=d_extent),
                    columns_of(1, row=MINE, slots=extras, amps=got_lead, extent=half),
                ],
                2,
            )
            fed = functools.partial(given_to, 0, extent=quarter)
            then = terms(
                [
                    fed(row=FED_1, panel=up_0, amp_at=half),
                    fed(row=FED_2, panel=far_0, amp_at=half),
                    fed(row=FED_2, panel=far_1, amp_at=half + quarter),
                    columns_of(1, row=MINE, slots=extras, amps=got_extra, extent=quarter),
                    columns_of(2, row=LIGHT, slots=ROUNDS, amps=got_l, extent=half),
                ],
                3,
            )
            low = terms(
                [
                    columns_of(0, row=LIGHT_0, slots=ROUNDS, amps=lead_down, extent=half),
                    columns_of(
                        0,
                        row=LIGHT_0,
                        slots=ROUNDS,
                        amps=lead_down,
                        extent=half,
                        panel_at=half,
                        slot_at=ROUNDS,
                    ),
                ],
                1,
            )
            sent = then[0]
            sent += terms([fed(row=FED_1, panel=up_1, amp_at=half + quarter)], 1)[0]
            last = terms(
                [
                    columns_of(
                        1, row=LIGHT, slots=ROUNDS, amps=got_h, extent=half, panel_at=half
                    ),
                    columns_of(
                        0,
                        row=MINE,
                        slots=extras,
                        amps=extra_down,
                        extent=quarter,
                        panel_at=quarter,
                    ),
                ],
                2,
            )
            one = first[0] + then[1] + low[0] + last[0]
            two = first[1] + then[2] + last[1]
        one += rotated(jnp.where(feeds_one, sent, 0.0), 1)
        two += rotated(jnp.where(feeds_two, sent, 0.0), 2)

        def add_round(r, running):
            one, two = running

            def only(row, count):
                sub = lax.dynamic_slice_in_dim(lists, row * ROW + r, 1)
                return jnp.concatenate([sub, jnp.zeros(MOST - 1, jnp.int32), count.reshape(1)])

            has = jnp.where((r < lists[OWN * ROW + MOST]) & ~is_full, 1, 0).astype(jnp.int32)
            own = only(OWN, has)
            moved = [
                rotated(
                    take_columns(only(row, has), amplitudes, 0, 1, width, 0, d_extent), by
                )
                for row, by in ((NEXT, 1), (AFTER, 2))
            ]
            more = pair_terms(
                own,
                factors_a,
                [
                    columns_of(into, row=0, slots=1, amps=columns, extent=d_extent)
                    for into, columns in enumerate(moved)
                ],
                2,
                width,
                d_rows,
            )
            return one + more[0], two + more[1]

        one, two = lax.fori_loop(ROUNDS, jnp.maximum(others, ROUNDS), add_round, (one, two))
        return jnp.stack([here[0], one, two])

    branches = [
        functools.partial(run, wrapped, odd) for wrapped in (False, True) for odd in (False, True)
    ]
    operands = (lists, factors_a, factors_b, amplitudes)
    terms = lax.switch(lists[MISC * ROW], branches, operands)
    a_rows = factors_a.shape[0]
    terms = terms.reshape(STEPS, a_rows, pairs, -1).swapaxes(1, 2).reshape(STEPS, 1, -1)
    return summed_over_narrow(terms)


def solution(mesh):
    return jax.shard_map(
        local,
        mesh=mesh,
        in_specs=(P(), P("blk", "narrow", None), P("blk", "narrow", None), P()),
        out_specs=P(None, "blk", "narrow"),
        check_vma=False,
    )
```

```python
import functools

import jax
import jax.numpy as jnp
from jax import lax
from jax.experimental import pallas as pl
from jax.experimental.pallas import tpu as pltpu
from jax.sharding import PartitionSpec as P

STEPS = 3
MOST = 8
ROUNDS = 3
GROUP = 16
LANES = 128
ROW = MOST + 1

(
    OWN,
    LIGHT,
    LIGHT_0,
    LIGHT_1,
    NEXT,
    AFTER,
    LEAD,
    PART,
    MINE,
    FED_1,
    FED_2,
    MISC,
) = range(12)
AHEAD = 4
SMALL = pl.CostEstimate(flops=1024, bytes_accessed=1024, transcendentals=0)


def send(value, pairs):
    return lax.ppermute(value, "blk", pairs)


def rotated(value, by):
    size = lax.axis_size("blk")
    return send(value, [(i, (i + by) % size) for i in range(size)])


def lists_kernel(position_ref, screen_ref, out_ref):
    tiles, subs = screen_ref.shape
    position = position_ref[0]

    def count_of(tile):
        return sum(jnp.where(screen_ref[tile, s] != 0, 1, 0) for s in range(subs))

    def look(tile, found):
        best, fullest, others = found
        count = count_of(tile)
        larger = count > best
        others = jnp.where(larger, best, jnp.maximum(others, count))
        return jnp.where(larger, count, best), jnp.where(larger, tile, fullest), others

    zero = jnp.int32(0)
    best, fullest, others = lax.fori_loop(0, tiles, look, (zero, zero, zero))

    def fill(row, tile, skip, count):
        for k in range(MOST):
            out_ref[row * ROW + k] = 0
        seen = jnp.int32(0)
        for s in range(subs):
            kept = screen_ref[tile, s] != 0

            @pl.when(kept & (seen >= skip))
            def _():
                out_ref[row * ROW + seen - skip] = s

            seen += jnp.where(kept, 1, 0)
        out_ref[row * ROW + MOST] = seen if count is None else count

    following = lax.rem(position + 1, tiles)
    second = lax.rem(position + 2, tiles)
    is_first = lax.rem(position, 2) == 0
    own_count = count_of(position)
    extra = jnp.maximum(best - ROUNDS, 0)
    light = jnp.minimum(own_count, ROUNDS)
    fill(OWN, position, 0, own_count)
    fill(LIGHT, position, 0, light)
    fill(LIGHT_0, position, 0, jnp.where(is_first, light, 0))
    fill(LIGHT_1, position, 0, jnp.where(is_first, 0, light))
    fill(NEXT, following, 0, None)
    fill(AFTER, second, 0, None)
    fill(MINE, fullest, ROUNDS, jnp.where(position == fullest, extra, 0))
    fill(FED_1, fullest, ROUNDS, jnp.where(following == fullest, extra, 0))
    fill(FED_2, fullest, ROUNDS, jnp.where(second == fullest, extra, 0))
    for k in range(ROW):
        other = out_ref[NEXT * ROW + k % ROUNDS] if k < 2 * ROUNDS else 0
        out_ref[LEAD * ROW + k] = jnp.where(is_first, out_ref[MINE * ROW + k], other)
        out_ref[PART * ROW + k] = jnp.where(is_first, 0, k // ROUNDS)
    out_ref[MISC * ROW] = jnp.where(fullest < 2, 2, 0) + lax.rem(fullest, 2)
    out_ref[MISC * ROW + 1] = fullest
    out_ref[MISC * ROW + 2] = others
    for k in range(3, ROW):
        out_ref[MISC * ROW + k] = 0


def kept_lists(position, screen):
    return pl.pallas_call(
        lists_kernel,
        in_specs=[pl.BlockSpec(memory_space=pltpu.SMEM)] * 2,
        out_specs=pl.BlockSpec(memory_space=pltpu.SMEM),
        out_shape=jax.ShapeDtypeStruct(((MISC + 1) * ROW,), jnp.int32),
        name="kept_lists",
    )(position.reshape(1), screen)


def take_kernel(row, slots, start, extent, part, lists_ref, source, *refs):
    out, sems = refs[-2:]
    width = out.shape[-1]
    copies = []
    for s in range(slots):
        sub = pl.multiple_of(lists_ref[row * ROW + s] * width, width)
        first = start
        if part is not None:
            first = pl.multiple_of(start + lists_ref[part * ROW + s] * extent, extent)
        piece = source.at[:, pl.ds(first, extent), pl.ds(sub, width)]
        copies.append(pltpu.make_async_copy(piece, out.at[s], sems.at[s]))
    for copy in copies:
        copy.start()
    for copy in copies:
        copy.wait()


def take_columns(lists, amplitudes, row, slots, width, start, extent, behind=(), part=None):
    pairs = amplitudes.shape[0]
    return pl.pallas_call(
        functools.partial(take_kernel, row, slots, start, extent, part),
        in_specs=[pl.BlockSpec(memory_space=pltpu.SMEM)]
        + [pl.BlockSpec(memory_space=pltpu.HBM)] * (1 + len(behind)),
        out_specs=pl.BlockSpec(memory_space=pltpu.HBM),
        out_shape=jax.ShapeDtypeStruct((slots, pairs, extent, width), amplitudes.dtype),
        scratch_shapes=[pltpu.SemaphoreType.DMA((slots,))],
        cost_estimate=SMALL,
        name="take_columns",
    )(lists, amplitudes, *behind)


def panel_kernel(start, panel, *refs):
    out, sems = refs[-2:]
    rows, extent, _ = out.shape
    parts = sems.shape[0]
    share = rows // parts
    copies = []
    for n in range(parts):
        piece = panel.at[pl.ds(n * share, share), pl.ds(start, extent), :]
        copies.append(pltpu.make_async_copy(piece, out.at[pl.ds(n * share, share)], sems.at[n]))
    for copy in copies:
        copy.start()
    for copy in copies:
        copy.wait()


def take_panel(panel, start, extent, behind=()):
    b_rows, _, aux = panel.shape
    return pl.pallas_call(
        functools.partial(panel_kernel, start),
        in_specs=[pl.BlockSpec(memory_space=pltpu.HBM)] * (1 + len(behind)),
        out_specs=pl.BlockSpec(memory_space=pltpu.HBM),
        out_shape=jax.ShapeDtypeStruct((b_rows, extent, aux), panel.dtype),
        scratch_shapes=[pltpu.SemaphoreType.DMA((4,))],
        cost_estimate=SMALL,
        name="take_panel",
    )(panel, *behind)


def tie_kernel(*refs):
    pass


def tied(value, *behind):
    return pl.pallas_call(
        tie_kernel,
        in_specs=[pl.BlockSpec(memory_space=pltpu.HBM)] * (1 + len(behind)),
        out_specs=pl.BlockSpec(memory_space=pltpu.HBM),
        out_shape=jax.ShapeDtypeStruct(value.shape, value.dtype),
        input_output_aliases={0: 0},
        cost_estimate=SMALL,
        name="tied",
    )(value, *behind)


class Segment:
    def __init__(self, into, row, slots, amps, panel, extent, amp_at=0, panel_at=0, slot_at=0):
        self.into, self.row, self.slots = into, row, slots
        self.amps, self.panel, self.extent = amps, panel, extent
        self.amp_at, self.panel_at, self.slot_at = amp_at, panel_at, slot_at


def terms_kernel(segments, places, d_rows, lists_ref, *refs):
    arrays = refs[: -8]
    out_ref, amp_buf, panel_buf, factor_buf, mixed, total, sems, factor_sems = refs[-8:]
    factors = arrays[0]
    outs = out_ref.shape[0]
    _, most, pairs, _, width = amp_buf.shape
    b_rows = panel_buf.shape[1]
    _, _, a_rows, _, aux = factor_buf.shape

    counts = [lists_ref[seg.row * ROW + MOST] for seg in segments]
    starts, orders = [], []
    begin = order = jnp.int32(0)
    for seg, count in zip(segments, counts):
        starts.append(begin)
        orders.append(order)
        begin = begin + jnp.where(count > 0, seg.extent // d_rows, 0)
        order = order + jnp.where(count > 0, 1, 0)
    items = begin

    def pick(at, values):
        found = values[0]
        for s in range(1, len(segments)):
            found = jnp.where(at == s, values[s], found)
        return found

    def locate(t):
        at = jnp.int32(0)
        for s in range(len(segments)):
            at = jnp.where((counts[s] > 0) & (t >= starts[s]), s, at)
        return at, t - pick(at, starts), lax.rem(pick(at, orders), AHEAD)

    def fetch(t):
        at, block, turn = locate(t)
        slot = lax.rem(t, AHEAD)
        for s, seg in enumerate(segments):
            amps, panel = arrays[places[s][0]], arrays[places[s][1]]

            @pl.when(at == s)
            def _():
                amp_d = pl.ds(pl.multiple_of(seg.amp_at + block * d_rows, d_rows), d_rows)
                panel_d = pl.ds(pl.multiple_of(seg.panel_at + block * d_rows, d_rows), d_rows)
                pltpu.make_async_copy(
                    panel.at[:, panel_d, :], panel_buf.at[slot], sems.at[slot, most]
                ).start()

                def one(k, carry):
                    sub = pl.multiple_of(lists_ref[seg.row * ROW + k] * width, width)
                    columns = pl.ds(sub, width)
                    if len(amps.shape) == 3:
                        source = amps.at[:, amp_d, columns]
                    else:
                        source = amps.at[seg.slot_at + k, :, amp_d, :]
                    pltpu.make_async_copy(
                        source, amp_buf.at[slot, k], sems.at[slot, k]
                    ).start()

                    @pl.when(block == 0)
                    def _():
                        pltpu.make_async_copy(
                            factors.at[:, columns, :],
                            factor_buf.at[turn, k],
                            factor_sems.at[turn, k],
                        ).start()

                    return carry

                lax.fori_loop(0, counts[s], one, 0)

    def arrive(slot, block, turn, count):
        pltpu.make_async_copy(
            panel_buf.at[slot], panel_buf.at[slot], sems.at[slot, most]
        ).wait()

        def one(k, carry):
            pltpu.make_async_copy(
                amp_buf.at[slot, k], amp_buf.at[slot, k], sems.at[slot, k]
            ).wait()

            @pl.when(block == 0)
            def _():
                pltpu.make_async_copy(
                    factor_buf.at[turn, k], factor_buf.at[turn, k], factor_sems.at[turn, k]
                ).wait()

            return carry

        lax.fori_loop(0, count, one, 0)

    total[...] = jnp.zeros_like(total)

    def mix(couples, slot, turn, count):
        slots = min(2 * couples, most)
        whole = slots - 1 < count
        columns = [amp_buf[slot, k].reshape(pairs * d_rows, width) for k in range(slots)]
        columns[-1] = jnp.where(whole, columns[-1], jnp.zeros_like(columns[-1]))
        lhs = jnp.concatenate(columns, axis=1)

        def one(a, carry):
            rows = [factor_buf[turn, k, a] for k in range(slots)]
            rows[-1] = jnp.where(whole, rows[-1], jnp.zeros_like(rows[-1]))
            product = jnp.dot(
                lhs, jnp.concatenate(rows, axis=0), preferred_element_type=jnp.float32
            )
            mixed[a] = product.astype(mixed.dtype).reshape(pairs, d_rows, aux)
            return carry

        lax.fori_loop(0, a_rows, one, 0)

    def step(n, carry):
        @pl.when(n < items)
        def _():
            fetch(n)

        @pl.when(n >= AHEAD - 1)
        def _():
            t = n - (AHEAD - 1)
            at, block, turn = locate(t)
            slot = lax.rem(t, AHEAD)
            count = pick(at, counts)
            into = pick(at, [seg.into for seg in segments])
            arrive(slot, block, turn, count)
            for couples in range(1, (most + 1) // 2 + 1):

                @pl.when((count > 2 * couples - 2) & (count <= 2 * couples))
                def _():
                    mix(couples, slot, turn, count)

            def group(g, carry):
                rows = pl.ds(pl.multiple_of(g * GROUP, GROUP), GROUP)
                lhs = jnp.concatenate(
                    [mixed[a, :, rows, :].reshape(-1, aux) for a in range(a_rows)], axis=0
                )
                rhs = panel_buf[slot, :, rows, :].reshape(b_rows * GROUP, aux)
                total[into] += lax.dot_general(
                    lhs, rhs, (((1,), (1,)), ((), ())), preferred_element_type=jnp.float32
                )
                return carry

            lax.fori_loop(0, d_rows // GROUP, group, 0)

        return carry

    lax.fori_loop(0, jnp.where(items > 0, items + AHEAD - 1, 0), step, 0)

    def finish(o, carry):
        _, rows, columns = total.shape
        row_d = lax.broadcasted_iota(jnp.int32, (rows, columns), 0) % GROUP
        column_d = lax.broadcasted_iota(jnp.int32, (rows, columns), 1) % GROUP
        kept = jnp.where(row_d == column_d, total[o], 0.0)
        kept = kept.reshape(rows // GROUP, GROUP, columns).sum(axis=1)
        from_b = lax.broadcasted_iota(jnp.int32, (columns, LANES), 0) // GROUP
        to_b = lax.broadcasted_iota(jnp.int32, (columns, LANES), 1)
        gather = jnp.where(from_b == to_b, 1.0, 0.0)
        out_ref[o] = jnp.dot(
            kept, gather, precision=lax.Precision.HIGHEST, preferred_element_type=jnp.float32
        )
        return carry

    lax.fori_loop(0, outs, finish, 0)


def pair_terms(lists, factors_a, segments, outs, width, d_rows):
    arrays, places = [factors_a], []
    for seg in segments:
        place = []
        for array in (seg.amps, seg.panel):
            known = [n for n, other in enumerate(arrays) if other is array]
            place.append(known[0] if known else len(arrays))
            if not known:
                arrays.append(array)
        places.append(place)
    a_rows, _, aux = factors_a.shape
    pairs = segments[0].amps.shape[-3]
    b_rows = segments[0].panel.shape[0]
    most = max(2, *(seg.slots for seg in segments))
    out = pl.pallas_call(
        functools.partial(terms_kernel, segments, places, d_rows),
        in_specs=[pl.BlockSpec(memory_space=pltpu.SMEM)]
        + [pl.BlockSpec(memory_space=pltpu.HBM)] * len(arrays),
        out_specs=pl.BlockSpec(memory_space=pltpu.VMEM),
        scratch_shapes=[
            pltpu.VMEM((AHEAD, most, pairs, d_rows, width), jnp.bfloat16),
            pltpu.VMEM((AHEAD, b_rows, d_rows, aux), jnp.bfloat16),
            pltpu.VMEM((AHEAD, most, a_rows, width, aux), jnp.bfloat16),
            pltpu.VMEM((a_rows, pairs, d_rows, aux), jnp.bfloat16),
            pltpu.VMEM((outs, a_rows * pairs * GROUP, b_rows * GROUP), jnp.float32),
            pltpu.SemaphoreType.DMA((AHEAD, most + 1)),
            pltpu.SemaphoreType.DMA((AHEAD, most)),
        ],
        out_shape=jax.ShapeDtypeStruct((outs, a_rows * pairs, LANES), jnp.float32),
        compiler_params=pltpu.CompilerParams(vmem_limit_bytes=32 * 1024 * 1024),
        cost_estimate=SMALL,
        name="pair_terms",
    )(lists, *arrays)
    return out[:, :, :b_rows]


def summed_over_narrow(value):
    size = lax.axis_size("narrow")
    me = lax.axis_index("narrow")
    share = value.shape[2] // size

    def part(owner):
        return lax.dynamic_slice_in_dim(value, owner * share, share, 2)

    parts = [part(me)]
    for k in range(1, size):
        to = [(i, (i + k) % size) for i in range(size)]
        parts.append(lax.ppermute(part((me + k) % size), "narrow", to))
    return sum(parts[1:], parts[0])


def local(factors_a, factors_b, amplitudes, screen):
    pairs, d_extent, virtuals = amplitudes.shape
    width = virtuals // screen.shape[1]
    tiles = lax.axis_size("blk")
    position = lax.axis_index("blk")
    extras = MOST - ROUNDS
    d_rows = min(64, d_extent // 4)

    lists = kept_lists(position, screen)
    fullest = lists[MISC * ROW + 1]
    others = lists[MISC * ROW + 2]
    is_first = position % 2 == 0
    is_full = position == fullest
    feeds_one = (position + 1) % tiles == fullest
    feeds_two = (position + 2) % tiles == fullest

    evens, odds = range(0, tiles, 2), range(1, tiles, 2)
    up = [(i, i + 1) for i in evens]
    down = [(i + 1, i) for i in evens]
    around = [(i, (i + 2) % tiles) for i in range(tiles)]

    def run(wrapped, odd, operands):
        lists, factors_a, factors_b, amplitudes = operands
        terms = functools.partial(pair_terms, lists, factors_a, width=width, d_rows=d_rows)
        columns_of = functools.partial(Segment, panel=factors_b)
        given_to = functools.partial(Segment, amps=amplitudes, slots=extras)
        take = functools.partial(take_columns, lists, amplitudes, width=width)
        cut = functools.partial(take_panel, factors_b)

        def ahead(at):
            return (at >= tiles - 2) == wrapped

        def hops(keep):
            return [(at, to) for at, to in around if keep(at)]

        def backs(keep):
            return [(to, at) for at, to in around if keep(at)]

        here = terms(
            [columns_of(0, row=OWN, slots=MOST, amps=amplitudes, extent=d_extent)], 1
        )
        half, quarter = d_extent // 2, d_extent // 4
        after = functools.partial(take, row=AFTER, slots=ROUNDS, extent=half)
        if odd:
            given = max(3 * d_extent // 8 // d_rows, 1) * d_rows
            moved = d_extent - given

            def seconds(at):
                return at in odds and ahead(at)

            near_l = take(row=NEXT, slots=ROUNDS, start=0, extent=half)
            side_l = send(near_l, up + down)
            near_h = take(row=NEXT, slots=ROUNDS, start=half, extent=half)
            side_h = send(near_h, up + down)
            direct = take(row=AFTER, slots=ROUNDS, start=0, extent=d_extent)
            got_direct = send(direct, hops(lambda at: at in evens))
            extra = take(row=MINE, slots=extras, start=0, extent=moved)
            extra_two = send(extra, hops(seconds))
            far = send(cut(start=moved, extent=given), backs(seconds))

            side_l = tied(side_l, here)
            after_h = after(start=half)
            pass_l = jnp.where(is_first, side_l, after(start=0))
            on_l = send(pass_l, around)
            beside = send(cut(start=moved, extent=given, behind=[side_l]), down)
            extra = take(row=MINE, slots=extras, start=0, extent=moved, behind=[side_l])
            extra = tied(extra, got_direct, extra_two, far, side_h, after_h, pass_l)
            extra_one = send(extra, up)
            on_h = send(jnp.where(is_first, side_h, after_h), around)

            first = terms(
                [
                    columns_of(1, row=LIGHT_0, slots=ROUNDS, amps=got_direct, extent=d_extent),
                    columns_of(0, row=LIGHT_1, slots=ROUNDS, amps=side_l, extent=half),
                    columns_of(
                        0, row=LIGHT_1, slots=ROUNDS, amps=side_h, extent=half, panel_at=half
                    ),
                    columns_of(1, row=MINE, slots=extras, amps=extra_two, extent=moved),
                ],
                2,
            )
            then = terms(
                [
                    columns_of(0, row=LIGHT_0, slots=ROUNDS, amps=on_l, extent=half),
                    columns_of(1, row=LIGHT_1, slots=ROUNDS, amps=on_l, extent=half),
                ],
                2,
            )
            sent = terms(
                [
                    given_to(0, row=FED_1, panel=beside, extent=given, amp_at=moved),
                    given_to(0, row=FED_2, panel=far, extent=given, amp_at=moved),
                ],
                1,
            )[0]
            last = terms(
                [
                    columns_of(
                        0, row=LIGHT_0, slots=ROUNDS, amps=on_h, extent=half, panel_at=half
                    ),
                    columns_of(
                        1, row=LIGHT_1, slots=ROUNDS, amps=on_h, extent=half, panel_at=half
                    ),
                    columns_of(0, row=MINE, slots=extras, amps=extra_one, extent=moved),
                ],
                2,
            )
            one = first[0] + then[0] + last[0]
            two = first[1] + then[1] + last[1]
        else:
            def firsts(at):
                return at in evens and ahead(at)

            lead = take(row=LEAD, part=PART, slots=2 * ROUNDS, start=0, extent=half)
            got_lead = send(lead, hops(lambda at: at in odds or ahead(at)))
            far_0 = send(cut(start=half, extent=quarter), backs(firsts))
            extra_0 = take(row=MINE, slots=extras, start=0, extent=quarter)
            cross = send(extra_0, down)
            near = take(row=NEXT, slots=ROUNDS, start=0, extent=d_extent)
            side = send(near, up)
            far_1 = send(cut(start=half + quarter, extent=quarter), backs(firsts))

            extra_1 = take(row=MINE, slots=extras, start=quarter, extent=quarter)
            cross = tied(cross, here)
            got_extra = send(jnp.where(is_first, cross, extra_1), hops(ahead))
            far_0 = tied(far_0, here, cross)
            up_0 = send(far_0, up)
            lead_down = send(got_lead, down)
            after_l = after(start=0, behind=[got_lead, side])
            got_l = send(after_l, around)
            far_1 = tied(far_1, after_l)
            up_1 = send(far_1, up)
            after_h = after(start=half, behind=[far_1, got_extra])
            got_h = send(after_h, around)
            extra_down = send(tied(got_extra, after_h), down)

            first = terms(
                [
                    columns_of(0, row=LIGHT_1, slots=ROUNDS, amps=side, extent=d_extent),
                    columns_of(1, row=MINE, slots=extras, amps=got_lead, extent=half),
                ],
                2,
            )
            fed = functools.partial(given_to, 0, extent=quarter)
            then = terms(
                [
                    fed(row=FED_1, panel=up_0, amp_at=half),
                    fed(row=FED_2, panel=far_0, amp_at=half),
                    fed(row=FED_2, panel=far_1, amp_at=half + quarter),
                    columns_of(1, row=MINE, slots=extras, amps=got_extra, extent=quarter),
                    columns_of(2, row=LIGHT, slots=ROUNDS, amps=got_l, extent=half),
                ],
                3,
            )
            low = terms(
                [
                    columns_of(0, row=LIGHT_0, slots=ROUNDS, amps=lead_down, extent=half),
                    columns_of(
                        0,
                        row=LIGHT_0,
                        slots=ROUNDS,
                        amps=lead_down,
                        extent=half,
                        panel_at=half,
                        slot_at=ROUNDS,
                    ),
                ],
                1,
            )
            sent = then[0]
            sent += terms([fed(row=FED_1, panel=up_1, amp_at=half + quarter)], 1)[0]
            last = terms(
                [
                    columns_of(
                        1, row=LIGHT, slots=ROUNDS, amps=got_h, extent=half, panel_at=half
                    ),
                    columns_of(
                        0,
                        row=MINE,
                        slots=extras,
                        amps=extra_down,
                        extent=quarter,
                        panel_at=quarter,
                    ),
                ],
                2,
            )
            one = first[0] + then[1] + low[0] + last[0]
            two = first[1] + then[2] + last[1]
        one += rotated(jnp.where(feeds_one, sent, 0.0), 1)
        two += rotated(jnp.where(feeds_two, sent, 0.0), 2)

        def add_round(r, running):
            one, two = running

            def only(row, count):
                sub = lax.dynamic_slice_in_dim(lists, row * ROW + r, 1)
                return jnp.concatenate([sub, jnp.zeros(MOST - 1, jnp.int32), count.reshape(1)])

            has = jnp.where((r < lists[OWN * ROW + MOST]) & ~is_full, 1, 0).astype(jnp.int32)
            own = only(OWN, has)
            moved = [
                rotated(
                    take_columns(only(row, has), amplitudes, 0, 1, width, 0, d_extent), by
                )
                for row, by in ((NEXT, 1), (AFTER, 2))
            ]
            more = pair_terms(
                own,
                factors_a,
                [
                    columns_of(into, row=0, slots=1, amps=columns, extent=d_extent)
                    for into, columns in enumerate(moved)
                ],
                2,
                width,
                d_rows,
            )
            return one + more[0], two + more[1]

        one, two = lax.fori_loop(ROUNDS, jnp.maximum(others, ROUNDS), add_round, (one, two))
        return jnp.stack([here[0], one, two])

    branches = [
        functools.partial(run, wrapped, odd) for wrapped in (False, True) for odd in (False, True)
    ]
    operands = (lists, factors_a, factors_b, amplitudes)
    terms = lax.switch(lists[MISC * ROW], branches, operands)
    a_rows = factors_a.shape[0]
    terms = terms.reshape(STEPS, a_rows, pairs, -1).swapaxes(1, 2).reshape(STEPS, 1, -1)
    return summed_over_narrow(terms)


def solution(mesh):
    return jax.shard_map(
        local,
        mesh=mesh,
        in_specs=(P(), P("blk", "narrow", None), P("blk", "narrow", None), P()),
        out_specs=P(None, "blk", "narrow"),
        check_vma=False,
    )
```

```python
import functools

import jax
import jax.numpy as jnp
from jax import lax
from jax.experimental import pallas as pl
from jax.experimental.pallas import tpu as pltpu
from jax.sharding import PartitionSpec as P

STEPS = 3
MOST = 8
ROUNDS = 3
GROUP = 16
LANES = 128
ROW = MOST + 1

(
    OWN,
    LIGHT,
    LIGHT_0,
    LIGHT_1,
    NEXT,
    AFTER,
    LEAD,
    PART,
    MINE,
    FED_1,
    FED_2,
    MISC,
) = range(12)
AHEAD = 4
SMALL = pl.CostEstimate(flops=1024, bytes_accessed=1024, transcendentals=0)


def send(value, pairs):
    return lax.ppermute(value, "blk", pairs)


def rotated(value, by):
    size = lax.axis_size("blk")
    return send(value, [(i, (i + by) % size) for i in range(size)])


def lists_kernel(position_ref, screen_ref, out_ref):
    tiles, subs = screen_ref.shape
    position = position_ref[0]

    def count_of(tile):
        return sum(jnp.where(screen_ref[tile, s] != 0, 1, 0) for s in range(subs))

    def look(tile, found):
        best, fullest, others = found
        count = count_of(tile)
        larger = count > best
        others = jnp.where(larger, best, jnp.maximum(others, count))
        return jnp.where(larger, count, best), jnp.where(larger, tile, fullest), others

    zero = jnp.int32(0)
    best, fullest, others = lax.fori_loop(0, tiles, look, (zero, zero, zero))

    def fill(row, tile, skip, count):
        for k in range(MOST):
            out_ref[row * ROW + k] = 0
        seen = jnp.int32(0)
        for s in range(subs):
            kept = screen_ref[tile, s] != 0

            @pl.when(kept & (seen >= skip))
            def _():
                out_ref[row * ROW + seen - skip] = s

            seen += jnp.where(kept, 1, 0)
        out_ref[row * ROW + MOST] = seen if count is None else count

    following = lax.rem(position + 1, tiles)
    second = lax.rem(position + 2, tiles)
    is_first = lax.rem(position, 2) == 0
    own_count = count_of(position)
    extra = jnp.maximum(best - ROUNDS, 0)
    light = jnp.minimum(own_count, ROUNDS)
    fill(OWN, position, 0, own_count)
    fill(LIGHT, position, 0, light)
    fill(LIGHT_0, position, 0, jnp.where(is_first, light, 0))
    fill(LIGHT_1, position, 0, jnp.where(is_first, 0, light))
    fill(NEXT, following, 0, None)
    fill(AFTER, second, 0, None)
    fill(MINE, fullest, ROUNDS, jnp.where(position == fullest, extra, 0))
    fill(FED_1, fullest, ROUNDS, jnp.where(following == fullest, extra, 0))
    fill(FED_2, fullest, ROUNDS, jnp.where(second == fullest, extra, 0))
    for k in range(ROW):
        other = out_ref[NEXT * ROW + k % ROUNDS] if k < 2 * ROUNDS else 0
        out_ref[LEAD * ROW + k] = jnp.where(is_first, out_ref[MINE * ROW + k], other)
        out_ref[PART * ROW + k] = jnp.where(is_first, 0, k // ROUNDS)
    out_ref[MISC * ROW] = jnp.where(fullest < 2, 2, 0) + lax.rem(fullest, 2)
    out_ref[MISC * ROW + 1] = fullest
    out_ref[MISC * ROW + 2] = others
    for k in range(3, ROW):
        out_ref[MISC * ROW + k] = 0


def kept_lists(position, screen):
    return pl.pallas_call(
        lists_kernel,
        in_specs=[pl.BlockSpec(memory_space=pltpu.SMEM)] * 2,
        out_specs=pl.BlockSpec(memory_space=pltpu.SMEM),
        out_shape=jax.ShapeDtypeStruct(((MISC + 1) * ROW,), jnp.int32),
        name="kept_lists",
    )(position.reshape(1), screen)


def staged(count, source_of, target_of, stage, sems):
    def load(n, carry):
        pltpu.make_async_copy(source_of(n), stage.at[n], sems.at[0, n]).start()
        return carry

    def store(n, carry):
        pltpu.make_async_copy(stage.at[n], stage.at[n], sems.at[0, n]).wait()
        pltpu.make_async_copy(stage.at[n], target_of(n), sems.at[1, n]).start()
        return carry

    def finish(n, carry):
        pltpu.make_async_copy(stage.at[n], stage.at[n], sems.at[1, n]).wait()
        return carry

    for act in (load, store, finish):
        lax.fori_loop(0, count, act, 0)


def take_kernel(row, slots, start, extent, part, lists_ref, source, *refs):
    out, stage, sems = refs[-3:]
    width = out.shape[-1]

    def source_of(s):
        sub = pl.multiple_of(lists_ref[row * ROW + s] * width, width)
        first = start
        if part is not None:
            first = pl.multiple_of(start + lists_ref[part * ROW + s] * extent, extent)
        return source.at[:, pl.ds(first, extent), pl.ds(sub, width)]

    staged(slots, source_of, lambda s: out.at[s], stage, sems)


def take_columns(lists, amplitudes, row, slots, width, start, extent, behind=(), part=None):
    pairs = amplitudes.shape[0]
    return pl.pallas_call(
        functools.partial(take_kernel, row, slots, start, extent, part),
        in_specs=[pl.BlockSpec(memory_space=pltpu.SMEM)]
        + [pl.BlockSpec(memory_space=pltpu.HBM)] * (1 + len(behind)),
        out_specs=pl.BlockSpec(memory_space=pltpu.HBM),
        out_shape=jax.ShapeDtypeStruct((slots, pairs, extent, width), amplitudes.dtype),
        scratch_shapes=[
            pltpu.VMEM((slots, pairs, extent, width), amplitudes.dtype),
            pltpu.SemaphoreType.DMA((2, slots)),
        ],
        compiler_params=pltpu.CompilerParams(vmem_limit_bytes=16 * 1024 * 1024),
        cost_estimate=SMALL,
        name="take_columns",
    )(lists, amplitudes, *behind)


def panel_kernel(start, panel, *refs):
    out, stage, sems = refs[-3:]
    parts, share, extent, _ = stage.shape

    def rows(n):
        return pl.ds(n * share, share)

    staged(
        parts,
        lambda n: panel.at[rows(n), pl.ds(start, extent), :],
        lambda n: out.at[rows(n)],
        stage,
        sems,
    )


def take_panel(panel, start, extent, behind=()):
    b_rows, _, aux = panel.shape
    return pl.pallas_call(
        functools.partial(panel_kernel, start),
        in_specs=[pl.BlockSpec(memory_space=pltpu.HBM)] * (1 + len(behind)),
        out_specs=pl.BlockSpec(memory_space=pltpu.HBM),
        out_shape=jax.ShapeDtypeStruct((b_rows, extent, aux), panel.dtype),
        scratch_shapes=[
            pltpu.VMEM((4, b_rows // 4, extent, aux), panel.dtype),
            pltpu.SemaphoreType.DMA((2, 4)),
        ],
        compiler_params=pltpu.CompilerParams(vmem_limit_bytes=16 * 1024 * 1024),
        cost_estimate=SMALL,
        name="take_panel",
    )(panel, *behind)


def tie_kernel(*refs):
    pass


def tied(value, *behind):
    return pl.pallas_call(
        tie_kernel,
        in_specs=[pl.BlockSpec(memory_space=pltpu.HBM)] * (1 + len(behind)),
        out_specs=pl.BlockSpec(memory_space=pltpu.HBM),
        out_shape=jax.ShapeDtypeStruct(value.shape, value.dtype),
        input_output_aliases={0: 0},
        cost_estimate=SMALL,
        name="tied",
    )(value, *behind)


class Segment:
    def __init__(self, into, row, slots, amps, panel, extent, amp_at=0, panel_at=0, slot_at=0):
        self.into, self.row, self.slots = into, row, slots
        self.amps, self.panel, self.extent = amps, panel, extent
        self.amp_at, self.panel_at, self.slot_at = amp_at, panel_at, slot_at


def terms_kernel(segments, places, d_rows, lists_ref, *refs):
    arrays = refs[: -8]
    out_ref, amp_buf, panel_buf, factor_buf, mixed, total, sems, factor_sems = refs[-8:]
    factors = arrays[0]
    outs = out_ref.shape[0]
    _, most, pairs, _, width = amp_buf.shape
    b_rows = panel_buf.shape[1]
    _, _, a_rows, _, aux = factor_buf.shape

    counts = [lists_ref[seg.row * ROW + MOST] for seg in segments]
    starts, orders = [], []
    begin = order = jnp.int32(0)
    for seg, count in zip(segments, counts):
        starts.append(begin)
        orders.append(order)
        begin = begin + jnp.where(count > 0, seg.extent // d_rows, 0)
        order = order + jnp.where(count > 0, 1, 0)
    items = begin

    def pick(at, values):
        found = values[0]
        for s in range(1, len(segments)):
            found = jnp.where(at == s, values[s], found)
        return found

    def locate(t):
        at = jnp.int32(0)
        for s in range(len(segments)):
            at = jnp.where((counts[s] > 0) & (t >= starts[s]), s, at)
        return at, t - pick(at, starts), lax.rem(pick(at, orders), AHEAD)

    def fetch(t):
        at, block, turn = locate(t)
        slot = lax.rem(t, AHEAD)
        for s, seg in enumerate(segments):
            amps, panel = arrays[places[s][0]], arrays[places[s][1]]

            @pl.when(at == s)
            def _():
                amp_d = pl.ds(pl.multiple_of(seg.amp_at + block * d_rows, d_rows), d_rows)
                panel_d = pl.ds(pl.multiple_of(seg.panel_at + block * d_rows, d_rows), d_rows)
                pltpu.make_async_copy(
                    panel.at[:, panel_d, :], panel_buf.at[slot], sems.at[slot, most]
                ).start()

                def one(k, carry):
                    sub = pl.multiple_of(lists_ref[seg.row * ROW + k] * width, width)
                    columns = pl.ds(sub, width)
                    if len(amps.shape) == 3:
                        source = amps.at[:, amp_d, columns]
                    else:
                        source = amps.at[seg.slot_at + k, :, amp_d, :]
                    pltpu.make_async_copy(
                        source, amp_buf.at[slot, k], sems.at[slot, k]
                    ).start()

                    @pl.when(block == 0)
                    def _():
                        pltpu.make_async_copy(
                            factors.at[:, columns, :],
                            factor_buf.at[turn, k],
                            factor_sems.at[turn, k],
                        ).start()

                    return carry

                lax.fori_loop(0, counts[s], one, 0)

    def arrive(slot, block, turn, count):
        pltpu.make_async_copy(
            panel_buf.at[slot], panel_buf.at[slot], sems.at[slot, most]
        ).wait()

        def one(k, carry):
            pltpu.make_async_copy(
                amp_buf.at[slot, k], amp_buf.at[slot, k], sems.at[slot, k]
            ).wait()

            @pl.when(block == 0)
            def _():
                pltpu.make_async_copy(
                    factor_buf.at[turn, k], factor_buf.at[turn, k], factor_sems.at[turn, k]
                ).wait()

            return carry

        lax.fori_loop(0, count, one, 0)

    total[...] = jnp.zeros_like(total)

    def mix(low, top, slot, turn, count):
        columns = [amp_buf[slot, k].reshape(pairs * d_rows, width) for k in range(top)]
        for k in range(low, top):
            columns[k] = jnp.where(k < count, columns[k], jnp.zeros_like(columns[k]))
        lhs = jnp.concatenate(columns, axis=1)
        for a in range(a_rows):
            rows = [factor_buf[turn, k, a] for k in range(top)]
            for k in range(low, top):
                rows[k] = jnp.where(k < count, rows[k], jnp.zeros_like(rows[k]))
            product = jnp.dot(
                lhs, jnp.concatenate(rows, axis=0), preferred_element_type=jnp.float32
            )
            mixed[a] = product.astype(mixed.dtype).reshape(pairs, d_rows, aux)

    def step(n, carry):
        @pl.when(n < items)
        def _():
            fetch(n)

        @pl.when(n >= AHEAD - 1)
        def _():
            t = n - (AHEAD - 1)
            at, block, turn = locate(t)
            slot = lax.rem(t, AHEAD)
            count = pick(at, counts)
            into = pick(at, [seg.into for seg in segments])
            arrive(slot, block, turn, count)
            tops = set()
            for slots in {seg.slots for seg in segments}:
                tops |= {slots} | ({2, 4} if slots == MOST else {2} if slots <= ROUNDS else set())
            tops = sorted(tops)
            for low, top in zip([0] + tops, tops):

                @pl.when((count > low) & (count <= top))
                def _():
                    mix(low + 1, top, slot, turn, count)

            partial = total[into]
            for g in range(0, d_rows, GROUP):
                lhs = jnp.concatenate(
                    [mixed[a, :, g : g + GROUP, :].reshape(-1, aux) for a in range(a_rows)],
                    axis=0,
                )
                rhs = panel_buf[slot, :, g : g + GROUP, :].reshape(b_rows * GROUP, aux)
                partial += lax.dot_general(
                    lhs, rhs, (((1,), (1,)), ((), ())), preferred_element_type=jnp.float32
                )
            total[into] = partial

        return carry

    lax.fori_loop(0, jnp.where(items > 0, items + AHEAD - 1, 0), step, 0)

    def finish(o, carry):
        _, rows, columns = total.shape
        row_d = lax.broadcasted_iota(jnp.int32, (rows, columns), 0) % GROUP
        column_d = lax.broadcasted_iota(jnp.int32, (rows, columns), 1) % GROUP
        kept = jnp.where(row_d == column_d, total[o], 0.0)
        kept = kept.reshape(rows // GROUP, GROUP, columns).sum(axis=1)
        from_b = lax.broadcasted_iota(jnp.int32, (columns, LANES), 0) // GROUP
        to_b = lax.broadcasted_iota(jnp.int32, (columns, LANES), 1)
        gather = jnp.where(from_b == to_b, 1.0, 0.0)
        out_ref[o] = jnp.dot(
            kept, gather, precision=lax.Precision.HIGHEST, preferred_element_type=jnp.float32
        )
        return carry

    lax.fori_loop(0, outs, finish, 0)


def pair_terms(lists, factors_a, segments, outs, width, d_rows):
    arrays, places = [factors_a], []
    for seg in segments:
        place = []
        for array in (seg.amps, seg.panel):
            known = [n for n, other in enumerate(arrays) if other is array]
            place.append(known[0] if known else len(arrays))
            if not known:
                arrays.append(array)
        places.append(place)
    a_rows, _, aux = factors_a.shape
    pairs = segments[0].amps.shape[-3]
    b_rows = segments[0].panel.shape[0]
    most = max(2, *(seg.slots for seg in segments))
    out = pl.pallas_call(
        functools.partial(terms_kernel, segments, places, d_rows),
        in_specs=[pl.BlockSpec(memory_space=pltpu.SMEM)]
        + [pl.BlockSpec(memory_space=pltpu.HBM)] * len(arrays),
        out_specs=pl.BlockSpec(memory_space=pltpu.VMEM),
        scratch_shapes=[
            pltpu.VMEM((AHEAD, most, pairs, d_rows, width), jnp.bfloat16),
            pltpu.VMEM((AHEAD, b_rows, d_rows, aux), jnp.bfloat16),
            pltpu.VMEM((AHEAD, most, a_rows, width, aux), jnp.bfloat16),
            pltpu.VMEM((a_rows, pairs, d_rows, aux), jnp.bfloat16),
            pltpu.VMEM((outs, a_rows * pairs * GROUP, b_rows * GROUP), jnp.float32),
            pltpu.SemaphoreType.DMA((AHEAD, most + 1)),
            pltpu.SemaphoreType.DMA((AHEAD, most)),
        ],
        out_shape=jax.ShapeDtypeStruct((outs, a_rows * pairs, LANES), jnp.float32),
        compiler_params=pltpu.CompilerParams(vmem_limit_bytes=32 * 1024 * 1024),
        cost_estimate=SMALL,
        name="pair_terms",
    )(lists, *arrays)
    return out[:, :, :b_rows]


def summed_over_narrow(value):
    size = lax.axis_size("narrow")
    me = lax.axis_index("narrow")
    share = value.shape[2] // size

    def part(owner):
        return lax.dynamic_slice_in_dim(value, owner * share, share, 2)

    parts = [part(me)]
    for k in range(1, size):
        to = [(i, (i + k) % size) for i in range(size)]
        parts.append(lax.ppermute(part((me + k) % size), "narrow", to))
    return sum(parts[1:], parts[0])


def local(factors_a, factors_b, amplitudes, screen):
    pairs, d_extent, virtuals = amplitudes.shape
    width = virtuals // screen.shape[1]
    tiles = lax.axis_size("blk")
    position = lax.axis_index("blk")
    extras = MOST - ROUNDS
    d_rows = min(64, d_extent // 4)

    lists = kept_lists(position, screen)
    fullest = lists[MISC * ROW + 1]
    others = lists[MISC * ROW + 2]
    is_first = position % 2 == 0
    is_full = position == fullest
    feeds_one = (position + 1) % tiles == fullest
    feeds_two = (position + 2) % tiles == fullest

    evens, odds = range(0, tiles, 2), range(1, tiles, 2)
    up = [(i, i + 1) for i in evens]
    down = [(i + 1, i) for i in evens]
    around = [(i, (i + 2) % tiles) for i in range(tiles)]

    def run(wrapped, odd, operands):
        lists, factors_a, factors_b, amplitudes = operands
        terms = functools.partial(pair_terms, lists, factors_a, width=width, d_rows=d_rows)
        columns_of = functools.partial(Segment, panel=factors_b)
        given_to = functools.partial(Segment, amps=amplitudes, slots=extras)
        take = functools.partial(take_columns, lists, amplitudes, width=width)
        cut = functools.partial(take_panel, factors_b)

        def ahead(at):
            return (at >= tiles - 2) == wrapped

        def hops(keep):
            return [(at, to) for at, to in around if keep(at)]

        def backs(keep):
            return [(to, at) for at, to in around if keep(at)]

        here = terms(
            [columns_of(0, row=OWN, slots=MOST, amps=amplitudes, extent=d_extent)], 1
        )
        half, quarter = d_extent // 2, d_extent // 4
        after = functools.partial(take, row=AFTER, slots=ROUNDS, extent=half)
        if odd:
            given = max(3 * d_extent // 8 // d_rows, 1) * d_rows
            moved = d_extent - given

            def seconds(at):
                return at in odds and ahead(at)

            near_l = take(row=NEXT, slots=ROUNDS, start=0, extent=half)
            side_l = send(near_l, up + down)
            near_h = take(row=NEXT, slots=ROUNDS, start=half, extent=half)
            side_h = send(near_h, up + down)
            direct = take(row=AFTER, slots=ROUNDS, start=0, extent=d_extent)
            got_direct = send(direct, hops(lambda at: at in evens))
            extra = take(row=MINE, slots=extras, start=0, extent=moved)
            extra_two = send(extra, hops(seconds))
            far = send(cut(start=moved, extent=given), backs(seconds))

            side_l = tied(side_l, here)
            after_h = after(start=half)
            pass_l = jnp.where(is_first, side_l, after(start=0))
            on_l = send(pass_l, around)
            beside = send(cut(start=moved, extent=given, behind=[side_l]), down)
            extra = take(row=MINE, slots=extras, start=0, extent=moved, behind=[side_l])
            extra = tied(extra, got_direct, extra_two, far, side_h, after_h, pass_l)
            extra_one = send(extra, up)
            on_h = send(jnp.where(is_first, side_h, after_h), around)

            first = terms(
                [
                    columns_of(1, row=LIGHT_0, slots=ROUNDS, amps=got_direct, extent=d_extent),
                    columns_of(0, row=LIGHT_1, slots=ROUNDS, amps=side_l, extent=half),
                    columns_of(
                        0, row=LIGHT_1, slots=ROUNDS, amps=side_h, extent=half, panel_at=half
                    ),
                    columns_of(1, row=MINE, slots=extras, amps=extra_two, extent=moved),
                ],
                2,
            )
            then = terms(
                [
                    columns_of(0, row=LIGHT_0, slots=ROUNDS, amps=on_l, extent=half),
                    columns_of(1, row=LIGHT_1, slots=ROUNDS, amps=on_l, extent=half),
                ],
                2,
            )
            sent = terms(
                [
                    given_to(0, row=FED_1, panel=beside, extent=given, amp_at=moved),
                    given_to(0, row=FED_2, panel=far, extent=given, amp_at=moved),
                ],
                1,
            )[0]
            last = terms(
                [
                    columns_of(
                        0, row=LIGHT_0, slots=ROUNDS, amps=on_h, extent=half, panel_at=half
                    ),
                    columns_of(
                        1, row=LIGHT_1, slots=ROUNDS, amps=on_h, extent=half, panel_at=half
                    ),
                    columns_of(0, row=MINE, slots=extras, amps=extra_one, extent=moved),
                ],
                2,
            )
            one = first[0] + then[0] + last[0]
            two = first[1] + then[1] + last[1]
        else:
            def firsts(at):
                return at in evens and ahead(at)

            lead = take(row=LEAD, part=PART, slots=2 * ROUNDS, start=0, extent=half)
            got_lead = send(lead, hops(lambda at: at in odds or ahead(at)))
            far_0 = send(cut(start=half, extent=quarter), backs(firsts))
            extra_0 = take(row=MINE, slots=extras, start=0, extent=quarter)
            cross = send(extra_0, down)
            near = take(row=NEXT, slots=ROUNDS, start=0, extent=d_extent)
            side = send(near, up)
            far_1 = send(cut(start=half + quarter, extent=quarter), backs(firsts))

            extra_1 = take(row=MINE, slots=extras, start=quarter, extent=quarter)
            cross = tied(cross, here)
            got_extra = send(jnp.where(is_first, cross, extra_1), hops(ahead))
            far_0 = tied(far_0, here, cross)
            up_0 = send(far_0, up)
            lead_down = send(got_lead, down)
            after_l = after(start=0, behind=[got_lead, side])
            got_l = send(after_l, around)
            far_1 = tied(far_1, after_l)
            up_1 = send(far_1, up)
            after_h = after(start=half, behind=[far_1, got_extra])
            got_h = send(after_h, around)
            extra_down = send(tied(got_extra, after_h), down)

            first = terms(
                [
                    columns_of(0, row=LIGHT_1, slots=ROUNDS, amps=side, extent=d_extent),
                    columns_of(1, row=MINE, slots=extras, amps=got_lead, extent=half),
                ],
                2,
            )
            fed = functools.partial(given_to, 0, extent=quarter)
            then = terms(
                [
                    fed(row=FED_1, panel=up_0, amp_at=half),
                    fed(row=FED_2, panel=far_0, amp_at=half),
                    fed(row=FED_2, panel=far_1, amp_at=half + quarter),
                    columns_of(1, row=MINE, slots=extras, amps=got_extra, extent=quarter),
                    columns_of(2, row=LIGHT, slots=ROUNDS, amps=got_l, extent=half),
                ],
                3,
            )
            low = terms(
                [
                    columns_of(0, row=LIGHT_0, slots=ROUNDS, amps=lead_down, extent=half),
                    columns_of(
                        0,
                        row=LIGHT_0,
                        slots=ROUNDS,
                        amps=lead_down,
                        extent=half,
                        panel_at=half,
                        slot_at=ROUNDS,
                    ),
                ],
                1,
            )
            sent = then[0]
            sent += terms([fed(row=FED_1, panel=up_1, amp_at=half + quarter)], 1)[0]
            last = terms(
                [
                    columns_of(
                        1, row=LIGHT, slots=ROUNDS, amps=got_h, extent=half, panel_at=half
                    ),
                    columns_of(
                        0,
                        row=MINE,
                        slots=extras,
                        amps=extra_down,
                        extent=quarter,
                        panel_at=quarter,
                    ),
                ],
                2,
            )
            one = first[0] + then[1] + low[0] + last[0]
            two = first[1] + then[2] + last[1]
        one += rotated(jnp.where(feeds_one, sent, 0.0), 1)
        two += rotated(jnp.where(feeds_two, sent, 0.0), 2)

        return jnp.stack([here[0], one, two])

    branches = [
        functools.partial(run, wrapped, odd) for wrapped in (False, True) for odd in (False, True)
    ]
    operands = (lists, factors_a, factors_b, amplitudes)
    terms = lax.switch(lists[MISC * ROW], branches, operands)
    def add_round(r, running):
        one, two = running

        def only(row, count):
            sub = lax.dynamic_slice_in_dim(lists, row * ROW + r, 1)
            return jnp.concatenate([sub, jnp.zeros(MOST - 1, jnp.int32), count.reshape(1)])

        has = jnp.where((r < lists[OWN * ROW + MOST]) & ~is_full, 1, 0).astype(jnp.int32)
        own = only(OWN, has)
        moved = [
            rotated(
                take_columns(only(row, has), amplitudes, 0, 1, width, 0, d_extent), by
            )
            for row, by in ((NEXT, 1), (AFTER, 2))
        ]
        more = pair_terms(
            own,
            factors_a,
            [
                Segment(into, 0, 1, columns, factors_b, d_extent)
                for into, columns in enumerate(moved)
            ],
            2,
            width,
            d_rows,
        )
        return one + more[0], two + more[1]

    one, two = lax.fori_loop(
        ROUNDS, jnp.maximum(others, ROUNDS), add_round, (terms[1], terms[2])
    )
    terms = jnp.stack([terms[0], one, two])
    a_rows = factors_a.shape[0]
    terms = terms.reshape(STEPS, a_rows, pairs, -1).swapaxes(1, 2).reshape(STEPS, 1, -1)
    return summed_over_narrow(terms)


def solution(mesh):
    return jax.shard_map(
        local,
        mesh=mesh,
        in_specs=(P(), P("blk", "narrow", None), P("blk", "narrow", None), P()),
        out_specs=P(None, "blk", "narrow"),
        check_vma=False,
    )
```

```python
import functools

import jax
import jax.numpy as jnp
from jax import lax
from jax.experimental import pallas as pl
from jax.experimental.pallas import tpu as pltpu
from jax.sharding import PartitionSpec as P

STEPS = 3
MOST = 8
ROUNDS = 3
GROUP = 16
LANES = 128
ROW = MOST + 1

(
    OWN,
    LIGHT,
    LIGHT_0,
    LIGHT_1,
    NEXT,
    AFTER,
    LEAD,
    PART,
    MINE,
    FED_1,
    FED_2,
    MISC,
) = range(12)
FIRST = MISC * ROW + 3
AHEAD = 4
VMEM = 60 * 1024 * 1024
SMALL = pl.CostEstimate(flops=1024, bytes_accessed=1024, transcendentals=0)


def send(value, pairs):
    return lax.ppermute(value, "blk", pairs)


def rotated(value, by):
    size = lax.axis_size("blk")
    return send(value, [(i, (i + by) % size) for i in range(size)])


def lists_kernel(position_ref, screen_ref, out_ref):
    tiles, subs = screen_ref.shape
    position = position_ref[0]

    def count_of(tile):
        return sum(jnp.where(screen_ref[tile, s] != 0, 1, 0) for s in range(subs))

    def look(tile, found):
        best, fullest, others = found
        count = count_of(tile)
        larger = count > best
        others = jnp.where(larger, best, jnp.maximum(others, count))
        return jnp.where(larger, count, best), jnp.where(larger, tile, fullest), others

    zero = jnp.int32(0)
    best, fullest, others = lax.fori_loop(0, tiles, look, (zero, zero, zero))

    def fill(row, tile, skip, count):
        for k in range(MOST):
            out_ref[row * ROW + k] = 0
        seen = jnp.int32(0)
        for s in range(subs):
            kept = screen_ref[tile, s] != 0

            @pl.when(kept & (seen >= skip))
            def _():
                out_ref[row * ROW + seen - skip] = s

            seen += jnp.where(kept, 1, 0)
        out_ref[row * ROW + MOST] = seen if count is None else count

    following = lax.rem(position + 1, tiles)
    second = lax.rem(position + 2, tiles)
    is_first = lax.rem(position, 2) == 0
    own_count = count_of(position)
    extra = jnp.maximum(best - ROUNDS, 0)
    light = jnp.minimum(own_count, ROUNDS)
    fill(OWN, position, 0, own_count)
    fill(LIGHT, position, 0, light)
    fill(LIGHT_0, position, 0, jnp.where(is_first, light, 0))
    fill(LIGHT_1, position, 0, jnp.where(is_first, 0, light))
    fill(NEXT, following, 0, None)
    fill(AFTER, second, 0, None)
    fill(MINE, fullest, ROUNDS, jnp.where(position == fullest, extra, 0))
    fill(FED_1, fullest, ROUNDS, jnp.where(following == fullest, extra, 0))
    fill(FED_2, fullest, ROUNDS, jnp.where(second == fullest, extra, 0))
    for k in range(ROW):
        other = out_ref[NEXT * ROW + k % ROUNDS] if k < 2 * ROUNDS else 0
        out_ref[LEAD * ROW + k] = jnp.where(is_first, out_ref[MINE * ROW + k], other)
        out_ref[PART * ROW + k] = jnp.where(is_first, 0, k // ROUNDS)
    out_ref[MISC * ROW] = jnp.where(fullest < 2, 2, 0) + lax.rem(fullest, 2)
    out_ref[MISC * ROW + 1] = fullest
    out_ref[MISC * ROW + 2] = others
    out_ref[FIRST] = jnp.where(is_first, 1, 0)
    for k in range(4, ROW):
        out_ref[MISC * ROW + k] = 0


def kept_lists(position, screen):
    return pl.pallas_call(
        lists_kernel,
        in_specs=[pl.BlockSpec(memory_space=pltpu.SMEM)] * 2,
        out_specs=pl.BlockSpec(memory_space=pltpu.SMEM),
        out_shape=jax.ShapeDtypeStruct(((MISC + 1) * ROW,), jnp.int32),
        name="kept_lists",
    )(position.reshape(1), screen)


def staged(count, load_from, target_of, stage, sems):
    def load(n, carry):
        load_from(
            n, lambda source: pltpu.make_async_copy(source, stage.at[n], sems.at[0, n]).start()
        )
        return carry

    def store(n, carry):
        pltpu.make_async_copy(stage.at[n], stage.at[n], sems.at[0, n]).wait()
        pltpu.make_async_copy(stage.at[n], target_of(n), sems.at[1, n]).start()
        return carry

    def finish(n, carry):
        pltpu.make_async_copy(stage.at[n], stage.at[n], sems.at[1, n]).wait()
        return carry

    for act in (load, store, finish):
        lax.fori_loop(0, count, act, 0)


def take_kernel(row, slots, start, extent, part, passes, lists_ref, source, *refs):
    out, stage, sems = refs[-3:]
    width = out.shape[-1]

    def columns(s, act):
        sub = pl.multiple_of(lists_ref[row * ROW + s] * width, width)
        first = start
        if part is not None:
            first = pl.multiple_of(start + lists_ref[part * ROW + s] * extent, extent)
        act(source.at[:, pl.ds(first, extent), pl.ds(sub, width)])

    def load_from(s, act):
        if passes:
            pl.when(lists_ref[FIRST] != 0)(lambda: act(refs[0].at[s]))
            pl.when(lists_ref[FIRST] == 0)(lambda: columns(s, act))
        else:
            columns(s, act)

    staged(slots, load_from, lambda s: out.at[s], stage, sems)


def take_columns(
    lists, amplitudes, row, slots, width, start, extent, behind=(), part=None, passing=None
):
    pairs = amplitudes.shape[0]
    others = ([] if passing is None else [passing]) + list(behind)
    return pl.pallas_call(
        functools.partial(take_kernel, row, slots, start, extent, part, passing is not None),
        in_specs=[pl.BlockSpec(memory_space=pltpu.SMEM)]
        + [pl.BlockSpec(memory_space=pltpu.HBM)] * (1 + len(others)),
        out_specs=pl.BlockSpec(memory_space=pltpu.HBM),
        out_shape=jax.ShapeDtypeStruct((slots, pairs, extent, width), amplitudes.dtype),
        scratch_shapes=[
            pltpu.VMEM((slots, pairs, extent, width), amplitudes.dtype),
            pltpu.SemaphoreType.DMA((2, slots)),
        ],
        compiler_params=pltpu.CompilerParams(vmem_limit_bytes=VMEM),
        cost_estimate=SMALL,
        name="take_columns",
    )(lists, amplitudes, *others)


def panel_kernel(start, panel, *refs):
    out, stage, sems = refs[-3:]
    parts, share, extent, _ = stage.shape

    def rows(n):
        return pl.ds(n * share, share)

    staged(
        parts,
        lambda n, act: act(panel.at[rows(n), pl.ds(start, extent), :]),
        lambda n: out.at[rows(n)],
        stage,
        sems,
    )


def take_panel(panel, start, extent, behind=()):
    b_rows, _, aux = panel.shape
    return pl.pallas_call(
        functools.partial(panel_kernel, start),
        in_specs=[pl.BlockSpec(memory_space=pltpu.HBM)] * (1 + len(behind)),
        out_specs=pl.BlockSpec(memory_space=pltpu.HBM),
        out_shape=jax.ShapeDtypeStruct((b_rows, extent, aux), panel.dtype),
        scratch_shapes=[
            pltpu.VMEM((4, b_rows // 4, extent, aux), panel.dtype),
            pltpu.SemaphoreType.DMA((2, 4)),
        ],
        compiler_params=pltpu.CompilerParams(vmem_limit_bytes=VMEM),
        cost_estimate=SMALL,
        name="take_panel",
    )(panel, *behind)


def tie_kernel(*refs):
    pass


def tied(value, *behind):
    return pl.pallas_call(
        tie_kernel,
        in_specs=[pl.BlockSpec(memory_space=pltpu.HBM)] * (1 + len(behind)),
        out_specs=pl.BlockSpec(memory_space=pltpu.HBM),
        out_shape=jax.ShapeDtypeStruct(value.shape, value.dtype),
        input_output_aliases={0: 0},
        cost_estimate=SMALL,
        name="tied",
    )(value, *behind)


class Segment:
    def __init__(self, into, row, slots, amps, panel, extent, amp_at=0, panel_at=0, slot_at=0):
        self.into, self.row, self.slots = into, row, slots
        self.amps, self.panel, self.extent = amps, panel, extent
        self.amp_at, self.panel_at, self.slot_at = amp_at, panel_at, slot_at


def terms_kernel(segments, places, d_rows, lists_ref, *refs):
    arrays = refs[: -8]
    out_ref, amp_buf, panel_buf, factor_buf, mixed, total, sems, factor_sems = refs[-8:]
    factors = arrays[0]
    outs = out_ref.shape[0]
    _, most, pairs, _, width = amp_buf.shape
    b_rows = panel_buf.shape[1]
    _, _, a_rows, _, aux = factor_buf.shape

    counts = [lists_ref[seg.row * ROW + MOST] for seg in segments]
    starts, orders = [], []
    begin = order = jnp.int32(0)
    for seg, count in zip(segments, counts):
        starts.append(begin)
        orders.append(order)
        begin = begin + jnp.where(count > 0, seg.extent // d_rows, 0)
        order = order + jnp.where(count > 0, 1, 0)
    items = begin

    def pick(at, values):
        found = values[0]
        for s in range(1, len(segments)):
            found = jnp.where(at == s, values[s], found)
        return found

    def locate(t):
        at = jnp.int32(0)
        for s in range(len(segments)):
            at = jnp.where((counts[s] > 0) & (t >= starts[s]), s, at)
        return at, t - pick(at, starts), lax.rem(pick(at, orders), AHEAD)

    def fetch(t):
        at, block, turn = locate(t)
        slot = lax.rem(t, AHEAD)
        for s, seg in enumerate(segments):
            amps, panel = arrays[places[s][0]], arrays[places[s][1]]

            @pl.when(at == s)
            def _():
                amp_d = pl.ds(pl.multiple_of(seg.amp_at + block * d_rows, d_rows), d_rows)
                panel_d = pl.ds(pl.multiple_of(seg.panel_at + block * d_rows, d_rows), d_rows)
                pltpu.make_async_copy(
                    panel.at[:, panel_d, :], panel_buf.at[slot], sems.at[slot, most]
                ).start()

                def one(k, carry):
                    sub = pl.multiple_of(lists_ref[seg.row * ROW + k] * width, width)
                    columns = pl.ds(sub, width)
                    if len(amps.shape) == 3:
                        source = amps.at[:, amp_d, columns]
                    else:
                        source = amps.at[seg.slot_at + k, :, amp_d, :]
                    pltpu.make_async_copy(
                        source, amp_buf.at[slot, k], sems.at[slot, k]
                    ).start()

                    @pl.when(block == 0)
                    def _():
                        pltpu.make_async_copy(
                            factors.at[:, columns, :],
                            factor_buf.at[turn, k],
                            factor_sems.at[turn, k],
                        ).start()

                    return carry

                lax.fori_loop(0, counts[s], one, 0)

    def arrive(slot, block, turn, count):
        pltpu.make_async_copy(
            panel_buf.at[slot], panel_buf.at[slot], sems.at[slot, most]
        ).wait()

        def one(k, carry):
            pltpu.make_async_copy(
                amp_buf.at[slot, k], amp_buf.at[slot, k], sems.at[slot, k]
            ).wait()

            @pl.when(block == 0)
            def _():
                pltpu.make_async_copy(
                    factor_buf.at[turn, k], factor_buf.at[turn, k], factor_sems.at[turn, k]
                ).wait()

            return carry

        lax.fori_loop(0, count, one, 0)

    total[...] = jnp.zeros_like(total)

    def mix(low, top, slot, turn, count):
        columns = [amp_buf[slot, k].reshape(pairs * d_rows, width) for k in range(top)]
        for k in range(low, top):
            columns[k] = jnp.where(k < count, columns[k], jnp.zeros_like(columns[k]))
        lhs = jnp.concatenate(columns, axis=1)
        for a in range(a_rows):
            rows = [factor_buf[turn, k, a] for k in range(top)]
            for k in range(low, top):
                rows[k] = jnp.where(k < count, rows[k], jnp.zeros_like(rows[k]))
            product = jnp.dot(
                lhs, jnp.concatenate(rows, axis=0), preferred_element_type=jnp.float32
            )
            mixed[a] = product.astype(mixed.dtype).reshape(pairs, d_rows, aux)

    def step(n, carry):
        @pl.when(n < items)
        def _():
            fetch(n)

        @pl.when(n >= AHEAD - 1)
        def _():
            t = n - (AHEAD - 1)
            at, block, turn = locate(t)
            slot = lax.rem(t, AHEAD)
            count = pick(at, counts)
            into = pick(at, [seg.into for seg in segments])
            arrive(slot, block, turn, count)
            tops = set()
            for slots in {seg.slots for seg in segments}:
                tops |= {slots} | ({2, 4} if slots == MOST else {2} if slots <= ROUNDS else set())
            tops = sorted(tops)
            for low, top in zip([0] + tops, tops):

                @pl.when((count > low) & (count <= top))
                def _():
                    mix(low + 1, top, slot, turn, count)

            partial = total[into]
            for g in range(0, d_rows, GROUP):
                lhs = jnp.concatenate(
                    [mixed[a, :, g : g + GROUP, :].reshape(-1, aux) for a in range(a_rows)],
                    axis=0,
                )
                rhs = panel_buf[slot, :, g : g + GROUP, :].reshape(b_rows * GROUP, aux)
                partial += lax.dot_general(
                    lhs, rhs, (((1,), (1,)), ((), ())), preferred_element_type=jnp.float32
                )
            total[into] = partial

        return carry

    lax.fori_loop(0, jnp.where(items > 0, items + AHEAD - 1, 0), step, 0)

    def finish(o, carry):
        _, rows, columns = total.shape
        row_d = lax.broadcasted_iota(jnp.int32, (rows, columns), 0) % GROUP
        column_d = lax.broadcasted_iota(jnp.int32, (rows, columns), 1) % GROUP
        kept = jnp.where(row_d == column_d, total[o], 0.0)
        kept = kept.reshape(rows // GROUP, GROUP, columns).sum(axis=1)
        from_b = lax.broadcasted_iota(jnp.int32, (columns, LANES), 0) // GROUP
        to_b = lax.broadcasted_iota(jnp.int32, (columns, LANES), 1)
        gather = jnp.where(from_b == to_b, 1.0, 0.0)
        out_ref[o] = jnp.dot(
            kept, gather, precision=lax.Precision.HIGHEST, preferred_element_type=jnp.float32
        )
        return carry

    lax.fori_loop(0, outs, finish, 0)


def pair_terms(lists, factors_a, segments, outs, width, d_rows, behind=()):
    arrays, places = [factors_a], []
    for seg in segments:
        place = []
        for array in (seg.amps, seg.panel):
            known = [n for n, other in enumerate(arrays) if other is array]
            place.append(known[0] if known else len(arrays))
            if not known:
                arrays.append(array)
        places.append(place)
    arrays += behind
    a_rows, _, aux = factors_a.shape
    pairs = segments[0].amps.shape[-3]
    b_rows = segments[0].panel.shape[0]
    most = max(2, *(seg.slots for seg in segments))
    return pl.pallas_call(
        functools.partial(terms_kernel, segments, places, d_rows),
        in_specs=[pl.BlockSpec(memory_space=pltpu.SMEM)]
        + [pl.BlockSpec(memory_space=pltpu.HBM)] * len(arrays),
        out_specs=pl.BlockSpec(memory_space=pltpu.VMEM),
        scratch_shapes=[
            pltpu.VMEM((AHEAD, most, pairs, d_rows, width), jnp.bfloat16),
            pltpu.VMEM((AHEAD, b_rows, d_rows, aux), jnp.bfloat16),
            pltpu.VMEM((AHEAD, most, a_rows, width, aux), jnp.bfloat16),
            pltpu.VMEM((a_rows, pairs, d_rows, aux), jnp.bfloat16),
            pltpu.VMEM((outs, a_rows * pairs * GROUP, b_rows * GROUP), jnp.float32),
            pltpu.SemaphoreType.DMA((AHEAD, most + 1)),
            pltpu.SemaphoreType.DMA((AHEAD, most)),
        ],
        out_shape=jax.ShapeDtypeStruct((outs, a_rows * pairs, LANES), jnp.float32),
        compiler_params=pltpu.CompilerParams(vmem_limit_bytes=VMEM),
        cost_estimate=SMALL,
        name="pair_terms",
    )(lists, *arrays)


def summed_over_narrow(value):
    size = lax.axis_size("narrow")
    me = lax.axis_index("narrow")
    share = value.shape[2] // size

    def part(owner):
        return lax.dynamic_slice_in_dim(value, owner * share, share, 2)

    parts = [part(me)]
    for k in range(1, size):
        to = [(i, (i + k) % size) for i in range(size)]
        parts.append(lax.ppermute(part((me + k) % size), "narrow", to))
    return sum(parts[1:], parts[0])


def local(factors_a, factors_b, amplitudes, screen):
    pairs, d_extent, virtuals = amplitudes.shape
    width = virtuals // screen.shape[1]
    tiles = lax.axis_size("blk")
    position = lax.axis_index("blk")
    extras = MOST - ROUNDS
    d_rows = min(64, d_extent // 4)

    lists = kept_lists(position, screen)
    fullest = lists[MISC * ROW + 1]
    others = lists[MISC * ROW + 2]
    is_first = position % 2 == 0
    is_full = position == fullest
    feeds_one = (position + 1) % tiles == fullest
    feeds_two = (position + 2) % tiles == fullest

    evens, odds = range(0, tiles, 2), range(1, tiles, 2)
    up = [(i, i + 1) for i in evens]
    down = [(i + 1, i) for i in evens]
    around = [(i, (i + 2) % tiles) for i in range(tiles)]

    def run(wrapped, odd, operands):
        lists, factors_a, factors_b, amplitudes = operands
        terms = functools.partial(pair_terms, lists, factors_a, width=width, d_rows=d_rows)
        columns_of = functools.partial(Segment, panel=factors_b)
        given_to = functools.partial(Segment, amps=amplitudes, slots=extras)
        take = functools.partial(take_columns, lists, amplitudes, width=width)
        cut = functools.partial(take_panel, factors_b)

        def ahead(at):
            return (at >= tiles - 2) == wrapped

        def hops(keep):
            return [(at, to) for at, to in around if keep(at)]

        def backs(keep):
            return [(to, at) for at, to in around if keep(at)]

        half, quarter = d_extent // 2, d_extent // 4
        own = [columns_of(0, row=OWN, slots=MOST, amps=amplitudes, extent=d_extent)]
        after = functools.partial(take, row=AFTER, slots=ROUNDS, extent=half)
        near = functools.partial(take, row=NEXT, slots=ROUNDS)
        light = functools.partial(columns_of, slots=ROUNDS)
        mine = functools.partial(columns_of, row=MINE, slots=extras)
        if odd:
            given = max(3 * d_extent // 8 // d_rows, 1) * d_rows
            moved = d_extent - given

            def seconds(at):
                return at in odds and ahead(at)

            near_l = near(start=0, extent=half)
            side_l = send(near_l, up + down)
            direct = take(
                row=AFTER, slots=ROUNDS, start=0, extent=d_extent, behind=[near_l]
            )
            got_direct = send(direct, hops(lambda at: at in evens))
            extra = take(row=MINE, slots=extras, start=0, extent=moved, behind=[direct])
            extra_two = send(extra, hops(seconds))
            near_h = near(start=half, extent=half, behind=[extra])
            side_h = send(near_h, up + down)
            panel = cut(start=moved, extent=given, behind=[near_h])
            far = send(panel, backs(seconds))
            here = terms(own, 1, behind=[panel])

            pass_l = after(start=0, passing=side_l, behind=[here])
            on_l = send(pass_l, around)
            panel = cut(start=moved, extent=given, behind=[pass_l])
            beside = send(panel, down)
            extra = take(row=MINE, slots=extras, start=0, extent=moved, behind=[panel])
            extra = tied(extra, side_h, got_direct, far)
            extra_one = send(extra, up)
            pass_h = after(start=half, passing=side_h, behind=[extra, extra_two])
            on_h = send(pass_h, around)

            first = terms(
                [
                    light(1, row=LIGHT_0, amps=got_direct, extent=d_extent),
                    light(0, row=LIGHT_1, amps=side_l, extent=half),
                    light(0, row=LIGHT_1, amps=side_h, extent=half, panel_at=half),
                    mine(1, amps=extra_two, extent=moved),
                ],
                2,
                behind=[pass_h],
            )
            then = terms(
                [
                    light(0, row=LIGHT_0, amps=on_l, extent=half),
                    light(1, row=LIGHT_1, amps=on_l, extent=half),
                ],
                2,
                behind=[first],
            )
            sent = terms(
                [
                    given_to(0, row=FED_1, panel=beside, extent=given, amp_at=moved),
                    given_to(0, row=FED_2, panel=far, extent=given, amp_at=moved),
                ],
                1,
                behind=[then],
            )
            last = terms(
                [
                    light(0, row=LIGHT_0, amps=on_h, extent=half, panel_at=half),
                    light(1, row=LIGHT_1, amps=on_h, extent=half, panel_at=half),
                    mine(0, amps=extra_one, extent=moved),
                ],
                2,
                behind=[sent],
            )
            sent = sent[0]
            one = first[0] + then[0] + last[0]
            two = first[1] + then[1] + last[1]
        else:
            def firsts(at):
                return at in evens and ahead(at)

            lead = take(row=LEAD, part=PART, slots=2 * ROUNDS, start=0, extent=half)
            got_lead = send(lead, hops(lambda at: at in odds or ahead(at)))
            extra = take(row=MINE, slots=extras, start=0, extent=quarter, behind=[lead])
            cross = send(extra, down)
            panel = cut(start=half, extent=quarter, behind=[extra])
            far_0 = send(panel, backs(firsts))
            beside = near(start=0, extent=d_extent, behind=[panel])
            side = send(beside, up)
            panel = cut(start=half + quarter, extent=quarter, behind=[beside])
            far_1 = send(panel, backs(firsts))
            here = terms(own, 1, behind=[panel])

            extra = take(
                row=MINE,
                slots=extras,
                start=quarter,
                extent=quarter,
                passing=cross,
                behind=[here],
            )
            got_extra = send(extra, hops(ahead))
            far_0 = tied(far_0, extra)
            up_0 = send(far_0, up)
            lead_down = send(got_lead, down)
            after_l = after(start=0, behind=[far_0, got_lead, side])
            got_l = send(after_l, around)
            far_1 = tied(far_1, after_l)
            up_1 = send(far_1, up)
            after_h = after(start=half, behind=[far_1, got_extra])
            got_h = send(after_h, around)

            first = terms(
                [
                    light(0, row=LIGHT_1, amps=side, extent=d_extent),
                    mine(1, amps=got_lead, extent=half),
                ],
                2,
                behind=[after_h],
            )
            got_extra = tied(got_extra, first, up_0)
            extra_down = send(got_extra, down)
            fed = functools.partial(given_to, 0, extent=quarter)
            then = terms(
                [
                    fed(row=FED_1, panel=up_0, amp_at=half),
                    fed(row=FED_2, panel=far_0, amp_at=half),
                    fed(row=FED_2, panel=far_1, amp_at=half + quarter),
                    mine(1, amps=got_extra, extent=quarter),
                    light(2, row=LIGHT, amps=got_l, extent=half),
                ],
                3,
            )
            down_part = functools.partial(light, 0, row=LIGHT_0, amps=lead_down, extent=half)
            low = terms(
                [down_part(), down_part(panel_at=half, slot_at=ROUNDS)], 1, behind=[then]
            )
            sent = terms(
                [fed(row=FED_1, panel=up_1, amp_at=half + quarter)], 1, behind=[low]
            )
            last = terms(
                [
                    light(1, row=LIGHT, amps=got_h, extent=half, panel_at=half),
                    mine(0, amps=extra_down, extent=quarter, panel_at=quarter),
                ],
                2,
                behind=[sent],
            )
            sent = then[0] + sent[0]
            one = first[0] + then[1] + low[0] + last[0]
            two = first[1] + then[2] + last[1]
        one += rotated(jnp.where(feeds_one, sent, 0.0), 1)
        two += rotated(jnp.where(feeds_two, sent, 0.0), 2)

        return jnp.stack([here[0], one, two])

    branches = [
        functools.partial(run, wrapped, odd) for wrapped in (False, True) for odd in (False, True)
    ]
    operands = (lists, factors_a, factors_b, amplitudes)
    terms = lax.switch(lists[MISC * ROW], branches, operands)
    def add_round(r, running):
        one, two = running

        def only(row, count):
            sub = lax.dynamic_slice_in_dim(lists, row * ROW + r, 1)
            return jnp.concatenate([sub, jnp.zeros(MOST - 1, jnp.int32), count.reshape(1)])

        has = jnp.where((r < lists[OWN * ROW + MOST]) & ~is_full, 1, 0).astype(jnp.int32)
        own = only(OWN, has)
        moved = [
            rotated(
                take_columns(only(row, has), amplitudes, 0, 1, width, 0, d_extent), by
            )
            for row, by in ((NEXT, 1), (AFTER, 2))
        ]
        more = pair_terms(
            own,
            factors_a,
            [
                Segment(into, 0, 1, columns, factors_b, d_extent)
                for into, columns in enumerate(moved)
            ],
            2,
            width,
            d_rows,
        )
        return one + more[0], two + more[1]

    one, two = lax.fori_loop(
        ROUNDS, jnp.maximum(others, ROUNDS), add_round, (terms[1], terms[2])
    )
    terms = jnp.stack([terms[0], one, two])
    a_rows = factors_a.shape[0]
    terms = terms[:, :, : factors_b.shape[0]]
    terms = terms.reshape(STEPS, a_rows, pairs, -1).swapaxes(1, 2).reshape(STEPS, 1, -1)
    return summed_over_narrow(terms)


def solution(mesh):
    return jax.shard_map(
        local,
        mesh=mesh,
        in_specs=(P(), P("blk", "narrow", None), P("blk", "narrow", None), P()),
        out_specs=P(None, "blk", "narrow"),
        check_vma=False,
    )
```

```python
import functools

import jax
import jax.numpy as jnp
from jax import lax
from jax.experimental import pallas as pl
from jax.experimental.pallas import tpu as pltpu
from jax.sharding import PartitionSpec as P

STEPS = 3
MOST = 8
ROUNDS = 3
GROUP = 16
LANES = 128
ROW = MOST + 1

(
    OWN,
    LIGHT,
    LIGHT_0,
    LIGHT_1,
    NEXT,
    AFTER,
    LEAD,
    PART,
    MINE,
    FED_1,
    FED_2,
    MISC,
) = range(12)
FIRST = MISC * ROW + 3
AHEAD = 4
PARTS = 4
VMEM = 60 * 1024 * 1024
SMALL = pl.CostEstimate(flops=1024, bytes_accessed=1024, transcendentals=0)


def send(value, pairs):
    return lax.ppermute(value, "blk", pairs)


def rotated(value, by):
    size = lax.axis_size("blk")
    return send(value, [(i, (i + by) % size) for i in range(size)])


def lists_kernel(position_ref, screen_ref, out_ref):
    tiles, subs = screen_ref.shape
    position = position_ref[0]

    def count_of(tile):
        return sum(jnp.where(screen_ref[tile, s] != 0, 1, 0) for s in range(subs))

    def look(tile, found):
        best, fullest, others = found
        count = count_of(tile)
        larger = count > best
        others = jnp.where(larger, best, jnp.maximum(others, count))
        return jnp.where(larger, count, best), jnp.where(larger, tile, fullest), others

    zero = jnp.int32(0)
    best, fullest, others = lax.fori_loop(0, tiles, look, (zero, zero, zero))

    def fill(row, tile, skip, count):
        for k in range(MOST):
            out_ref[row * ROW + k] = 0
        seen = jnp.int32(0)
        for s in range(subs):
            kept = screen_ref[tile, s] != 0

            @pl.when(kept & (seen >= skip))
            def _():
                out_ref[row * ROW + seen - skip] = s

            seen += jnp.where(kept, 1, 0)
        out_ref[row * ROW + MOST] = seen if count is None else count

    following = lax.rem(position + 1, tiles)
    second = lax.rem(position + 2, tiles)
    is_first = lax.rem(position, 2) == 0
    own_count = count_of(position)
    extra = jnp.maximum(best - ROUNDS, 0)
    light = jnp.minimum(own_count, ROUNDS)
    fill(OWN, position, 0, own_count)
    fill(LIGHT, position, 0, light)
    fill(LIGHT_0, position, 0, jnp.where(is_first, light, 0))
    fill(LIGHT_1, position, 0, jnp.where(is_first, 0, light))
    fill(NEXT, following, 0, None)
    fill(AFTER, second, 0, None)
    fill(MINE, fullest, ROUNDS, jnp.where(position == fullest, extra, 0))
    fill(FED_1, fullest, ROUNDS, jnp.where(following == fullest, extra, 0))
    fill(FED_2, fullest, ROUNDS, jnp.where(second == fullest, extra, 0))
    for k in range(ROW):
        other = out_ref[NEXT * ROW + k % ROUNDS] if k < 2 * ROUNDS else 0
        out_ref[LEAD * ROW + k] = jnp.where(is_first, out_ref[MINE * ROW + k], other)
        out_ref[PART * ROW + k] = jnp.where(is_first, 0, k // ROUNDS)
    out_ref[MISC * ROW] = jnp.where(fullest < 2, 2, 0) + lax.rem(fullest, 2)
    out_ref[MISC * ROW + 1] = fullest
    out_ref[MISC * ROW + 2] = others
    out_ref[FIRST] = jnp.where(is_first, 1, 0)
    for k in range(4, ROW):
        out_ref[MISC * ROW + k] = 0


def kept_lists(position, screen):
    return pl.pallas_call(
        lists_kernel,
        in_specs=[pl.BlockSpec(memory_space=pltpu.SMEM)] * 2,
        out_specs=pl.BlockSpec(memory_space=pltpu.SMEM),
        out_shape=jax.ShapeDtypeStruct(((MISC + 1) * ROW,), jnp.int32),
        name="kept_lists",
    )(position.reshape(1), screen)


def staged(count, load_from, target_of, stage, sems):
    def load(n, carry):
        load_from(
            n, lambda source: pltpu.make_async_copy(source, stage.at[n], sems.at[0, n]).start()
        )
        return carry

    def store(n, carry):
        pltpu.make_async_copy(stage.at[n], stage.at[n], sems.at[0, n]).wait()
        pltpu.make_async_copy(stage.at[n], target_of(n), sems.at[1, n]).start()
        return carry

    def finish(n, carry):
        pltpu.make_async_copy(stage.at[n], stage.at[n], sems.at[1, n]).wait()
        return carry

    for act in (load, store, finish):
        lax.fori_loop(0, count, act, 0)


def take_kernel(row, slots, start, extent, part, passes, lists_ref, source, *refs):
    out, stage, sems = refs[-3:]
    width = out.shape[-1]

    def columns(s, act):
        sub = pl.multiple_of(lists_ref[row * ROW + s] * width, width)
        first = start
        if part is not None:
            first = pl.multiple_of(start + lists_ref[part * ROW + s] * extent, extent)
        act(source.at[:, pl.ds(first, extent), pl.ds(sub, width)])

    def load_from(s, act):
        if passes:
            pl.when(lists_ref[FIRST] != 0)(lambda: act(refs[0].at[s]))
            pl.when(lists_ref[FIRST] == 0)(lambda: columns(s, act))
        else:
            columns(s, act)

    staged(slots, load_from, lambda s: out.at[s], stage, sems)


def take_columns(
    lists, amplitudes, row, slots, width, start, extent, behind=(), part=None, passing=None
):
    pairs = amplitudes.shape[0]
    others = ([] if passing is None else [passing]) + list(behind)
    return pl.pallas_call(
        functools.partial(take_kernel, row, slots, start, extent, part, passing is not None),
        in_specs=[pl.BlockSpec(memory_space=pltpu.SMEM)]
        + [pl.BlockSpec(memory_space=pltpu.HBM)] * (1 + len(others)),
        out_specs=pl.BlockSpec(memory_space=pltpu.HBM),
        out_shape=jax.ShapeDtypeStruct((slots, pairs, extent, width), amplitudes.dtype),
        scratch_shapes=[
            pltpu.VMEM((slots, pairs, extent, width), amplitudes.dtype),
            pltpu.SemaphoreType.DMA((2, slots)),
        ],
        compiler_params=pltpu.CompilerParams(vmem_limit_bytes=VMEM),
        cost_estimate=SMALL,
        name="take_columns",
    )(lists, amplitudes, *others)


def panel_kernel(start, panel, *refs):
    out, stage, sems = refs[-3:]
    parts, share, extent, _ = stage.shape

    def rows(n):
        return pl.ds(n * share, share)

    staged(
        parts,
        lambda n, act: act(panel.at[rows(n), pl.ds(start, extent), :]),
        lambda n: out.at[rows(n)],
        stage,
        sems,
    )


def take_panel(panel, start, extent, behind=()):
    b_rows, _, aux = panel.shape
    return pl.pallas_call(
        functools.partial(panel_kernel, start),
        in_specs=[pl.BlockSpec(memory_space=pltpu.HBM)] * (1 + len(behind)),
        out_specs=pl.BlockSpec(memory_space=pltpu.HBM),
        out_shape=jax.ShapeDtypeStruct((b_rows, extent, aux), panel.dtype),
        scratch_shapes=[
            pltpu.VMEM((PARTS, b_rows // PARTS, extent, aux), panel.dtype),
            pltpu.SemaphoreType.DMA((2, PARTS)),
        ],
        compiler_params=pltpu.CompilerParams(vmem_limit_bytes=VMEM),
        cost_estimate=SMALL,
        name="take_panel",
    )(panel, *behind)


def tie_kernel(*refs):
    pass


def tied(value, *behind):
    return pl.pallas_call(
        tie_kernel,
        in_specs=[pl.BlockSpec(memory_space=pltpu.HBM)] * (1 + len(behind)),
        out_specs=pl.BlockSpec(memory_space=pltpu.HBM),
        out_shape=jax.ShapeDtypeStruct(value.shape, value.dtype),
        input_output_aliases={0: 0},
        cost_estimate=SMALL,
        name="tied",
    )(value, *behind)


class Segment:
    def __init__(self, into, row, slots, amps, panel, extent, amp_at=0, panel_at=0, slot_at=0):
        self.into, self.row, self.slots = into, row, slots
        self.amps, self.panel, self.extent = amps, panel, extent
        self.amp_at, self.panel_at, self.slot_at = amp_at, panel_at, slot_at


def terms_kernel(segments, places, d_rows, lists_ref, *refs):
    arrays = refs[: -8]
    out_ref, amp_buf, panel_buf, factor_buf, mixed, total, sems, factor_sems = refs[-8:]
    factors = arrays[0]
    outs = out_ref.shape[0]
    _, most, pairs, _, width = amp_buf.shape
    b_rows = panel_buf.shape[1]
    share = b_rows // PARTS
    _, _, a_rows, _, aux = factor_buf.shape

    counts = [lists_ref[seg.row * ROW + MOST] for seg in segments]
    starts, orders = [], []
    begin = order = jnp.int32(0)
    for seg, count in zip(segments, counts):
        starts.append(begin)
        orders.append(order)
        begin = begin + jnp.where(count > 0, seg.extent // d_rows, 0)
        order = order + jnp.where(count > 0, 1, 0)
    items = begin

    def pick(at, values):
        found = values[0]
        for s in range(1, len(segments)):
            found = jnp.where(at == s, values[s], found)
        return found

    def locate(t):
        at = jnp.int32(0)
        for s in range(len(segments)):
            at = jnp.where((counts[s] > 0) & (t >= starts[s]), s, at)
        return at, t - pick(at, starts), lax.rem(pick(at, orders), AHEAD)

    def fetch(t):
        at, block, turn = locate(t)
        slot = lax.rem(t, AHEAD)
        for s, seg in enumerate(segments):
            amps, panel = arrays[places[s][0]], arrays[places[s][1]]

            @pl.when(at == s)
            def _():
                amp_d = pl.ds(pl.multiple_of(seg.amp_at + block * d_rows, d_rows), d_rows)
                panel_d = pl.ds(pl.multiple_of(seg.panel_at + block * d_rows, d_rows), d_rows)

                def part(n, carry):
                    rows = pl.ds(n * share, share)
                    pltpu.make_async_copy(
                        panel.at[rows, panel_d, :],
                        panel_buf.at[slot, rows],
                        sems.at[slot, most + n],
                    ).start()
                    return carry

                lax.fori_loop(0, PARTS, part, 0)

                def one(k, carry):
                    sub = pl.multiple_of(lists_ref[seg.row * ROW + k] * width, width)
                    columns = pl.ds(sub, width)
                    if len(amps.shape) == 3:
                        source = amps.at[:, amp_d, columns]
                    else:
                        source = amps.at[seg.slot_at + k, :, amp_d, :]
                    pltpu.make_async_copy(
                        source, amp_buf.at[slot, k], sems.at[slot, k]
                    ).start()

                    @pl.when(block == 0)
                    def _():
                        pltpu.make_async_copy(
                            factors.at[:, columns, :],
                            factor_buf.at[turn, k],
                            factor_sems.at[turn, k],
                        ).start()

                    return carry

                lax.fori_loop(0, counts[s], one, 0)

    def arrive(slot, block, turn, count):
        def part(n, carry):
            rows = panel_buf.at[slot, pl.ds(n * share, share)]
            pltpu.make_async_copy(rows, rows, sems.at[slot, most + n]).wait()
            return carry

        lax.fori_loop(0, PARTS, part, 0)

        def one(k, carry):
            pltpu.make_async_copy(
                amp_buf.at[slot, k], amp_buf.at[slot, k], sems.at[slot, k]
            ).wait()

            @pl.when(block == 0)
            def _():
                pltpu.make_async_copy(
                    factor_buf.at[turn, k], factor_buf.at[turn, k], factor_sems.at[turn, k]
                ).wait()

            return carry

        lax.fori_loop(0, count, one, 0)

    @pl.when(items > 0)
    def _():
        total[...] = jnp.zeros_like(total)

    def mix(low, top, slot, turn, count):
        columns = [amp_buf[slot, k].reshape(pairs * d_rows, width) for k in range(top)]
        for k in range(low, top):
            columns[k] = jnp.where(k < count, columns[k], jnp.zeros_like(columns[k]))
        lhs = jnp.concatenate(columns, axis=1)

        def one(a, carry):
            rows = [factor_buf[turn, k, a] for k in range(top)]
            for k in range(low, top):
                rows[k] = jnp.where(k < count, rows[k], jnp.zeros_like(rows[k]))
            product = jnp.dot(
                lhs, jnp.concatenate(rows, axis=0), preferred_element_type=jnp.float32
            )
            mixed[a] = product.astype(mixed.dtype).reshape(pairs, d_rows, aux)
            return carry

        lax.fori_loop(0, a_rows, one, 0)

    def step(n, carry):
        @pl.when(n < items)
        def _():
            fetch(n)

        @pl.when(n >= AHEAD - 1)
        def _():
            t = n - (AHEAD - 1)
            at, block, turn = locate(t)
            slot = lax.rem(t, AHEAD)
            count = pick(at, counts)
            into = pick(at, [seg.into for seg in segments])
            arrive(slot, block, turn, count)
            tops = set()
            for slots in {seg.slots for seg in segments}:
                tops |= {slots} | ({2, 4} if slots == MOST else {2} if slots <= ROUNDS else set())
            tops = sorted(tops)
            for low, top in zip([0] + tops, tops):

                @pl.when((count > low) & (count <= top))
                def _():
                    mix(low + 1, top, slot, turn, count)

            partial = total[into]
            for g in range(0, d_rows, GROUP):
                lhs = jnp.concatenate(
                    [mixed[a, :, g : g + GROUP, :].reshape(-1, aux) for a in range(a_rows)],
                    axis=0,
                )
                rhs = panel_buf[slot, :, g : g + GROUP, :].reshape(b_rows * GROUP, aux)
                partial += lax.dot_general(
                    lhs, rhs, (((1,), (1,)), ((), ())), preferred_element_type=jnp.float32
                )
            total[into] = partial

        return carry

    lax.fori_loop(0, jnp.where(items > 0, items + AHEAD - 1, 0), step, 0)

    def finish(o, carry):
        _, rows, columns = total.shape
        row_d = lax.broadcasted_iota(jnp.int32, (rows, columns), 0) % GROUP
        column_d = lax.broadcasted_iota(jnp.int32, (rows, columns), 1) % GROUP
        kept = jnp.where(row_d == column_d, total[o], 0.0)
        kept = kept.reshape(rows // GROUP, GROUP, columns).sum(axis=1)
        from_b = lax.broadcasted_iota(jnp.int32, (columns, LANES), 0) // GROUP
        to_b = lax.broadcasted_iota(jnp.int32, (columns, LANES), 1)
        gather = jnp.where(from_b == to_b, 1.0, 0.0)
        out_ref[o] = jnp.dot(
            kept, gather, precision=lax.Precision.HIGHEST, preferred_element_type=jnp.float32
        )
        return carry

    @pl.when(items > 0)
    def _():
        lax.fori_loop(0, outs, finish, 0)

    @pl.when(items == 0)
    def _():
        out_ref[...] = jnp.zeros_like(out_ref)


def pair_terms(lists, factors_a, segments, outs, width, d_rows, behind=()):
    arrays, places = [factors_a], []
    for seg in segments:
        place = []
        for array in (seg.amps, seg.panel):
            known = [n for n, other in enumerate(arrays) if other is array]
            place.append(known[0] if known else len(arrays))
            if not known:
                arrays.append(array)
        places.append(place)
    arrays += behind
    a_rows, _, aux = factors_a.shape
    pairs = segments[0].amps.shape[-3]
    b_rows = segments[0].panel.shape[0]
    most = max(2, *(seg.slots for seg in segments))
    return pl.pallas_call(
        functools.partial(terms_kernel, segments, places, d_rows),
        in_specs=[pl.BlockSpec(memory_space=pltpu.SMEM)]
        + [pl.BlockSpec(memory_space=pltpu.HBM)] * len(arrays),
        out_specs=pl.BlockSpec(memory_space=pltpu.VMEM),
        scratch_shapes=[
            pltpu.VMEM((AHEAD, most, pairs, d_rows, width), jnp.bfloat16),
            pltpu.VMEM((AHEAD, b_rows, d_rows, aux), jnp.bfloat16),
            pltpu.VMEM((AHEAD, most, a_rows, width, aux), jnp.bfloat16),
            pltpu.VMEM((a_rows, pairs, d_rows, aux), jnp.bfloat16),
            pltpu.VMEM((outs, a_rows * pairs * GROUP, b_rows * GROUP), jnp.float32),
            pltpu.SemaphoreType.DMA((AHEAD, most + PARTS)),
            pltpu.SemaphoreType.DMA((AHEAD, most)),
        ],
        out_shape=jax.ShapeDtypeStruct((outs, a_rows * pairs, LANES), jnp.float32),
        compiler_params=pltpu.CompilerParams(vmem_limit_bytes=VMEM),
        cost_estimate=SMALL,
        name="pair_terms",
    )(lists, *arrays)


def summed_over_narrow(value):
    size = lax.axis_size("narrow")
    me = lax.axis_index("narrow")
    share = value.shape[2] // size

    def part(owner):
        return lax.dynamic_slice_in_dim(value, owner * share, share, 2)

    parts = [part(me)]
    for k in range(1, size):
        to = [(i, (i + k) % size) for i in range(size)]
        parts.append(lax.ppermute(part((me + k) % size), "narrow", to))
    return sum(parts[1:], parts[0])


def local(factors_a, factors_b, amplitudes, screen):
    pairs, d_extent, virtuals = amplitudes.shape
    width = virtuals // screen.shape[1]
    tiles = lax.axis_size("blk")
    position = lax.axis_index("blk")
    extras = MOST - ROUNDS
    d_rows = min(64, d_extent // 4)

    lists = kept_lists(position, screen)
    fullest = lists[MISC * ROW + 1]
    others = lists[MISC * ROW + 2]
    is_first = position % 2 == 0
    is_full = position == fullest
    feeds_one = (position + 1) % tiles == fullest
    feeds_two = (position + 2) % tiles == fullest

    evens, odds = range(0, tiles, 2), range(1, tiles, 2)
    up = [(i, i + 1) for i in evens]
    down = [(i + 1, i) for i in evens]
    around = [(i, (i + 2) % tiles) for i in range(tiles)]

    def run(wrapped, odd, operands):
        lists, factors_a, factors_b, amplitudes = operands
        terms = functools.partial(pair_terms, lists, factors_a, width=width, d_rows=d_rows)
        columns_of = functools.partial(Segment, panel=factors_b)
        given_to = functools.partial(Segment, amps=amplitudes, slots=extras)
        take = functools.partial(take_columns, lists, amplitudes, width=width)
        cut = functools.partial(take_panel, factors_b)

        def ahead(at):
            return (at >= tiles - 2) == wrapped

        def hops(keep):
            return [(at, to) for at, to in around if keep(at)]

        def backs(keep):
            return [(to, at) for at, to in around if keep(at)]

        half, quarter = d_extent // 2, d_extent // 4
        own = [columns_of(0, row=OWN, slots=MOST, amps=amplitudes, extent=d_extent)]
        after = functools.partial(take, row=AFTER, slots=ROUNDS, extent=half)
        near = functools.partial(take, row=NEXT, slots=ROUNDS)
        light = functools.partial(columns_of, slots=ROUNDS)
        mine = functools.partial(columns_of, row=MINE, slots=extras)
        if odd:
            given = max(3 * d_extent // 8 // d_rows, 1) * d_rows
            moved = d_extent - given

            def seconds(at):
                return at in odds and ahead(at)

            near_l = near(start=0, extent=half)
            side_l = send(near_l, up + down)
            direct = take(
                row=AFTER, slots=ROUNDS, start=0, extent=d_extent, behind=[near_l]
            )
            got_direct = send(direct, hops(lambda at: at in evens))
            extra = take(row=MINE, slots=extras, start=0, extent=moved, behind=[near_l])
            extra_two = send(extra, hops(seconds))
            near_h = near(start=half, extent=half, behind=[near_l])
            side_h = send(near_h, up + down)
            panel = cut(start=moved, extent=given, behind=[near_l])
            far = send(panel, backs(seconds))
            here = terms(own, 1, behind=[near_l])

            pass_l = after(start=0, passing=side_l, behind=[here])
            on_l = send(pass_l, around)
            panel = cut(start=moved, extent=given, behind=[pass_l])
            beside = send(panel, down)
            extra = take(row=MINE, slots=extras, start=0, extent=moved, behind=[panel])
            extra = tied(extra, side_h, got_direct, far)
            extra_one = send(extra, up)
            pass_h = after(start=half, passing=side_h, behind=[extra, extra_two])
            on_h = send(pass_h, around)

            first = terms(
                [
                    light(1, row=LIGHT_0, amps=got_direct, extent=d_extent),
                    light(0, row=LIGHT_1, amps=side_l, extent=half),
                    light(0, row=LIGHT_1, amps=side_h, extent=half, panel_at=half),
                    mine(1, amps=extra_two, extent=moved),
                ],
                2,
                behind=[pass_h],
            )
            then = terms(
                [
                    light(0, row=LIGHT_0, amps=on_l, extent=half),
                    light(1, row=LIGHT_1, amps=on_l, extent=half),
                ],
                2,
                behind=[first],
            )
            sent = terms(
                [
                    given_to(0, row=FED_1, panel=beside, extent=given, amp_at=moved),
                    given_to(0, row=FED_2, panel=far, extent=given, amp_at=moved),
                ],
                1,
                behind=[then],
            )
            last = terms(
                [
                    light(0, row=LIGHT_0, amps=on_h, extent=half, panel_at=half),
                    light(1, row=LIGHT_1, amps=on_h, extent=half, panel_at=half),
                    mine(0, amps=extra_one, extent=moved),
                ],
                2,
                behind=[sent],
            )
            sent = sent[0]
            one = first[0] + then[0] + last[0]
            two = first[1] + then[1] + last[1]
        else:
            def firsts(at):
                return at in evens and ahead(at)

            beside = near(start=0, extent=d_extent)
            side = send(beside, up)
            lead = take(
                row=LEAD, part=PART, slots=2 * ROUNDS, start=0, extent=half, behind=[beside]
            )
            got_lead = send(lead, hops(lambda at: at in odds or ahead(at)))
            extra = take(row=MINE, slots=extras, start=0, extent=quarter, behind=[lead])
            cross = send(extra, down)
            panel = cut(start=half, extent=quarter, behind=[extra])
            far_0 = send(panel, backs(firsts))
            panel = cut(start=half + quarter, extent=quarter, behind=[panel])
            far_1 = send(panel, backs(firsts))
            here = terms(own, 1, behind=[panel])

            extra = take(
                row=MINE,
                slots=extras,
                start=quarter,
                extent=quarter,
                passing=cross,
                behind=[here],
            )
            got_extra = send(extra, hops(ahead))
            far_0 = tied(far_0, extra, side)
            up_0 = send(far_0, up)
            lead_down = send(got_lead, down)
            after_l = after(start=0, behind=[far_0, got_lead, side])
            got_l = send(after_l, around)
            far_1 = tied(far_1, after_l)
            up_1 = send(far_1, up)
            after_h = after(start=half, behind=[far_1, got_extra])
            got_h = send(after_h, around)

            first = terms(
                [
                    light(0, row=LIGHT_1, amps=side, extent=d_extent),
                    mine(1, amps=got_lead, extent=half),
                ],
                2,
                behind=[after_h],
            )
            got_extra = tied(got_extra, first, up_0)
            extra_down = send(got_extra, down)
            fed = functools.partial(given_to, 0, extent=quarter)
            then = terms(
                [
                    fed(row=FED_1, panel=up_0, amp_at=half),
                    fed(row=FED_2, panel=far_0, amp_at=half),
                    fed(row=FED_2, panel=far_1, amp_at=half + quarter),
                    mine(1, amps=got_extra, extent=quarter),
                    light(2, row=LIGHT, amps=got_l, extent=half),
                ],
                3,
            )
            down_part = functools.partial(light, 0, row=LIGHT_0, amps=lead_down, extent=half)
            low = terms(
                [down_part(), down_part(panel_at=half, slot_at=ROUNDS)], 1, behind=[then]
            )
            sent = terms(
                [fed(row=FED_1, panel=up_1, amp_at=half + quarter)], 1, behind=[low]
            )
            last = terms(
                [
                    light(1, row=LIGHT, amps=got_h, extent=half, panel_at=half),
                    mine(0, amps=extra_down, extent=quarter, panel_at=quarter),
                ],
                2,
                behind=[sent],
            )
            sent = then[0] + sent[0]
            one = first[0] + then[1] + low[0] + last[0]
            two = first[1] + then[2] + last[1]
        one += rotated(jnp.where(feeds_one, sent, 0.0), 1)
        two += rotated(jnp.where(feeds_two, sent, 0.0), 2)

        return jnp.stack([here[0], one, two])

    branches = [
        functools.partial(run, wrapped, odd) for wrapped in (False, True) for odd in (False, True)
    ]
    operands = (lists, factors_a, factors_b, amplitudes)
    terms = lax.switch(lists[MISC * ROW], branches, operands)
    def add_round(r, running):
        one, two = running

        def only(row, count):
            sub = lax.dynamic_slice_in_dim(lists, row * ROW + r, 1)
            return jnp.concatenate([sub, jnp.zeros(MOST - 1, jnp.int32), count.reshape(1)])

        has = jnp.where((r < lists[OWN * ROW + MOST]) & ~is_full, 1, 0).astype(jnp.int32)
        own = only(OWN, has)
        moved = [
            rotated(
                take_columns(only(row, has), amplitudes, 0, 1, width, 0, d_extent), by
            )
            for row, by in ((NEXT, 1), (AFTER, 2))
        ]
        more = pair_terms(
            own,
            factors_a,
            [
                Segment(into, 0, 1, columns, factors_b, d_extent)
                for into, columns in enumerate(moved)
            ],
            2,
            width,
            d_rows,
        )
        return one + more[0], two + more[1]

    one, two = lax.fori_loop(
        ROUNDS, jnp.maximum(others, ROUNDS), add_round, (terms[1], terms[2])
    )
    terms = jnp.stack([terms[0], one, two])
    a_rows = factors_a.shape[0]
    terms = terms[:, :, : factors_b.shape[0]]
    terms = terms.reshape(STEPS, a_rows, pairs, -1).swapaxes(1, 2).reshape(STEPS, 1, -1)
    return summed_over_narrow(terms)


def solution(mesh):
    return jax.shard_map(
        local,
        mesh=mesh,
        in_specs=(P(), P("blk", "narrow", None), P("blk", "narrow", None), P()),
        out_specs=P(None, "blk", "narrow"),
        check_vma=False,
    )
```

```python
import functools

import jax
import jax.numpy as jnp
from jax import lax
from jax.experimental import pallas as pl
from jax.experimental.pallas import tpu as pltpu
from jax.sharding import PartitionSpec as P

STEPS = 3
MOST = 8
ROUNDS = 3
GROUP = 16
LANES = 128
ROW = MOST + 1

(
    OWN,
    LIGHT,
    LIGHT_0,
    LIGHT_1,
    NEXT,
    AFTER,
    LEAD,
    PART,
    MINE,
    FED_1,
    FED_2,
    MISC,
) = range(12)
FIRST = MISC * ROW + 3
AHEAD = 4
PARTS = 4
VMEM = 60 * 1024 * 1024
SMALL = pl.CostEstimate(flops=1024, bytes_accessed=1024, transcendentals=0)


def send(value, pairs):
    return lax.ppermute(value, "blk", pairs)


def rotated(value, by):
    size = lax.axis_size("blk")
    return send(value, [(i, (i + by) % size) for i in range(size)])


def lists_kernel(position_ref, screen_ref, out_ref):
    tiles, subs = screen_ref.shape
    position = position_ref[0]

    def count_of(tile):
        return sum(jnp.where(screen_ref[tile, s] != 0, 1, 0) for s in range(subs))

    def look(tile, found):
        best, fullest, others = found
        count = count_of(tile)
        larger = count > best
        others = jnp.where(larger, best, jnp.maximum(others, count))
        return jnp.where(larger, count, best), jnp.where(larger, tile, fullest), others

    zero = jnp.int32(0)
    best, fullest, others = lax.fori_loop(0, tiles, look, (zero, zero, zero))

    def fill(row, tile, skip, count):
        for k in range(MOST):
            out_ref[row * ROW + k] = 0
        seen = jnp.int32(0)
        for s in range(subs):
            kept = screen_ref[tile, s] != 0

            @pl.when(kept & (seen >= skip))
            def _():
                out_ref[row * ROW + seen - skip] = s

            seen += jnp.where(kept, 1, 0)
        out_ref[row * ROW + MOST] = seen if count is None else count

    following = lax.rem(position + 1, tiles)
    second = lax.rem(position + 2, tiles)
    is_first = lax.rem(position, 2) == 0
    own_count = count_of(position)
    extra = jnp.maximum(best - ROUNDS, 0)
    light = jnp.minimum(own_count, ROUNDS)
    fill(OWN, position, 0, own_count)
    fill(LIGHT, position, 0, light)
    fill(LIGHT_0, position, 0, jnp.where(is_first, light, 0))
    fill(LIGHT_1, position, 0, jnp.where(is_first, 0, light))
    fill(NEXT, following, 0, None)
    fill(AFTER, second, 0, None)
    fill(MINE, fullest, ROUNDS, jnp.where(position == fullest, extra, 0))
    fill(FED_1, fullest, ROUNDS, jnp.where(following == fullest, extra, 0))
    fill(FED_2, fullest, ROUNDS, jnp.where(second == fullest, extra, 0))
    for k in range(ROW):
        other = out_ref[NEXT * ROW + k % ROUNDS] if k < 2 * ROUNDS else 0
        out_ref[LEAD * ROW + k] = jnp.where(is_first, out_ref[MINE * ROW + k], other)
        out_ref[PART * ROW + k] = jnp.where(is_first, 0, k // ROUNDS)
    out_ref[MISC * ROW] = jnp.where(fullest < 2, 2, 0) + lax.rem(fullest, 2)
    out_ref[MISC * ROW + 1] = fullest
    out_ref[MISC * ROW + 2] = others
    out_ref[FIRST] = jnp.where(is_first, 1, 0)
    for k in range(4, ROW):
        out_ref[MISC * ROW + k] = 0


def kept_lists(position, screen):
    return pl.pallas_call(
        lists_kernel,
        in_specs=[pl.BlockSpec(memory_space=pltpu.SMEM)] * 2,
        out_specs=pl.BlockSpec(memory_space=pltpu.SMEM),
        out_shape=jax.ShapeDtypeStruct(((MISC + 1) * ROW,), jnp.int32),
        name="kept_lists",
    )(position.reshape(1), screen)


def staged(count, load_from, target_of, stage, sems):
    def load(n, carry):
        load_from(
            n, lambda source: pltpu.make_async_copy(source, stage.at[n], sems.at[0, n]).start()
        )
        return carry

    def store(n, carry):
        pltpu.make_async_copy(stage.at[n], stage.at[n], sems.at[0, n]).wait()
        pltpu.make_async_copy(stage.at[n], target_of(n), sems.at[1, n]).start()
        return carry

    def finish(n, carry):
        pltpu.make_async_copy(stage.at[n], stage.at[n], sems.at[1, n]).wait()
        return carry

    for act in (load, store, finish):
        lax.fori_loop(0, count, act, 0)


def take_kernel(row, slots, start, extent, part, passes, lists_ref, source, *refs):
    out, stage, sems = refs[-3:]
    width = out.shape[-1]

    def columns(s, act):
        sub = pl.multiple_of(lists_ref[row * ROW + s] * width, width)
        first = start
        if part is not None:
            first = pl.multiple_of(start + lists_ref[part * ROW + s] * extent, extent)
        act(source.at[:, pl.ds(first, extent), pl.ds(sub, width)])

    def load_from(s, act):
        if passes:
            pl.when(lists_ref[FIRST] != 0)(lambda: act(refs[0].at[s]))
            pl.when(lists_ref[FIRST] == 0)(lambda: columns(s, act))
        else:
            columns(s, act)

    staged(slots, load_from, lambda s: out.at[s], stage, sems)


def take_columns(
    lists, amplitudes, row, slots, width, start, extent, behind=(), part=None, passing=None
):
    pairs = amplitudes.shape[0]
    others = ([] if passing is None else [passing]) + list(behind)
    return pl.pallas_call(
        functools.partial(take_kernel, row, slots, start, extent, part, passing is not None),
        in_specs=[pl.BlockSpec(memory_space=pltpu.SMEM)]
        + [pl.BlockSpec(memory_space=pltpu.HBM)] * (1 + len(others)),
        out_specs=pl.BlockSpec(memory_space=pltpu.HBM),
        out_shape=jax.ShapeDtypeStruct((slots, pairs, extent, width), amplitudes.dtype),
        scratch_shapes=[
            pltpu.VMEM((slots, pairs, extent, width), amplitudes.dtype),
            pltpu.SemaphoreType.DMA((2, slots)),
        ],
        compiler_params=pltpu.CompilerParams(vmem_limit_bytes=VMEM),
        cost_estimate=SMALL,
        name="take_columns",
    )(lists, amplitudes, *others)


def panel_kernel(start, panel, *refs):
    out, stage, sems = refs[-3:]
    parts, share, extent, _ = stage.shape

    def rows(n):
        return pl.ds(n * share, share)

    staged(
        parts,
        lambda n, act: act(panel.at[rows(n), pl.ds(start, extent), :]),
        lambda n: out.at[rows(n)],
        stage,
        sems,
    )


def take_panel(panel, start, extent, behind=()):
    b_rows, _, aux = panel.shape
    return pl.pallas_call(
        functools.partial(panel_kernel, start),
        in_specs=[pl.BlockSpec(memory_space=pltpu.HBM)] * (1 + len(behind)),
        out_specs=pl.BlockSpec(memory_space=pltpu.HBM),
        out_shape=jax.ShapeDtypeStruct((b_rows, extent, aux), panel.dtype),
        scratch_shapes=[
            pltpu.VMEM((PARTS, b_rows // PARTS, extent, aux), panel.dtype),
            pltpu.SemaphoreType.DMA((2, PARTS)),
        ],
        compiler_params=pltpu.CompilerParams(vmem_limit_bytes=VMEM),
        cost_estimate=SMALL,
        name="take_panel",
    )(panel, *behind)


def tie_kernel(*refs):
    pass


def tied(value, *behind):
    return pl.pallas_call(
        tie_kernel,
        in_specs=[pl.BlockSpec(memory_space=pltpu.HBM)] * (1 + len(behind)),
        out_specs=pl.BlockSpec(memory_space=pltpu.HBM),
        out_shape=jax.ShapeDtypeStruct(value.shape, value.dtype),
        input_output_aliases={0: 0},
        cost_estimate=SMALL,
        name="tied",
    )(value, *behind)


class Segment:
    def __init__(self, into, row, slots, amps, panel, extent, amp_at=0, panel_at=0, slot_at=0):
        self.into, self.row, self.slots = into, row, slots
        self.amps, self.panel, self.extent = amps, panel, extent
        self.amp_at, self.panel_at, self.slot_at = amp_at, panel_at, slot_at


def rows_of(extent, d_rows):
    return 2 * d_rows if extent % (2 * d_rows) == 0 else d_rows


def terms_kernel(segments, places, d_rows, lists_ref, *refs):
    arrays = refs[:-8]
    out_ref, amp_buf, panel_buf, factor_buf, mixed, total, sems, factor_sems = refs[-8:]
    factors = arrays[0]
    outs = out_ref.shape[0]
    _, most, pairs, _, width = amp_buf.shape
    b_rows = panel_buf.shape[1]
    _, _, a_rows, _, aux = factor_buf.shape

    counts = [lists_ref[seg.row * ROW + MOST] for seg in segments]
    brought = [rows_of(seg.extent, d_rows) for seg in segments]
    starts, orders = [], []
    begin = order = jnp.int32(0)
    for seg, count, rows in zip(segments, counts, brought):
        starts.append(begin)
        orders.append(order)
        begin = begin + jnp.where(count > 0, seg.extent // rows, 0)
        order = order + jnp.where(count > 0, 1, 0)
    items = begin

    def pick(at, values):
        found = values[0]
        for s in range(1, len(segments)):
            found = jnp.where(at == s, values[s], found)
        return found

    def locate(t):
        at = jnp.int32(0)
        for s in range(len(segments)):
            at = jnp.where((counts[s] > 0) & (t >= starts[s]), s, at)
        return at, t - pick(at, starts), lax.rem(pick(at, orders), AHEAD)

    def fetch(t):
        at, block, turn = locate(t)
        slot = lax.rem(t, AHEAD)
        for s, (seg, rows) in enumerate(zip(segments, brought)):
            amps, panel = arrays[places[s][0]], arrays[places[s][1]]

            @pl.when(at == s)
            def _():
                amp_d = pl.ds(pl.multiple_of(seg.amp_at + block * rows, d_rows), rows)
                panel_d = pl.ds(pl.multiple_of(seg.panel_at + block * rows, d_rows), rows)
                pltpu.make_async_copy(
                    panel.at[:, panel_d, :],
                    panel_buf.at[slot, :, pl.ds(0, rows)],
                    sems.at[slot, most],
                ).start()

                def one(k, carry):
                    sub = pl.multiple_of(lists_ref[seg.row * ROW + k] * width, width)
                    columns = pl.ds(sub, width)
                    if len(amps.shape) == 3:
                        source = amps.at[:, amp_d, columns]
                    else:
                        source = amps.at[seg.slot_at + k, :, amp_d, :]
                    pltpu.make_async_copy(
                        source, amp_buf.at[slot, k, :, pl.ds(0, rows)], sems.at[slot, k]
                    ).start()

                    @pl.when(block == 0)
                    def _():
                        pltpu.make_async_copy(
                            factors.at[:, columns, :],
                            factor_buf.at[turn, k],
                            factor_sems.at[turn, k],
                        ).start()

                    return carry

                lax.fori_loop(0, counts[s], one, 0)

    def arrive(slot, rows, block, turn, count):
        piece = panel_buf.at[slot, :, pl.ds(0, rows)]
        pltpu.make_async_copy(piece, piece, sems.at[slot, most]).wait()

        def one(k, carry):
            piece = amp_buf.at[slot, k, :, pl.ds(0, rows)]
            pltpu.make_async_copy(piece, piece, sems.at[slot, k]).wait()

            @pl.when(block == 0)
            def _():
                piece = factor_buf.at[turn, k]
                pltpu.make_async_copy(piece, piece, factor_sems.at[turn, k]).wait()

            return carry

        lax.fori_loop(0, count, one, 0)

    @pl.when(items > 0)
    def _():
        total[...] = jnp.zeros_like(total)

    def mix(low, top, slot, half, turn, count):
        columns = [
            amp_buf[slot, k, :, half, :].reshape(pairs * d_rows, width) for k in range(top)
        ]
        for k in range(low, top):
            columns[k] = jnp.where(k < count, columns[k], jnp.zeros_like(columns[k]))
        lhs = jnp.concatenate(columns, axis=1)

        def one(a, carry):
            rows = [factor_buf[turn, k, a] for k in range(top)]
            for k in range(low, top):
                rows[k] = jnp.where(k < count, rows[k], jnp.zeros_like(rows[k]))
            product = jnp.dot(
                lhs, jnp.concatenate(rows, axis=0), preferred_element_type=jnp.float32
            )
            mixed[a] = product.astype(mixed.dtype).reshape(pairs, d_rows, aux)
            return carry

        lax.fori_loop(0, a_rows, one, 0)

    tops = set()
    for slots in {seg.slots for seg in segments}:
        tops |= {2, 3, 5, slots} if slots == MOST else {min(2, slots), slots}
    tops = sorted(tops)

    def step(n, carry):
        @pl.when(n < items)
        def _():
            fetch(n)

        @pl.when(n >= AHEAD - 1)
        def _():
            t = n - (AHEAD - 1)
            at, block, turn = locate(t)
            slot = lax.rem(t, AHEAD)
            count = pick(at, counts)
            into = pick(at, [seg.into for seg in segments])
            parts = pick(at, [rows // d_rows for rows in brought])
            for rows in set(brought):
                pl.when(parts == rows // d_rows)(
                    functools.partial(arrive, slot, rows, block, turn, count)
                )

            def compute(part, carry):
                first = pl.multiple_of(part * d_rows, d_rows)
                for low, top in zip([0] + tops, tops):

                    @pl.when((count > low) & (count <= top))
                    def _():
                        mix(low + 1, top, slot, pl.ds(first, d_rows), turn, count)

                partial = total[into]
                for g in range(0, d_rows, GROUP):
                    lhs = jnp.concatenate(
                        [mixed[a, :, g : g + GROUP, :].reshape(-1, aux) for a in range(a_rows)],
                        axis=0,
                    )
                    rhs = panel_buf[slot, :, pl.ds(first + g, GROUP), :]
                    partial += lax.dot_general(
                        lhs,
                        rhs.reshape(b_rows * GROUP, aux),
                        (((1,), (1,)), ((), ())),
                        preferred_element_type=jnp.float32,
                    )
                total[into] = partial
                return carry

            lax.fori_loop(0, parts, compute, 0)

        return carry

    lax.fori_loop(0, jnp.where(items > 0, items + AHEAD - 1, 0), step, 0)

    def finish(o, carry):
        _, rows, columns = total.shape
        row_d = lax.broadcasted_iota(jnp.int32, (rows, columns), 0) % GROUP
        column_d = lax.broadcasted_iota(jnp.int32, (rows, columns), 1) % GROUP
        kept = jnp.where(row_d == column_d, total[o], 0.0)
        kept = kept.reshape(rows // GROUP, GROUP, columns).sum(axis=1)
        from_b = lax.broadcasted_iota(jnp.int32, (columns, LANES), 0) // GROUP
        to_b = lax.broadcasted_iota(jnp.int32, (columns, LANES), 1)
        gather = jnp.where(from_b == to_b, 1.0, 0.0)
        out_ref[o] = jnp.dot(
            kept, gather, precision=lax.Precision.HIGHEST, preferred_element_type=jnp.float32
        )
        return carry

    @pl.when(items > 0)
    def _():
        lax.fori_loop(0, outs, finish, 0)

    @pl.when(items == 0)
    def _():
        out_ref[...] = jnp.zeros_like(out_ref)


def pair_terms(lists, factors_a, segments, outs, width, d_rows, behind=()):
    arrays, places = [factors_a], []
    for seg in segments:
        place = []
        for array in (seg.amps, seg.panel):
            known = [n for n, other in enumerate(arrays) if other is array]
            place.append(known[0] if known else len(arrays))
            if not known:
                arrays.append(array)
        places.append(place)
    arrays += behind
    a_rows, _, aux = factors_a.shape
    pairs = segments[0].amps.shape[-3]
    b_rows = segments[0].panel.shape[0]
    most = max(2, *(seg.slots for seg in segments))
    largest = max(rows_of(seg.extent, d_rows) for seg in segments)
    return pl.pallas_call(
        functools.partial(terms_kernel, segments, places, d_rows),
        in_specs=[pl.BlockSpec(memory_space=pltpu.SMEM)]
        + [pl.BlockSpec(memory_space=pltpu.HBM)] * len(arrays),
        out_specs=pl.BlockSpec(memory_space=pltpu.VMEM),
        scratch_shapes=[
            pltpu.VMEM((AHEAD, most, pairs, largest, width), jnp.bfloat16),
            pltpu.VMEM((AHEAD, b_rows, largest, aux), jnp.bfloat16),
            pltpu.VMEM((AHEAD, most, a_rows, width, aux), jnp.bfloat16),
            pltpu.VMEM((a_rows, pairs, d_rows, aux), jnp.bfloat16),
            pltpu.VMEM((outs, a_rows * pairs * GROUP, b_rows * GROUP), jnp.float32),
            pltpu.SemaphoreType.DMA((AHEAD, most + 1)),
            pltpu.SemaphoreType.DMA((AHEAD, most)),
        ],
        out_shape=jax.ShapeDtypeStruct((outs, a_rows * pairs, LANES), jnp.float32),
        compiler_params=pltpu.CompilerParams(vmem_limit_bytes=VMEM),
        cost_estimate=SMALL,
        name="pair_terms",
    )(lists, *arrays)


def summed_over_narrow(value):
    size = lax.axis_size("narrow")
    me = lax.axis_index("narrow")
    share = value.shape[2] // size

    def part(owner):
        return lax.dynamic_slice_in_dim(value, owner * share, share, 2)

    parts = [part(me)]
    for k in range(1, size):
        to = [(i, (i + k) % size) for i in range(size)]
        parts.append(lax.ppermute(part((me + k) % size), "narrow", to))
    return sum(parts[1:], parts[0])


def local(factors_a, factors_b, amplitudes, screen):
    pairs, d_extent, virtuals = amplitudes.shape
    width = virtuals // screen.shape[1]
    tiles = lax.axis_size("blk")
    position = lax.axis_index("blk")
    extras = MOST - ROUNDS
    d_rows = min(64, d_extent // 4)

    lists = kept_lists(position, screen)
    fullest = lists[MISC * ROW + 1]
    others = lists[MISC * ROW + 2]
    is_first = position % 2 == 0
    is_full = position == fullest
    feeds_one = (position + 1) % tiles == fullest
    feeds_two = (position + 2) % tiles == fullest

    evens, odds = range(0, tiles, 2), range(1, tiles, 2)
    up = [(i, i + 1) for i in evens]
    down = [(i + 1, i) for i in evens]
    around = [(i, (i + 2) % tiles) for i in range(tiles)]

    def run(wrapped, odd, operands):
        lists, factors_a, factors_b, amplitudes = operands
        terms = functools.partial(pair_terms, lists, factors_a, width=width, d_rows=d_rows)
        columns_of = functools.partial(Segment, panel=factors_b)
        given_to = functools.partial(Segment, amps=amplitudes, slots=extras)
        take = functools.partial(take_columns, lists, amplitudes, width=width)
        cut = functools.partial(take_panel, factors_b)

        def ahead(at):
            return (at >= tiles - 2) == wrapped

        def hops(keep):
            return [(at, to) for at, to in around if keep(at)]

        def backs(keep):
            return [(to, at) for at, to in around if keep(at)]

        half, quarter = d_extent // 2, d_extent // 4
        own = columns_of(0, row=OWN, slots=MOST, amps=amplitudes, extent=d_extent)
        after = functools.partial(take, row=AFTER, slots=ROUNDS, extent=half)
        near = functools.partial(take, row=NEXT, slots=ROUNDS)
        light = functools.partial(columns_of, slots=ROUNDS)
        mine = functools.partial(columns_of, row=MINE, slots=extras)
        if odd:
            given = max(3 * d_extent // 8 // d_rows, 1) * d_rows
            moved = d_extent - given

            def seconds(at):
                return at in odds and ahead(at)

            near_l = near(start=0, extent=half)
            side_l = send(near_l, up + down)
            direct = take(
                row=AFTER, slots=ROUNDS, start=0, extent=d_extent, behind=[near_l]
            )
            got_direct = send(direct, hops(lambda at: at in evens))
            extra = take(row=MINE, slots=extras, start=0, extent=moved, behind=[near_l])
            extra_two = send(extra, hops(seconds))
            near_h = near(start=half, extent=half, behind=[near_l])
            side_h = send(near_h, up + down)
            panel = cut(start=moved, extent=given, behind=[near_l])
            far = send(panel, backs(seconds))

            pass_l = after(start=0, passing=side_l)
            on_l = send(pass_l, around)
            panel = cut(start=moved, extent=given, behind=[pass_l])
            beside = send(panel, down)
            extra = take(row=MINE, slots=extras, start=0, extent=moved, behind=[panel])
            extra = tied(extra, side_h, got_direct, far)
            extra_one = send(extra, up)
            pass_h = after(start=half, passing=side_h, behind=[extra, extra_two])
            on_h = send(pass_h, around)

            first = terms(
                [
                    own,
                    light(2, row=LIGHT_0, amps=got_direct, extent=d_extent),
                    light(1, row=LIGHT_1, amps=side_l, extent=half),
                    light(1, row=LIGHT_1, amps=side_h, extent=half, panel_at=half),
                    mine(2, amps=extra_two, extent=moved),
                ],
                3,
                behind=[pass_h],
            )
            then = terms(
                [
                    light(0, row=LIGHT_0, amps=on_l, extent=half),
                    light(1, row=LIGHT_1, amps=on_l, extent=half),
                ],
                2,
                behind=[first],
            )
            sent = terms(
                [
                    given_to(0, row=FED_1, panel=beside, extent=given, amp_at=moved),
                    given_to(0, row=FED_2, panel=far, extent=given, amp_at=moved),
                ],
                1,
                behind=[then],
            )
            last = terms(
                [
                    light(0, row=LIGHT_0, amps=on_h, extent=half, panel_at=half),
                    light(1, row=LIGHT_1, amps=on_h, extent=half, panel_at=half),
                    mine(0, amps=extra_one, extent=moved),
                ],
                2,
                behind=[sent],
            )
            sent = sent[0]
            one = first[1] + then[0] + last[0]
            two = first[2] + then[1] + last[1]
        else:
            def firsts(at):
                return at in evens and ahead(at)

            beside = near(start=0, extent=d_extent)
            side = send(beside, up)
            lead = take(
                row=LEAD, part=PART, slots=2 * ROUNDS, start=0, extent=half, behind=[beside]
            )
            got_lead = send(lead, hops(lambda at: at in odds or ahead(at)))
            extra = take(row=MINE, slots=extras, start=0, extent=quarter, behind=[lead])
            cross = send(extra, down)
            panel = cut(start=half, extent=quarter, behind=[extra])
            far_0 = send(panel, backs(firsts))
            panel = cut(start=half + quarter, extent=quarter, behind=[panel])
            far_1 = send(panel, backs(firsts))

            extra = take(
                row=MINE,
                slots=extras,
                start=quarter,
                extent=quarter,
                passing=cross,
                behind=[panel],
            )
            got_extra = send(extra, hops(ahead))
            far_0 = tied(far_0, extra, side)
            up_0 = send(far_0, up)
            lead_down = send(got_lead, down)
            after_l = after(start=0, behind=[far_0, got_lead, side])
            got_l = send(after_l, around)
            far_1 = tied(far_1, after_l)
            up_1 = send(far_1, up)
            after_h = after(start=half, behind=[far_1, got_extra])
            got_h = send(after_h, around)

            first = terms(
                [
                    own,
                    light(1, row=LIGHT_1, amps=side, extent=d_extent),
                    mine(2, amps=got_lead, extent=half),
                ],
                3,
                behind=[after_h],
            )
            got_extra = tied(got_extra, first, up_0)
            extra_down = send(got_extra, down)
            fed = functools.partial(given_to, 0, extent=quarter)
            down_part = functools.partial(light, 1, row=LIGHT_0, amps=lead_down, extent=half)
            then = terms(
                [
                    light(2, row=LIGHT, amps=got_l, extent=half),
                    fed(row=FED_1, panel=up_0, amp_at=half),
                    fed(row=FED_2, panel=far_0, amp_at=half),
                    fed(row=FED_2, panel=far_1, amp_at=half + quarter),
                    mine(1, amps=got_extra, extent=quarter),
                    down_part(),
                    down_part(panel_at=half, slot_at=ROUNDS),
                ],
                3,
            )
            sent = terms(
                [fed(row=FED_1, panel=up_1, amp_at=half + quarter)], 1, behind=[then]
            )
            last = terms(
                [
                    light(1, row=LIGHT, amps=got_h, extent=half, panel_at=half),
                    mine(0, amps=extra_down, extent=quarter, panel_at=quarter),
                ],
                2,
                behind=[sent],
            )
            sent = then[0] + sent[0]
            one = first[1] + then[1] + last[0]
            two = first[2] + then[2] + last[1]
        return jnp.stack([first[0], one, two, sent])

    branches = [
        functools.partial(run, wrapped, odd) for wrapped in (False, True) for odd in (False, True)
    ]
    operands = (lists, factors_a, factors_b, amplitudes)
    terms = lax.switch(lists[MISC * ROW], branches, operands)
    def add_round(r, running):
        one, two = running

        def only(row, count):
            sub = lax.dynamic_slice_in_dim(lists, row * ROW + r, 1)
            return jnp.concatenate([sub, jnp.zeros(MOST - 1, jnp.int32), count.reshape(1)])

        has = jnp.where((r < lists[OWN * ROW + MOST]) & ~is_full, 1, 0).astype(jnp.int32)
        own = only(OWN, has)
        moved = [
            rotated(
                take_columns(only(row, has), amplitudes, 0, 1, width, 0, d_extent), by
            )
            for row, by in ((NEXT, 1), (AFTER, 2))
        ]
        more = pair_terms(
            own,
            factors_a,
            [
                Segment(into, 0, 1, columns, factors_b, d_extent)
                for into, columns in enumerate(moved)
            ],
            2,
            width,
            d_rows,
        )
        return one + more[0], two + more[1]

    one, two = lax.fori_loop(
        ROUNDS, jnp.maximum(others, ROUNDS), add_round, (terms[1], terms[2])
    )
    terms = jnp.stack([terms[0], one, two, terms[3]])
    a_rows = factors_a.shape[0]
    terms = terms[:, :, : factors_b.shape[0]]
    terms = terms.reshape(STEPS + 1, a_rows, pairs, -1).swapaxes(1, 2)
    summed = summed_over_narrow(terms.reshape(STEPS + 1, 1, -1))
    given_one = rotated(jnp.where(feeds_one, summed[STEPS:], 0.0), 1)
    given_two = rotated(jnp.where(feeds_two, summed[STEPS:], 0.0), 2)
    return jnp.concatenate([summed[:1], summed[1:2] + given_one, summed[2:3] + given_two])


def solution(mesh):
    return jax.shard_map(
        local,
        mesh=mesh,
        in_specs=(P(), P("blk", "narrow", None), P("blk", "narrow", None), P()),
        out_specs=P(None, "blk", "narrow"),
        check_vma=False,
    )
```

```python
import functools

import jax
import jax.numpy as jnp
from jax import lax
from jax.experimental import pallas as pl
from jax.experimental.pallas import tpu as pltpu
from jax.sharding import PartitionSpec as P

STEPS = 3
MOST = 8
ROUNDS = 3
GROUP = 16
LANES = 128
ROW = MOST + 1

(
    OWN,
    LIGHT,
    LIGHT_0,
    LIGHT_1,
    NEXT,
    AFTER,
    LEAD,
    PART,
    MINE,
    FED_1,
    FED_2,
    MISC,
) = range(12)
FIRST = MISC * ROW + 3
AHEAD = 4
PARTS = 4
VMEM = 60 * 1024 * 1024
SMALL = pl.CostEstimate(flops=1024, bytes_accessed=1024, transcendentals=0)


def send(value, pairs):
    return lax.ppermute(value, "blk", pairs)


def rotated(value, by):
    size = lax.axis_size("blk")
    return send(value, [(i, (i + by) % size) for i in range(size)])


def lists_kernel(position_ref, screen_ref, out_ref):
    tiles, subs = screen_ref.shape
    position = position_ref[0]

    def count_of(tile):
        return sum(jnp.where(screen_ref[tile, s] != 0, 1, 0) for s in range(subs))

    def look(tile, found):
        best, fullest, others = found
        count = count_of(tile)
        larger = count > best
        others = jnp.where(larger, best, jnp.maximum(others, count))
        return jnp.where(larger, count, best), jnp.where(larger, tile, fullest), others

    zero = jnp.int32(0)
    best, fullest, others = lax.fori_loop(0, tiles, look, (zero, zero, zero))

    def fill(row, tile, skip, count):
        for k in range(MOST):
            out_ref[row * ROW + k] = 0
        seen = jnp.int32(0)
        for s in range(subs):
            kept = screen_ref[tile, s] != 0

            @pl.when(kept & (seen >= skip))
            def _():
                out_ref[row * ROW + seen - skip] = s

            seen += jnp.where(kept, 1, 0)
        out_ref[row * ROW + MOST] = seen if count is None else count

    following = lax.rem(position + 1, tiles)
    second = lax.rem(position + 2, tiles)
    is_first = lax.rem(position, 2) == 0
    own_count = count_of(position)
    extra = jnp.maximum(best - ROUNDS, 0)
    light = jnp.minimum(own_count, ROUNDS)
    fill(OWN, position, 0, own_count)
    fill(LIGHT, position, 0, light)
    fill(LIGHT_0, position, 0, jnp.where(is_first, light, 0))
    fill(LIGHT_1, position, 0, jnp.where(is_first, 0, light))
    fill(NEXT, following, 0, None)
    fill(AFTER, second, 0, None)
    fill(MINE, fullest, ROUNDS, jnp.where(position == fullest, extra, 0))
    fill(FED_1, fullest, ROUNDS, jnp.where(following == fullest, extra, 0))
    fill(FED_2, fullest, ROUNDS, jnp.where(second == fullest, extra, 0))
    for k in range(ROW):
        other = out_ref[NEXT * ROW + k % ROUNDS] if k < 2 * ROUNDS else 0
        out_ref[LEAD * ROW + k] = jnp.where(is_first, out_ref[MINE * ROW + k], other)
        out_ref[PART * ROW + k] = jnp.where(is_first, 0, k // ROUNDS)
    out_ref[MISC * ROW] = jnp.where(fullest < 2, 2, 0) + lax.rem(fullest, 2)
    out_ref[MISC * ROW + 1] = fullest
    out_ref[MISC * ROW + 2] = others
    out_ref[FIRST] = jnp.where(is_first, 1, 0)
    for k in range(4, ROW):
        out_ref[MISC * ROW + k] = 0


def kept_lists(position, screen):
    return pl.pallas_call(
        lists_kernel,
        in_specs=[pl.BlockSpec(memory_space=pltpu.SMEM)] * 2,
        out_specs=pl.BlockSpec(memory_space=pltpu.SMEM),
        out_shape=jax.ShapeDtypeStruct(((MISC + 1) * ROW,), jnp.int32),
        name="kept_lists",
    )(position.reshape(1), screen)


def staged(count, load_from, target_of, stage, sems):
    def load(n, carry):
        load_from(
            n, lambda source: pltpu.make_async_copy(source, stage.at[n], sems.at[0, n]).start()
        )
        return carry

    def store(n, carry):
        pltpu.make_async_copy(stage.at[n], stage.at[n], sems.at[0, n]).wait()
        pltpu.make_async_copy(stage.at[n], target_of(n), sems.at[1, n]).start()
        return carry

    def finish(n, carry):
        pltpu.make_async_copy(stage.at[n], stage.at[n], sems.at[1, n]).wait()
        return carry

    for act in (load, store, finish):
        lax.fori_loop(0, count, act, 0)


def take_kernel(row, slots, start, extent, part, passes, lists_ref, source, *refs):
    out, stage, sems = refs[-3:]
    width = out.shape[-1]

    def columns(s, act):
        sub = pl.multiple_of(lists_ref[row * ROW + s] * width, width)
        first = start
        if part is not None:
            first = pl.multiple_of(start + lists_ref[part * ROW + s] * extent, extent)
        act(source.at[:, pl.ds(first, extent), pl.ds(sub, width)])

    def load_from(s, act):
        if passes:
            pl.when(lists_ref[FIRST] != 0)(lambda: act(refs[0].at[s]))
            pl.when(lists_ref[FIRST] == 0)(lambda: columns(s, act))
        else:
            columns(s, act)

    staged(slots, load_from, lambda s: out.at[s], stage, sems)


def take_columns(
    lists, amplitudes, row, slots, width, start, extent, behind=(), part=None, passing=None
):
    pairs = amplitudes.shape[0]
    others = ([] if passing is None else [passing]) + list(behind)
    return pl.pallas_call(
        functools.partial(take_kernel, row, slots, start, extent, part, passing is not None),
        in_specs=[pl.BlockSpec(memory_space=pltpu.SMEM)]
        + [pl.BlockSpec(memory_space=pltpu.HBM)] * (1 + len(others)),
        out_specs=pl.BlockSpec(memory_space=pltpu.HBM),
        out_shape=jax.ShapeDtypeStruct((slots, pairs, extent, width), amplitudes.dtype),
        scratch_shapes=[
            pltpu.VMEM((slots, pairs, extent, width), amplitudes.dtype),
            pltpu.SemaphoreType.DMA((2, slots)),
        ],
        compiler_params=pltpu.CompilerParams(vmem_limit_bytes=VMEM),
        cost_estimate=SMALL,
        name="take_columns",
    )(lists, amplitudes, *others)


def panel_kernel(start, panel, *refs):
    out, stage, sems = refs[-3:]
    parts, share, extent, _ = stage.shape

    def rows(n):
        return pl.ds(n * share, share)

    staged(
        parts,
        lambda n, act: act(panel.at[rows(n), pl.ds(start, extent), :]),
        lambda n: out.at[rows(n)],
        stage,
        sems,
    )


def take_panel(panel, start, extent, behind=()):
    b_rows, _, aux = panel.shape
    return pl.pallas_call(
        functools.partial(panel_kernel, start),
        in_specs=[pl.BlockSpec(memory_space=pltpu.HBM)] * (1 + len(behind)),
        out_specs=pl.BlockSpec(memory_space=pltpu.HBM),
        out_shape=jax.ShapeDtypeStruct((b_rows, extent, aux), panel.dtype),
        scratch_shapes=[
            pltpu.VMEM((PARTS, b_rows // PARTS, extent, aux), panel.dtype),
            pltpu.SemaphoreType.DMA((2, PARTS)),
        ],
        compiler_params=pltpu.CompilerParams(vmem_limit_bytes=VMEM),
        cost_estimate=SMALL,
        name="take_panel",
    )(panel, *behind)


def tie_kernel(*refs):
    pass


def tied(value, *behind):
    return pl.pallas_call(
        tie_kernel,
        in_specs=[pl.BlockSpec(memory_space=pltpu.HBM)] * (1 + len(behind)),
        out_specs=pl.BlockSpec(memory_space=pltpu.HBM),
        out_shape=jax.ShapeDtypeStruct(value.shape, value.dtype),
        input_output_aliases={0: 0},
        cost_estimate=SMALL,
        name="tied",
    )(value, *behind)


class Segment:
    def __init__(self, into, row, slots, amps, panel, extent, amp_at=0, panel_at=0, slot_at=0):
        self.into, self.row, self.slots = into, row, slots
        self.amps, self.panel, self.extent = amps, panel, extent
        self.amp_at, self.panel_at, self.slot_at = amp_at, panel_at, slot_at


def rows_of(extent, d_rows):
    return 2 * d_rows if extent % (2 * d_rows) == 0 else d_rows


def terms_kernel(segments, places, moves, d_rows, lists_ref, *refs):
    added, arrays = refs[: len(moves)], refs[len(moves) : -8]
    out_ref, amp_buf, panel_buf, factor_buf, mixed, total, sems, factor_sems = refs[-8:]
    factors = arrays[0]
    outs = out_ref.shape[0]
    _, most, pairs, _, width = amp_buf.shape
    b_rows = panel_buf.shape[1]
    _, _, a_rows, _, aux = factor_buf.shape

    counts = [lists_ref[seg.row * ROW + MOST] for seg in segments]
    brought = [rows_of(seg.extent, d_rows) for seg in segments]
    starts, orders = [], []
    begin = order = jnp.int32(0)
    for seg, count, rows in zip(segments, counts, brought):
        starts.append(begin)
        orders.append(order)
        begin = begin + jnp.where(count > 0, seg.extent // rows, 0)
        order = order + jnp.where(count > 0, 1, 0)
    items = begin

    def pick(at, values):
        found = values[0]
        for s in range(1, len(segments)):
            found = jnp.where(at == s, values[s], found)
        return found

    def locate(t):
        at = jnp.int32(0)
        for s in range(len(segments)):
            at = jnp.where((counts[s] > 0) & (t >= starts[s]), s, at)
        return at, t - pick(at, starts), lax.rem(pick(at, orders), AHEAD)

    def fetch(t):
        at, block, turn = locate(t)
        slot = lax.rem(t, AHEAD)
        for s, (seg, rows) in enumerate(zip(segments, brought)):
            amps, panel = arrays[places[s][0]], arrays[places[s][1]]

            @pl.when(at == s)
            def _():
                amp_d = pl.ds(pl.multiple_of(seg.amp_at + block * rows, d_rows), rows)
                panel_d = pl.ds(pl.multiple_of(seg.panel_at + block * rows, d_rows), rows)
                pltpu.make_async_copy(
                    panel.at[:, panel_d, :],
                    panel_buf.at[slot, :, pl.ds(0, rows)],
                    sems.at[slot, most],
                ).start()

                def one(k, carry):
                    sub = pl.multiple_of(lists_ref[seg.row * ROW + k] * width, width)
                    columns = pl.ds(sub, width)
                    if len(amps.shape) == 3:
                        source = amps.at[:, amp_d, columns]
                    else:
                        source = amps.at[seg.slot_at + k, :, amp_d, :]
                    pltpu.make_async_copy(
                        source, amp_buf.at[slot, k, :, pl.ds(0, rows)], sems.at[slot, k]
                    ).start()

                    @pl.when(block == 0)
                    def _():
                        pltpu.make_async_copy(
                            factors.at[:, columns, :],
                            factor_buf.at[turn, k],
                            factor_sems.at[turn, k],
                        ).start()

                    return carry

                lax.fori_loop(0, counts[s], one, 0)

    def arrive(slot, rows, block, turn, count):
        piece = panel_buf.at[slot, :, pl.ds(0, rows)]
        pltpu.make_async_copy(piece, piece, sems.at[slot, most]).wait()

        def one(k, carry):
            piece = amp_buf.at[slot, k, :, pl.ds(0, rows)]
            pltpu.make_async_copy(piece, piece, sems.at[slot, k]).wait()

            @pl.when(block == 0)
            def _():
                piece = factor_buf.at[turn, k]
                pltpu.make_async_copy(piece, piece, factor_sems.at[turn, k]).wait()

            return carry

        lax.fori_loop(0, count, one, 0)

    @pl.when(items > 0)
    def _():
        total[...] = jnp.zeros_like(total)

    def mix(low, top, slot, half, turn, count):
        columns = [
            amp_buf[slot, k, :, half, :].reshape(pairs * d_rows, width) for k in range(top)
        ]
        for k in range(low, top):
            columns[k] = jnp.where(k < count, columns[k], jnp.zeros_like(columns[k]))
        lhs = jnp.concatenate(columns, axis=1)
        for a in range(a_rows):
            rows = [factor_buf[turn, k, a] for k in range(top)]
            for k in range(low, top):
                rows[k] = jnp.where(k < count, rows[k], jnp.zeros_like(rows[k]))
            product = jnp.dot(
                lhs, jnp.concatenate(rows, axis=0), preferred_element_type=jnp.float32
            )
            mixed[a] = product.astype(mixed.dtype).reshape(pairs, d_rows, aux)

    tops = set()
    for slots in {seg.slots for seg in segments}:
        tops |= {2, 5, slots} if slots == MOST else {min(2, slots), slots}
    tops = sorted(tops)

    def step(n, carry):
        @pl.when(n < items)
        def _():
            fetch(n)

        @pl.when(n >= AHEAD - 1)
        def _():
            t = n - (AHEAD - 1)
            at, block, turn = locate(t)
            slot = lax.rem(t, AHEAD)
            count = pick(at, counts)
            into = pick(at, [seg.into for seg in segments])
            parts = pick(at, [rows // d_rows for rows in brought])
            for rows in set(brought):
                pl.when(parts == rows // d_rows)(
                    functools.partial(arrive, slot, rows, block, turn, count)
                )

            def compute(part, carry):
                first = pl.multiple_of(part * d_rows, d_rows)
                for low, top in zip([0] + tops, tops):

                    @pl.when((count > low) & (count <= top))
                    def _():
                        mix(low + 1, top, slot, pl.ds(first, d_rows), turn, count)

                partial = total[into]
                for g in range(0, d_rows, GROUP):
                    lhs = jnp.concatenate(
                        [mixed[a, :, g : g + GROUP, :].reshape(-1, aux) for a in range(a_rows)],
                        axis=0,
                    )
                    rhs = panel_buf[slot, :, pl.ds(first + g, GROUP), :]
                    partial += lax.dot_general(
                        lhs,
                        rhs.reshape(b_rows * GROUP, aux),
                        (((1,), (1,)), ((), ())),
                        preferred_element_type=jnp.float32,
                    )
                total[into] = partial
                return carry

            lax.fori_loop(0, parts, compute, 0)

        return carry

    lax.fori_loop(0, jnp.where(items > 0, items + AHEAD - 1, 0), step, 0)

    def finish(o, carry):
        _, rows, columns = total.shape
        row_d = lax.broadcasted_iota(jnp.int32, (rows, columns), 0) % GROUP
        column_d = lax.broadcasted_iota(jnp.int32, (rows, columns), 1) % GROUP
        kept = jnp.where(row_d == column_d, total[o], 0.0)
        kept = kept.reshape(rows // GROUP, GROUP, columns).sum(axis=1)
        from_b = lax.broadcasted_iota(jnp.int32, (columns, LANES), 0) // GROUP
        to_b = lax.broadcasted_iota(jnp.int32, (columns, LANES), 1)
        gather = jnp.where(from_b == to_b, 1.0, 0.0)
        out_ref[o] = jnp.dot(
            kept, gather, precision=lax.Precision.HIGHEST, preferred_element_type=jnp.float32
        )
        return carry

    @pl.when(items > 0)
    def _():
        lax.fori_loop(0, outs, finish, 0)

    @pl.when(items == 0)
    def _():
        out_ref[...] = jnp.zeros_like(out_ref)

    for ref, pairs_of in zip(added, moves):
        for source, target in pairs_of:
            out_ref[target] += ref[source]


def pair_terms(lists, factors_a, segments, outs, width, d_rows, behind=(), added=()):
    arrays, places = [factors_a], []
    for seg in segments:
        place = []
        for array in (seg.amps, seg.panel):
            known = [n for n, other in enumerate(arrays) if other is array]
            place.append(known[0] if known else len(arrays))
            if not known:
                arrays.append(array)
        places.append(place)
    arrays += behind
    a_rows, _, aux = factors_a.shape
    pairs = segments[0].amps.shape[-3]
    b_rows = segments[0].panel.shape[0]
    most = max(2, *(seg.slots for seg in segments))
    largest = max(rows_of(seg.extent, d_rows) for seg in segments)
    return pl.pallas_call(
        functools.partial(terms_kernel, segments, places, [moves for _, moves in added], d_rows),
        in_specs=[pl.BlockSpec(memory_space=pltpu.SMEM)]
        + [pl.BlockSpec(memory_space=pltpu.VMEM)] * len(added)
        + [pl.BlockSpec(memory_space=pltpu.HBM)] * len(arrays),
        out_specs=pl.BlockSpec(memory_space=pltpu.VMEM),
        scratch_shapes=[
            pltpu.VMEM((AHEAD, most, pairs, largest, width), jnp.bfloat16),
            pltpu.VMEM((AHEAD, b_rows, largest, aux), jnp.bfloat16),
            pltpu.VMEM((AHEAD, most, a_rows, width, aux), jnp.bfloat16),
            pltpu.VMEM((a_rows, pairs, d_rows, aux), jnp.bfloat16),
            pltpu.VMEM((outs, a_rows * pairs * GROUP, b_rows * GROUP), jnp.float32),
            pltpu.SemaphoreType.DMA((AHEAD, most + 1)),
            pltpu.SemaphoreType.DMA((AHEAD, most)),
        ],
        out_shape=jax.ShapeDtypeStruct((outs, a_rows * pairs, LANES), jnp.float32),
        compiler_params=pltpu.CompilerParams(vmem_limit_bytes=VMEM),
        cost_estimate=SMALL,
        name="pair_terms",
    )(lists, *(array for array, _ in added), *arrays)


def summed_over_narrow(value):
    size = lax.axis_size("narrow")
    me = lax.axis_index("narrow")
    share = value.shape[2] // size

    def part(owner):
        return lax.dynamic_slice_in_dim(value, owner * share, share, 2)

    parts = [part(me)]
    for k in range(1, size):
        to = [(i, (i + k) % size) for i in range(size)]
        parts.append(lax.ppermute(part((me + k) % size), "narrow", to))
    return sum(parts[1:], parts[0])


def local(factors_a, factors_b, amplitudes, screen):
    pairs, d_extent, virtuals = amplitudes.shape
    width = virtuals // screen.shape[1]
    tiles = lax.axis_size("blk")
    position = lax.axis_index("blk")
    extras = MOST - ROUNDS
    d_rows = min(64, d_extent // 4)

    lists = kept_lists(position, screen)
    fullest = lists[MISC * ROW + 1]
    others = lists[MISC * ROW + 2]
    is_first = position % 2 == 0
    is_full = position == fullest
    feeds_one = (position + 1) % tiles == fullest
    feeds_two = (position + 2) % tiles == fullest

    evens, odds = range(0, tiles, 2), range(1, tiles, 2)
    up = [(i, i + 1) for i in evens]
    down = [(i + 1, i) for i in evens]
    around = [(i, (i + 2) % tiles) for i in range(tiles)]

    def run(wrapped, odd, operands):
        lists, factors_a, factors_b, amplitudes = operands
        terms = functools.partial(pair_terms, lists, factors_a, width=width, d_rows=d_rows)
        columns_of = functools.partial(Segment, panel=factors_b)
        given_to = functools.partial(Segment, amps=amplitudes, slots=extras)
        take = functools.partial(take_columns, lists, amplitudes, width=width)
        cut = functools.partial(take_panel, factors_b)

        def ahead(at):
            return (at >= tiles - 2) == wrapped

        def hops(keep):
            return [(at, to) for at, to in around if keep(at)]

        def backs(keep):
            return [(to, at) for at, to in around if keep(at)]

        half, quarter = d_extent // 2, d_extent // 4
        own = columns_of(0, row=OWN, slots=MOST, amps=amplitudes, extent=d_extent)
        after = functools.partial(take, row=AFTER, slots=ROUNDS, extent=half)
        near = functools.partial(take, row=NEXT, slots=ROUNDS)
        light = functools.partial(columns_of, slots=ROUNDS)
        mine = functools.partial(columns_of, row=MINE, slots=extras)
        if odd:
            given = max(3 * d_extent // 8 // d_rows, 1) * d_rows
            moved = d_extent - given

            def seconds(at):
                return at in odds and ahead(at)

            near_l = near(start=0, extent=half)
            side_l = send(near_l, down)
            extra = take(row=MINE, slots=extras, start=0, extent=moved, behind=[near_l])
            extra_one = send(extra, up)
            extra_two = send(extra, hops(seconds))
            direct = take(
                row=AFTER, slots=ROUNDS, start=0, extent=d_extent, behind=[near_l]
            )
            got_direct = send(direct, hops(lambda at: at in evens))
            panel = cut(start=moved, extent=given, behind=[near_l])
            far = send(panel, backs(seconds))

            near_h = near(start=half, extent=half, behind=[side_l])
            side_h = send(near_h, down)
            pass_l = after(start=0, passing=side_l)
            panel = cut(start=moved, extent=given, behind=[side_l])
            near_l = near(start=0, extent=half, behind=[side_l])
            panel = tied(panel, side_h, got_direct, far, pass_l, near_l)
            beside = send(panel, down)
            near_l = tied(near_l, panel, extra_one)
            own_l = send(near_l, up)
            pass_l = tied(pass_l, near_l, extra_two)
            on_l = send(pass_l, around)
            near_h = near(start=half, extent=half, behind=[pass_l])
            own_h = send(near_h, up)
            pass_h = after(start=half, passing=side_h, behind=[near_h])
            on_h = send(pass_h, around)

            first = terms(
                [
                    own,
                    light(2, row=LIGHT_0, amps=got_direct, extent=d_extent),
                    mine(1, amps=extra_one, extent=moved),
                    mine(2, amps=extra_two, extent=moved),
                ],
                3,
                behind=[pass_h],
            )
            then = terms(
                [
                    light(0, row=LIGHT_0, amps=on_l, extent=half),
                    light(1, row=LIGHT_1, amps=on_l, extent=half),
                    light(0, row=LIGHT_1, amps=own_l, extent=half),
                ],
                2,
                behind=[first],
            )
            return terms(
                [
                    light(1, row=LIGHT_0, amps=on_h, extent=half, panel_at=half),
                    light(2, row=LIGHT_1, amps=on_h, extent=half, panel_at=half),
                    light(1, row=LIGHT_1, amps=own_h, extent=half, panel_at=half),
                    given_to(3, row=FED_1, panel=beside, extent=given, amp_at=moved),
                    given_to(3, row=FED_2, panel=far, extent=given, amp_at=moved),
                ],
                4,
                added=[(first, [(0, 0), (1, 1), (2, 2)]), (then, [(0, 1), (1, 2)])],
            )
        else:
            def firsts(at):
                return at in evens and ahead(at)

            lead = take(row=LEAD, part=PART, slots=2 * ROUNDS, start=0, extent=half)
            got_lead = send(lead, hops(lambda at: at in odds or ahead(at)))
            beside = near(start=0, extent=d_extent, behind=[lead])
            side = send(beside, up)
            extra = take(row=MINE, slots=extras, start=0, extent=quarter, behind=[beside])
            cross = send(extra, down)
            panel = cut(start=half, extent=quarter, behind=[extra])
            far_0 = send(panel, backs(firsts))
            panel = cut(start=half + quarter, extent=quarter, behind=[panel])
            far_1 = send(panel, backs(firsts))

            extra = take(
                row=MINE,
                slots=extras,
                start=quarter,
                extent=quarter,
                passing=cross,
                behind=[panel],
            )
            got_extra = send(extra, hops(ahead))
            far_0 = tied(far_0, extra, side)
            up_0 = send(far_0, up)
            lead_down = send(got_lead, down)
            after_l = after(start=0, behind=[far_0, got_lead, side])
            got_l = send(after_l, around)
            far_1 = tied(far_1, after_l, got_extra)
            up_1 = send(far_1, up)
            after_h = after(start=half, behind=[far_1, got_extra])
            got_h = send(after_h, around)

            first = terms(
                [
                    own,
                    light(1, row=LIGHT_1, amps=side, extent=d_extent),
                    mine(2, amps=got_lead, extent=half),
                ],
                3,
                behind=[after_h],
            )
            got_extra = tied(got_extra, first, up_0)
            extra_down = send(got_extra, down)
            fed = functools.partial(given_to, into=0, extent=quarter)
            down_part = functools.partial(light, 1, row=LIGHT_0, amps=lead_down, extent=half)
            then = terms(
                [
                    light(2, row=LIGHT, amps=got_l, extent=half),
                    fed(row=FED_1, panel=up_0, amp_at=half),
                    fed(row=FED_2, panel=far_0, amp_at=half),
                    fed(row=FED_2, panel=far_1, amp_at=half + quarter),
                    mine(1, amps=got_extra, extent=quarter),
                    down_part(),
                    down_part(panel_at=half, slot_at=ROUNDS),
                ],
                3,
            )
            return terms(
                [
                    light(2, row=LIGHT, amps=got_h, extent=half, panel_at=half),
                    mine(1, amps=extra_down, extent=quarter, panel_at=quarter),
                    fed(row=FED_1, panel=up_1, amp_at=half + quarter, into=3),
                ],
                4,
                added=[
                    (first, [(0, 0), (1, 1), (2, 2)]),
                    (then, [(0, 3), (1, 1), (2, 2)]),
                ],
            )

    branches = [
        functools.partial(run, wrapped, odd) for wrapped in (False, True) for odd in (False, True)
    ]
    operands = (lists, factors_a, factors_b, amplitudes)
    terms = lax.switch(lists[MISC * ROW], branches, operands)
    def add_round(r, terms):

        def only(row, count):
            sub = lax.dynamic_slice_in_dim(lists, row * ROW + r, 1)
            return jnp.concatenate([sub, jnp.zeros(MOST - 1, jnp.int32), count.reshape(1)])

        has = jnp.where((r < lists[OWN * ROW + MOST]) & ~is_full, 1, 0).astype(jnp.int32)
        own = only(OWN, has)
        moved = [
            rotated(
                take_columns(only(row, has), amplitudes, 0, 1, width, 0, d_extent), by
            )
            for row, by in ((NEXT, 1), (AFTER, 2))
        ]
        segments = [
            Segment(1 + n, 0, 1, columns, factors_b, d_extent) for n, columns in enumerate(moved)
        ]
        kept = [(n, n) for n in range(STEPS + 1)]
        return pair_terms(
            own, factors_a, segments, STEPS + 1, width, d_rows, added=[(terms, kept)]
        )

    terms = lax.fori_loop(ROUNDS, jnp.maximum(others, ROUNDS), add_round, terms)
    a_rows = factors_a.shape[0]
    terms = terms[:, :, : factors_b.shape[0]]
    terms = terms.reshape(STEPS + 1, a_rows, pairs, -1).swapaxes(1, 2)
    summed = summed_over_narrow(terms.reshape(STEPS + 1, 1, -1))
    given_one = rotated(jnp.where(feeds_one, summed[STEPS:], 0.0), 1)
    given_two = rotated(jnp.where(feeds_two, summed[STEPS:], 0.0), 2)
    return jnp.concatenate([summed[:1], summed[1:2] + given_one, summed[2:3] + given_two])


def solution(mesh):
    return jax.shard_map(
        local,
        mesh=mesh,
        in_specs=(P(), P("blk", "narrow", None), P("blk", "narrow", None), P()),
        out_specs=P(None, "blk", "narrow"),
        check_vma=False,
    )
```

```python
import functools

import jax
import jax.numpy as jnp
from jax import lax
from jax.experimental import pallas as pl
from jax.experimental.pallas import tpu as pltpu
from jax.sharding import PartitionSpec as P

STEPS = 3
MOST = 8
ROUNDS = 3
GROUP = 16
LANES = 128
ROW = MOST + 1

(
    OWN,
    LIGHT,
    LIGHT_0,
    LIGHT_1,
    NEXT,
    AFTER,
    LEAD,
    PART,
    MINE,
    FED_1,
    FED_2,
    MISC,
) = range(12)
FIRST = MISC * ROW + 3
AHEAD = 4
PARTS = 4
VMEM = 60 * 1024 * 1024
SMALL = pl.CostEstimate(flops=1024, bytes_accessed=1024, transcendentals=0)


def send(value, pairs):
    return lax.ppermute(value, "blk", pairs)


def rotated(value, by):
    size = lax.axis_size("blk")
    return send(value, [(i, (i + by) % size) for i in range(size)])


def lists_kernel(position_ref, screen_ref, out_ref):
    tiles, subs = screen_ref.shape
    position = position_ref[0]

    def count_of(tile):
        return sum(jnp.where(screen_ref[tile, s] != 0, 1, 0) for s in range(subs))

    def look(tile, found):
        best, fullest, others = found
        count = count_of(tile)
        larger = count > best
        others = jnp.where(larger, best, jnp.maximum(others, count))
        return jnp.where(larger, count, best), jnp.where(larger, tile, fullest), others

    zero = jnp.int32(0)
    best, fullest, others = lax.fori_loop(0, tiles, look, (zero, zero, zero))

    def fill(row, tile, skip, count):
        for k in range(MOST):
            out_ref[row * ROW + k] = 0
        seen = jnp.int32(0)
        for s in range(subs):
            kept = screen_ref[tile, s] != 0

            @pl.when(kept & (seen >= skip))
            def _():
                out_ref[row * ROW + seen - skip] = s

            seen += jnp.where(kept, 1, 0)
        out_ref[row * ROW + MOST] = seen if count is None else count

    following = lax.rem(position + 1, tiles)
    second = lax.rem(position + 2, tiles)
    is_first = lax.rem(position, 2) == 0
    own_count = count_of(position)
    extra = jnp.maximum(best - ROUNDS, 0)
    light = jnp.minimum(own_count, ROUNDS)
    fill(OWN, position, 0, own_count)
    fill(LIGHT, position, 0, light)
    fill(LIGHT_0, position, 0, jnp.where(is_first, light, 0))
    fill(LIGHT_1, position, 0, jnp.where(is_first, 0, light))
    fill(NEXT, following, 0, None)
    fill(AFTER, second, 0, None)
    fill(MINE, fullest, ROUNDS, jnp.where(position == fullest, extra, 0))
    fill(FED_1, fullest, ROUNDS, jnp.where(following == fullest, extra, 0))
    fill(FED_2, fullest, ROUNDS, jnp.where(second == fullest, extra, 0))
    for k in range(ROW):
        other = out_ref[NEXT * ROW + k % ROUNDS] if k < 2 * ROUNDS else 0
        out_ref[LEAD * ROW + k] = jnp.where(is_first, out_ref[MINE * ROW + k], other)
        out_ref[PART * ROW + k] = jnp.where(is_first, 0, k // ROUNDS)
    out_ref[MISC * ROW] = jnp.where(fullest < 2, 2, 0) + lax.rem(fullest, 2)
    out_ref[MISC * ROW + 1] = fullest
    out_ref[MISC * ROW + 2] = others
    out_ref[FIRST] = jnp.where(is_first, 1, 0)
    for k in range(4, ROW):
        out_ref[MISC * ROW + k] = 0


def kept_lists(position, screen):
    return pl.pallas_call(
        lists_kernel,
        in_specs=[pl.BlockSpec(memory_space=pltpu.SMEM)] * 2,
        out_specs=pl.BlockSpec(memory_space=pltpu.SMEM),
        out_shape=jax.ShapeDtypeStruct(((MISC + 1) * ROW,), jnp.int32),
        name="kept_lists",
    )(position.reshape(1), screen)


class Columns:
    def __init__(self, row, slots, start, extent, part=None, passing=None):
        self.row, self.slots, self.start, self.extent = row, slots, start, extent
        self.part, self.passing = part, passing


class Panel:
    def __init__(self, start, extent):
        self.start, self.extent = start, extent


def take_kernel(kinds, lists_ref, amplitudes, panel, *refs):
    count = len(kinds)
    sems = refs[-1]
    stages, outs = refs[-1 - count : -1], refs[-1 - 2 * count : -1 - count]

    def columns_load(kind, passing, width):
        def load(s, act):
            def own():
                sub = pl.multiple_of(lists_ref[kind.row * ROW + s] * width, width)
                first = kind.start
                if kind.part is not None:
                    further = lists_ref[kind.part * ROW + s] * kind.extent
                    first = pl.multiple_of(first + further, kind.extent)
                act(amplitudes.at[:, pl.ds(first, kind.extent), pl.ds(sub, width)])

            if passing is None:
                own()
            else:
                pl.when(lists_ref[FIRST] != 0)(lambda: act(passing.at[s]))
                pl.when(lists_ref[FIRST] == 0)(own)

        return load

    def panel_load(kind, share):
        def load(n, act):
            act(panel.at[pl.ds(n * share, share), pl.ds(kind.start, kind.extent), :])

        return load

    jobs = []
    given = 0
    for n, kind in enumerate(kinds):
        if isinstance(kind, Columns):
            passing = None
            if kind.passing is not None:
                passing = refs[given]
                given += 1
            load = columns_load(kind, passing, outs[n].shape[-1])
            jobs.append((load, lambda s, n=n: outs[n].at[s], kind.slots))
        else:
            share = stages[n].shape[1]
            load = panel_load(kind, share)
            jobs.append((load, lambda s, n=n, share=share: outs[n].at[pl.ds(s * share, share)], PARTS))

    def loops(act):
        for n, (load, target, pieces) in enumerate(jobs):

            def body(s, carry):
                act(n, s, load, target)
                return carry

            lax.fori_loop(0, pieces, body, 0)

    def start(n, s, load, target):
        stage = stages[n].at[s]
        load(s, lambda source: pltpu.make_async_copy(source, stage, sems.at[0, n, s]).start())

    def pass_on(n, s, load, target):
        stage = stages[n].at[s]
        pltpu.make_async_copy(stage, stage, sems.at[0, n, s]).wait()
        pltpu.make_async_copy(stage, target(s), sems.at[1, n, s]).start()

    def finish(n, s, load, target):
        stage = stages[n].at[s]
        pltpu.make_async_copy(stage, stage, sems.at[1, n, s]).wait()

    for act in (start, pass_on, finish):
        loops(act)


def take(lists, amplitudes, panel, kinds, width, behind=()):
    pairs = amplitudes.shape[0]
    b_rows, _, aux = panel.shape
    shapes, stages = [], []
    for kind in kinds:
        if isinstance(kind, Columns):
            shapes.append((kind.slots, pairs, kind.extent, width))
            stages.append(shapes[-1])
        else:
            shapes.append((b_rows, kind.extent, aux))
            stages.append((PARTS, b_rows // PARTS, kind.extent, aux))
    passed = [kind.passing for kind in kinds if getattr(kind, "passing", None) is not None]
    others = passed + list(behind)
    return pl.pallas_call(
        functools.partial(take_kernel, kinds),
        in_specs=[pl.BlockSpec(memory_space=pltpu.SMEM)]
        + [pl.BlockSpec(memory_space=pltpu.HBM)] * (2 + len(others)),
        out_specs=[pl.BlockSpec(memory_space=pltpu.HBM)] * len(kinds),
        out_shape=[jax.ShapeDtypeStruct(shape, amplitudes.dtype) for shape in shapes],
        scratch_shapes=[pltpu.VMEM(shape, amplitudes.dtype) for shape in stages]
        + [pltpu.SemaphoreType.DMA((2, len(kinds), max(shape[0] for shape in stages)))],
        compiler_params=pltpu.CompilerParams(vmem_limit_bytes=VMEM),
        cost_estimate=SMALL,
        name="take",
    )(lists, amplitudes, panel, *others)


def tie_kernel(*refs):
    pass


def tied(value, *behind):
    return pl.pallas_call(
        tie_kernel,
        in_specs=[pl.BlockSpec(memory_space=pltpu.HBM)] * (1 + len(behind)),
        out_specs=pl.BlockSpec(memory_space=pltpu.HBM),
        out_shape=jax.ShapeDtypeStruct(value.shape, value.dtype),
        input_output_aliases={0: 0},
        cost_estimate=SMALL,
        name="tied",
    )(value, *behind)


class Segment:
    def __init__(self, into, row, slots, amps, panel, extent, amp_at=0, panel_at=0, slot_at=0):
        self.into, self.row, self.slots = into, row, slots
        self.amps, self.panel, self.extent = amps, panel, extent
        self.amp_at, self.panel_at, self.slot_at = amp_at, panel_at, slot_at


def terms_kernel(segments, places, moves, d_rows, lists_ref, *refs):
    added, arrays = refs[: len(moves)], refs[len(moves) : -8]
    out_ref, amp_buf, panel_buf, factor_buf, mixed, total, sems, factor_sems = refs[-8:]
    factors = arrays[0]
    outs = out_ref.shape[0]
    _, most, pairs, _, width = amp_buf.shape
    b_rows = panel_buf.shape[1]
    _, _, a_rows, _, aux = factor_buf.shape

    counts = [lists_ref[seg.row * ROW + MOST] for seg in segments]
    starts, orders = [], []
    begin = order = jnp.int32(0)
    for seg, count in zip(segments, counts):
        starts.append(begin)
        orders.append(order)
        begin = begin + jnp.where(count > 0, seg.extent // d_rows, 0)
        order = order + jnp.where(count > 0, 1, 0)
    items = begin

    def pick(at, values):
        found = values[0]
        for s in range(1, len(segments)):
            found = jnp.where(at == s, values[s], found)
        return found

    def locate(t):
        at = jnp.int32(0)
        for s in range(len(segments)):
            at = jnp.where((counts[s] > 0) & (t >= starts[s]), s, at)
        return at, t - pick(at, starts), lax.rem(pick(at, orders), AHEAD)

    def fetch(t):
        at, block, turn = locate(t)
        slot = lax.rem(t, AHEAD)
        for s, seg in enumerate(segments):
            amps, panel = arrays[places[s][0]], arrays[places[s][1]]

            @pl.when(at == s)
            def _():
                amp_d = pl.ds(pl.multiple_of(seg.amp_at + block * d_rows, d_rows), d_rows)
                panel_d = pl.ds(pl.multiple_of(seg.panel_at + block * d_rows, d_rows), d_rows)
                pltpu.make_async_copy(
                    panel.at[:, panel_d, :], panel_buf.at[slot], sems.at[slot, most]
                ).start()

                def one(k, carry):
                    sub = pl.multiple_of(lists_ref[seg.row * ROW + k] * width, width)
                    columns = pl.ds(sub, width)
                    if len(amps.shape) == 3:
                        source = amps.at[:, amp_d, columns]
                    else:
                        source = amps.at[seg.slot_at + k, :, amp_d, :]
                    pltpu.make_async_copy(
                        source, amp_buf.at[slot, k], sems.at[slot, k]
                    ).start()

                    @pl.when(block == 0)
                    def _():
                        pltpu.make_async_copy(
                            factors.at[:, columns, :],
                            factor_buf.at[turn, k],
                            factor_sems.at[turn, k],
                        ).start()

                    return carry

                lax.fori_loop(0, counts[s], one, 0)

    def arrive(slot, block, turn, count):
        piece = panel_buf.at[slot]
        pltpu.make_async_copy(piece, piece, sems.at[slot, most]).wait()

        def one(k, carry):
            piece = amp_buf.at[slot, k]
            pltpu.make_async_copy(piece, piece, sems.at[slot, k]).wait()

            @pl.when(block == 0)
            def _():
                piece = factor_buf.at[turn, k]
                pltpu.make_async_copy(piece, piece, factor_sems.at[turn, k]).wait()

            return carry

        lax.fori_loop(0, count, one, 0)

    @pl.when(items > 0)
    def _():
        total[...] = jnp.zeros_like(total)

    def mix(low, top, slot, turn, count):
        columns = [amp_buf[slot, k].reshape(pairs * d_rows, width) for k in range(top)]
        for k in range(low, top):
            columns[k] = jnp.where(k < count, columns[k], jnp.zeros_like(columns[k]))
        lhs = jnp.concatenate(columns, axis=1)
        for a in range(a_rows):
            rows = [factor_buf[turn, k, a] for k in range(top)]
            for k in range(low, top):
                rows[k] = jnp.where(k < count, rows[k], jnp.zeros_like(rows[k]))
            product = jnp.dot(
                lhs, jnp.concatenate(rows, axis=0), preferred_element_type=jnp.float32
            )
            mixed[a] = product.astype(mixed.dtype).reshape(pairs, d_rows, aux)

    tops = set()
    for slots in {seg.slots for seg in segments}:
        tops |= {ROUNDS, slots} if slots == MOST else {slots}
    tops = sorted(top for top in tops if top <= ROUNDS or top == most)

    def step(n, carry):
        @pl.when(n < items)
        def _():
            fetch(n)

        @pl.when(n >= AHEAD - 1)
        def _():
            t = n - (AHEAD - 1)
            at, block, turn = locate(t)
            slot = lax.rem(t, AHEAD)
            count = pick(at, counts)
            into = pick(at, [seg.into for seg in segments])
            arrive(slot, block, turn, count)
            for low, top in zip([0] + tops, tops):

                @pl.when((count > low) & (count <= top))
                def _():
                    mix(low + 1, top, slot, turn, count)

            partial = total[into]
            for g in range(0, d_rows, GROUP):
                lhs = jnp.concatenate(
                    [mixed[a, :, g : g + GROUP, :].reshape(-1, aux) for a in range(a_rows)],
                    axis=0,
                )
                rhs = panel_buf[slot, :, g : g + GROUP, :].reshape(b_rows * GROUP, aux)
                partial += lax.dot_general(
                    lhs, rhs, (((1,), (1,)), ((), ())), preferred_element_type=jnp.float32
                )
            total[into] = partial

        return carry

    lax.fori_loop(0, jnp.where(items > 0, items + AHEAD - 1, 0), step, 0)

    def finish(o, carry):
        _, rows, columns = total.shape
        row_d = lax.broadcasted_iota(jnp.int32, (rows, columns), 0) % GROUP
        column_d = lax.broadcasted_iota(jnp.int32, (rows, columns), 1) % GROUP
        kept = jnp.where(row_d == column_d, total[o], 0.0)
        kept = kept.reshape(rows // GROUP, GROUP, columns).sum(axis=1)
        from_b = lax.broadcasted_iota(jnp.int32, (columns, LANES), 0) // GROUP
        to_b = lax.broadcasted_iota(jnp.int32, (columns, LANES), 1)
        gather = jnp.where(from_b == to_b, 1.0, 0.0)
        out_ref[o] = jnp.dot(
            kept, gather, precision=lax.Precision.HIGHEST, preferred_element_type=jnp.float32
        )
        return carry

    @pl.when(items > 0)
    def _():
        lax.fori_loop(0, outs, finish, 0)

    @pl.when(items == 0)
    def _():
        out_ref[...] = jnp.zeros_like(out_ref)

    for ref, pairs_of in zip(added, moves):
        for source, target in pairs_of:
            out_ref[target] += ref[source]


def pair_terms(lists, factors_a, segments, outs, width, d_rows, behind=(), added=()):
    arrays, places = [factors_a], []
    for seg in segments:
        place = []
        for array in (seg.amps, seg.panel):
            known = [n for n, other in enumerate(arrays) if other is array]
            place.append(known[0] if known else len(arrays))
            if not known:
                arrays.append(array)
        places.append(place)
    arrays += behind
    a_rows, _, aux = factors_a.shape
    pairs = segments[0].amps.shape[-3]
    b_rows = segments[0].panel.shape[0]
    most = max(2, *(seg.slots for seg in segments))
    return pl.pallas_call(
        functools.partial(terms_kernel, segments, places, [moves for _, moves in added], d_rows),
        in_specs=[pl.BlockSpec(memory_space=pltpu.SMEM)]
        + [pl.BlockSpec(memory_space=pltpu.VMEM)] * len(added)
        + [pl.BlockSpec(memory_space=pltpu.HBM)] * len(arrays),
        out_specs=pl.BlockSpec(memory_space=pltpu.VMEM),
        scratch_shapes=[
            pltpu.VMEM((AHEAD, most, pairs, d_rows, width), jnp.bfloat16),
            pltpu.VMEM((AHEAD, b_rows, d_rows, aux), jnp.bfloat16),
            pltpu.VMEM((AHEAD, most, a_rows, width, aux), jnp.bfloat16),
            pltpu.VMEM((a_rows, pairs, d_rows, aux), jnp.bfloat16),
            pltpu.VMEM((outs, a_rows * pairs * GROUP, b_rows * GROUP), jnp.float32),
            pltpu.SemaphoreType.DMA((AHEAD, most + 1)),
            pltpu.SemaphoreType.DMA((AHEAD, most)),
        ],
        out_shape=jax.ShapeDtypeStruct((outs, a_rows * pairs, LANES), jnp.float32),
        compiler_params=pltpu.CompilerParams(vmem_limit_bytes=VMEM),
        cost_estimate=SMALL,
        name="pair_terms",
    )(lists, *(array for array, _ in added), *arrays)


def summed_over_narrow(value):
    size = lax.axis_size("narrow")
    me = lax.axis_index("narrow")
    share = value.shape[2] // size

    def part(owner):
        return lax.dynamic_slice_in_dim(value, owner * share, share, 2)

    parts = [part(me)]
    for k in range(1, size):
        to = [(i, (i + k) % size) for i in range(size)]
        parts.append(lax.ppermute(part((me + k) % size), "narrow", to))
    return sum(parts[1:], parts[0])


def local(factors_a, factors_b, amplitudes, screen):
    pairs, d_extent, virtuals = amplitudes.shape
    width = virtuals // screen.shape[1]
    tiles = lax.axis_size("blk")
    position = lax.axis_index("blk")
    extras = MOST - ROUNDS
    d_rows = min(64, d_extent // 4)

    lists = kept_lists(position, screen)
    fullest = lists[MISC * ROW + 1]
    others = lists[MISC * ROW + 2]
    is_first = position % 2 == 0
    is_full = position == fullest
    feeds_one = (position + 1) % tiles == fullest
    feeds_two = (position + 2) % tiles == fullest

    evens, odds = range(0, tiles, 2), range(1, tiles, 2)
    up = [(i, i + 1) for i in evens]
    down = [(i + 1, i) for i in evens]
    around = [(i, (i + 2) % tiles) for i in range(tiles)]

    def run(wrapped, odd, operands):
        lists, factors_a, factors_b, amplitudes = operands
        terms = functools.partial(pair_terms, lists, factors_a, width=width, d_rows=d_rows)
        copy = functools.partial(take, lists, amplitudes, factors_b, width=width)
        columns_of = functools.partial(Segment, panel=factors_b)
        given_to = functools.partial(Segment, amps=amplitudes, slots=extras)

        def ahead(at):
            return (at >= tiles - 2) == wrapped

        def hops(keep):
            return [(at, to) for at, to in around if keep(at)]

        def backs(keep):
            return [(to, at) for at, to in around if keep(at)]

        half, quarter = d_extent // 2, d_extent // 4
        own = columns_of(0, row=OWN, slots=MOST, amps=amplitudes, extent=d_extent)
        after = functools.partial(Columns, AFTER, ROUNDS)
        near = functools.partial(Columns, NEXT, ROUNDS)
        light = functools.partial(columns_of, slots=ROUNDS)
        mine = functools.partial(columns_of, row=MINE, slots=extras)
        if odd:
            given = max(3 * d_extent // 8 // d_rows, 1) * d_rows
            moved = d_extent - given

            def seconds(at):
                return at in odds and ahead(at)

            (extra,) = copy([Columns(MINE, extras, 0, moved)])
            extra_one = send(extra, up)
            extra_two = send(extra, hops(seconds))
            near_l, direct, panel = copy(
                [near(0, half), after(0, d_extent), Panel(moved, given)], behind=[extra]
            )
            side_l = send(near_l, down)
            got_direct = send(direct, hops(lambda at: at in evens))
            far = send(panel, backs(seconds))

            near_h, near_l, panel, pass_l = copy(
                [
                    near(half, half),
                    near(0, half),
                    Panel(moved, given),
                    after(0, half, passing=side_l),
                ]
            )
            side_h = send(near_h, down)
            panel = tied(panel, side_h, got_direct, far)
            beside = send(panel, down)
            pass_l = tied(pass_l, panel)
            on_l = send(pass_l, around)
            near_h, pass_h = copy(
                [near(half, half), after(half, half, passing=side_h)], behind=[pass_l]
            )
            near_l = tied(near_l, extra_one, near_h)
            own_l = send(near_l, up)
            pass_h = tied(pass_h, near_l)
            on_h = send(pass_h, around)
            near_h = tied(near_h, pass_h, extra_two)
            own_h = send(near_h, up)

            first = terms(
                [
                    own,
                    light(2, row=LIGHT_0, amps=got_direct, extent=d_extent),
                    mine(1, amps=extra_one, extent=moved),
                    mine(2, amps=extra_two, extent=moved),
                ],
                3,
                behind=[near_h],
            )
            then = terms(
                [
                    light(0, row=LIGHT_0, amps=on_l, extent=half),
                    light(1, row=LIGHT_1, amps=on_l, extent=half),
                    light(0, row=LIGHT_1, amps=own_l, extent=half),
                ],
                2,
                behind=[first],
            )
            return terms(
                [
                    light(1, row=LIGHT_0, amps=on_h, extent=half, panel_at=half),
                    light(2, row=LIGHT_1, amps=on_h, extent=half, panel_at=half),
                    light(1, row=LIGHT_1, amps=own_h, extent=half, panel_at=half),
                    given_to(3, row=FED_1, panel=beside, extent=given, amp_at=moved),
                    given_to(3, row=FED_2, panel=far, extent=given, amp_at=moved),
                ],
                4,
                added=[(first, [(0, 0), (1, 1), (2, 2)]), (then, [(0, 1), (1, 2)])],
            )
        else:
            def firsts(at):
                return at in evens and ahead(at)

            lead, beside = copy(
                [Columns(LEAD, 2 * ROUNDS, 0, half, part=PART), near(0, d_extent)]
            )
            got_lead = send(lead, hops(lambda at: at in odds or ahead(at)))
            side = send(beside, up)
            extra, panel_0, panel_1 = copy(
                [
                    Columns(MINE, extras, 0, quarter),
                    Panel(half, quarter),
                    Panel(half + quarter, quarter),
                ],
                behind=[lead],
            )
            cross = send(extra, down)
            far_0 = send(panel_0, backs(firsts))
            far_1 = send(panel_1, backs(firsts))

            extra, after_l, after_h = copy(
                [
                    Columns(MINE, extras, quarter, quarter, passing=cross),
                    after(0, half),
                    after(half, half),
                ]
            )
            got_extra = send(extra, hops(ahead))
            far_0 = tied(far_0, extra, side)
            up_0 = send(far_0, up)
            lead_down = send(got_lead, down)
            after_l = tied(after_l, far_0, got_lead)
            got_l = send(after_l, around)
            far_1 = tied(far_1, after_l, got_extra)
            up_1 = send(far_1, up)
            after_h = tied(after_h, far_1)
            got_h = send(after_h, around)

            first = terms(
                [
                    own,
                    light(1, row=LIGHT_1, amps=side, extent=d_extent),
                    mine(2, amps=got_lead, extent=half),
                ],
                3,
                behind=[after_h],
            )
            got_extra = tied(got_extra, first, up_0)
            extra_down = send(got_extra, down)
            fed = functools.partial(given_to, into=0, extent=quarter)
            down_part = functools.partial(light, 1, row=LIGHT_0, amps=lead_down, extent=half)
            then = terms(
                [
                    light(2, row=LIGHT, amps=got_l, extent=half),
                    fed(row=FED_1, panel=up_0, amp_at=half),
                    fed(row=FED_2, panel=far_0, amp_at=half),
                    fed(row=FED_2, panel=far_1, amp_at=half + quarter),
                    mine(1, amps=got_extra, extent=quarter),
                    down_part(),
                    down_part(panel_at=half, slot_at=ROUNDS),
                ],
                3,
            )
            return terms(
                [
                    light(2, row=LIGHT, amps=got_h, extent=half, panel_at=half),
                    mine(1, amps=extra_down, extent=quarter, panel_at=quarter),
                    fed(row=FED_1, panel=up_1, amp_at=half + quarter, into=3),
                ],
                4,
                added=[
                    (first, [(0, 0), (1, 1), (2, 2)]),
                    (then, [(0, 3), (1, 1), (2, 2)]),
                ],
            )

    branches = [
        functools.partial(run, wrapped, odd) for wrapped in (False, True) for odd in (False, True)
    ]
    operands = (lists, factors_a, factors_b, amplitudes)
    terms = lax.switch(lists[MISC * ROW], branches, operands)
    def add_round(r, terms):

        def only(row, count):
            sub = lax.dynamic_slice_in_dim(lists, row * ROW + r, 1)
            return jnp.concatenate([sub, jnp.zeros(MOST - 1, jnp.int32), count.reshape(1)])

        has = jnp.where((r < lists[OWN * ROW + MOST]) & ~is_full, 1, 0).astype(jnp.int32)
        own = only(OWN, has)
        moved = [
            rotated(
                take(
                    only(row, has), amplitudes, factors_b, [Columns(0, 1, 0, d_extent)], width
                )[0],
                by,
            )
            for row, by in ((NEXT, 1), (AFTER, 2))
        ]
        segments = [
            Segment(1 + n, 0, 1, columns, factors_b, d_extent) for n, columns in enumerate(moved)
        ]
        kept = [(n, n) for n in range(STEPS + 1)]
        return pair_terms(
            own, factors_a, segments, STEPS + 1, width, d_rows, added=[(terms, kept)]
        )

    terms = lax.fori_loop(ROUNDS, jnp.maximum(others, ROUNDS), add_round, terms)
    a_rows = factors_a.shape[0]
    terms = terms[:, :, : factors_b.shape[0]]
    terms = terms.reshape(STEPS + 1, a_rows, pairs, -1).swapaxes(1, 2)
    summed = summed_over_narrow(terms.reshape(STEPS + 1, 1, -1))
    given_one = rotated(jnp.where(feeds_one, summed[STEPS:], 0.0), 1)
    given_two = rotated(jnp.where(feeds_two, summed[STEPS:], 0.0), 2)
    return jnp.concatenate([summed[:1], summed[1:2] + given_one, summed[2:3] + given_two])


def solution(mesh):
    return jax.shard_map(
        local,
        mesh=mesh,
        in_specs=(P(), P("blk", "narrow", None), P("blk", "narrow", None), P()),
        out_specs=P(None, "blk", "narrow"),
        check_vma=False,
    )
```

```python
import functools

import jax
import jax.numpy as jnp
from jax import lax
from jax.experimental import pallas as pl
from jax.experimental.pallas import tpu as pltpu
from jax.sharding import PartitionSpec as P

STEPS = 3
MOST = 8
ROUNDS = 3
GROUP = 16
LANES = 128
ROW = MOST + 1

(
    OWN,
    LIGHT,
    LIGHT_0,
    LIGHT_1,
    NEXT,
    AFTER,
    LEAD,
    PART,
    MINE,
    FED_1,
    FED_2,
    MISC,
) = range(12)
FIRST = MISC * ROW + 3
AHEAD = 4
PARTS = 4
VMEM = 60 * 1024 * 1024
SMALL = pl.CostEstimate(flops=1024, bytes_accessed=1024, transcendentals=0)


def send(value, pairs):
    return lax.ppermute(value, "blk", pairs)


def rotated(value, by):
    size = lax.axis_size("blk")
    return send(value, [(i, (i + by) % size) for i in range(size)])


def lists_kernel(position_ref, screen_ref, out_ref):
    tiles, subs = screen_ref.shape
    position = position_ref[0]

    def count_of(tile):
        return sum(jnp.where(screen_ref[tile, s] != 0, 1, 0) for s in range(subs))

    def look(tile, found):
        best, fullest, others = found
        count = count_of(tile)
        larger = count > best
        others = jnp.where(larger, best, jnp.maximum(others, count))
        return jnp.where(larger, count, best), jnp.where(larger, tile, fullest), others

    zero = jnp.int32(0)
    best, fullest, others = lax.fori_loop(0, tiles, look, (zero, zero, zero))

    def fill(row, tile, skip, count):
        for k in range(MOST):
            out_ref[row * ROW + k] = 0
        seen = jnp.int32(0)
        for s in range(subs):
            kept = screen_ref[tile, s] != 0

            @pl.when(kept & (seen >= skip))
            def _():
                out_ref[row * ROW + seen - skip] = s

            seen += jnp.where(kept, 1, 0)
        out_ref[row * ROW + MOST] = seen if count is None else count

    following = lax.rem(position + 1, tiles)
    second = lax.rem(position + 2, tiles)
    is_first = lax.rem(position, 2) == 0
    own_count = count_of(position)
    extra = jnp.maximum(best - ROUNDS, 0)
    light = jnp.minimum(own_count, ROUNDS)
    fill(OWN, position, 0, own_count)
    fill(LIGHT, position, 0, light)
    fill(LIGHT_0, position, 0, jnp.where(is_first, light, 0))
    fill(LIGHT_1, position, 0, jnp.where(is_first, 0, light))
    fill(NEXT, following, 0, None)
    fill(AFTER, second, 0, None)
    fill(MINE, fullest, ROUNDS, jnp.where(position == fullest, extra, 0))
    fill(FED_1, fullest, ROUNDS, jnp.where(following == fullest, extra, 0))
    fill(FED_2, fullest, ROUNDS, jnp.where(second == fullest, extra, 0))
    for k in range(ROW):
        other = out_ref[NEXT * ROW + k % ROUNDS] if k < 2 * ROUNDS else 0
        out_ref[LEAD * ROW + k] = jnp.where(is_first, out_ref[MINE * ROW + k], other)
        out_ref[PART * ROW + k] = jnp.where(is_first, 0, k // ROUNDS)
    out_ref[MISC * ROW] = jnp.where(fullest < 2, 2, 0) + lax.rem(fullest, 2)
    out_ref[MISC * ROW + 1] = fullest
    out_ref[MISC * ROW + 2] = others
    out_ref[FIRST] = jnp.where(is_first, 1, 0)
    for k in range(4, ROW):
        out_ref[MISC * ROW + k] = 0


def kept_lists(position, screen):
    return pl.pallas_call(
        lists_kernel,
        in_specs=[pl.BlockSpec(memory_space=pltpu.SMEM)] * 2,
        out_specs=pl.BlockSpec(memory_space=pltpu.SMEM),
        out_shape=jax.ShapeDtypeStruct(((MISC + 1) * ROW,), jnp.int32),
        name="kept_lists",
    )(position.reshape(1), screen)


class Columns:
    def __init__(self, row, slots, start, extent, part=None, passing=None):
        self.row, self.slots, self.start, self.extent = row, slots, start, extent
        self.part, self.passing = part, passing


class Panel:
    def __init__(self, start, extent):
        self.start, self.extent = start, extent


def take_kernel(kinds, lists_ref, amplitudes, panel, *refs):
    count = len(kinds)
    sems = refs[-1]
    stages, outs = refs[-1 - count : -1], refs[-1 - 2 * count : -1 - count]

    def columns_load(kind, passing, width):
        def load(s, act):
            def own():
                sub = pl.multiple_of(lists_ref[kind.row * ROW + s] * width, width)
                first = kind.start
                if kind.part is not None:
                    further = lists_ref[kind.part * ROW + s] * kind.extent
                    first = pl.multiple_of(first + further, kind.extent)
                act(amplitudes.at[:, pl.ds(first, kind.extent), pl.ds(sub, width)])

            if passing is None:
                own()
            else:
                pl.when(lists_ref[FIRST] != 0)(lambda: act(passing.at[s]))
                pl.when(lists_ref[FIRST] == 0)(own)

        return load

    def panel_load(kind, share):
        def load(n, act):
            act(panel.at[pl.ds(n * share, share), pl.ds(kind.start, kind.extent), :])

        return load

    jobs = []
    given = 0
    for n, kind in enumerate(kinds):
        if isinstance(kind, Columns):
            passing = None
            if kind.passing is not None:
                passing = refs[given]
                given += 1
            load = columns_load(kind, passing, outs[n].shape[-1])
            jobs.append((load, lambda s, n=n: outs[n].at[s], kind.slots))
        else:
            share = stages[n].shape[1]
            load = panel_load(kind, share)
            jobs.append((load, lambda s, n=n, share=share: outs[n].at[pl.ds(s * share, share)], PARTS))

    def loops(act):
        for n, (load, target, pieces) in enumerate(jobs):

            def body(s, carry):
                act(n, s, load, target)
                return carry

            lax.fori_loop(0, pieces, body, 0)

    def start(n, s, load, target):
        stage = stages[n].at[s]
        load(s, lambda source: pltpu.make_async_copy(source, stage, sems.at[0, n, s]).start())

    def pass_on(n, s, load, target):
        stage = stages[n].at[s]
        pltpu.make_async_copy(stage, stage, sems.at[0, n, s]).wait()
        pltpu.make_async_copy(stage, target(s), sems.at[1, n, s]).start()

    def finish(n, s, load, target):
        stage = stages[n].at[s]
        pltpu.make_async_copy(stage, stage, sems.at[1, n, s]).wait()

    for act in (start, pass_on, finish):
        loops(act)


def take(lists, amplitudes, panel, kinds, width, behind=()):
    pairs = amplitudes.shape[0]
    b_rows, _, aux = panel.shape
    shapes, stages = [], []
    for kind in kinds:
        if isinstance(kind, Columns):
            shapes.append((kind.slots, pairs, kind.extent, width))
            stages.append(shapes[-1])
        else:
            shapes.append((b_rows, kind.extent, aux))
            stages.append((PARTS, b_rows // PARTS, kind.extent, aux))
    passed = [kind.passing for kind in kinds if getattr(kind, "passing", None) is not None]
    others = passed + list(behind)
    return pl.pallas_call(
        functools.partial(take_kernel, kinds),
        in_specs=[pl.BlockSpec(memory_space=pltpu.SMEM)]
        + [pl.BlockSpec(memory_space=pltpu.HBM)] * (2 + len(others)),
        out_specs=[pl.BlockSpec(memory_space=pltpu.HBM)] * len(kinds),
        out_shape=[jax.ShapeDtypeStruct(shape, amplitudes.dtype) for shape in shapes],
        scratch_shapes=[pltpu.VMEM(shape, amplitudes.dtype) for shape in stages]
        + [pltpu.SemaphoreType.DMA((2, len(kinds), max(shape[0] for shape in stages)))],
        compiler_params=pltpu.CompilerParams(vmem_limit_bytes=VMEM),
        cost_estimate=SMALL,
        name="take",
    )(lists, amplitudes, panel, *others)


def tie_kernel(*refs):
    pass


def tied(value, *behind):
    return pl.pallas_call(
        tie_kernel,
        in_specs=[pl.BlockSpec(memory_space=pltpu.HBM)] * (1 + len(behind)),
        out_specs=pl.BlockSpec(memory_space=pltpu.HBM),
        out_shape=jax.ShapeDtypeStruct(value.shape, value.dtype),
        input_output_aliases={0: 0},
        cost_estimate=SMALL,
        name="tied",
    )(value, *behind)


class Segment:
    def __init__(self, into, row, slots, amps, panel, extent, amp_at=0, panel_at=0, slot_at=0):
        self.into, self.row, self.slots = into, row, slots
        self.amps, self.panel, self.extent = amps, panel, extent
        self.amp_at, self.panel_at, self.slot_at = amp_at, panel_at, slot_at


def terms_kernel(segments, places, moves, d_rows, lists_ref, *refs):
    added, arrays = refs[: len(moves)], refs[len(moves) : -8]
    out_ref, amp_buf, panel_buf, factor_buf, mixed, total, sems, factor_sems = refs[-8:]
    factors = arrays[0]
    outs = out_ref.shape[0]
    _, most, pairs, _, width = amp_buf.shape
    b_rows = panel_buf.shape[1]
    _, _, a_rows, _, aux = factor_buf.shape

    counts = [lists_ref[seg.row * ROW + MOST] for seg in segments]
    starts, orders = [], []
    begin = order = jnp.int32(0)
    for seg, count in zip(segments, counts):
        starts.append(begin)
        orders.append(order)
        begin = begin + jnp.where(count > 0, seg.extent // d_rows, 0)
        order = order + jnp.where(count > 0, 1, 0)
    items = begin

    def pick(at, values):
        found = values[0]
        for s in range(1, len(segments)):
            found = jnp.where(at == s, values[s], found)
        return found

    def pick_row(o, values):
        found = values[0]
        for n in range(1, len(values)):
            found = jnp.where(o == n, values[n], found)
        return found

    def locate(t):
        at = jnp.int32(0)
        for s in range(len(segments)):
            at = jnp.where((counts[s] > 0) & (t >= starts[s]), s, at)
        return at, t - pick(at, starts), lax.rem(pick(at, orders), AHEAD)

    def fetch(t):
        at, block, turn = locate(t)
        slot = lax.rem(t, AHEAD)
        for s, seg in enumerate(segments):
            amps, panel = arrays[places[s][0]], arrays[places[s][1]]

            @pl.when(at == s)
            def _():
                amp_d = pl.ds(pl.multiple_of(seg.amp_at + block * d_rows, d_rows), d_rows)
                panel_d = pl.ds(pl.multiple_of(seg.panel_at + block * d_rows, d_rows), d_rows)
                pltpu.make_async_copy(
                    panel.at[:, panel_d, :], panel_buf.at[slot], sems.at[slot, most]
                ).start()

                def one(k, carry):
                    sub = pl.multiple_of(lists_ref[seg.row * ROW + k] * width, width)
                    columns = pl.ds(sub, width)
                    if len(amps.shape) == 3:
                        source = amps.at[:, amp_d, columns]
                    else:
                        source = amps.at[seg.slot_at + k, :, amp_d, :]
                    pltpu.make_async_copy(
                        source, amp_buf.at[slot, k], sems.at[slot, k]
                    ).start()

                    @pl.when(block == 0)
                    def _():
                        pltpu.make_async_copy(
                            factors.at[:, columns, :],
                            factor_buf.at[turn, k],
                            factor_sems.at[turn, k],
                        ).start()

                    return carry

                lax.fori_loop(0, counts[s], one, 0)

    def arrive(slot, block, turn, count):
        piece = panel_buf.at[slot]
        pltpu.make_async_copy(piece, piece, sems.at[slot, most]).wait()

        def one(k, carry):
            piece = amp_buf.at[slot, k]
            pltpu.make_async_copy(piece, piece, sems.at[slot, k]).wait()

            @pl.when(block == 0)
            def _():
                piece = factor_buf.at[turn, k]
                pltpu.make_async_copy(piece, piece, factor_sems.at[turn, k]).wait()

            return carry

        lax.fori_loop(0, count, one, 0)

    @pl.when(items > 0)
    def _():
        total[...] = jnp.zeros_like(total)

    def mix(low, top, slot, turn, count):
        columns = [amp_buf[slot, k].reshape(pairs * d_rows, width) for k in range(top)]
        for k in range(low, top):
            columns[k] = jnp.where(k < count, columns[k], jnp.zeros_like(columns[k]))
        lhs = jnp.concatenate(columns, axis=1)
        for a in range(a_rows):
            rows = [factor_buf[turn, k, a] for k in range(top)]
            for k in range(low, top):
                rows[k] = jnp.where(k < count, rows[k], jnp.zeros_like(rows[k]))
            product = jnp.dot(
                lhs, jnp.concatenate(rows, axis=0), preferred_element_type=jnp.float32
            )
            mixed[a] = product.astype(mixed.dtype).reshape(pairs, d_rows, aux)

    tops = set()
    for slots in {seg.slots for seg in segments}:
        tops |= {ROUNDS, slots} if slots == MOST else {slots}
    tops = sorted(top for top in tops if top <= ROUNDS or top == most)

    def step(n, carry):
        @pl.when(n < items)
        def _():
            fetch(n)

        @pl.when(n >= AHEAD - 1)
        def _():
            t = n - (AHEAD - 1)
            at, block, turn = locate(t)
            slot = lax.rem(t, AHEAD)
            count = pick(at, counts)
            into = pick(at, [seg.into for seg in segments])
            arrive(slot, block, turn, count)
            for low, top in zip([0] + tops, tops):

                @pl.when((count > low) & (count <= top))
                def _():
                    mix(low + 1, top, slot, turn, count)

            partial = total[into]
            for g in range(0, d_rows, GROUP):
                lhs = jnp.concatenate(
                    [mixed[a, :, g : g + GROUP, :].reshape(-1, aux) for a in range(a_rows)],
                    axis=0,
                )
                rhs = panel_buf[slot, :, g : g + GROUP, :].reshape(b_rows * GROUP, aux)
                partial += lax.dot_general(
                    lhs, rhs, (((1,), (1,)), ((), ())), preferred_element_type=jnp.float32
                )
            total[into] = partial

        return carry

    lax.fori_loop(0, jnp.where(items > 0, items + AHEAD - 1, 0), step, 0)

    out_ref[...] = jnp.zeros_like(out_ref)
    used = [jnp.int32(0)] * outs
    for seg, count in zip(segments, counts):
        used[seg.into] = used[seg.into] + count

    def finish(o, carry):
        @pl.when(pick_row(o, used) > 0)
        def _():
            _, rows, columns = total.shape
            row_d = lax.broadcasted_iota(jnp.int32, (rows, columns), 0) % GROUP
            column_d = lax.broadcasted_iota(jnp.int32, (rows, columns), 1) % GROUP
            kept = jnp.where(row_d == column_d, total[o], 0.0)
            kept = kept.reshape(rows // GROUP, GROUP, columns).sum(axis=1)
            from_b = lax.broadcasted_iota(jnp.int32, (columns, LANES), 0) // GROUP
            to_b = lax.broadcasted_iota(jnp.int32, (columns, LANES), 1)
            gather = jnp.where(from_b == to_b, 1.0, 0.0)
            out_ref[o] = jnp.dot(
                kept,
                gather,
                precision=lax.Precision.HIGHEST,
                preferred_element_type=jnp.float32,
            )

        return carry

    lax.fori_loop(0, outs, finish, 0)

    for ref, pairs_of in zip(added, moves):
        for source, target in pairs_of:
            out_ref[target] += ref[source]


def pair_terms(lists, factors_a, segments, outs, width, d_rows, behind=(), added=()):
    arrays, places = [factors_a], []
    for seg in segments:
        place = []
        for array in (seg.amps, seg.panel):
            known = [n for n, other in enumerate(arrays) if other is array]
            place.append(known[0] if known else len(arrays))
            if not known:
                arrays.append(array)
        places.append(place)
    arrays += behind
    a_rows, _, aux = factors_a.shape
    pairs = segments[0].amps.shape[-3]
    b_rows = segments[0].panel.shape[0]
    most = max(2, *(seg.slots for seg in segments))
    return pl.pallas_call(
        functools.partial(terms_kernel, segments, places, [moves for _, moves in added], d_rows),
        in_specs=[pl.BlockSpec(memory_space=pltpu.SMEM)]
        + [pl.BlockSpec(memory_space=pltpu.VMEM)] * len(added)
        + [pl.BlockSpec(memory_space=pltpu.HBM)] * len(arrays),
        out_specs=pl.BlockSpec(memory_space=pltpu.VMEM),
        scratch_shapes=[
            pltpu.VMEM((AHEAD, most, pairs, d_rows, width), jnp.bfloat16),
            pltpu.VMEM((AHEAD, b_rows, d_rows, aux), jnp.bfloat16),
            pltpu.VMEM((AHEAD, most, a_rows, width, aux), jnp.bfloat16),
            pltpu.VMEM((a_rows, pairs, d_rows, aux), jnp.bfloat16),
            pltpu.VMEM((outs, a_rows * pairs * GROUP, b_rows * GROUP), jnp.float32),
            pltpu.SemaphoreType.DMA((AHEAD, most + 1)),
            pltpu.SemaphoreType.DMA((AHEAD, most)),
        ],
        out_shape=jax.ShapeDtypeStruct((outs, a_rows * pairs, LANES), jnp.float32),
        compiler_params=pltpu.CompilerParams(vmem_limit_bytes=VMEM),
        cost_estimate=SMALL,
        name="pair_terms",
    )(lists, *(array for array, _ in added), *arrays)


def summed_over_narrow(value):
    size = lax.axis_size("narrow")
    me = lax.axis_index("narrow")
    share = value.shape[2] // size

    def part(owner):
        return lax.dynamic_slice_in_dim(value, owner * share, share, 2)

    parts = [part(me)]
    for k in range(1, size):
        to = [(i, (i + k) % size) for i in range(size)]
        parts.append(lax.ppermute(part((me + k) % size), "narrow", to))
    return sum(parts[1:], parts[0])


def local(factors_a, factors_b, amplitudes, screen):
    pairs, d_extent, virtuals = amplitudes.shape
    width = virtuals // screen.shape[1]
    tiles = lax.axis_size("blk")
    position = lax.axis_index("blk")
    extras = MOST - ROUNDS
    d_rows = min(64, d_extent // 4)

    lists = kept_lists(position, screen)
    fullest = lists[MISC * ROW + 1]
    others = lists[MISC * ROW + 2]
    is_first = position % 2 == 0
    is_full = position == fullest
    feeds_one = (position + 1) % tiles == fullest
    feeds_two = (position + 2) % tiles == fullest

    evens, odds = range(0, tiles, 2), range(1, tiles, 2)
    up = [(i, i + 1) for i in evens]
    down = [(i + 1, i) for i in evens]
    around = [(i, (i + 2) % tiles) for i in range(tiles)]

    def run(wrapped, odd, operands):
        lists, factors_a, factors_b, amplitudes = operands
        terms = functools.partial(pair_terms, lists, factors_a, width=width, d_rows=d_rows)
        copy = functools.partial(take, lists, amplitudes, factors_b, width=width)
        columns_of = functools.partial(Segment, panel=factors_b)
        given_to = functools.partial(Segment, amps=amplitudes, slots=extras)

        def ahead(at):
            return (at >= tiles - 2) == wrapped

        def hops(keep):
            return [(at, to) for at, to in around if keep(at)]

        def backs(keep):
            return [(to, at) for at, to in around if keep(at)]

        half, quarter = d_extent // 2, d_extent // 4
        own = columns_of(0, row=OWN, slots=MOST, amps=amplitudes, extent=d_extent)
        after = functools.partial(Columns, AFTER, ROUNDS)
        near = functools.partial(Columns, NEXT, ROUNDS)
        light = functools.partial(columns_of, slots=ROUNDS)
        mine = functools.partial(columns_of, row=MINE, slots=extras)
        if odd:
            given = max(3 * d_extent // 8 // d_rows, 1) * d_rows
            moved = d_extent - given

            def seconds(at):
                return at in odds and ahead(at)

            (extra,) = copy([Columns(MINE, extras, 0, moved)])
            extra_one = send(extra, up)
            extra_two = send(extra, hops(seconds))
            near_l, direct, panel = copy(
                [near(0, half), after(0, d_extent), Panel(moved, given)], behind=[extra]
            )
            side_l = send(near_l, down)
            got_direct = send(direct, hops(lambda at: at in evens))
            far = send(panel, backs(seconds))

            near_h, near_l, panel, pass_l = copy(
                [
                    near(half, half),
                    near(0, half),
                    Panel(moved, given),
                    after(0, half, passing=side_l),
                ]
            )
            side_h = send(near_h, down)
            panel = tied(panel, side_h, got_direct, far)
            beside = send(panel, down)
            pass_l = tied(pass_l, panel)
            on_l = send(pass_l, around)
            near_l = tied(near_l, pass_l)
            own_l = send(near_l, up)
            near_h, pass_h = copy(
                [near(half, half), after(half, half, passing=side_h)], behind=[near_l]
            )
            pass_h = tied(pass_h, extra_one)
            on_h = send(pass_h, around)
            near_h = tied(near_h, pass_h, extra_two)
            own_h = send(near_h, up)

            first = terms(
                [
                    own,
                    light(2, row=LIGHT_0, amps=got_direct, extent=d_extent),
                    mine(1, amps=extra_one, extent=moved),
                    mine(2, amps=extra_two, extent=moved),
                    given_to(3, row=FED_2, panel=far, extent=given, amp_at=moved),
                ],
                4,
                behind=[near_h],
            )
            then = terms(
                [
                    light(0, row=LIGHT_0, amps=on_l, extent=half),
                    light(1, row=LIGHT_1, amps=on_l, extent=half),
                    light(0, row=LIGHT_1, amps=own_l, extent=half),
                ],
                2,
                behind=[first],
            )
            return terms(
                [
                    light(1, row=LIGHT_0, amps=on_h, extent=half, panel_at=half),
                    light(2, row=LIGHT_1, amps=on_h, extent=half, panel_at=half),
                    light(1, row=LIGHT_1, amps=own_h, extent=half, panel_at=half),
                    given_to(3, row=FED_1, panel=beside, extent=given, amp_at=moved),
                ],
                4,
                added=[(first, [(0, 0), (1, 1), (2, 2), (3, 3)]), (then, [(0, 1), (1, 2)])],
            )
        else:
            def firsts(at):
                return at in evens and ahead(at)

            lead, beside = copy(
                [Columns(LEAD, 2 * ROUNDS, 0, half, part=PART), near(0, d_extent)]
            )
            got_lead = send(lead, hops(lambda at: at in odds or ahead(at)))
            side = send(beside, up)
            extra, panel_0, panel_1 = copy(
                [
                    Columns(MINE, extras, 0, quarter),
                    Panel(half, quarter),
                    Panel(half + quarter, quarter),
                ],
                behind=[lead],
            )
            cross = send(extra, down)
            far_0 = send(panel_0, backs(firsts))
            far_1 = send(panel_1, backs(firsts))

            extra, after_l, after_h = copy(
                [
                    Columns(MINE, extras, quarter, quarter, passing=cross),
                    after(0, half),
                    after(half, half),
                ]
            )
            got_extra = send(extra, hops(ahead))
            far_0 = tied(far_0, extra)
            up_0 = send(far_0, up)
            lead_down = send(got_lead, down)
            after_l = tied(after_l, far_0, got_lead, side)
            got_l = send(after_l, around)
            far_1 = tied(far_1, after_l, got_extra)
            up_1 = send(far_1, up)
            after_h = tied(after_h, far_1)
            got_h = send(after_h, around)

            first = terms(
                [
                    own,
                    light(1, row=LIGHT_1, amps=side, extent=d_extent),
                    mine(2, amps=got_lead, extent=half),
                ],
                3,
                behind=[after_h],
            )
            got_extra = tied(got_extra, first, up_0)
            extra_down = send(got_extra, down)
            fed = functools.partial(given_to, into=0, extent=quarter)
            down_part = functools.partial(light, 1, row=LIGHT_0, amps=lead_down, extent=half)
            then = terms(
                [
                    light(2, row=LIGHT, amps=got_l, extent=half),
                    fed(row=FED_1, panel=up_0, amp_at=half),
                    fed(row=FED_2, panel=far_0, amp_at=half),
                    fed(row=FED_2, panel=far_1, amp_at=half + quarter),
                    mine(1, amps=got_extra, extent=quarter),
                    down_part(),
                    down_part(panel_at=half, slot_at=ROUNDS),
                ],
                3,
            )
            return terms(
                [
                    light(2, row=LIGHT, amps=got_h, extent=half, panel_at=half),
                    mine(1, amps=extra_down, extent=quarter, panel_at=quarter),
                    fed(row=FED_1, panel=up_1, amp_at=half + quarter, into=3),
                ],
                4,
                added=[
                    (first, [(0, 0), (1, 1), (2, 2)]),
                    (then, [(0, 3), (1, 1), (2, 2)]),
                ],
            )

    branches = [
        functools.partial(run, wrapped, odd) for wrapped in (False, True) for odd in (False, True)
    ]
    operands = (lists, factors_a, factors_b, amplitudes)
    terms = lax.switch(lists[MISC * ROW], branches, operands)
    def add_round(r, terms):

        def only(row, count):
            sub = lax.dynamic_slice_in_dim(lists, row * ROW + r, 1)
            return jnp.concatenate([sub, jnp.zeros(MOST - 1, jnp.int32), count.reshape(1)])

        has = jnp.where((r < lists[OWN * ROW + MOST]) & ~is_full, 1, 0).astype(jnp.int32)
        own = only(OWN, has)
        moved = [
            rotated(
                take(
                    only(row, has), amplitudes, factors_b, [Columns(0, 1, 0, d_extent)], width
                )[0],
                by,
            )
            for row, by in ((NEXT, 1), (AFTER, 2))
        ]
        segments = [
            Segment(1 + n, 0, 1, columns, factors_b, d_extent) for n, columns in enumerate(moved)
        ]
        kept = [(n, n) for n in range(STEPS + 1)]
        return pair_terms(
            own, factors_a, segments, STEPS + 1, width, d_rows, added=[(terms, kept)]
        )

    terms = lax.fori_loop(ROUNDS, jnp.maximum(others, ROUNDS), add_round, terms)
    a_rows = factors_a.shape[0]
    terms = terms[:, :, : factors_b.shape[0]]
    terms = terms.reshape(STEPS + 1, a_rows, pairs, -1).swapaxes(1, 2)
    summed = summed_over_narrow(terms.reshape(STEPS + 1, 1, -1))
    given_one = rotated(jnp.where(feeds_one, summed[STEPS:], 0.0), 1)
    given_two = rotated(jnp.where(feeds_two, summed[STEPS:], 0.0), 2)
    return jnp.concatenate([summed[:1], summed[1:2] + given_one, summed[2:3] + given_two])


def solution(mesh):
    return jax.shard_map(
        local,
        mesh=mesh,
        in_specs=(P(), P("blk", "narrow", None), P("blk", "narrow", None), P()),
        out_specs=P(None, "blk", "narrow"),
        check_vma=False,
    )
```

```python
import functools

import jax
import jax.numpy as jnp
from jax import lax
from jax.experimental import pallas as pl
from jax.experimental.pallas import tpu as pltpu
from jax.sharding import PartitionSpec as P

STEPS = 3
MOST = 8
ROUNDS = 3
GROUP = 16
LANES = 128
ROW = MOST + 1

(
    OWN,
    LIGHT,
    LIGHT_0,
    LIGHT_1,
    NEXT,
    AFTER,
    LEAD,
    PART,
    MINE,
    FED_1,
    FED_2,
    MISC,
) = range(12)
FIRST = MISC * ROW + 3
AHEAD = 4
PARTS = 4
VMEM = 60 * 1024 * 1024
SMALL = pl.CostEstimate(flops=1024, bytes_accessed=1024, transcendentals=0)


def send(value, pairs):
    return lax.ppermute(value, "blk", pairs)


def rotated(value, by):
    size = lax.axis_size("blk")
    return send(value, [(i, (i + by) % size) for i in range(size)])


def lists_kernel(position_ref, screen_ref, out_ref):
    tiles, subs = screen_ref.shape
    position = position_ref[0]

    def count_of(tile):
        return sum(jnp.where(screen_ref[tile, s] != 0, 1, 0) for s in range(subs))

    def look(tile, found):
        best, fullest, others = found
        count = count_of(tile)
        larger = count > best
        others = jnp.where(larger, best, jnp.maximum(others, count))
        return jnp.where(larger, count, best), jnp.where(larger, tile, fullest), others

    zero = jnp.int32(0)
    best, fullest, others = lax.fori_loop(0, tiles, look, (zero, zero, zero))

    def fill(row, tile, skip, count):
        for k in range(MOST):
            out_ref[row * ROW + k] = 0
        seen = jnp.int32(0)
        for s in range(subs):
            kept = screen_ref[tile, s] != 0

            @pl.when(kept & (seen >= skip))
            def _():
                out_ref[row * ROW + seen - skip] = s

            seen += jnp.where(kept, 1, 0)
        out_ref[row * ROW + MOST] = seen if count is None else count

    following = lax.rem(position + 1, tiles)
    second = lax.rem(position + 2, tiles)
    is_first = lax.rem(position, 2) == 0
    own_count = count_of(position)
    extra = jnp.maximum(best - ROUNDS, 0)
    light = jnp.minimum(own_count, ROUNDS)
    fill(OWN, position, 0, own_count)
    fill(LIGHT, position, 0, light)
    fill(LIGHT_0, position, 0, jnp.where(is_first, light, 0))
    fill(LIGHT_1, position, 0, jnp.where(is_first, 0, light))
    fill(NEXT, following, 0, None)
    fill(AFTER, second, 0, None)
    fill(MINE, fullest, ROUNDS, jnp.where(position == fullest, extra, 0))
    fill(FED_1, fullest, ROUNDS, jnp.where(following == fullest, extra, 0))
    fill(FED_2, fullest, ROUNDS, jnp.where(second == fullest, extra, 0))
    for k in range(ROW):
        other = out_ref[NEXT * ROW + k % ROUNDS] if k < 2 * ROUNDS else 0
        out_ref[LEAD * ROW + k] = jnp.where(is_first, out_ref[MINE * ROW + k], other)
        out_ref[PART * ROW + k] = jnp.where(is_first, 0, k // ROUNDS)
    out_ref[MISC * ROW] = jnp.where(fullest < 2, 2, 0) + lax.rem(fullest, 2)
    out_ref[MISC * ROW + 1] = fullest
    out_ref[MISC * ROW + 2] = others
    out_ref[FIRST] = jnp.where(is_first, 1, 0)
    for k in range(4, ROW):
        out_ref[MISC * ROW + k] = 0


def kept_lists(position, screen):
    return pl.pallas_call(
        lists_kernel,
        in_specs=[pl.BlockSpec(memory_space=pltpu.SMEM)] * 2,
        out_specs=pl.BlockSpec(memory_space=pltpu.SMEM),
        out_shape=jax.ShapeDtypeStruct(((MISC + 1) * ROW,), jnp.int32),
        name="kept_lists",
    )(position.reshape(1), screen)


class Columns:
    def __init__(self, row, slots, start, extent, part=None, passing=None):
        self.row, self.slots, self.start, self.extent = row, slots, start, extent
        self.part, self.passing = part, passing


class Panel:
    def __init__(self, start, extent):
        self.start, self.extent = start, extent


def take_kernel(kinds, lists_ref, amplitudes, panel, *refs):
    count = len(kinds)
    sems = refs[-1]
    stages, outs = refs[-1 - count : -1], refs[-1 - 2 * count : -1 - count]

    def columns_load(kind, passing, width):
        def load(s, act):
            def own():
                sub = pl.multiple_of(lists_ref[kind.row * ROW + s] * width, width)
                first = kind.start
                if kind.part is not None:
                    further = lists_ref[kind.part * ROW + s] * kind.extent
                    first = pl.multiple_of(first + further, kind.extent)
                act(amplitudes.at[:, pl.ds(first, kind.extent), pl.ds(sub, width)])

            if passing is None:
                own()
            else:
                pl.when(lists_ref[FIRST] != 0)(lambda: act(passing.at[s]))
                pl.when(lists_ref[FIRST] == 0)(own)

        return load

    def panel_load(kind, share):
        def load(n, act):
            act(panel.at[pl.ds(n * share, share), pl.ds(kind.start, kind.extent), :])

        return load

    jobs = []
    given = 0
    for n, kind in enumerate(kinds):
        if isinstance(kind, Columns):
            passing = None
            if kind.passing is not None:
                passing = refs[given]
                given += 1
            load = columns_load(kind, passing, outs[n].shape[-1])
            jobs.append((load, lambda s, n=n: outs[n].at[s], kind.slots))
        else:
            share = stages[n].shape[1]
            load = panel_load(kind, share)
            jobs.append((load, lambda s, n=n, share=share: outs[n].at[pl.ds(s * share, share)], PARTS))

    def loops(act):
        for n, (load, target, pieces) in enumerate(jobs):

            def body(s, carry):
                act(n, s, load, target)
                return carry

            lax.fori_loop(0, pieces, body, 0)

    def start(n, s, load, target):
        stage = stages[n].at[s]
        load(s, lambda source: pltpu.make_async_copy(source, stage, sems.at[0, n, s]).start())

    def pass_on(n, s, load, target):
        stage = stages[n].at[s]
        pltpu.make_async_copy(stage, stage, sems.at[0, n, s]).wait()
        pltpu.make_async_copy(stage, target(s), sems.at[1, n, s]).start()

    def finish(n, s, load, target):
        stage = stages[n].at[s]
        pltpu.make_async_copy(stage, stage, sems.at[1, n, s]).wait()

    for act in (start, pass_on, finish):
        loops(act)


def take(lists, amplitudes, panel, kinds, width, behind=()):
    pairs = amplitudes.shape[0]
    b_rows, _, aux = panel.shape
    shapes, stages = [], []
    for kind in kinds:
        if isinstance(kind, Columns):
            shapes.append((kind.slots, pairs, kind.extent, width))
            stages.append(shapes[-1])
        else:
            shapes.append((b_rows, kind.extent, aux))
            stages.append((PARTS, b_rows // PARTS, kind.extent, aux))
    passed = [kind.passing for kind in kinds if getattr(kind, "passing", None) is not None]
    others = passed + list(behind)
    return pl.pallas_call(
        functools.partial(take_kernel, kinds),
        in_specs=[pl.BlockSpec(memory_space=pltpu.SMEM)]
        + [pl.BlockSpec(memory_space=pltpu.HBM)] * (2 + len(others)),
        out_specs=[pl.BlockSpec(memory_space=pltpu.HBM)] * len(kinds),
        out_shape=[jax.ShapeDtypeStruct(shape, amplitudes.dtype) for shape in shapes],
        scratch_shapes=[pltpu.VMEM(shape, amplitudes.dtype) for shape in stages]
        + [pltpu.SemaphoreType.DMA((2, len(kinds), max(shape[0] for shape in stages)))],
        compiler_params=pltpu.CompilerParams(vmem_limit_bytes=VMEM),
        cost_estimate=SMALL,
        name="take",
    )(lists, amplitudes, panel, *others)


def tie_kernel(*refs):
    pass


def tied(value, *behind):
    return pl.pallas_call(
        tie_kernel,
        in_specs=[pl.BlockSpec(memory_space=pltpu.HBM)] * (1 + len(behind)),
        out_specs=pl.BlockSpec(memory_space=pltpu.HBM),
        out_shape=jax.ShapeDtypeStruct(value.shape, value.dtype),
        input_output_aliases={0: 0},
        cost_estimate=SMALL,
        name="tied",
    )(value, *behind)


class Segment:
    def __init__(self, into, row, slots, amps, panel, extent, amp_at=0, panel_at=0, slot_at=0):
        self.into, self.row, self.slots = into, row, slots
        self.amps, self.panel, self.extent = amps, panel, extent
        self.amp_at, self.panel_at, self.slot_at = amp_at, panel_at, slot_at


def terms_kernel(segments, places, moves, d_rows, lists_ref, *refs):
    added, arrays = refs[: len(moves)], refs[len(moves) : -8]
    out_ref, amp_buf, panel_buf, factor_buf, mixed, total, sems, factor_sems = refs[-8:]
    factors = arrays[0]
    outs = out_ref.shape[0]
    _, most, pairs, _, width = amp_buf.shape
    b_rows = panel_buf.shape[1]
    _, _, a_rows, _, aux = factor_buf.shape

    counts = [lists_ref[seg.row * ROW + MOST] for seg in segments]
    starts, orders = [], []
    begin = order = jnp.int32(0)
    for seg, count in zip(segments, counts):
        starts.append(begin)
        orders.append(order)
        begin = begin + jnp.where(count > 0, seg.extent // d_rows, 0)
        order = order + jnp.where(count > 0, 1, 0)
    items = begin

    def pick(at, values):
        found = values[0]
        for s in range(1, len(segments)):
            found = jnp.where(at == s, values[s], found)
        return found

    def pick_row(o, values):
        found = values[0]
        for n in range(1, len(values)):
            found = jnp.where(o == n, values[n], found)
        return found

    def locate(t):
        at = jnp.int32(0)
        for s in range(len(segments)):
            at = jnp.where((counts[s] > 0) & (t >= starts[s]), s, at)
        return at, t - pick(at, starts), lax.rem(pick(at, orders), AHEAD)

    def fetch(t):
        at, block, turn = locate(t)
        slot = lax.rem(t, AHEAD)
        for s, seg in enumerate(segments):
            amps, panel = arrays[places[s][0]], arrays[places[s][1]]

            @pl.when(at == s)
            def _():
                amp_d = pl.ds(pl.multiple_of(seg.amp_at + block * d_rows, d_rows), d_rows)
                panel_d = pl.ds(pl.multiple_of(seg.panel_at + block * d_rows, d_rows), d_rows)
                pltpu.make_async_copy(
                    panel.at[:, panel_d, :], panel_buf.at[slot], sems.at[slot, most]
                ).start()

                def one(k, carry):
                    sub = pl.multiple_of(lists_ref[seg.row * ROW + k] * width, width)
                    columns = pl.ds(sub, width)
                    if len(amps.shape) == 3:
                        source = amps.at[:, amp_d, columns]
                    else:
                        source = amps.at[seg.slot_at + k, :, amp_d, :]
                    pltpu.make_async_copy(
                        source, amp_buf.at[slot, k], sems.at[slot, k]
                    ).start()

                    @pl.when(block == 0)
                    def _():
                        pltpu.make_async_copy(
                            factors.at[:, columns, :],
                            factor_buf.at[turn, k],
                            factor_sems.at[turn, k],
                        ).start()

                    return carry

                lax.fori_loop(0, counts[s], one, 0)

    def arrive(slot, block, turn, count):
        piece = panel_buf.at[slot]
        pltpu.make_async_copy(piece, piece, sems.at[slot, most]).wait()

        def one(k, carry):
            piece = amp_buf.at[slot, k]
            pltpu.make_async_copy(piece, piece, sems.at[slot, k]).wait()

            @pl.when(block == 0)
            def _():
                piece = factor_buf.at[turn, k]
                pltpu.make_async_copy(piece, piece, factor_sems.at[turn, k]).wait()

            return carry

        lax.fori_loop(0, count, one, 0)

    @pl.when(items > 0)
    def _():
        total[...] = jnp.zeros_like(total)

    def mix(low, top, slot, turn, count):
        columns = [amp_buf[slot, k].reshape(pairs * d_rows, width) for k in range(top)]
        for k in range(low, top):
            columns[k] = jnp.where(k < count, columns[k], jnp.zeros_like(columns[k]))
        lhs = jnp.concatenate(columns, axis=1)
        for a in range(a_rows):
            rows = [factor_buf[turn, k, a] for k in range(top)]
            for k in range(low, top):
                rows[k] = jnp.where(k < count, rows[k], jnp.zeros_like(rows[k]))
            product = jnp.dot(
                lhs, jnp.concatenate(rows, axis=0), preferred_element_type=jnp.float32
            )
            mixed[a] = product.astype(mixed.dtype).reshape(pairs, d_rows, aux)

    tops = set()
    for slots in {seg.slots for seg in segments}:
        tops |= {ROUNDS, slots} if slots == MOST else {slots}
    tops = sorted(top for top in tops if top <= ROUNDS or top == most)

    def step(n, carry):
        @pl.when(n < items)
        def _():
            fetch(n)

        @pl.when(n >= AHEAD - 1)
        def _():
            t = n - (AHEAD - 1)
            at, block, turn = locate(t)
            slot = lax.rem(t, AHEAD)
            count = pick(at, counts)
            into = pick(at, [seg.into for seg in segments])
            arrive(slot, block, turn, count)
            for low, top in zip([0] + tops, tops):

                @pl.when((count > low) & (count <= top))
                def _():
                    mix(low + 1, top, slot, turn, count)

            partial = total[into]
            for g in range(0, d_rows, GROUP):
                lhs = jnp.concatenate(
                    [mixed[a, :, g : g + GROUP, :].reshape(-1, aux) for a in range(a_rows)],
                    axis=0,
                )
                rhs = panel_buf[slot, :, g : g + GROUP, :].reshape(b_rows * GROUP, aux)
                partial += lax.dot_general(
                    lhs, rhs, (((1,), (1,)), ((), ())), preferred_element_type=jnp.float32
                )
            total[into] = partial

        return carry

    lax.fori_loop(0, jnp.where(items > 0, items + AHEAD - 1, 0), step, 0)

    out_ref[...] = jnp.zeros_like(out_ref)
    used = [jnp.int32(0)] * outs
    for seg, count in zip(segments, counts):
        used[seg.into] = used[seg.into] + count

    def finish(o, carry):
        @pl.when(pick_row(o, used) > 0)
        def _():
            _, rows, columns = total.shape
            row_d = lax.broadcasted_iota(jnp.int32, (rows, columns), 0) % GROUP
            column_d = lax.broadcasted_iota(jnp.int32, (rows, columns), 1) % GROUP
            kept = jnp.where(row_d == column_d, total[o], 0.0)
            kept = kept.reshape(rows // GROUP, GROUP, columns).sum(axis=1)
            from_b = lax.broadcasted_iota(jnp.int32, (columns, LANES), 0) // GROUP
            to_b = lax.broadcasted_iota(jnp.int32, (columns, LANES), 1)
            gather = jnp.where(from_b == to_b, 1.0, 0.0)
            out_ref[o] = jnp.dot(
                kept,
                gather,
                precision=lax.Precision.HIGHEST,
                preferred_element_type=jnp.float32,
            )

        return carry

    lax.fori_loop(0, outs, finish, 0)

    for ref, pairs_of in zip(added, moves):
        for source, target in pairs_of:
            out_ref[target] += ref[source]


def pair_terms(lists, factors_a, segments, outs, width, d_rows, behind=(), added=()):
    arrays, places = [factors_a], []
    for seg in segments:
        place = []
        for array in (seg.amps, seg.panel):
            known = [n for n, other in enumerate(arrays) if other is array]
            place.append(known[0] if known else len(arrays))
            if not known:
                arrays.append(array)
        places.append(place)
    arrays += behind
    a_rows, _, aux = factors_a.shape
    pairs = segments[0].amps.shape[-3]
    b_rows = segments[0].panel.shape[0]
    most = max(2, *(seg.slots for seg in segments))
    return pl.pallas_call(
        functools.partial(terms_kernel, segments, places, [moves for _, moves in added], d_rows),
        in_specs=[pl.BlockSpec(memory_space=pltpu.SMEM)]
        + [pl.BlockSpec(memory_space=pltpu.VMEM)] * len(added)
        + [pl.BlockSpec(memory_space=pltpu.HBM)] * len(arrays),
        out_specs=pl.BlockSpec(memory_space=pltpu.VMEM),
        scratch_shapes=[
            pltpu.VMEM((AHEAD, most, pairs, d_rows, width), jnp.bfloat16),
            pltpu.VMEM((AHEAD, b_rows, d_rows, aux), jnp.bfloat16),
            pltpu.VMEM((AHEAD, most, a_rows, width, aux), jnp.bfloat16),
            pltpu.VMEM((a_rows, pairs, d_rows, aux), jnp.bfloat16),
            pltpu.VMEM((outs, a_rows * pairs * GROUP, b_rows * GROUP), jnp.float32),
            pltpu.SemaphoreType.DMA((AHEAD, most + 1)),
            pltpu.SemaphoreType.DMA((AHEAD, most)),
        ],
        out_shape=jax.ShapeDtypeStruct((outs, a_rows * pairs, LANES), jnp.float32),
        compiler_params=pltpu.CompilerParams(vmem_limit_bytes=VMEM),
        cost_estimate=SMALL,
        name="pair_terms",
    )(lists, *(array for array, _ in added), *arrays)


def summed_over_narrow(value):
    size = lax.axis_size("narrow")
    me = lax.axis_index("narrow")
    share = value.shape[2] // size

    def part(owner):
        return lax.dynamic_slice_in_dim(value, owner * share, share, 2)

    parts = [part(me)]
    for k in range(1, size):
        to = [(i, (i + k) % size) for i in range(size)]
        parts.append(lax.ppermute(part((me + k) % size), "narrow", to))
    return sum(parts[1:], parts[0])


def local(factors_a, factors_b, amplitudes, screen):
    pairs, d_extent, virtuals = amplitudes.shape
    width = virtuals // screen.shape[1]
    tiles = lax.axis_size("blk")
    position = lax.axis_index("blk")
    extras = MOST - ROUNDS
    d_rows = min(64, d_extent // 4)

    lists = kept_lists(position, screen)
    fullest = lists[MISC * ROW + 1]
    others = lists[MISC * ROW + 2]
    is_first = position % 2 == 0
    is_full = position == fullest
    feeds_one = (position + 1) % tiles == fullest
    feeds_two = (position + 2) % tiles == fullest

    evens, odds = range(0, tiles, 2), range(1, tiles, 2)
    up = [(i, i + 1) for i in evens]
    down = [(i + 1, i) for i in evens]
    around = [(i, (i + 2) % tiles) for i in range(tiles)]

    def run(wrapped, odd, operands):
        lists, factors_a, factors_b, amplitudes = operands
        terms = functools.partial(pair_terms, lists, factors_a, width=width, d_rows=d_rows)
        copy = functools.partial(take, lists, amplitudes, factors_b, width=width)
        columns_of = functools.partial(Segment, panel=factors_b)
        given_to = functools.partial(Segment, amps=amplitudes, slots=extras)

        def ahead(at):
            return (at >= tiles - 2) == wrapped

        def hops(keep):
            return [(at, to) for at, to in around if keep(at)]

        def backs(keep):
            return [(to, at) for at, to in around if keep(at)]

        half, quarter = d_extent // 2, d_extent // 4
        low = 5 * d_extent // 8 // d_rows * d_rows
        high = d_extent - low
        own = columns_of(0, row=OWN, slots=MOST, amps=amplitudes, extent=d_extent)
        after = functools.partial(Columns, AFTER, ROUNDS)
        near = functools.partial(Columns, NEXT, ROUNDS)
        light = functools.partial(columns_of, slots=ROUNDS)
        mine = functools.partial(columns_of, row=MINE, slots=extras)
        if odd:
            given = max(3 * d_extent // 8 // d_rows, 1) * d_rows
            moved = d_extent - given

            def seconds(at):
                return at in odds and ahead(at)

            (extra,) = copy([Columns(MINE, extras, 0, moved)])
            extra_one = send(extra, up)
            extra_two = send(extra, hops(seconds))
            near_l, direct, panel = copy(
                [near(0, low), after(0, d_extent), Panel(moved, given)], behind=[extra]
            )
            side_l = send(near_l, down)
            got_direct = send(direct, hops(lambda at: at in evens))
            far = send(panel, backs(seconds))

            near_h, near_l, own_near_h, panel = copy(
                [near(low, high), near(0, low), near(low, high), Panel(moved, given)],
                behind=[near_l],
            )
            near_h = tied(near_h, side_l)
            side_h = send(near_h, down)
            (pass_l,) = copy([after(0, low, passing=side_l)], behind=[near_h])
            panel = tied(panel, side_h, got_direct, far, pass_l)
            beside = send(panel, down)
            pass_l = tied(pass_l, panel)
            on_l = send(pass_l, around)
            near_l = tied(near_l, pass_l)
            own_l = send(near_l, up)
            (pass_h,) = copy([after(low, high, passing=side_h)], behind=[near_l])
            pass_h = tied(pass_h, extra_one)
            on_h = send(pass_h, around)
            near_h = tied(own_near_h, pass_h, extra_two)
            own_h = send(near_h, up)

            first = terms(
                [
                    own,
                    light(2, row=LIGHT_0, amps=got_direct, extent=d_extent),
                    mine(1, amps=extra_one, extent=moved),
                    mine(2, amps=extra_two, extent=moved),
                    given_to(3, row=FED_2, panel=far, extent=given, amp_at=moved),
                ],
                4,
                behind=[near_h],
            )
            then = terms(
                [
                    light(0, row=LIGHT_0, amps=on_l, extent=low),
                    light(1, row=LIGHT_1, amps=on_l, extent=low),
                    light(0, row=LIGHT_1, amps=own_l, extent=low),
                ],
                2,
                behind=[first],
            )
            return terms(
                [
                    light(1, row=LIGHT_0, amps=on_h, extent=high, panel_at=low),
                    light(2, row=LIGHT_1, amps=on_h, extent=high, panel_at=low),
                    light(1, row=LIGHT_1, amps=own_h, extent=high, panel_at=low),
                    given_to(3, row=FED_1, panel=beside, extent=given, amp_at=moved),
                ],
                4,
                added=[(first, [(0, 0), (1, 1), (2, 2), (3, 3)]), (then, [(0, 1), (1, 2)])],
            )
        else:
            def firsts(at):
                return at in evens and ahead(at)

            lead, beside = copy(
                [Columns(LEAD, 2 * ROUNDS, 0, half, part=PART), near(0, d_extent)]
            )
            got_lead = send(lead, hops(lambda at: at in odds or ahead(at)))
            side = send(beside, up)
            extra, panel_0, panel_1 = copy(
                [
                    Columns(MINE, extras, 0, quarter),
                    Panel(half, quarter),
                    Panel(half + quarter, quarter),
                ],
                behind=[lead],
            )
            cross = send(extra, down)
            far_0 = send(panel_0, backs(firsts))
            far_1 = send(panel_1, backs(firsts))

            extra, after_l, after_h = copy(
                [
                    Columns(MINE, extras, quarter, quarter, passing=cross),
                    after(0, low),
                    after(low, high),
                ]
            )
            got_extra = send(extra, hops(ahead))
            far_0 = tied(far_0, extra)
            up_0 = send(far_0, up)
            lead_down = send(got_lead, down)
            after_l = tied(after_l, far_0, got_lead, side)
            got_l = send(after_l, around)
            far_1 = tied(far_1, after_l, got_extra)
            up_1 = send(far_1, up)
            after_h = tied(after_h, far_1)
            got_h = send(after_h, around)

            first = terms(
                [
                    own,
                    light(1, row=LIGHT_1, amps=side, extent=d_extent),
                    mine(2, amps=got_lead, extent=half),
                ],
                3,
                behind=[after_h],
            )
            got_extra = tied(got_extra, first, up_0)
            extra_down = send(got_extra, down)
            fed = functools.partial(given_to, into=0, extent=quarter)
            down_part = functools.partial(light, 1, row=LIGHT_0, amps=lead_down, extent=half)
            then = terms(
                [
                    light(2, row=LIGHT, amps=got_l, extent=low),
                    fed(row=FED_1, panel=up_0, amp_at=half),
                    fed(row=FED_2, panel=far_0, amp_at=half),
                    fed(row=FED_2, panel=far_1, amp_at=half + quarter),
                    mine(1, amps=got_extra, extent=quarter),
                    down_part(),
                    down_part(panel_at=half, slot_at=ROUNDS),
                ],
                3,
            )
            return terms(
                [
                    light(2, row=LIGHT, amps=got_h, extent=high, panel_at=low),
                    mine(1, amps=extra_down, extent=quarter, panel_at=quarter),
                    fed(row=FED_1, panel=up_1, amp_at=half + quarter, into=3),
                ],
                4,
                added=[
                    (first, [(0, 0), (1, 1), (2, 2)]),
                    (then, [(0, 3), (1, 1), (2, 2)]),
                ],
            )

    branches = [
        functools.partial(run, wrapped, odd) for wrapped in (False, True) for odd in (False, True)
    ]
    operands = (lists, factors_a, factors_b, amplitudes)
    terms = lax.switch(lists[MISC * ROW], branches, operands)
    def add_round(r, terms):

        def only(row, count):
            sub = lax.dynamic_slice_in_dim(lists, row * ROW + r, 1)
            return jnp.concatenate([sub, jnp.zeros(MOST - 1, jnp.int32), count.reshape(1)])

        has = jnp.where((r < lists[OWN * ROW + MOST]) & ~is_full, 1, 0).astype(jnp.int32)
        own = only(OWN, has)
        moved = [
            rotated(
                take(
                    only(row, has), amplitudes, factors_b, [Columns(0, 1, 0, d_extent)], width
                )[0],
                by,
            )
            for row, by in ((NEXT, 1), (AFTER, 2))
        ]
        segments = [
            Segment(1 + n, 0, 1, columns, factors_b, d_extent) for n, columns in enumerate(moved)
        ]
        kept = [(n, n) for n in range(STEPS + 1)]
        return pair_terms(
            own, factors_a, segments, STEPS + 1, width, d_rows, added=[(terms, kept)]
        )

    terms = lax.fori_loop(ROUNDS, jnp.maximum(others, ROUNDS), add_round, terms)
    a_rows = factors_a.shape[0]
    terms = terms[:, :, : factors_b.shape[0]]
    terms = terms.reshape(STEPS + 1, a_rows, pairs, -1).swapaxes(1, 2)
    summed = summed_over_narrow(terms.reshape(STEPS + 1, 1, -1))
    given_one = rotated(jnp.where(feeds_one, summed[STEPS:], 0.0), 1)
    given_two = rotated(jnp.where(feeds_two, summed[STEPS:], 0.0), 2)
    return jnp.concatenate([summed[:1], summed[1:2] + given_one, summed[2:3] + given_two])


def solution(mesh):
    return jax.shard_map(
        local,
        mesh=mesh,
        in_specs=(P(), P("blk", "narrow", None), P("blk", "narrow", None), P()),
        out_specs=P(None, "blk", "narrow"),
        check_vma=False,
    )
```

```python
import functools

import jax
import jax.numpy as jnp
from jax import lax
from jax.experimental import pallas as pl
from jax.experimental.pallas import tpu as pltpu
from jax.sharding import PartitionSpec as P

STEPS = 3
MOST = 8
ROUNDS = 3
GROUP = 16
LANES = 128
ROW = MOST + 1

(
    OWN,
    LIGHT,
    LIGHT_0,
    LIGHT_1,
    NEXT,
    AFTER,
    LEAD,
    PART,
    REST,
    REST_PART,
    MINE,
    MINE_L,
    MINE_H,
    FED_1,
    FED_2,
    MISC,
) = range(16)
FIRST = MISC * ROW + 3
AHEAD = 4
PARTS = 4
VMEM = 60 * 1024 * 1024
SMALL = pl.CostEstimate(flops=1024, bytes_accessed=1024, transcendentals=0)


def send(value, pairs):
    return lax.ppermute(value, "blk", pairs)


def rotated(value, by):
    size = lax.axis_size("blk")
    return send(value, [(i, (i + by) % size) for i in range(size)])


def lists_kernel(position_ref, screen_ref, out_ref):
    tiles, subs = screen_ref.shape
    position = position_ref[0]

    def count_of(tile):
        return sum(jnp.where(screen_ref[tile, s] != 0, 1, 0) for s in range(subs))

    def look(tile, found):
        best, fullest, others = found
        count = count_of(tile)
        larger = count > best
        others = jnp.where(larger, best, jnp.maximum(others, count))
        return jnp.where(larger, count, best), jnp.where(larger, tile, fullest), others

    zero = jnp.int32(0)
    best, fullest, others = lax.fori_loop(0, tiles, look, (zero, zero, zero))

    def fill(row, tile, skip, count):
        for k in range(MOST):
            out_ref[row * ROW + k] = 0
        seen = jnp.int32(0)
        for s in range(subs):
            kept = screen_ref[tile, s] != 0

            @pl.when(kept & (seen >= skip))
            def _():
                out_ref[row * ROW + seen - skip] = s

            seen += jnp.where(kept, 1, 0)
        out_ref[row * ROW + MOST] = seen if count is None else count

    following = lax.rem(position + 1, tiles)
    second = lax.rem(position + 2, tiles)
    is_first = lax.rem(position, 2) == 0
    own_count = count_of(position)
    extra = jnp.maximum(best - ROUNDS, 0)
    light = jnp.minimum(own_count, ROUNDS)
    fill(OWN, position, 0, own_count)
    fill(LIGHT, position, 0, light)
    fill(LIGHT_0, position, 0, jnp.where(is_first, light, 0))
    fill(LIGHT_1, position, 0, jnp.where(is_first, 0, light))
    fill(NEXT, following, 0, None)
    fill(AFTER, second, 0, None)
    fill(MINE, fullest, ROUNDS, jnp.where(position == fullest, extra, 0))
    fill(FED_1, fullest, ROUNDS, jnp.where(following == fullest, extra, 0))
    fill(FED_2, fullest, ROUNDS, jnp.where(second == fullest, extra, 0))
    mine = jnp.where(position == fullest, extra, 0)
    fill(MINE_L, fullest, ROUNDS, jnp.minimum(mine, ROUNDS))
    fill(MINE_H, fullest, 2 * ROUNDS, jnp.maximum(mine - ROUNDS, 0))
    for k in range(ROW):
        for row, part, source in ((LEAD, PART, MINE_L), (REST, REST_PART, MINE_H)):
            other = out_ref[NEXT * ROW + k] if k < ROUNDS else 0
            out_ref[row * ROW + k] = jnp.where(is_first, out_ref[source * ROW + k], other)
            out_ref[part * ROW + k] = jnp.where(is_first, 0, 0 if part == PART else 1)
    out_ref[MISC * ROW] = jnp.where(fullest < 2, 2, 0) + lax.rem(fullest, 2)
    out_ref[MISC * ROW + 1] = fullest
    out_ref[MISC * ROW + 2] = others
    out_ref[FIRST] = jnp.where(is_first, 1, 0)
    for k in range(4, ROW):
        out_ref[MISC * ROW + k] = 0


def kept_lists(position, screen):
    return pl.pallas_call(
        lists_kernel,
        in_specs=[pl.BlockSpec(memory_space=pltpu.SMEM)] * 2,
        out_specs=pl.BlockSpec(memory_space=pltpu.SMEM),
        out_shape=jax.ShapeDtypeStruct(((MISC + 1) * ROW,), jnp.int32),
        name="kept_lists",
    )(position.reshape(1), screen)


class Columns:
    def __init__(self, row, slots, start, extent, part=None, passing=None):
        self.row, self.slots, self.start, self.extent = row, slots, start, extent
        self.part, self.passing = part, passing


class Panel:
    def __init__(self, start, extent):
        self.start, self.extent = start, extent


def take_kernel(kinds, lists_ref, amplitudes, panel, *refs):
    count = len(kinds)
    sems = refs[-1]
    stages, outs = refs[-1 - count : -1], refs[-1 - 2 * count : -1 - count]

    def columns_load(kind, passing, width):
        def load(s, act):
            def own():
                sub = pl.multiple_of(lists_ref[kind.row * ROW + s] * width, width)
                first = kind.start
                if kind.part is not None:
                    further = lists_ref[kind.part * ROW + s] * kind.extent
                    first = pl.multiple_of(first + further, kind.extent)
                act(amplitudes.at[:, pl.ds(first, kind.extent), pl.ds(sub, width)])

            if passing is None:
                own()
            else:
                pl.when(lists_ref[FIRST] != 0)(lambda: act(passing.at[s]))
                pl.when(lists_ref[FIRST] == 0)(own)

        return load

    def panel_load(kind, share):
        def load(n, act):
            act(panel.at[pl.ds(n * share, share), pl.ds(kind.start, kind.extent), :])

        return load

    jobs = []
    given = 0
    for n, kind in enumerate(kinds):
        if isinstance(kind, Columns):
            passing = None
            if kind.passing is not None:
                passing = refs[given]
                given += 1
            load = columns_load(kind, passing, outs[n].shape[-1])
            jobs.append((load, lambda s, n=n: outs[n].at[s], kind.slots))
        else:
            share = stages[n].shape[1]
            load = panel_load(kind, share)
            jobs.append((load, lambda s, n=n, share=share: outs[n].at[pl.ds(s * share, share)], PARTS))

    def loops(act):
        for n, (load, target, pieces) in enumerate(jobs):

            def body(s, carry):
                act(n, s, load, target)
                return carry

            lax.fori_loop(0, pieces, body, 0)

    def start(n, s, load, target):
        stage = stages[n].at[s]
        load(s, lambda source: pltpu.make_async_copy(source, stage, sems.at[0, n, s]).start())

    def pass_on(n, s, load, target):
        stage = stages[n].at[s]
        pltpu.make_async_copy(stage, stage, sems.at[0, n, s]).wait()
        pltpu.make_async_copy(stage, target(s), sems.at[1, n, s]).start()

    def finish(n, s, load, target):
        stage = stages[n].at[s]
        pltpu.make_async_copy(stage, stage, sems.at[1, n, s]).wait()

    for act in (start, pass_on, finish):
        loops(act)


def take(lists, amplitudes, panel, kinds, width, behind=()):
    pairs = amplitudes.shape[0]
    b_rows, _, aux = panel.shape
    shapes, stages = [], []
    for kind in kinds:
        if isinstance(kind, Columns):
            shapes.append((kind.slots, pairs, kind.extent, width))
            stages.append(shapes[-1])
        else:
            shapes.append((b_rows, kind.extent, aux))
            stages.append((PARTS, b_rows // PARTS, kind.extent, aux))
    passed = [kind.passing for kind in kinds if getattr(kind, "passing", None) is not None]
    others = passed + list(behind)
    return pl.pallas_call(
        functools.partial(take_kernel, kinds),
        in_specs=[pl.BlockSpec(memory_space=pltpu.SMEM)]
        + [pl.BlockSpec(memory_space=pltpu.HBM)] * (2 + len(others)),
        out_specs=[pl.BlockSpec(memory_space=pltpu.HBM)] * len(kinds),
        out_shape=[jax.ShapeDtypeStruct(shape, amplitudes.dtype) for shape in shapes],
        scratch_shapes=[pltpu.VMEM(shape, amplitudes.dtype) for shape in stages]
        + [pltpu.SemaphoreType.DMA((2, len(kinds), max(shape[0] for shape in stages)))],
        compiler_params=pltpu.CompilerParams(vmem_limit_bytes=VMEM),
        cost_estimate=SMALL,
        name="take",
    )(lists, amplitudes, panel, *others)


def tie_kernel(*refs):
    pass


def tied(value, *behind):
    return pl.pallas_call(
        tie_kernel,
        in_specs=[pl.BlockSpec(memory_space=pltpu.HBM)] * (1 + len(behind)),
        out_specs=pl.BlockSpec(memory_space=pltpu.HBM),
        out_shape=jax.ShapeDtypeStruct(value.shape, value.dtype),
        input_output_aliases={0: 0},
        cost_estimate=SMALL,
        name="tied",
    )(value, *behind)


class Segment:
    def __init__(self, into, row, slots, amps, panel, extent, amp_at=0, panel_at=0, slot_at=0):
        self.into, self.row, self.slots = into, row, slots
        self.amps, self.panel, self.extent = amps, panel, extent
        self.amp_at, self.panel_at, self.slot_at = amp_at, panel_at, slot_at


def terms_kernel(segments, places, moves, d_rows, lists_ref, *refs):
    added, arrays = refs[: len(moves)], refs[len(moves) : -8]
    out_ref, amp_buf, panel_buf, factor_buf, mixed, total, sems, factor_sems = refs[-8:]
    factors = arrays[0]
    outs = out_ref.shape[0]
    _, most, pairs, _, width = amp_buf.shape
    b_rows = panel_buf.shape[1]
    _, _, a_rows, _, aux = factor_buf.shape

    counts = [lists_ref[seg.row * ROW + MOST] for seg in segments]
    starts, orders = [], []
    begin = order = jnp.int32(0)
    for seg, count in zip(segments, counts):
        starts.append(begin)
        orders.append(order)
        begin = begin + jnp.where(count > 0, seg.extent // d_rows, 0)
        order = order + jnp.where(count > 0, 1, 0)
    items = begin

    def pick(at, values):
        found = values[0]
        for s in range(1, len(segments)):
            found = jnp.where(at == s, values[s], found)
        return found

    def pick_row(o, values):
        found = values[0]
        for n in range(1, len(values)):
            found = jnp.where(o == n, values[n], found)
        return found

    def locate(t):
        at = jnp.int32(0)
        for s in range(len(segments)):
            at = jnp.where((counts[s] > 0) & (t >= starts[s]), s, at)
        return at, t - pick(at, starts), lax.rem(pick(at, orders), AHEAD)

    def fetch(t):
        at, block, turn = locate(t)
        slot = lax.rem(t, AHEAD)
        for s, seg in enumerate(segments):
            amps, panel = arrays[places[s][0]], arrays[places[s][1]]

            @pl.when(at == s)
            def _():
                amp_d = pl.ds(pl.multiple_of(seg.amp_at + block * d_rows, d_rows), d_rows)
                panel_d = pl.ds(pl.multiple_of(seg.panel_at + block * d_rows, d_rows), d_rows)
                pltpu.make_async_copy(
                    panel.at[:, panel_d, :], panel_buf.at[slot], sems.at[slot, most]
                ).start()

                def one(k, carry):
                    sub = pl.multiple_of(lists_ref[seg.row * ROW + k] * width, width)
                    columns = pl.ds(sub, width)
                    if len(amps.shape) == 3:
                        source = amps.at[:, amp_d, columns]
                    else:
                        source = amps.at[seg.slot_at + k, :, amp_d, :]
                    pltpu.make_async_copy(
                        source, amp_buf.at[slot, k], sems.at[slot, k]
                    ).start()

                    @pl.when(block == 0)
                    def _():
                        pltpu.make_async_copy(
                            factors.at[:, columns, :],
                            factor_buf.at[turn, k],
                            factor_sems.at[turn, k],
                        ).start()

                    return carry

                lax.fori_loop(0, counts[s], one, 0)

    def arrive(slot, block, turn, count):
        piece = panel_buf.at[slot]
        pltpu.make_async_copy(piece, piece, sems.at[slot, most]).wait()

        def one(k, carry):
            piece = amp_buf.at[slot, k]
            pltpu.make_async_copy(piece, piece, sems.at[slot, k]).wait()

            @pl.when(block == 0)
            def _():
                piece = factor_buf.at[turn, k]
                pltpu.make_async_copy(piece, piece, factor_sems.at[turn, k]).wait()

            return carry

        lax.fori_loop(0, count, one, 0)

    @pl.when(items > 0)
    def _():
        total[...] = jnp.zeros_like(total)

    def mix(low, top, slot, turn, count):
        columns = [amp_buf[slot, k].reshape(pairs * d_rows, width) for k in range(top)]
        for k in range(low, top):
            columns[k] = jnp.where(k < count, columns[k], jnp.zeros_like(columns[k]))
        lhs = jnp.concatenate(columns, axis=1)
        for a in range(a_rows):
            rows = [factor_buf[turn, k, a] for k in range(top)]
            for k in range(low, top):
                rows[k] = jnp.where(k < count, rows[k], jnp.zeros_like(rows[k]))
            product = jnp.dot(
                lhs, jnp.concatenate(rows, axis=0), preferred_element_type=jnp.float32
            )
            mixed[a] = product.astype(mixed.dtype).reshape(pairs, d_rows, aux)

    tops = set()
    for slots in {seg.slots for seg in segments}:
        tops |= {ROUNDS, slots} if slots == MOST else {slots}
    tops = sorted(top for top in tops if top <= ROUNDS or top == most)

    def step(n, carry):
        @pl.when(n < items)
        def _():
            fetch(n)

        @pl.when(n >= AHEAD - 1)
        def _():
            t = n - (AHEAD - 1)
            at, block, turn = locate(t)
            slot = lax.rem(t, AHEAD)
            count = pick(at, counts)
            into = pick(at, [seg.into for seg in segments])
            arrive(slot, block, turn, count)
            for low, top in zip([0] + tops, tops):

                @pl.when((count > low) & (count <= top))
                def _():
                    mix(low + 1, top, slot, turn, count)

            partial = total[into]
            for g in range(0, d_rows, GROUP):
                lhs = jnp.concatenate(
                    [mixed[a, :, g : g + GROUP, :].reshape(-1, aux) for a in range(a_rows)],
                    axis=0,
                )
                rhs = panel_buf[slot, :, g : g + GROUP, :].reshape(b_rows * GROUP, aux)
                partial += lax.dot_general(
                    lhs, rhs, (((1,), (1,)), ((), ())), preferred_element_type=jnp.float32
                )
            total[into] = partial

        return carry

    lax.fori_loop(0, jnp.where(items > 0, items + AHEAD - 1, 0), step, 0)

    out_ref[...] = jnp.zeros_like(out_ref)
    used = [jnp.int32(0)] * outs
    for seg, count in zip(segments, counts):
        used[seg.into] = used[seg.into] + count

    def finish(o, carry):
        @pl.when(pick_row(o, used) > 0)
        def _():
            _, rows, columns = total.shape
            row_d = lax.broadcasted_iota(jnp.int32, (rows, columns), 0) % GROUP
            column_d = lax.broadcasted_iota(jnp.int32, (rows, columns), 1) % GROUP
            kept = jnp.where(row_d == column_d, total[o], 0.0)
            kept = kept.reshape(rows // GROUP, GROUP, columns).sum(axis=1)
            from_b = lax.broadcasted_iota(jnp.int32, (columns, LANES), 0) // GROUP
            to_b = lax.broadcasted_iota(jnp.int32, (columns, LANES), 1)
            gather = jnp.where(from_b == to_b, 1.0, 0.0)
            out_ref[o] = jnp.dot(
                kept,
                gather,
                precision=lax.Precision.HIGHEST,
                preferred_element_type=jnp.float32,
            )

        return carry

    lax.fori_loop(0, outs, finish, 0)

    for ref, pairs_of in zip(added, moves):
        for source, target in pairs_of:
            out_ref[target] += ref[source]


def pair_terms(lists, factors_a, segments, outs, width, d_rows, behind=(), added=()):
    arrays, places = [factors_a], []
    for seg in segments:
        place = []
        for array in (seg.amps, seg.panel):
            known = [n for n, other in enumerate(arrays) if other is array]
            place.append(known[0] if known else len(arrays))
            if not known:
                arrays.append(array)
        places.append(place)
    arrays += behind
    a_rows, _, aux = factors_a.shape
    pairs = segments[0].amps.shape[-3]
    b_rows = segments[0].panel.shape[0]
    most = max(2, *(seg.slots for seg in segments))
    return pl.pallas_call(
        functools.partial(terms_kernel, segments, places, [moves for _, moves in added], d_rows),
        in_specs=[pl.BlockSpec(memory_space=pltpu.SMEM)]
        + [pl.BlockSpec(memory_space=pltpu.VMEM)] * len(added)
        + [pl.BlockSpec(memory_space=pltpu.HBM)] * len(arrays),
        out_specs=pl.BlockSpec(memory_space=pltpu.VMEM),
        scratch_shapes=[
            pltpu.VMEM((AHEAD, most, pairs, d_rows, width), jnp.bfloat16),
            pltpu.VMEM((AHEAD, b_rows, d_rows, aux), jnp.bfloat16),
            pltpu.VMEM((AHEAD, most, a_rows, width, aux), jnp.bfloat16),
            pltpu.VMEM((a_rows, pairs, d_rows, aux), jnp.bfloat16),
            pltpu.VMEM((outs, a_rows * pairs * GROUP, b_rows * GROUP), jnp.float32),
            pltpu.SemaphoreType.DMA((AHEAD, most + 1)),
            pltpu.SemaphoreType.DMA((AHEAD, most)),
        ],
        out_shape=jax.ShapeDtypeStruct((outs, a_rows * pairs, LANES), jnp.float32),
        compiler_params=pltpu.CompilerParams(vmem_limit_bytes=VMEM),
        cost_estimate=SMALL,
        name="pair_terms",
    )(lists, *(array for array, _ in added), *arrays)


def summed_over_narrow(value):
    size = lax.axis_size("narrow")
    me = lax.axis_index("narrow")
    share = value.shape[2] // size

    def part(owner):
        return lax.dynamic_slice_in_dim(value, owner * share, share, 2)

    parts = [part(me)]
    for k in range(1, size):
        to = [(i, (i + k) % size) for i in range(size)]
        parts.append(lax.ppermute(part((me + k) % size), "narrow", to))
    return sum(parts[1:], parts[0])


def local(factors_a, factors_b, amplitudes, screen):
    pairs, d_extent, virtuals = amplitudes.shape
    width = virtuals // screen.shape[1]
    tiles = lax.axis_size("blk")
    position = lax.axis_index("blk")
    extras = MOST - ROUNDS
    d_rows = min(64, d_extent // 4)

    lists = kept_lists(position, screen)
    fullest = lists[MISC * ROW + 1]
    others = lists[MISC * ROW + 2]
    is_first = position % 2 == 0
    is_full = position == fullest
    feeds_one = (position + 1) % tiles == fullest
    feeds_two = (position + 2) % tiles == fullest

    evens, odds = range(0, tiles, 2), range(1, tiles, 2)
    up = [(i, i + 1) for i in evens]
    down = [(i + 1, i) for i in evens]
    around = [(i, (i + 2) % tiles) for i in range(tiles)]

    def run(wrapped, odd, operands):
        lists, factors_a, factors_b, amplitudes = operands
        terms = functools.partial(pair_terms, lists, factors_a, width=width, d_rows=d_rows)
        copy = functools.partial(take, lists, amplitudes, factors_b, width=width)
        columns_of = functools.partial(Segment, panel=factors_b)
        given_to = functools.partial(Segment, amps=amplitudes, slots=extras)

        def ahead(at):
            return (at >= tiles - 2) == wrapped

        def hops(keep):
            return [(at, to) for at, to in around if keep(at)]

        def backs(keep):
            return [(to, at) for at, to in around if keep(at)]

        half, quarter = d_extent // 2, d_extent // 4
        low = 5 * d_extent // 8 // d_rows * d_rows
        high = d_extent - low
        own = columns_of(0, row=OWN, slots=MOST, amps=amplitudes, extent=d_extent)
        after = functools.partial(Columns, AFTER, ROUNDS)
        near = functools.partial(Columns, NEXT, ROUNDS)
        light = functools.partial(columns_of, slots=ROUNDS)
        mine = functools.partial(columns_of, row=MINE, slots=extras)
        if odd:
            given = max(3 * d_extent // 8 // d_rows, 1) * d_rows
            moved = d_extent - given

            def seconds(at):
                return at in odds and ahead(at)

            (extra,) = copy([Columns(MINE, extras, 0, moved)])
            extra_one = send(extra, up)
            extra_two = send(extra, hops(seconds))
            near_l, direct, panel = copy(
                [near(0, low), after(0, d_extent), Panel(moved, given)], behind=[extra]
            )
            side_l = send(near_l, down)
            got_direct = send(direct, hops(lambda at: at in evens))
            far = send(panel, backs(seconds))

            near_h, near_l, own_near_h, panel = copy(
                [near(low, high), near(0, low), near(low, high), Panel(moved, given)],
                behind=[near_l],
            )
            near_h = tied(near_h, side_l)
            side_h = send(near_h, down)
            (pass_l,) = copy([after(0, low, passing=side_l)], behind=[near_h])
            panel = tied(panel, side_h, extra_one, pass_l)
            beside = send(panel, down)
            near_l = tied(near_l, panel)
            own_l = send(near_l, up)
            pass_l = tied(pass_l, near_l, got_direct, extra_two)
            on_l = send(pass_l, around)
            (pass_h,) = copy([after(low, high, passing=side_h)], behind=[panel])
            pass_h = tied(pass_h, pass_l, far)
            on_h = send(pass_h, around)
            near_h = tied(own_near_h, pass_h)
            own_h = send(near_h, up)

            first = terms(
                [
                    own,
                    light(2, row=LIGHT_0, amps=got_direct, extent=d_extent),
                    mine(1, amps=extra_one, extent=moved),
                    mine(2, amps=extra_two, extent=moved),
                    given_to(3, row=FED_2, panel=far, extent=given, amp_at=moved),
                ],
                4,
                behind=[near_h],
            )
            then = terms(
                [
                    light(0, row=LIGHT_0, amps=on_l, extent=low),
                    light(1, row=LIGHT_1, amps=on_l, extent=low),
                    light(0, row=LIGHT_1, amps=own_l, extent=low),
                ],
                2,
                behind=[first],
            )
            return terms(
                [
                    light(1, row=LIGHT_0, amps=on_h, extent=high, panel_at=low),
                    light(2, row=LIGHT_1, amps=on_h, extent=high, panel_at=low),
                    light(1, row=LIGHT_1, amps=own_h, extent=high, panel_at=low),
                    given_to(3, row=FED_1, panel=beside, extent=given, amp_at=moved),
                ],
                4,
                added=[(first, [(0, 0), (1, 1), (2, 2), (3, 3)]), (then, [(0, 1), (1, 2)])],
            )
        else:
            def firsts(at):
                return at in evens and ahead(at)

            def early(at):
                return at in odds or ahead(at)

            lead = functools.partial(Columns, LEAD, ROUNDS, 0, half)
            rest = functools.partial(Columns, REST, ROUNDS, 0, half)
            lead_l, lead_h, beside = copy(
                [lead(part=PART), rest(part=REST_PART), near(0, d_extent)]
            )
            got_lead_l = send(lead_l, hops(early))
            got_lead_h = send(lead_h, hops(early))
            side = send(beside, up)
            extra, panel_0 = copy(
                [Columns(MINE, extras, 0, quarter), Panel(half, quarter)], behind=[lead_l]
            )
            cross = send(extra, down)
            far_0 = send(panel_0, backs(firsts))
            panel_1, after_l, after_h = copy(
                [Panel(half + quarter, quarter), after(0, low), after(low, high)],
                behind=[extra],
            )

            lead_down_l = send(got_lead_l, down)
            panel_1 = tied(panel_1, cross)
            far_1 = send(panel_1, backs(firsts))
            (extra,) = copy(
                [Columns(MINE, extras, quarter, quarter, passing=cross)], behind=[panel_1]
            )
            far_0 = tied(far_0, extra, got_lead_l)
            up_0 = send(far_0, up)
            extra = tied(extra, got_lead_h)
            got_extra = send(extra, hops(ahead))
            lead_down_h = send(got_lead_h, down)
            after_l = tied(after_l, extra, side, lead_down_l)
            got_l = send(after_l, around)
            far_1 = tied(far_1, after_l)
            up_1 = send(far_1, up)
            got_extra = tied(got_extra, far_1)
            extra_down = send(got_extra, down)
            after_h = tied(after_h, got_extra, lead_down_h)
            got_h = send(after_h, around)

            first = terms(
                [
                    own,
                    light(1, row=LIGHT_1, amps=side, extent=d_extent),
                    light(1, row=LIGHT_0, amps=lead_down_l, extent=half),
                    light(1, row=LIGHT_0, amps=lead_down_h, extent=half, panel_at=half),
                    columns_of(2, row=MINE_L, slots=ROUNDS, amps=got_lead_l, extent=half),
                    columns_of(2, row=MINE_H, slots=ROUNDS, amps=got_lead_h, extent=half),
                ],
                3,
                behind=[after_h],
            )
            fed = functools.partial(given_to, into=0, extent=quarter)
            then = terms(
                [
                    fed(row=FED_1, panel=up_0, amp_at=half),
                    fed(row=FED_2, panel=far_0, amp_at=half),
                    fed(row=FED_2, panel=far_1, amp_at=half + quarter),
                    mine(1, amps=got_extra, extent=quarter),
                    mine(1, amps=extra_down, extent=quarter, panel_at=quarter),
                    light(2, row=LIGHT, amps=got_l, extent=low),
                ],
                3,
                behind=[first],
            )
            return terms(
                [
                    light(2, row=LIGHT, amps=got_h, extent=high, panel_at=low),
                    fed(row=FED_1, panel=up_1, amp_at=half + quarter, into=3),
                ],
                4,
                added=[
                    (first, [(0, 0), (1, 1), (2, 2)]),
                    (then, [(0, 3), (1, 1), (2, 2)]),
                ],
            )

    branches = [
        functools.partial(run, wrapped, odd) for wrapped in (False, True) for odd in (False, True)
    ]
    operands = (lists, factors_a, factors_b, amplitudes)
    terms = lax.switch(lists[MISC * ROW], branches, operands)
    def add_round(r, terms):

        def only(row, count):
            sub = lax.dynamic_slice_in_dim(lists, row * ROW + r, 1)
            return jnp.concatenate([sub, jnp.zeros(MOST - 1, jnp.int32), count.reshape(1)])

        has = jnp.where((r < lists[OWN * ROW + MOST]) & ~is_full, 1, 0).astype(jnp.int32)
        own = only(OWN, has)
        moved = [
            rotated(
                take(
                    only(row, has), amplitudes, factors_b, [Columns(0, 1, 0, d_extent)], width
                )[0],
                by,
            )
            for row, by in ((NEXT, 1), (AFTER, 2))
        ]
        segments = [
            Segment(1 + n, 0, 1, columns, factors_b, d_extent) for n, columns in enumerate(moved)
        ]
        kept = [(n, n) for n in range(STEPS + 1)]
        return pair_terms(
            own, factors_a, segments, STEPS + 1, width, d_rows, added=[(terms, kept)]
        )

    terms = lax.fori_loop(ROUNDS, jnp.maximum(others, ROUNDS), add_round, terms)
    a_rows = factors_a.shape[0]
    terms = terms[:, :, : factors_b.shape[0]]
    terms = terms.reshape(STEPS + 1, a_rows, pairs, -1).swapaxes(1, 2)
    summed = summed_over_narrow(terms.reshape(STEPS + 1, 1, -1))
    given_one = rotated(jnp.where(feeds_one, summed[STEPS:], 0.0), 1)
    given_two = rotated(jnp.where(feeds_two, summed[STEPS:], 0.0), 2)
    return jnp.concatenate([summed[:1], summed[1:2] + given_one, summed[2:3] + given_two])


def solution(mesh):
    return jax.shard_map(
        local,
        mesh=mesh,
        in_specs=(P(), P("blk", "narrow", None), P("blk", "narrow", None), P()),
        out_specs=P(None, "blk", "narrow"),
        check_vma=False,
    )
```

```python
import functools

import jax
import jax.numpy as jnp
from jax import lax
from jax.experimental import pallas as pl
from jax.experimental.pallas import tpu as pltpu
from jax.sharding import PartitionSpec as P

STEPS = 3
MOST = 8
ROUNDS = 3
GROUP = 16
LANES = 128
ROW = MOST + 1

(
    OWN,
    LIGHT,
    LIGHT_0,
    LIGHT_1,
    NEXT,
    AFTER,
    LEAD,
    PART,
    REST,
    REST_PART,
    MINE,
    MINE_L,
    MINE_H,
    FED_1,
    FED_2,
    MISC,
) = range(16)
FIRST = MISC * ROW + 3
AHEAD = 4
PARTS = 4
VMEM = 60 * 1024 * 1024
SMALL = pl.CostEstimate(flops=1024, bytes_accessed=1024, transcendentals=0)


def send(value, pairs):
    return lax.ppermute(value, "blk", pairs)


def rotated(value, by):
    size = lax.axis_size("blk")
    return send(value, [(i, (i + by) % size) for i in range(size)])


def lists_kernel(position_ref, screen_ref, out_ref):
    tiles, subs = screen_ref.shape
    position = position_ref[0]

    def count_of(tile):
        return sum(jnp.where(screen_ref[tile, s] != 0, 1, 0) for s in range(subs))

    def look(tile, found):
        best, fullest, others = found
        count = count_of(tile)
        larger = count > best
        others = jnp.where(larger, best, jnp.maximum(others, count))
        return jnp.where(larger, count, best), jnp.where(larger, tile, fullest), others

    zero = jnp.int32(0)
    best, fullest, others = lax.fori_loop(0, tiles, look, (zero, zero, zero))

    def fill(row, tile, skip, count):
        for k in range(MOST):
            out_ref[row * ROW + k] = 0
        seen = jnp.int32(0)
        for s in range(subs):
            kept = screen_ref[tile, s] != 0

            @pl.when(kept & (seen >= skip))
            def _():
                out_ref[row * ROW + seen - skip] = s

            seen += jnp.where(kept, 1, 0)
        out_ref[row * ROW + MOST] = seen if count is None else count

    following = lax.rem(position + 1, tiles)
    second = lax.rem(position + 2, tiles)
    is_first = lax.rem(position, 2) == 0
    own_count = count_of(position)
    extra = jnp.maximum(best - ROUNDS, 0)
    light = jnp.minimum(own_count, ROUNDS)
    fill(OWN, position, 0, own_count)
    fill(LIGHT, position, 0, light)
    fill(LIGHT_0, position, 0, jnp.where(is_first, light, 0))
    fill(LIGHT_1, position, 0, jnp.where(is_first, 0, light))
    fill(NEXT, following, 0, None)
    fill(AFTER, second, 0, None)
    fill(MINE, fullest, ROUNDS, jnp.where(position == fullest, extra, 0))
    fill(FED_1, fullest, ROUNDS, jnp.where(following == fullest, extra, 0))
    fill(FED_2, fullest, ROUNDS, jnp.where(second == fullest, extra, 0))
    mine = jnp.where(position == fullest, extra, 0)
    fill(MINE_L, fullest, ROUNDS, jnp.minimum(mine, ROUNDS))
    fill(MINE_H, fullest, 2 * ROUNDS, jnp.maximum(mine - ROUNDS, 0))
    for k in range(ROW):
        for row, part, source in ((LEAD, PART, MINE_L), (REST, REST_PART, MINE_H)):
            other = out_ref[NEXT * ROW + k] if k < ROUNDS else 0
            out_ref[row * ROW + k] = jnp.where(is_first, out_ref[source * ROW + k], other)
            out_ref[part * ROW + k] = jnp.where(is_first, 0, 0 if part == PART else 1)
    out_ref[MISC * ROW] = jnp.where(fullest < 2, 2, 0) + lax.rem(fullest, 2)
    out_ref[MISC * ROW + 1] = fullest
    out_ref[MISC * ROW + 2] = others
    out_ref[FIRST] = jnp.where(is_first, 1, 0)
    for k in range(4, ROW):
        out_ref[MISC * ROW + k] = 0


def kept_lists(position, screen):
    return pl.pallas_call(
        lists_kernel,
        in_specs=[pl.BlockSpec(memory_space=pltpu.SMEM)] * 2,
        out_specs=pl.BlockSpec(memory_space=pltpu.SMEM),
        out_shape=jax.ShapeDtypeStruct(((MISC + 1) * ROW,), jnp.int32),
        name="kept_lists",
    )(position.reshape(1), screen)


class Columns:
    def __init__(self, row, slots, start, extent, part=None, passing=None):
        self.row, self.slots, self.start, self.extent = row, slots, start, extent
        self.part, self.passing = part, passing


class Panel:
    def __init__(self, start, extent):
        self.start, self.extent = start, extent


def take_kernel(kinds, lists_ref, amplitudes, panel, *refs):
    count = len(kinds)
    sems = refs[-1]
    stages, outs = refs[-1 - count : -1], refs[-1 - 2 * count : -1 - count]

    def columns_load(kind, passing, width):
        def load(s, act):
            def own():
                sub = pl.multiple_of(lists_ref[kind.row * ROW + s] * width, width)
                first = kind.start
                if kind.part is not None:
                    further = lists_ref[kind.part * ROW + s] * kind.extent
                    first = pl.multiple_of(first + further, kind.extent)
                act(amplitudes.at[:, pl.ds(first, kind.extent), pl.ds(sub, width)])

            if passing is None:
                own()
            else:
                pl.when(lists_ref[FIRST] != 0)(lambda: act(passing.at[s]))
                pl.when(lists_ref[FIRST] == 0)(own)

        return load

    def panel_load(kind, share):
        def load(n, act):
            act(panel.at[pl.ds(n * share, share), pl.ds(kind.start, kind.extent), :])

        return load

    jobs = []
    given = 0
    for n, kind in enumerate(kinds):
        if isinstance(kind, Columns):
            passing = None
            if kind.passing is not None:
                passing = refs[given]
                given += 1
            load = columns_load(kind, passing, outs[n].shape[-1])
            jobs.append((load, lambda s, n=n: outs[n].at[s], kind.slots))
        else:
            share = stages[n].shape[1]
            load = panel_load(kind, share)
            jobs.append((load, lambda s, n=n, share=share: outs[n].at[pl.ds(s * share, share)], PARTS))

    def loops(act):
        for n, (load, target, pieces) in enumerate(jobs):

            def body(s, carry):
                act(n, s, load, target)
                return carry

            lax.fori_loop(0, pieces, body, 0)

    def start(n, s, load, target):
        stage = stages[n].at[s]
        load(s, lambda source: pltpu.make_async_copy(source, stage, sems.at[0, n, s]).start())

    def pass_on(n, s, load, target):
        stage = stages[n].at[s]
        pltpu.make_async_copy(stage, stage, sems.at[0, n, s]).wait()
        pltpu.make_async_copy(stage, target(s), sems.at[1, n, s]).start()

    def finish(n, s, load, target):
        stage = stages[n].at[s]
        pltpu.make_async_copy(stage, stage, sems.at[1, n, s]).wait()

    for act in (start, pass_on, finish):
        loops(act)


def take(lists, amplitudes, panel, kinds, width, behind=()):
    pairs = amplitudes.shape[0]
    b_rows, _, aux = panel.shape
    shapes, stages = [], []
    for kind in kinds:
        if isinstance(kind, Columns):
            shapes.append((kind.slots, pairs, kind.extent, width))
            stages.append(shapes[-1])
        else:
            shapes.append((b_rows, kind.extent, aux))
            stages.append((PARTS, b_rows // PARTS, kind.extent, aux))
    passed = [kind.passing for kind in kinds if getattr(kind, "passing", None) is not None]
    others = passed + list(behind)
    return pl.pallas_call(
        functools.partial(take_kernel, kinds),
        in_specs=[pl.BlockSpec(memory_space=pltpu.SMEM)]
        + [pl.BlockSpec(memory_space=pltpu.HBM)] * (2 + len(others)),
        out_specs=[pl.BlockSpec(memory_space=pltpu.HBM)] * len(kinds),
        out_shape=[jax.ShapeDtypeStruct(shape, amplitudes.dtype) for shape in shapes],
        scratch_shapes=[pltpu.VMEM(shape, amplitudes.dtype) for shape in stages]
        + [pltpu.SemaphoreType.DMA((2, len(kinds), max(shape[0] for shape in stages)))],
        compiler_params=pltpu.CompilerParams(vmem_limit_bytes=VMEM),
        cost_estimate=SMALL,
        name="take",
    )(lists, amplitudes, panel, *others)


def tie_kernel(*refs):
    pass


def tied(value, *behind):
    return pl.pallas_call(
        tie_kernel,
        in_specs=[pl.BlockSpec(memory_space=pltpu.HBM)] * (1 + len(behind)),
        out_specs=pl.BlockSpec(memory_space=pltpu.HBM),
        out_shape=jax.ShapeDtypeStruct(value.shape, value.dtype),
        input_output_aliases={0: 0},
        cost_estimate=SMALL,
        name="tied",
    )(value, *behind)


class Segment:
    def __init__(self, into, row, slots, amps, panel, extent, amp_at=0, panel_at=0, slot_at=0):
        self.into, self.row, self.slots = into, row, slots
        self.amps, self.panel, self.extent = amps, panel, extent
        self.amp_at, self.panel_at, self.slot_at = amp_at, panel_at, slot_at


def terms_kernel(segments, places, moves, d_rows, lists_ref, *refs):
    added, arrays = refs[: len(moves)], refs[len(moves) : -8]
    out_ref, amp_buf, panel_buf, factor_buf, mixed, total, sems, factor_sems = refs[-8:]
    factors = arrays[0]
    outs = out_ref.shape[0]
    _, most, pairs, _, width = amp_buf.shape
    b_rows = panel_buf.shape[1]
    _, _, a_rows, _, aux = factor_buf.shape

    counts = [lists_ref[seg.row * ROW + MOST] for seg in segments]
    starts, orders = [], []
    begin = order = jnp.int32(0)
    for seg, count in zip(segments, counts):
        starts.append(begin)
        orders.append(order)
        begin = begin + jnp.where(count > 0, seg.extent // d_rows, 0)
        order = order + jnp.where(count > 0, 1, 0)
    items = begin

    def pick(at, values):
        found = values[0]
        for s in range(1, len(segments)):
            found = jnp.where(at == s, values[s], found)
        return found

    def pick_row(o, values):
        found = values[0]
        for n in range(1, len(values)):
            found = jnp.where(o == n, values[n], found)
        return found

    def locate(t):
        at = jnp.int32(0)
        for s in range(len(segments)):
            at = jnp.where((counts[s] > 0) & (t >= starts[s]), s, at)
        return at, t - pick(at, starts), lax.rem(pick(at, orders), AHEAD)

    def fetch(t):
        at, block, turn = locate(t)
        slot = lax.rem(t, AHEAD)
        for s, seg in enumerate(segments):
            amps, panel = arrays[places[s][0]], arrays[places[s][1]]

            @pl.when(at == s)
            def _():
                amp_d = pl.ds(pl.multiple_of(seg.amp_at + block * d_rows, d_rows), d_rows)
                panel_d = pl.ds(pl.multiple_of(seg.panel_at + block * d_rows, d_rows), d_rows)
                pltpu.make_async_copy(
                    panel.at[:, panel_d, :], panel_buf.at[slot], sems.at[slot, most]
                ).start()

                def one(k, carry):
                    sub = pl.multiple_of(lists_ref[seg.row * ROW + k] * width, width)
                    columns = pl.ds(sub, width)
                    if len(amps.shape) == 3:
                        source = amps.at[:, amp_d, columns]
                    else:
                        source = amps.at[seg.slot_at + k, :, amp_d, :]
                    pltpu.make_async_copy(
                        source, amp_buf.at[slot, k], sems.at[slot, k]
                    ).start()

                    @pl.when(block == 0)
                    def _():
                        pltpu.make_async_copy(
                            factors.at[:, columns, :],
                            factor_buf.at[turn, k],
                            factor_sems.at[turn, k],
                        ).start()

                    return carry

                lax.fori_loop(0, counts[s], one, 0)

    def arrive(slot, block, turn, count):
        piece = panel_buf.at[slot]
        pltpu.make_async_copy(piece, piece, sems.at[slot, most]).wait()

        def one(k, carry):
            piece = amp_buf.at[slot, k]
            pltpu.make_async_copy(piece, piece, sems.at[slot, k]).wait()

            @pl.when(block == 0)
            def _():
                piece = factor_buf.at[turn, k]
                pltpu.make_async_copy(piece, piece, factor_sems.at[turn, k]).wait()

            return carry

        lax.fori_loop(0, count, one, 0)

    @pl.when(items > 0)
    def _():
        total[...] = jnp.zeros_like(total)

    def mix(low, top, slot, turn, count):
        columns = [amp_buf[slot, k].reshape(pairs * d_rows, width) for k in range(top)]
        for k in range(low, top):
            columns[k] = jnp.where(k < count, columns[k], jnp.zeros_like(columns[k]))
        lhs = jnp.concatenate(columns, axis=1)
        for a in range(a_rows):
            rows = [factor_buf[turn, k, a] for k in range(top)]
            for k in range(low, top):
                rows[k] = jnp.where(k < count, rows[k], jnp.zeros_like(rows[k]))
            product = jnp.dot(
                lhs, jnp.concatenate(rows, axis=0), preferred_element_type=jnp.float32
            )
            mixed[a] = product.astype(mixed.dtype).reshape(pairs, d_rows, aux)

    tops = set()
    for slots in {seg.slots for seg in segments}:
        tops |= {ROUNDS, slots} if slots == MOST else {slots}
    tops = sorted(top for top in tops if top <= ROUNDS or top == most)

    def step(n, carry):
        @pl.when(n < items)
        def _():
            fetch(n)

        @pl.when(n >= AHEAD - 1)
        def _():
            t = n - (AHEAD - 1)
            at, block, turn = locate(t)
            slot = lax.rem(t, AHEAD)
            count = pick(at, counts)
            into = pick(at, [seg.into for seg in segments])
            arrive(slot, block, turn, count)
            for low, top in zip([0] + tops, tops):

                @pl.when((count > low) & (count <= top))
                def _():
                    mix(low + 1, top, slot, turn, count)

            partial = total[into]
            for g in range(0, d_rows, GROUP):
                lhs = jnp.concatenate(
                    [mixed[a, :, g : g + GROUP, :].reshape(-1, aux) for a in range(a_rows)],
                    axis=0,
                )
                rhs = panel_buf[slot, :, g : g + GROUP, :].reshape(b_rows * GROUP, aux)
                partial += lax.dot_general(
                    lhs, rhs, (((1,), (1,)), ((), ())), preferred_element_type=jnp.float32
                )
            total[into] = partial

        return carry

    lax.fori_loop(0, jnp.where(items > 0, items + AHEAD - 1, 0), step, 0)

    out_ref[...] = jnp.zeros_like(out_ref)
    used = [jnp.int32(0)] * outs
    for seg, count in zip(segments, counts):
        used[seg.into] = used[seg.into] + count

    def finish(o, carry):
        @pl.when(pick_row(o, used) > 0)
        def _():
            _, rows, columns = total.shape
            row_d = lax.broadcasted_iota(jnp.int32, (rows, columns), 0) % GROUP
            column_d = lax.broadcasted_iota(jnp.int32, (rows, columns), 1) % GROUP
            kept = jnp.where(row_d == column_d, total[o], 0.0)
            kept = kept.reshape(rows // GROUP, GROUP, columns).sum(axis=1)
            from_b = lax.broadcasted_iota(jnp.int32, (columns, LANES), 0) // GROUP
            to_b = lax.broadcasted_iota(jnp.int32, (columns, LANES), 1)
            gather = jnp.where(from_b == to_b, 1.0, 0.0)
            out_ref[o] = jnp.dot(
                kept,
                gather,
                precision=lax.Precision.HIGHEST,
                preferred_element_type=jnp.float32,
            )

        return carry

    lax.fori_loop(0, outs, finish, 0)

    for ref, pairs_of in zip(added, moves):
        for source, target in pairs_of:
            out_ref[target] += ref[source]


def pair_terms(lists, factors_a, segments, outs, width, d_rows, behind=(), added=()):
    arrays, places = [factors_a], []
    for seg in segments:
        place = []
        for array in (seg.amps, seg.panel):
            known = [n for n, other in enumerate(arrays) if other is array]
            place.append(known[0] if known else len(arrays))
            if not known:
                arrays.append(array)
        places.append(place)
    arrays += behind
    a_rows, _, aux = factors_a.shape
    pairs = segments[0].amps.shape[-3]
    b_rows = segments[0].panel.shape[0]
    most = max(2, *(seg.slots for seg in segments))
    return pl.pallas_call(
        functools.partial(terms_kernel, segments, places, [moves for _, moves in added], d_rows),
        in_specs=[pl.BlockSpec(memory_space=pltpu.SMEM)]
        + [pl.BlockSpec(memory_space=pltpu.VMEM)] * len(added)
        + [pl.BlockSpec(memory_space=pltpu.HBM)] * len(arrays),
        out_specs=pl.BlockSpec(memory_space=pltpu.VMEM),
        scratch_shapes=[
            pltpu.VMEM((AHEAD, most, pairs, d_rows, width), jnp.bfloat16),
            pltpu.VMEM((AHEAD, b_rows, d_rows, aux), jnp.bfloat16),
            pltpu.VMEM((AHEAD, most, a_rows, width, aux), jnp.bfloat16),
            pltpu.VMEM((a_rows, pairs, d_rows, aux), jnp.bfloat16),
            pltpu.VMEM((outs, a_rows * pairs * GROUP, b_rows * GROUP), jnp.float32),
            pltpu.SemaphoreType.DMA((AHEAD, most + 1)),
            pltpu.SemaphoreType.DMA((AHEAD, most)),
        ],
        out_shape=jax.ShapeDtypeStruct((outs, a_rows * pairs, LANES), jnp.float32),
        compiler_params=pltpu.CompilerParams(vmem_limit_bytes=VMEM),
        cost_estimate=SMALL,
        name="pair_terms",
    )(lists, *(array for array, _ in added), *arrays)


def summed_over_narrow(value):
    size = lax.axis_size("narrow")
    me = lax.axis_index("narrow")
    share = value.shape[2] // size

    def part(owner):
        return lax.dynamic_slice_in_dim(value, owner * share, share, 2)

    parts = [part(me)]
    for k in range(1, size):
        to = [(i, (i + k) % size) for i in range(size)]
        parts.append(lax.ppermute(part((me + k) % size), "narrow", to))
    return sum(parts[1:], parts[0])


def local(factors_a, factors_b, amplitudes, screen):
    pairs, d_extent, virtuals = amplitudes.shape
    width = virtuals // screen.shape[1]
    tiles = lax.axis_size("blk")
    position = lax.axis_index("blk")
    extras = MOST - ROUNDS
    d_rows = min(64, d_extent // 4)

    lists = kept_lists(position, screen)
    fullest = lists[MISC * ROW + 1]
    others = lists[MISC * ROW + 2]
    is_first = position % 2 == 0
    is_full = position == fullest
    feeds_one = (position + 1) % tiles == fullest
    feeds_two = (position + 2) % tiles == fullest

    evens, odds = range(0, tiles, 2), range(1, tiles, 2)
    up = [(i, i + 1) for i in evens]
    down = [(i + 1, i) for i in evens]
    around = [(i, (i + 2) % tiles) for i in range(tiles)]

    def run(wrapped, odd, operands):
        lists, factors_a, factors_b, amplitudes = operands
        terms = functools.partial(pair_terms, lists, factors_a, width=width, d_rows=d_rows)
        copy = functools.partial(take, lists, amplitudes, factors_b, width=width)
        columns_of = functools.partial(Segment, panel=factors_b)
        given_to = functools.partial(Segment, amps=amplitudes, slots=extras)

        def ahead(at):
            return (at >= tiles - 2) == wrapped

        def hops(keep):
            return [(at, to) for at, to in around if keep(at)]

        def backs(keep):
            return [(to, at) for at, to in around if keep(at)]

        half, quarter = d_extent // 2, d_extent // 4
        low = 3 * d_extent // 4 // d_rows * d_rows
        high = d_extent - low
        own = columns_of(0, row=OWN, slots=MOST, amps=amplitudes, extent=d_extent)
        after = functools.partial(Columns, AFTER, ROUNDS)
        near = functools.partial(Columns, NEXT, ROUNDS)
        light = functools.partial(columns_of, slots=ROUNDS)
        mine = functools.partial(columns_of, row=MINE, slots=extras)
        if odd:
            given = max(3 * d_extent // 8 // d_rows, 1) * d_rows
            moved = d_extent - given

            def seconds(at):
                return at in odds and ahead(at)

            (extra,) = copy([Columns(MINE, extras, 0, moved)])
            extra_one = send(extra, up)
            extra_two = send(extra, hops(seconds))
            near_l, direct, panel = copy(
                [near(0, low), after(0, d_extent), Panel(moved, given)], behind=[extra]
            )
            side_l = send(near_l, down)
            got_direct = send(direct, hops(lambda at: at in evens))
            far = send(panel, backs(seconds))

            near_h, near_l, own_near_h, panel = copy(
                [near(low, high), near(0, low), near(low, high), Panel(moved, given)],
                behind=[near_l],
            )
            near_h = tied(near_h, side_l)
            side_h = send(near_h, down)
            (pass_l,) = copy([after(0, low, passing=side_l)], behind=[near_h])
            near_l = tied(near_l, extra_one, pass_l)
            own_l = send(near_l, up)
            panel = tied(panel, side_h, near_l)
            beside = send(panel, down)
            pass_l = tied(pass_l, panel, got_direct, extra_two)
            on_l = send(pass_l, around)
            (pass_h,) = copy([after(low, high, passing=side_h)], behind=[panel])
            pass_h = tied(pass_h, pass_l, far)
            on_h = send(pass_h, around)
            near_h = tied(own_near_h, pass_h)
            own_h = send(near_h, up)

            first = terms(
                [
                    own,
                    light(2, row=LIGHT_0, amps=got_direct, extent=d_extent),
                    mine(1, amps=extra_one, extent=moved),
                    mine(2, amps=extra_two, extent=moved),
                    given_to(3, row=FED_2, panel=far, extent=given, amp_at=moved),
                ],
                4,
                behind=[near_h],
            )
            then = terms(
                [
                    light(0, row=LIGHT_0, amps=on_l, extent=low),
                    light(1, row=LIGHT_1, amps=on_l, extent=low),
                    light(0, row=LIGHT_1, amps=own_l, extent=low),
                ],
                2,
                behind=[first],
            )
            return terms(
                [
                    light(1, row=LIGHT_0, amps=on_h, extent=high, panel_at=low),
                    light(2, row=LIGHT_1, amps=on_h, extent=high, panel_at=low),
                    light(1, row=LIGHT_1, amps=own_h, extent=high, panel_at=low),
                    given_to(3, row=FED_1, panel=beside, extent=given, amp_at=moved),
                ],
                4,
                added=[(first, [(0, 0), (1, 1), (2, 2), (3, 3)]), (then, [(0, 1), (1, 2)])],
            )
        else:
            def firsts(at):
                return at in evens and ahead(at)

            def early(at):
                return at in odds or ahead(at)

            lead = functools.partial(Columns, LEAD, ROUNDS, 0, half)
            rest = functools.partial(Columns, REST, ROUNDS, 0, half)
            lead_l, lead_h, beside = copy(
                [lead(part=PART), rest(part=REST_PART), near(0, d_extent)]
            )
            got_lead_l = send(lead_l, hops(early))
            got_lead_h = send(lead_h, hops(early))
            side = send(beside, up)
            extra, panel_0 = copy(
                [Columns(MINE, extras, 0, quarter), Panel(half, quarter)], behind=[lead_l]
            )
            cross = send(extra, down)
            far_0 = send(panel_0, backs(firsts))
            panel_1, after_l, after_h = copy(
                [Panel(half + quarter, quarter), after(0, low), after(low, high)],
                behind=[extra],
            )

            lead_down_l = send(got_lead_l, down)
            panel_1 = tied(panel_1, cross)
            far_1 = send(panel_1, backs(firsts))
            (extra,) = copy(
                [Columns(MINE, extras, quarter, quarter, passing=cross)], behind=[panel_1]
            )
            far_0 = tied(far_0, extra, got_lead_l)
            up_0 = send(far_0, up)
            extra = tied(extra, got_lead_h)
            got_extra = send(extra, hops(ahead))
            lead_down_h = send(got_lead_h, down)
            after_l = tied(after_l, extra, side, lead_down_l)
            got_l = send(after_l, around)
            far_1 = tied(far_1, after_l)
            up_1 = send(far_1, up)
            got_extra = tied(got_extra, far_1)
            extra_down = send(got_extra, down)
            after_h = tied(after_h, got_extra, lead_down_h)
            got_h = send(after_h, around)

            first = terms(
                [
                    own,
                    light(1, row=LIGHT_1, amps=side, extent=d_extent),
                    light(1, row=LIGHT_0, amps=lead_down_l, extent=half),
                    light(1, row=LIGHT_0, amps=lead_down_h, extent=half, panel_at=half),
                    columns_of(2, row=MINE_L, slots=ROUNDS, amps=got_lead_l, extent=half),
                    columns_of(2, row=MINE_H, slots=ROUNDS, amps=got_lead_h, extent=half),
                ],
                3,
                behind=[after_h],
            )
            fed = functools.partial(given_to, into=0, extent=quarter)
            then = terms(
                [
                    fed(row=FED_1, panel=up_0, amp_at=half),
                    fed(row=FED_2, panel=far_0, amp_at=half),
                    fed(row=FED_2, panel=far_1, amp_at=half + quarter),
                    mine(1, amps=got_extra, extent=quarter),
                    mine(1, amps=extra_down, extent=quarter, panel_at=quarter),
                    light(2, row=LIGHT, amps=got_l, extent=low),
                ],
                3,
                behind=[first],
            )
            return terms(
                [
                    light(2, row=LIGHT, amps=got_h, extent=high, panel_at=low),
                    fed(row=FED_1, panel=up_1, amp_at=half + quarter, into=3),
                ],
                4,
                added=[
                    (first, [(0, 0), (1, 1), (2, 2)]),
                    (then, [(0, 3), (1, 1), (2, 2)]),
                ],
            )

    branches = [
        functools.partial(run, wrapped, odd) for wrapped in (False, True) for odd in (False, True)
    ]
    operands = (lists, factors_a, factors_b, amplitudes)
    terms = lax.switch(lists[MISC * ROW], branches, operands)
    def add_round(r, terms):

        def only(row, count):
            sub = lax.dynamic_slice_in_dim(lists, row * ROW + r, 1)
            return jnp.concatenate([sub, jnp.zeros(MOST - 1, jnp.int32), count.reshape(1)])

        has = jnp.where((r < lists[OWN * ROW + MOST]) & ~is_full, 1, 0).astype(jnp.int32)
        own = only(OWN, has)
        moved = [
            rotated(
                take(
                    only(row, has), amplitudes, factors_b, [Columns(0, 1, 0, d_extent)], width
                )[0],
                by,
            )
            for row, by in ((NEXT, 1), (AFTER, 2))
        ]
        segments = [
            Segment(1 + n, 0, 1, columns, factors_b, d_extent) for n, columns in enumerate(moved)
        ]
        kept = [(n, n) for n in range(STEPS + 1)]
        return pair_terms(
            own, factors_a, segments, STEPS + 1, width, d_rows, added=[(terms, kept)]
        )

    terms = lax.fori_loop(ROUNDS, jnp.maximum(others, ROUNDS), add_round, terms)
    a_rows = factors_a.shape[0]
    terms = terms[:, :, : factors_b.shape[0]]
    terms = terms.reshape(STEPS + 1, a_rows, pairs, -1).swapaxes(1, 2)
    summed = summed_over_narrow(terms.reshape(STEPS + 1, 1, -1))
    given_one = rotated(jnp.where(feeds_one, summed[STEPS:], 0.0), 1)
    given_two = rotated(jnp.where(feeds_two, summed[STEPS:], 0.0), 2)
    return jnp.concatenate([summed[:1], summed[1:2] + given_one, summed[2:3] + given_two])


def solution(mesh):
    return jax.shard_map(
        local,
        mesh=mesh,
        in_specs=(P(), P("blk", "narrow", None), P("blk", "narrow", None), P()),
        out_specs=P(None, "blk", "narrow"),
        check_vma=False,
    )
```

```python
import functools

import jax
import jax.numpy as jnp
from jax import lax
from jax.experimental import pallas as pl
from jax.experimental.pallas import tpu as pltpu
from jax.sharding import PartitionSpec as P

STEPS = 3
MOST = 8
ROUNDS = 3
GROUP = 16
LANES = 128
ROW = MOST + 1

(
    OWN,
    LIGHT,
    LIGHT_0,
    LIGHT_1,
    NEXT,
    AFTER,
    LEAD,
    PART,
    REST,
    REST_PART,
    MINE,
    MINE_L,
    MINE_H,
    FED_1,
    FED_2,
    FED_1_L,
    FED_1_H,
    FED_2_L,
    FED_2_H,
    MISC,
) = range(20)
FIRST = MISC * ROW + 3
AHEAD = 4
PARTS = 4
VMEM = 60 * 1024 * 1024
SMALL = pl.CostEstimate(flops=1024, bytes_accessed=1024, transcendentals=0)


def send(value, pairs):
    return lax.ppermute(value, "blk", pairs)


def rotated(value, by):
    size = lax.axis_size("blk")
    return send(value, [(i, (i + by) % size) for i in range(size)])


def lists_kernel(position_ref, screen_ref, out_ref):
    tiles, subs = screen_ref.shape
    position = position_ref[0]

    def count_of(tile):
        return sum(jnp.where(screen_ref[tile, s] != 0, 1, 0) for s in range(subs))

    def look(tile, found):
        best, fullest, others = found
        count = count_of(tile)
        larger = count > best
        others = jnp.where(larger, best, jnp.maximum(others, count))
        return jnp.where(larger, count, best), jnp.where(larger, tile, fullest), others

    zero = jnp.int32(0)
    best, fullest, others = lax.fori_loop(0, tiles, look, (zero, zero, zero))

    def fill(row, tile, skip, count):
        for k in range(MOST):
            out_ref[row * ROW + k] = 0
        seen = jnp.int32(0)
        for s in range(subs):
            kept = screen_ref[tile, s] != 0

            @pl.when(kept & (seen >= skip))
            def _():
                out_ref[row * ROW + seen - skip] = s

            seen += jnp.where(kept, 1, 0)
        out_ref[row * ROW + MOST] = seen if count is None else count

    following = lax.rem(position + 1, tiles)
    second = lax.rem(position + 2, tiles)
    is_first = lax.rem(position, 2) == 0
    own_count = count_of(position)
    extra = jnp.maximum(best - ROUNDS, 0)
    light = jnp.minimum(own_count, ROUNDS)
    fill(OWN, position, 0, own_count)
    fill(LIGHT, position, 0, light)
    fill(LIGHT_0, position, 0, jnp.where(is_first, light, 0))
    fill(LIGHT_1, position, 0, jnp.where(is_first, 0, light))
    fill(NEXT, following, 0, None)
    fill(AFTER, second, 0, None)
    fill(MINE, fullest, ROUNDS, jnp.where(position == fullest, extra, 0))
    fill(FED_1, fullest, ROUNDS, jnp.where(following == fullest, extra, 0))
    fill(FED_2, fullest, ROUNDS, jnp.where(second == fullest, extra, 0))
    for lower, upper, deals in (
        (MINE_L, MINE_H, position == fullest),
        (FED_1_L, FED_1_H, following == fullest),
        (FED_2_L, FED_2_H, second == fullest),
    ):
        all_of = jnp.where(deals, extra, 0)
        fill(lower, fullest, ROUNDS, jnp.minimum(all_of, ROUNDS))
        fill(upper, fullest, 2 * ROUNDS, jnp.maximum(all_of - ROUNDS, 0))
    for k in range(ROW):
        for row, part, source in ((LEAD, PART, MINE_L), (REST, REST_PART, MINE_H)):
            other = out_ref[NEXT * ROW + k] if k < ROUNDS else 0
            out_ref[row * ROW + k] = jnp.where(is_first, out_ref[source * ROW + k], other)
            out_ref[part * ROW + k] = jnp.where(is_first, 0, 0 if part == PART else 1)
    out_ref[MISC * ROW] = jnp.where(fullest < 2, 2, 0) + lax.rem(fullest, 2)
    out_ref[MISC * ROW + 1] = fullest
    out_ref[MISC * ROW + 2] = others
    out_ref[FIRST] = jnp.where(is_first, 1, 0)
    for k in range(4, ROW):
        out_ref[MISC * ROW + k] = 0


def kept_lists(position, screen):
    return pl.pallas_call(
        lists_kernel,
        in_specs=[pl.BlockSpec(memory_space=pltpu.SMEM)] * 2,
        out_specs=pl.BlockSpec(memory_space=pltpu.SMEM),
        out_shape=jax.ShapeDtypeStruct(((MISC + 1) * ROW,), jnp.int32),
        name="kept_lists",
    )(position.reshape(1), screen)


class Columns:
    def __init__(self, row, slots, start, extent, part=None, passing=None):
        self.row, self.slots, self.start, self.extent = row, slots, start, extent
        self.part, self.passing = part, passing


class Panel:
    def __init__(self, start, extent):
        self.start, self.extent = start, extent


def take_kernel(kinds, lists_ref, amplitudes, panel, *refs):
    count = len(kinds)
    sems = refs[-1]
    stages, outs = refs[-1 - count : -1], refs[-1 - 2 * count : -1 - count]

    def columns_load(kind, passing, width):
        def load(s, act):
            def own():
                sub = pl.multiple_of(lists_ref[kind.row * ROW + s] * width, width)
                first = kind.start
                if kind.part is not None:
                    further = lists_ref[kind.part * ROW + s] * kind.extent
                    first = pl.multiple_of(first + further, kind.extent)
                act(amplitudes.at[:, pl.ds(first, kind.extent), pl.ds(sub, width)])

            if passing is None:
                own()
            else:
                pl.when(lists_ref[FIRST] != 0)(lambda: act(passing.at[s]))
                pl.when(lists_ref[FIRST] == 0)(own)

        return load

    def panel_load(kind, share):
        def load(n, act):
            act(panel.at[pl.ds(n * share, share), pl.ds(kind.start, kind.extent), :])

        return load

    jobs = []
    given = 0
    for n, kind in enumerate(kinds):
        if isinstance(kind, Columns):
            passing = None
            if kind.passing is not None:
                passing = refs[given]
                given += 1
            load = columns_load(kind, passing, outs[n].shape[-1])
            jobs.append((load, lambda s, n=n: outs[n].at[s], kind.slots))
        else:
            share = stages[n].shape[1]
            load = panel_load(kind, share)
            jobs.append((load, lambda s, n=n, share=share: outs[n].at[pl.ds(s * share, share)], PARTS))

    def loops(act):
        for n, (load, target, pieces) in enumerate(jobs):

            def body(s, carry):
                act(n, s, load, target)
                return carry

            lax.fori_loop(0, pieces, body, 0)

    def start(n, s, load, target):
        stage = stages[n].at[s]
        load(s, lambda source: pltpu.make_async_copy(source, stage, sems.at[0, n, s]).start())

    def pass_on(n, s, load, target):
        stage = stages[n].at[s]
        pltpu.make_async_copy(stage, stage, sems.at[0, n, s]).wait()
        pltpu.make_async_copy(stage, target(s), sems.at[1, n, s]).start()

    def finish(n, s, load, target):
        stage = stages[n].at[s]
        pltpu.make_async_copy(stage, stage, sems.at[1, n, s]).wait()

    for act in (start, pass_on, finish):
        loops(act)


def take(lists, amplitudes, panel, kinds, width, behind=()):
    pairs = amplitudes.shape[0]
    b_rows, _, aux = panel.shape
    shapes, stages = [], []
    for kind in kinds:
        if isinstance(kind, Columns):
            shapes.append((kind.slots, pairs, kind.extent, width))
            stages.append(shapes[-1])
        else:
            shapes.append((b_rows, kind.extent, aux))
            stages.append((PARTS, b_rows // PARTS, kind.extent, aux))
    passed = [kind.passing for kind in kinds if getattr(kind, "passing", None) is not None]
    others = passed + list(behind)
    return pl.pallas_call(
        functools.partial(take_kernel, kinds),
        in_specs=[pl.BlockSpec(memory_space=pltpu.SMEM)]
        + [pl.BlockSpec(memory_space=pltpu.HBM)] * (2 + len(others)),
        out_specs=[pl.BlockSpec(memory_space=pltpu.HBM)] * len(kinds),
        out_shape=[jax.ShapeDtypeStruct(shape, amplitudes.dtype) for shape in shapes],
        scratch_shapes=[pltpu.VMEM(shape, amplitudes.dtype) for shape in stages]
        + [pltpu.SemaphoreType.DMA((2, len(kinds), max(shape[0] for shape in stages)))],
        compiler_params=pltpu.CompilerParams(vmem_limit_bytes=VMEM),
        cost_estimate=SMALL,
        name="take",
    )(lists, amplitudes, panel, *others)


def tie_kernel(*refs):
    pass


def tied(value, *behind):
    return pl.pallas_call(
        tie_kernel,
        in_specs=[pl.BlockSpec(memory_space=pltpu.HBM)] * (1 + len(behind)),
        out_specs=pl.BlockSpec(memory_space=pltpu.HBM),
        out_shape=jax.ShapeDtypeStruct(value.shape, value.dtype),
        input_output_aliases={0: 0},
        cost_estimate=SMALL,
        name="tied",
    )(value, *behind)


class Segment:
    def __init__(self, into, row, slots, amps, panel, extent, amp_at=0, panel_at=0, slot_at=0):
        self.into, self.row, self.slots = into, row, slots
        self.amps, self.panel, self.extent = amps, panel, extent
        self.amp_at, self.panel_at, self.slot_at = amp_at, panel_at, slot_at


def terms_kernel(segments, places, moves, d_rows, lists_ref, *refs):
    added, arrays = refs[: len(moves)], refs[len(moves) : -8]
    out_ref, amp_buf, panel_buf, factor_buf, mixed, total, sems, factor_sems = refs[-8:]
    factors = arrays[0]
    outs = out_ref.shape[0]
    _, most, pairs, _, width = amp_buf.shape
    b_rows = panel_buf.shape[1]
    _, _, a_rows, _, aux = factor_buf.shape

    counts = [lists_ref[seg.row * ROW + MOST] for seg in segments]
    starts, orders = [], []
    begin = order = jnp.int32(0)
    for seg, count in zip(segments, counts):
        starts.append(begin)
        orders.append(order)
        begin = begin + jnp.where(count > 0, seg.extent // d_rows, 0)
        order = order + jnp.where(count > 0, 1, 0)
    items = begin

    def pick(at, values):
        found = values[0]
        for s in range(1, len(segments)):
            found = jnp.where(at == s, values[s], found)
        return found

    def pick_row(o, values):
        found = values[0]
        for n in range(1, len(values)):
            found = jnp.where(o == n, values[n], found)
        return found

    def locate(t):
        at = jnp.int32(0)
        for s in range(len(segments)):
            at = jnp.where((counts[s] > 0) & (t >= starts[s]), s, at)
        return at, t - pick(at, starts), lax.rem(pick(at, orders), AHEAD)

    def fetch(t):
        at, block, turn = locate(t)
        slot = lax.rem(t, AHEAD)
        for s, seg in enumerate(segments):
            amps, panel = arrays[places[s][0]], arrays[places[s][1]]

            @pl.when(at == s)
            def _():
                amp_d = pl.ds(pl.multiple_of(seg.amp_at + block * d_rows, d_rows), d_rows)
                panel_d = pl.ds(pl.multiple_of(seg.panel_at + block * d_rows, d_rows), d_rows)
                pltpu.make_async_copy(
                    panel.at[:, panel_d, :], panel_buf.at[slot], sems.at[slot, most]
                ).start()

                def one(k, carry):
                    sub = pl.multiple_of(lists_ref[seg.row * ROW + k] * width, width)
                    columns = pl.ds(sub, width)
                    if len(amps.shape) == 3:
                        source = amps.at[:, amp_d, columns]
                    else:
                        source = amps.at[seg.slot_at + k, :, amp_d, :]
                    pltpu.make_async_copy(
                        source, amp_buf.at[slot, k], sems.at[slot, k]
                    ).start()

                    @pl.when(block == 0)
                    def _():
                        pltpu.make_async_copy(
                            factors.at[:, columns, :],
                            factor_buf.at[turn, k],
                            factor_sems.at[turn, k],
                        ).start()

                    return carry

                lax.fori_loop(0, counts[s], one, 0)

    def arrive(slot, block, turn, count):
        piece = panel_buf.at[slot]
        pltpu.make_async_copy(piece, piece, sems.at[slot, most]).wait()

        def one(k, carry):
            piece = amp_buf.at[slot, k]
            pltpu.make_async_copy(piece, piece, sems.at[slot, k]).wait()

            @pl.when(block == 0)
            def _():
                piece = factor_buf.at[turn, k]
                pltpu.make_async_copy(piece, piece, factor_sems.at[turn, k]).wait()

            return carry

        lax.fori_loop(0, count, one, 0)

    @pl.when(items > 0)
    def _():
        total[...] = jnp.zeros_like(total)

    def mix(low, top, slot, turn, count):
        columns = [amp_buf[slot, k].reshape(pairs * d_rows, width) for k in range(top)]
        for k in range(low, top):
            columns[k] = jnp.where(k < count, columns[k], jnp.zeros_like(columns[k]))
        lhs = jnp.concatenate(columns, axis=1)
        for a in range(a_rows):
            rows = [factor_buf[turn, k, a] for k in range(top)]
            for k in range(low, top):
                rows[k] = jnp.where(k < count, rows[k], jnp.zeros_like(rows[k]))
            product = jnp.dot(
                lhs, jnp.concatenate(rows, axis=0), preferred_element_type=jnp.float32
            )
            mixed[a] = product.astype(mixed.dtype).reshape(pairs, d_rows, aux)

    tops = set()
    for slots in {seg.slots for seg in segments}:
        tops |= {ROUNDS, slots} if slots == MOST else {slots}
    tops = sorted(top for top in tops if top <= ROUNDS or top == most)

    def step(n, carry):
        @pl.when(n < items)
        def _():
            fetch(n)

        @pl.when(n >= AHEAD - 1)
        def _():
            t = n - (AHEAD - 1)
            at, block, turn = locate(t)
            slot = lax.rem(t, AHEAD)
            count = pick(at, counts)
            into = pick(at, [seg.into for seg in segments])
            arrive(slot, block, turn, count)
            for low, top in zip([0] + tops, tops):

                @pl.when((count > low) & (count <= top))
                def _():
                    mix(low + 1, top, slot, turn, count)

            partial = total[into]
            for g in range(0, d_rows, GROUP):
                lhs = jnp.concatenate(
                    [mixed[a, :, g : g + GROUP, :].reshape(-1, aux) for a in range(a_rows)],
                    axis=0,
                )
                rhs = panel_buf[slot, :, g : g + GROUP, :].reshape(b_rows * GROUP, aux)
                partial += lax.dot_general(
                    lhs, rhs, (((1,), (1,)), ((), ())), preferred_element_type=jnp.float32
                )
            total[into] = partial

        return carry

    lax.fori_loop(0, jnp.where(items > 0, items + AHEAD - 1, 0), step, 0)

    out_ref[...] = jnp.zeros_like(out_ref)
    used = [jnp.int32(0)] * outs
    for seg, count in zip(segments, counts):
        used[seg.into] = used[seg.into] + count

    def finish(o, carry):
        @pl.when(pick_row(o, used) > 0)
        def _():
            _, rows, columns = total.shape
            row_d = lax.broadcasted_iota(jnp.int32, (rows, columns), 0) % GROUP
            column_d = lax.broadcasted_iota(jnp.int32, (rows, columns), 1) % GROUP
            kept = jnp.where(row_d == column_d, total[o], 0.0)
            kept = kept.reshape(rows // GROUP, GROUP, columns).sum(axis=1)
            from_b = lax.broadcasted_iota(jnp.int32, (columns, LANES), 0) // GROUP
            to_b = lax.broadcasted_iota(jnp.int32, (columns, LANES), 1)
            gather = jnp.where(from_b == to_b, 1.0, 0.0)
            out_ref[o] = jnp.dot(
                kept,
                gather,
                precision=lax.Precision.HIGHEST,
                preferred_element_type=jnp.float32,
            )

        return carry

    lax.fori_loop(0, outs, finish, 0)

    for ref, pairs_of in zip(added, moves):
        for source, target in pairs_of:
            out_ref[target] += ref[source]


def pair_terms(lists, factors_a, segments, outs, width, d_rows, behind=(), added=()):
    arrays, places = [factors_a], []
    for seg in segments:
        place = []
        for array in (seg.amps, seg.panel):
            known = [n for n, other in enumerate(arrays) if other is array]
            place.append(known[0] if known else len(arrays))
            if not known:
                arrays.append(array)
        places.append(place)
    arrays += behind
    a_rows, _, aux = factors_a.shape
    pairs = segments[0].amps.shape[-3]
    b_rows = segments[0].panel.shape[0]
    most = max(2, *(seg.slots for seg in segments))
    return pl.pallas_call(
        functools.partial(terms_kernel, segments, places, [moves for _, moves in added], d_rows),
        in_specs=[pl.BlockSpec(memory_space=pltpu.SMEM)]
        + [pl.BlockSpec(memory_space=pltpu.VMEM)] * len(added)
        + [pl.BlockSpec(memory_space=pltpu.HBM)] * len(arrays),
        out_specs=pl.BlockSpec(memory_space=pltpu.VMEM),
        scratch_shapes=[
            pltpu.VMEM((AHEAD, most, pairs, d_rows, width), jnp.bfloat16),
            pltpu.VMEM((AHEAD, b_rows, d_rows, aux), jnp.bfloat16),
            pltpu.VMEM((AHEAD, most, a_rows, width, aux), jnp.bfloat16),
            pltpu.VMEM((a_rows, pairs, d_rows, aux), jnp.bfloat16),
            pltpu.VMEM((outs, a_rows * pairs * GROUP, b_rows * GROUP), jnp.float32),
            pltpu.SemaphoreType.DMA((AHEAD, most + 1)),
            pltpu.SemaphoreType.DMA((AHEAD, most)),
        ],
        out_shape=jax.ShapeDtypeStruct((outs, a_rows * pairs, LANES), jnp.float32),
        compiler_params=pltpu.CompilerParams(vmem_limit_bytes=VMEM),
        cost_estimate=SMALL,
        name="pair_terms",
    )(lists, *(array for array, _ in added), *arrays)


def summed_over_narrow(value):
    size = lax.axis_size("narrow")
    me = lax.axis_index("narrow")
    share = value.shape[2] // size

    def part(owner):
        return lax.dynamic_slice_in_dim(value, owner * share, share, 2)

    parts = [part(me)]
    for k in range(1, size):
        to = [(i, (i + k) % size) for i in range(size)]
        parts.append(lax.ppermute(part((me + k) % size), "narrow", to))
    return sum(parts[1:], parts[0])


def local(factors_a, factors_b, amplitudes, screen):
    pairs, d_extent, virtuals = amplitudes.shape
    width = virtuals // screen.shape[1]
    tiles = lax.axis_size("blk")
    position = lax.axis_index("blk")
    extras = MOST - ROUNDS
    d_rows = min(64, d_extent // 4)

    lists = kept_lists(position, screen)
    fullest = lists[MISC * ROW + 1]
    others = lists[MISC * ROW + 2]
    is_first = position % 2 == 0
    is_full = position == fullest
    feeds_one = (position + 1) % tiles == fullest
    feeds_two = (position + 2) % tiles == fullest

    evens, odds = range(0, tiles, 2), range(1, tiles, 2)
    up = [(i, i + 1) for i in evens]
    down = [(i + 1, i) for i in evens]
    around = [(i, (i + 2) % tiles) for i in range(tiles)]

    def run(wrapped, odd, operands):
        lists, factors_a, factors_b, amplitudes = operands
        terms = functools.partial(pair_terms, lists, factors_a, width=width, d_rows=d_rows)
        copy = functools.partial(take, lists, amplitudes, factors_b, width=width)
        columns_of = functools.partial(Segment, panel=factors_b)
        given_to = functools.partial(Segment, amps=amplitudes, slots=extras)

        def ahead(at):
            return (at >= tiles - 2) == wrapped

        def hops(keep):
            return [(at, to) for at, to in around if keep(at)]

        def backs(keep):
            return [(to, at) for at, to in around if keep(at)]

        half, quarter = d_extent // 2, d_extent // 4
        low = 5 * d_extent // 8 // d_rows * d_rows
        high = d_extent - low
        own = columns_of(0, row=OWN, slots=MOST, amps=amplitudes, extent=d_extent)
        after = functools.partial(Columns, AFTER, ROUNDS)
        near = functools.partial(Columns, NEXT, ROUNDS)
        light = functools.partial(columns_of, slots=ROUNDS)
        mine = functools.partial(columns_of, row=MINE, slots=extras)
        if odd:
            given = max(3 * d_extent // 8 // d_rows, 1) * d_rows
            moved = d_extent - given

            def seconds(at):
                return at in odds and ahead(at)

            (extra,) = copy([Columns(MINE, extras, 0, moved)])
            extra_one = send(extra, up)
            extra_two = send(extra, hops(seconds))
            near_l, direct, panel = copy(
                [near(0, low), after(0, d_extent), Panel(moved, given)], behind=[extra]
            )
            side_l = send(near_l, down)
            got_direct = send(direct, hops(lambda at: at in evens))
            far = send(panel, backs(seconds))

            near_h, near_l, own_near_h, panel = copy(
                [near(low, high), near(0, low), near(low, high), Panel(moved, given)],
                behind=[near_l],
            )
            near_h = tied(near_h, side_l)
            side_h = send(near_h, down)
            (pass_l,) = copy([after(0, low, passing=side_l)], behind=[near_h])
            panel = tied(panel, side_h, extra_one, pass_l)
            beside = send(panel, down)
            near_l = tied(near_l, panel)
            own_l = send(near_l, up)
            pass_l = tied(pass_l, near_l, got_direct, extra_two)
            on_l = send(pass_l, around)
            (pass_h,) = copy([after(low, high, passing=side_h)], behind=[panel])
            pass_h = tied(pass_h, pass_l, far)
            on_h = send(pass_h, around)
            near_h = tied(own_near_h, pass_h)
            own_h = send(near_h, up)

            first = terms(
                [
                    own,
                    light(2, row=LIGHT_0, amps=got_direct, extent=d_extent),
                    mine(1, amps=extra_one, extent=moved),
                    mine(2, amps=extra_two, extent=moved),
                    given_to(3, row=FED_2, panel=far, extent=given, amp_at=moved),
                ],
                4,
                behind=[near_h],
            )
            then = terms(
                [
                    light(0, row=LIGHT_0, amps=on_l, extent=low),
                    light(1, row=LIGHT_1, amps=on_l, extent=low),
                    light(0, row=LIGHT_1, amps=own_l, extent=low),
                ],
                2,
                behind=[first],
            )
            return terms(
                [
                    light(1, row=LIGHT_0, amps=on_h, extent=high, panel_at=low),
                    light(2, row=LIGHT_1, amps=on_h, extent=high, panel_at=low),
                    light(1, row=LIGHT_1, amps=own_h, extent=high, panel_at=low),
                    given_to(3, row=FED_1, panel=beside, extent=given, amp_at=moved),
                ],
                4,
                added=[(first, [(0, 0), (1, 1), (2, 2), (3, 3)]), (then, [(0, 1), (1, 2)])],
            )
        else:
            def firsts(at):
                return at in evens and ahead(at)

            def early(at):
                return at in odds or ahead(at)

            lead = functools.partial(Columns, LEAD, ROUNDS, 0, half)
            rest = functools.partial(Columns, REST, ROUNDS, 0, half)
            lead_l, lead_h, beside = copy(
                [lead(part=PART), rest(part=REST_PART), near(0, d_extent)]
            )
            got_lead_l = send(lead_l, hops(early))
            got_lead_h = send(lead_h, hops(early))
            side = send(beside, up)
            extra, panel_0 = copy(
                [Columns(MINE, extras, 0, quarter), Panel(half, quarter)], behind=[lead_l]
            )
            cross = send(extra, down)
            far_0 = send(panel_0, backs(firsts))
            panel_1, after_l, after_h = copy(
                [Panel(half + quarter, quarter), after(0, low), after(low, high)],
                behind=[extra],
            )

            lead_down_l = send(got_lead_l, down)
            here = terms([own], 1, behind=[panel_1])
            panel_1 = tied(panel_1, cross, here)
            far_1 = send(panel_1, backs(firsts))
            (extra,) = copy(
                [Columns(MINE, extras, quarter, quarter, passing=cross)], behind=[panel_1]
            )
            far_0 = tied(far_0, extra, got_lead_l)
            up_0 = send(far_0, up)
            extra = tied(extra, got_lead_h)
            got_extra = send(extra, hops(ahead))
            lead_down_h = send(got_lead_h, down)
            after_l = tied(after_l, extra, side, lead_down_l)
            got_l = send(after_l, around)
            first = terms(
                [
                    light(0, row=LIGHT_1, amps=side, extent=d_extent),
                    light(0, row=LIGHT_0, amps=lead_down_l, extent=half),
                    light(1, row=MINE_L, amps=got_lead_l, extent=half),
                    light(1, row=MINE_H, amps=got_lead_h, extent=half),
                ],
                2,
                behind=[after_l],
            )
            far_1 = tied(far_1, first)
            up_1 = send(far_1, up)
            got_extra = tied(got_extra, far_1)
            extra_down = send(got_extra, down)
            after_h = tied(after_h, got_extra, lead_down_h)
            got_h = send(after_h, around)


            def both(segment, *rows, **more):
                return [
                    segment(row=row, slot_at=n * ROUNDS, **more) for n, row in enumerate(rows)
                ]

            fed = functools.partial(Segment, amps=amplitudes, slots=ROUNDS, extent=quarter)
            extras_of = functools.partial(light, 1, extent=quarter)
            then = terms(
                both(fed, FED_1_L, FED_1_H, into=0, panel=up_0, amp_at=half)
                + both(fed, FED_2_L, FED_2_H, into=0, panel=far_0, amp_at=half)
                + both(fed, FED_2_L, FED_2_H, into=0, panel=far_1, amp_at=half + quarter)
                + both(extras_of, MINE_L, MINE_H, amps=got_extra)
                + both(extras_of, MINE_L, MINE_H, amps=extra_down, panel_at=quarter)
                + [
                    light(1, row=LIGHT_0, amps=lead_down_h, extent=half, panel_at=half),
                    light(2, row=LIGHT, amps=got_l, extent=low),
                ],
                3,
                behind=[after_h],
            )
            return terms(
                [light(2, row=LIGHT, amps=got_h, extent=high, panel_at=low)]
                + both(fed, FED_1_L, FED_1_H, into=3, panel=up_1, amp_at=half + quarter),
                4,
                added=[
                    (here, [(0, 0)]),
                    (first, [(0, 1), (1, 2)]),
                    (then, [(0, 3), (1, 1), (2, 2)]),
                ],
            )

    branches = [
        functools.partial(run, wrapped, odd) for wrapped in (False, True) for odd in (False, True)
    ]
    operands = (lists, factors_a, factors_b, amplitudes)
    terms = lax.switch(lists[MISC * ROW], branches, operands)
    def add_round(r, terms):

        def only(row, count):
            sub = lax.dynamic_slice_in_dim(lists, row * ROW + r, 1)
            return jnp.concatenate([sub, jnp.zeros(MOST - 1, jnp.int32), count.reshape(1)])

        has = jnp.where((r < lists[OWN * ROW + MOST]) & ~is_full, 1, 0).astype(jnp.int32)
        own = only(OWN, has)
        moved = [
            rotated(
                take(
                    only(row, has), amplitudes, factors_b, [Columns(0, 1, 0, d_extent)], width
                )[0],
                by,
            )
            for row, by in ((NEXT, 1), (AFTER, 2))
        ]
        segments = [
            Segment(1 + n, 0, 1, columns, factors_b, d_extent) for n, columns in enumerate(moved)
        ]
        kept = [(n, n) for n in range(STEPS + 1)]
        return pair_terms(
            own, factors_a, segments, STEPS + 1, width, d_rows, added=[(terms, kept)]
        )

    terms = lax.fori_loop(ROUNDS, jnp.maximum(others, ROUNDS), add_round, terms)
    a_rows = factors_a.shape[0]
    terms = terms[:, :, : factors_b.shape[0]]
    terms = terms.reshape(STEPS + 1, a_rows, pairs, -1).swapaxes(1, 2)
    summed = summed_over_narrow(terms.reshape(STEPS + 1, 1, -1))
    given_one = rotated(jnp.where(feeds_one, summed[STEPS:], 0.0), 1)
    given_two = rotated(jnp.where(feeds_two, summed[STEPS:], 0.0), 2)
    return jnp.concatenate([summed[:1], summed[1:2] + given_one, summed[2:3] + given_two])


def solution(mesh):
    return jax.shard_map(
        local,
        mesh=mesh,
        in_specs=(P(), P("blk", "narrow", None), P("blk", "narrow", None), P()),
        out_specs=P(None, "blk", "narrow"),
        check_vma=False,
    )
```

```python
import functools

import jax
import jax.numpy as jnp
from jax import lax
from jax.experimental import pallas as pl
from jax.experimental.pallas import tpu as pltpu
from jax.sharding import PartitionSpec as P

STEPS = 3
MOST = 8
ROUNDS = 3
GROUP = 16
LANES = 128
ROW = MOST + 1

(
    OWN,
    LIGHT,
    LIGHT_0,
    LIGHT_1,
    NEXT,
    AFTER,
    LEAD,
    PART,
    REST,
    REST_PART,
    MINE,
    MINE_L,
    MINE_H,
    FED_1,
    FED_2,
    FED_1_L,
    FED_1_H,
    FED_2_L,
    FED_2_H,
    MISC,
) = range(20)
FIRST = MISC * ROW + 3
AHEAD = 4
PARTS = 4
VMEM = 60 * 1024 * 1024
SMALL = pl.CostEstimate(flops=1024, bytes_accessed=1024, transcendentals=0)


def send(value, pairs):
    return lax.ppermute(value, "blk", pairs)


def rotated(value, by):
    size = lax.axis_size("blk")
    return send(value, [(i, (i + by) % size) for i in range(size)])


def lists_kernel(position_ref, screen_ref, out_ref):
    tiles, subs = screen_ref.shape
    position = position_ref[0]

    def count_of(tile):
        return sum(jnp.where(screen_ref[tile, s] != 0, 1, 0) for s in range(subs))

    def look(tile, found):
        best, fullest, others = found
        count = count_of(tile)
        larger = count > best
        others = jnp.where(larger, best, jnp.maximum(others, count))
        return jnp.where(larger, count, best), jnp.where(larger, tile, fullest), others

    zero = jnp.int32(0)
    best, fullest, others = lax.fori_loop(0, tiles, look, (zero, zero, zero))

    def fill(row, tile, skip, count):
        for k in range(MOST):
            out_ref[row * ROW + k] = 0
        seen = jnp.int32(0)
        for s in range(subs):
            kept = screen_ref[tile, s] != 0

            @pl.when(kept & (seen >= skip))
            def _():
                out_ref[row * ROW + seen - skip] = s

            seen += jnp.where(kept, 1, 0)
        out_ref[row * ROW + MOST] = seen if count is None else count

    following = lax.rem(position + 1, tiles)
    second = lax.rem(position + 2, tiles)
    is_first = lax.rem(position, 2) == 0
    own_count = count_of(position)
    extra = jnp.maximum(best - ROUNDS, 0)
    light = jnp.minimum(own_count, ROUNDS)
    fill(OWN, position, 0, own_count)
    fill(LIGHT, position, 0, light)
    fill(LIGHT_0, position, 0, jnp.where(is_first, light, 0))
    fill(LIGHT_1, position, 0, jnp.where(is_first, 0, light))
    fill(NEXT, following, 0, None)
    fill(AFTER, second, 0, None)
    fill(MINE, fullest, ROUNDS, jnp.where(position == fullest, extra, 0))
    fill(FED_1, fullest, ROUNDS, jnp.where(following == fullest, extra, 0))
    fill(FED_2, fullest, ROUNDS, jnp.where(second == fullest, extra, 0))
    for lower, upper, deals in (
        (MINE_L, MINE_H, position == fullest),
        (FED_1_L, FED_1_H, following == fullest),
        (FED_2_L, FED_2_H, second == fullest),
    ):
        all_of = jnp.where(deals, extra, 0)
        fill(lower, fullest, ROUNDS, jnp.minimum(all_of, ROUNDS))
        fill(upper, fullest, 2 * ROUNDS, jnp.maximum(all_of - ROUNDS, 0))
    for k in range(ROW):
        for row, part, source in ((LEAD, PART, MINE_L), (REST, REST_PART, MINE_H)):
            other = out_ref[NEXT * ROW + k] if k < ROUNDS else 0
            out_ref[row * ROW + k] = jnp.where(is_first, out_ref[source * ROW + k], other)
            out_ref[part * ROW + k] = jnp.where(is_first, 0, 0 if part == PART else 1)
    out_ref[MISC * ROW] = jnp.where(fullest < 2, 2, 0) + lax.rem(fullest, 2)
    out_ref[MISC * ROW + 1] = fullest
    out_ref[MISC * ROW + 2] = others
    out_ref[FIRST] = jnp.where(is_first, 1, 0)
    for k in range(4, ROW):
        out_ref[MISC * ROW + k] = 0


def kept_lists(position, screen):
    return pl.pallas_call(
        lists_kernel,
        in_specs=[pl.BlockSpec(memory_space=pltpu.SMEM)] * 2,
        out_specs=pl.BlockSpec(memory_space=pltpu.SMEM),
        out_shape=jax.ShapeDtypeStruct(((MISC + 1) * ROW,), jnp.int32),
        name="kept_lists",
    )(position.reshape(1), screen)


class Columns:
    def __init__(self, row, slots, start, extent, part=None, passing=None):
        self.row, self.slots, self.start, self.extent = row, slots, start, extent
        self.part, self.passing = part, passing


class Panel:
    def __init__(self, start, extent):
        self.start, self.extent = start, extent


def take_kernel(kinds, lists_ref, amplitudes, panel, *refs):
    count = len(kinds)
    sems = refs[-1]
    stages, outs = refs[-1 - count : -1], refs[-1 - 2 * count : -1 - count]

    def columns_load(kind, passing, width):
        def load(s, act):
            def own():
                sub = pl.multiple_of(lists_ref[kind.row * ROW + s] * width, width)
                first = kind.start
                if kind.part is not None:
                    further = lists_ref[kind.part * ROW + s] * kind.extent
                    first = pl.multiple_of(first + further, kind.extent)
                act(amplitudes.at[:, pl.ds(first, kind.extent), pl.ds(sub, width)])

            if passing is None:
                own()
            else:
                pl.when(lists_ref[FIRST] != 0)(lambda: act(passing.at[s]))
                pl.when(lists_ref[FIRST] == 0)(own)

        return load

    def panel_load(kind, share):
        def load(n, act):
            act(panel.at[pl.ds(n * share, share), pl.ds(kind.start, kind.extent), :])

        return load

    jobs = []
    given = 0
    for n, kind in enumerate(kinds):
        if isinstance(kind, Columns):
            passing = None
            if kind.passing is not None:
                passing = refs[given]
                given += 1
            load = columns_load(kind, passing, outs[n].shape[-1])
            jobs.append((load, lambda s, n=n: outs[n].at[s], kind.slots))
        else:
            share = stages[n].shape[1]
            load = panel_load(kind, share)
            jobs.append((load, lambda s, n=n, share=share: outs[n].at[pl.ds(s * share, share)], PARTS))

    def loops(act):
        for n, (load, target, pieces) in enumerate(jobs):

            def body(s, carry):
                act(n, s, load, target)
                return carry

            lax.fori_loop(0, pieces, body, 0)

    def start(n, s, load, target):
        stage = stages[n].at[s]
        load(s, lambda source: pltpu.make_async_copy(source, stage, sems.at[0, n, s]).start())

    def pass_on(n, s, load, target):
        stage = stages[n].at[s]
        pltpu.make_async_copy(stage, stage, sems.at[0, n, s]).wait()
        pltpu.make_async_copy(stage, target(s), sems.at[1, n, s]).start()

    def finish(n, s, load, target):
        stage = stages[n].at[s]
        pltpu.make_async_copy(stage, stage, sems.at[1, n, s]).wait()

    for act in (start, pass_on, finish):
        loops(act)


def take(lists, amplitudes, panel, kinds, width, behind=()):
    pairs = amplitudes.shape[0]
    b_rows, _, aux = panel.shape
    shapes, stages = [], []
    for kind in kinds:
        if isinstance(kind, Columns):
            shapes.append((kind.slots, pairs, kind.extent, width))
            stages.append(shapes[-1])
        else:
            shapes.append((b_rows, kind.extent, aux))
            stages.append((PARTS, b_rows // PARTS, kind.extent, aux))
    passed = [kind.passing for kind in kinds if getattr(kind, "passing", None) is not None]
    others = passed + list(behind)
    return pl.pallas_call(
        functools.partial(take_kernel, kinds),
        in_specs=[pl.BlockSpec(memory_space=pltpu.SMEM)]
        + [pl.BlockSpec(memory_space=pltpu.HBM)] * (2 + len(others)),
        out_specs=[pl.BlockSpec(memory_space=pltpu.HBM)] * len(kinds),
        out_shape=[jax.ShapeDtypeStruct(shape, amplitudes.dtype) for shape in shapes],
        scratch_shapes=[pltpu.VMEM(shape, amplitudes.dtype) for shape in stages]
        + [pltpu.SemaphoreType.DMA((2, len(kinds), max(shape[0] for shape in stages)))],
        compiler_params=pltpu.CompilerParams(vmem_limit_bytes=VMEM),
        cost_estimate=SMALL,
        name="take",
    )(lists, amplitudes, panel, *others)


def tie_kernel(*refs):
    pass


def tied(value, *behind):
    return pl.pallas_call(
        tie_kernel,
        in_specs=[pl.BlockSpec(memory_space=pltpu.HBM)] * (1 + len(behind)),
        out_specs=pl.BlockSpec(memory_space=pltpu.HBM),
        out_shape=jax.ShapeDtypeStruct(value.shape, value.dtype),
        input_output_aliases={0: 0},
        cost_estimate=SMALL,
        name="tied",
    )(value, *behind)


class Segment:
    def __init__(self, into, row, slots, amps, panel, extent, amp_at=0, panel_at=0, slot_at=0):
        self.into, self.row, self.slots = into, row, slots
        self.amps, self.panel, self.extent = amps, panel, extent
        self.amp_at, self.panel_at, self.slot_at = amp_at, panel_at, slot_at


def terms_kernel(segments, places, moves, d_rows, lists_ref, *refs):
    added, arrays = refs[: len(moves)], refs[len(moves) : -8]
    out_ref, amp_buf, panel_buf, factor_buf, mixed, total, sems, factor_sems = refs[-8:]
    factors = arrays[0]
    outs = out_ref.shape[0]
    _, most, pairs, _, width = amp_buf.shape
    b_rows = panel_buf.shape[1]
    _, _, a_rows, _, aux = factor_buf.shape

    counts = [lists_ref[seg.row * ROW + MOST] for seg in segments]
    starts, orders = [], []
    begin = order = jnp.int32(0)
    for seg, count in zip(segments, counts):
        starts.append(begin)
        orders.append(order)
        begin = begin + jnp.where(count > 0, seg.extent // d_rows, 0)
        order = order + jnp.where(count > 0, 1, 0)
    items = begin

    def pick(at, values):
        found = values[0]
        for s in range(1, len(segments)):
            found = jnp.where(at == s, values[s], found)
        return found

    def pick_row(o, values):
        found = values[0]
        for n in range(1, len(values)):
            found = jnp.where(o == n, values[n], found)
        return found

    def locate(t):
        at = jnp.int32(0)
        for s in range(len(segments)):
            at = jnp.where((counts[s] > 0) & (t >= starts[s]), s, at)
        return at, t - pick(at, starts), lax.rem(pick(at, orders), AHEAD)

    def fetch(t):
        at, block, turn = locate(t)
        slot = lax.rem(t, AHEAD)
        for s, seg in enumerate(segments):
            amps, panel = arrays[places[s][0]], arrays[places[s][1]]

            @pl.when(at == s)
            def _():
                amp_d = pl.ds(pl.multiple_of(seg.amp_at + block * d_rows, d_rows), d_rows)
                panel_d = pl.ds(pl.multiple_of(seg.panel_at + block * d_rows, d_rows), d_rows)
                pltpu.make_async_copy(
                    panel.at[:, panel_d, :], panel_buf.at[slot], sems.at[slot, most]
                ).start()

                def one(k, carry):
                    sub = pl.multiple_of(lists_ref[seg.row * ROW + k] * width, width)
                    columns = pl.ds(sub, width)
                    if len(amps.shape) == 3:
                        source = amps.at[:, amp_d, columns]
                    else:
                        source = amps.at[seg.slot_at + k, :, amp_d, :]
                    pltpu.make_async_copy(
                        source, amp_buf.at[slot, k], sems.at[slot, k]
                    ).start()

                    @pl.when(block == 0)
                    def _():
                        pltpu.make_async_copy(
                            factors.at[:, columns, :],
                            factor_buf.at[turn, k],
                            factor_sems.at[turn, k],
                        ).start()

                    return carry

                lax.fori_loop(0, counts[s], one, 0)

    def arrive(slot, block, turn, count):
        piece = panel_buf.at[slot]
        pltpu.make_async_copy(piece, piece, sems.at[slot, most]).wait()

        def one(k, carry):
            piece = amp_buf.at[slot, k]
            pltpu.make_async_copy(piece, piece, sems.at[slot, k]).wait()

            @pl.when(block == 0)
            def _():
                piece = factor_buf.at[turn, k]
                pltpu.make_async_copy(piece, piece, factor_sems.at[turn, k]).wait()

            return carry

        lax.fori_loop(0, count, one, 0)

    @pl.when(items > 0)
    def _():
        total[...] = jnp.zeros_like(total)

    def mix(low, top, slot, turn, count):
        columns = [amp_buf[slot, k].reshape(pairs * d_rows, width) for k in range(top)]
        for k in range(low, top):
            columns[k] = jnp.where(k < count, columns[k], jnp.zeros_like(columns[k]))
        lhs = jnp.concatenate(columns, axis=1)
        for a in range(a_rows):
            rows = [factor_buf[turn, k, a] for k in range(top)]
            for k in range(low, top):
                rows[k] = jnp.where(k < count, rows[k], jnp.zeros_like(rows[k]))
            product = jnp.dot(
                lhs, jnp.concatenate(rows, axis=0), preferred_element_type=jnp.float32
            )
            mixed[a] = product.astype(mixed.dtype).reshape(pairs, d_rows, aux)

    tops = set()
    for slots in {seg.slots for seg in segments}:
        tops |= {ROUNDS, slots} if slots == MOST else {slots}
    tops = sorted(top for top in tops if top <= ROUNDS or top == most)

    def step(n, carry):
        @pl.when(n < items)
        def _():
            fetch(n)

        @pl.when(n >= AHEAD - 1)
        def _():
            t = n - (AHEAD - 1)
            at, block, turn = locate(t)
            slot = lax.rem(t, AHEAD)
            count = pick(at, counts)
            into = pick(at, [seg.into for seg in segments])
            arrive(slot, block, turn, count)
            for low, top in zip([0] + tops, tops):

                @pl.when((count > low) & (count <= top))
                def _():
                    mix(low + 1, top, slot, turn, count)

            partial = total[into]
            for g in range(0, d_rows, GROUP):
                lhs = jnp.concatenate(
                    [mixed[a, :, g : g + GROUP, :].reshape(-1, aux) for a in range(a_rows)],
                    axis=0,
                )
                rhs = panel_buf[slot, :, g : g + GROUP, :].reshape(b_rows * GROUP, aux)
                partial += lax.dot_general(
                    lhs, rhs, (((1,), (1,)), ((), ())), preferred_element_type=jnp.float32
                )
            total[into] = partial

        return carry

    lax.fori_loop(0, jnp.where(items > 0, items + AHEAD - 1, 0), step, 0)

    out_ref[...] = jnp.zeros_like(out_ref)
    used = [jnp.int32(0)] * outs
    for seg, count in zip(segments, counts):
        used[seg.into] = used[seg.into] + count

    def finish(o, carry):
        @pl.when(pick_row(o, used) > 0)
        def _():
            _, rows, columns = total.shape
            row_d = lax.broadcasted_iota(jnp.int32, (rows, columns), 0) % GROUP
            column_d = lax.broadcasted_iota(jnp.int32, (rows, columns), 1) % GROUP
            kept = jnp.where(row_d == column_d, total[o], 0.0)
            kept = kept.reshape(rows // GROUP, GROUP, columns).sum(axis=1)
            from_b = lax.broadcasted_iota(jnp.int32, (columns, LANES), 0) // GROUP
            to_b = lax.broadcasted_iota(jnp.int32, (columns, LANES), 1)
            gather = jnp.where(from_b == to_b, 1.0, 0.0)
            out_ref[o] = jnp.dot(
                kept,
                gather,
                precision=lax.Precision.HIGHEST,
                preferred_element_type=jnp.float32,
            )

        return carry

    lax.fori_loop(0, outs, finish, 0)

    for ref, pairs_of in zip(added, moves):
        for source, target in pairs_of:
            out_ref[target] += ref[source]


def pair_terms(lists, factors_a, segments, outs, width, d_rows, behind=(), added=()):
    arrays, places = [factors_a], []
    for seg in segments:
        place = []
        for array in (seg.amps, seg.panel):
            known = [n for n, other in enumerate(arrays) if other is array]
            place.append(known[0] if known else len(arrays))
            if not known:
                arrays.append(array)
        places.append(place)
    arrays += behind
    a_rows, _, aux = factors_a.shape
    pairs = segments[0].amps.shape[-3]
    b_rows = segments[0].panel.shape[0]
    most = max(2, *(seg.slots for seg in segments))
    return pl.pallas_call(
        functools.partial(terms_kernel, segments, places, [moves for _, moves in added], d_rows),
        in_specs=[pl.BlockSpec(memory_space=pltpu.SMEM)]
        + [pl.BlockSpec(memory_space=pltpu.VMEM)] * len(added)
        + [pl.BlockSpec(memory_space=pltpu.HBM)] * len(arrays),
        out_specs=pl.BlockSpec(memory_space=pltpu.VMEM),
        scratch_shapes=[
            pltpu.VMEM((AHEAD, most, pairs, d_rows, width), jnp.bfloat16),
            pltpu.VMEM((AHEAD, b_rows, d_rows, aux), jnp.bfloat16),
            pltpu.VMEM((AHEAD, most, a_rows, width, aux), jnp.bfloat16),
            pltpu.VMEM((a_rows, pairs, d_rows, aux), jnp.bfloat16),
            pltpu.VMEM((outs, a_rows * pairs * GROUP, b_rows * GROUP), jnp.float32),
            pltpu.SemaphoreType.DMA((AHEAD, most + 1)),
            pltpu.SemaphoreType.DMA((AHEAD, most)),
        ],
        out_shape=jax.ShapeDtypeStruct((outs, a_rows * pairs, LANES), jnp.float32),
        compiler_params=pltpu.CompilerParams(vmem_limit_bytes=VMEM),
        cost_estimate=SMALL,
        name="pair_terms",
    )(lists, *(array for array, _ in added), *arrays)


def summed_over_narrow(value):
    size = lax.axis_size("narrow")
    me = lax.axis_index("narrow")
    share = value.shape[2] // size

    def part(owner):
        return lax.dynamic_slice_in_dim(value, owner * share, share, 2)

    parts = [part(me)]
    for k in range(1, size):
        to = [(i, (i + k) % size) for i in range(size)]
        parts.append(lax.ppermute(part((me + k) % size), "narrow", to))
    return sum(parts[1:], parts[0])


def local(factors_a, factors_b, amplitudes, screen):
    pairs, d_extent, virtuals = amplitudes.shape
    width = virtuals // screen.shape[1]
    tiles = lax.axis_size("blk")
    position = lax.axis_index("blk")
    extras = MOST - ROUNDS
    d_rows = min(64, d_extent // 4)

    lists = kept_lists(position, screen)
    fullest = lists[MISC * ROW + 1]
    others = lists[MISC * ROW + 2]
    is_first = position % 2 == 0
    is_full = position == fullest
    feeds_one = (position + 1) % tiles == fullest
    feeds_two = (position + 2) % tiles == fullest

    evens, odds = range(0, tiles, 2), range(1, tiles, 2)
    up = [(i, i + 1) for i in evens]
    down = [(i + 1, i) for i in evens]
    around = [(i, (i + 2) % tiles) for i in range(tiles)]

    def run(wrapped, odd, operands):
        lists, factors_a, factors_b, amplitudes = operands
        terms = functools.partial(pair_terms, lists, factors_a, width=width, d_rows=d_rows)
        copy = functools.partial(take, lists, amplitudes, factors_b, width=width)
        columns_of = functools.partial(Segment, panel=factors_b)
        given_to = functools.partial(Segment, amps=amplitudes, slots=extras)

        def ahead(at):
            return (at >= tiles - 2) == wrapped

        def hops(keep):
            return [(at, to) for at, to in around if keep(at)]

        def backs(keep):
            return [(to, at) for at, to in around if keep(at)]

        half, quarter = d_extent // 2, d_extent // 4
        low = 5 * d_extent // 8 // d_rows * d_rows
        high = d_extent - low
        own = columns_of(0, row=OWN, slots=MOST, amps=amplitudes, extent=d_extent)
        after = functools.partial(Columns, AFTER, ROUNDS)
        near = functools.partial(Columns, NEXT, ROUNDS)
        light = functools.partial(columns_of, slots=ROUNDS)
        mine = functools.partial(columns_of, row=MINE, slots=extras)
        if odd:
            given = max(3 * d_extent // 8 // d_rows, 1) * d_rows
            moved = d_extent - given

            def seconds(at):
                return at in odds and ahead(at)

            (extra,) = copy([Columns(MINE, extras, 0, moved)])
            extra_one = send(extra, up)
            extra_two = send(extra, hops(seconds))
            near_l, direct, panel = copy(
                [near(0, low), after(0, d_extent), Panel(moved, given)], behind=[extra]
            )
            side_l = send(near_l, down)
            got_direct = send(direct, hops(lambda at: at in evens))
            far = send(panel, backs(seconds))

            near_h, near_l, own_near_h, panel = copy(
                [near(low, high), near(0, low), near(low, high), Panel(moved, given)],
                behind=[near_l],
            )
            near_h = tied(near_h, side_l)
            side_h = send(near_h, down)
            (pass_l,) = copy([after(0, low, passing=side_l)], behind=[near_h])
            panel = tied(panel, side_h, extra_one, pass_l)
            beside = send(panel, down)
            near_l = tied(near_l, panel)
            own_l = send(near_l, up)
            pass_l = tied(pass_l, near_l, got_direct, extra_two)
            on_l = send(pass_l, around)
            (pass_h,) = copy([after(low, high, passing=side_h)], behind=[panel])
            pass_h = tied(pass_h, pass_l, far)
            on_h = send(pass_h, around)
            near_h = tied(own_near_h, pass_h)
            own_h = send(near_h, up)

            first = terms(
                [
                    own,
                    light(2, row=LIGHT_0, amps=got_direct, extent=d_extent),
                    mine(1, amps=extra_one, extent=moved),
                    mine(2, amps=extra_two, extent=moved),
                    given_to(3, row=FED_2, panel=far, extent=given, amp_at=moved),
                ],
                4,
                behind=[near_h],
            )
            then = terms(
                [
                    light(0, row=LIGHT_0, amps=on_l, extent=low),
                    light(1, row=LIGHT_1, amps=on_l, extent=low),
                    light(0, row=LIGHT_1, amps=own_l, extent=low),
                ],
                2,
                behind=[first],
            )
            return terms(
                [
                    light(1, row=LIGHT_0, amps=on_h, extent=high, panel_at=low),
                    light(2, row=LIGHT_1, amps=on_h, extent=high, panel_at=low),
                    light(1, row=LIGHT_1, amps=own_h, extent=high, panel_at=low),
                    given_to(3, row=FED_1, panel=beside, extent=given, amp_at=moved),
                ],
                4,
                added=[(first, [(0, 0), (1, 1), (2, 2), (3, 3)]), (then, [(0, 1), (1, 2)])],
            )
        else:
            def firsts(at):
                return at in evens and ahead(at)

            def early(at):
                return at in odds or ahead(at)

            lead = functools.partial(Columns, LEAD, ROUNDS, 0, half)
            rest = functools.partial(Columns, REST, ROUNDS, 0, half)
            lead_l, lead_h, beside = copy(
                [lead(part=PART), rest(part=REST_PART), near(0, d_extent)]
            )
            got_lead_l = send(lead_l, hops(early))
            got_lead_h = send(lead_h, hops(early))
            side = send(beside, up)
            extra, panel_0 = copy(
                [Columns(MINE, extras, 0, quarter), Panel(half, quarter)], behind=[lead_l]
            )
            cross = send(extra, down)
            far_0 = send(panel_0, backs(firsts))
            panel_1, after_l, after_h = copy(
                [Panel(half + quarter, quarter), after(0, low), after(low, high)],
                behind=[extra],
            )

            lead_down_l = send(got_lead_l, down)
            here = terms([own], 1, behind=[panel_1])
            panel_1 = tied(panel_1, cross, here)
            far_1 = send(panel_1, backs(firsts))
            (extra,) = copy(
                [Columns(MINE, extras, quarter, quarter, passing=cross)], behind=[panel_1]
            )
            got_lead_l = tied(got_lead_l, extra)
            lead_down_l = send(got_lead_l, down)
            far_0 = tied(far_0, extra, got_lead_l)
            up_0 = send(far_0, up)
            extra = tied(extra, got_lead_h)
            got_extra = send(extra, hops(ahead))
            got_lead_h = tied(got_lead_h, extra)
            lead_down_h = send(got_lead_h, down)
            after_l = tied(after_l, extra, side, lead_down_l)
            got_l = send(after_l, around)
            far_1 = tied(far_1, after_l)
            up_1 = send(far_1, up)
            got_extra = tied(got_extra, far_1)
            extra_down = send(got_extra, down)
            after_h = tied(after_h, got_extra, lead_down_h)
            got_h = send(after_h, around)

            first = terms(
                [
                    light(0, row=LIGHT_1, amps=side, extent=d_extent),
                    light(0, row=LIGHT_0, amps=lead_down_l, extent=half),
                    light(0, row=LIGHT_0, amps=lead_down_h, extent=half, panel_at=half),
                    light(1, row=MINE_L, amps=got_lead_l, extent=half),
                    light(1, row=MINE_H, amps=got_lead_h, extent=half),
                ],
                2,
                behind=[after_h],
            )

            def both(segment, *rows, **more):
                return [
                    segment(row=row, slot_at=n * ROUNDS, **more) for n, row in enumerate(rows)
                ]

            fed = functools.partial(Segment, amps=amplitudes, slots=ROUNDS, extent=quarter)
            extras_of = functools.partial(light, 1, extent=quarter)
            then = terms(
                both(fed, FED_1_L, FED_1_H, into=0, panel=up_0, amp_at=half)
                + both(fed, FED_2_L, FED_2_H, into=0, panel=far_0, amp_at=half)
                + both(fed, FED_2_L, FED_2_H, into=0, panel=far_1, amp_at=half + quarter)
                + both(extras_of, MINE_L, MINE_H, amps=got_extra)
                + both(extras_of, MINE_L, MINE_H, amps=extra_down, panel_at=quarter)
                + [light(2, row=LIGHT, amps=got_l, extent=low)],
                3,
                behind=[first],
            )
            return terms(
                [light(2, row=LIGHT, amps=got_h, extent=high, panel_at=low)]
                + both(fed, FED_1_L, FED_1_H, into=3, panel=up_1, amp_at=half + quarter),
                4,
                added=[
                    (here, [(0, 0)]),
                    (first, [(0, 1), (1, 2)]),
                    (then, [(0, 3), (1, 1), (2, 2)]),
                ],
            )

    branches = [
        functools.partial(run, wrapped, odd) for wrapped in (False, True) for odd in (False, True)
    ]
    operands = (lists, factors_a, factors_b, amplitudes)
    terms = lax.switch(lists[MISC * ROW], branches, operands)
    def add_round(r, terms):

        def only(row, count):
            sub = lax.dynamic_slice_in_dim(lists, row * ROW + r, 1)
            return jnp.concatenate([sub, jnp.zeros(MOST - 1, jnp.int32), count.reshape(1)])

        has = jnp.where((r < lists[OWN * ROW + MOST]) & ~is_full, 1, 0).astype(jnp.int32)
        own = only(OWN, has)
        moved = [
            rotated(
                take(
                    only(row, has), amplitudes, factors_b, [Columns(0, 1, 0, d_extent)], width
                )[0],
                by,
            )
            for row, by in ((NEXT, 1), (AFTER, 2))
        ]
        segments = [
            Segment(1 + n, 0, 1, columns, factors_b, d_extent) for n, columns in enumerate(moved)
        ]
        kept = [(n, n) for n in range(STEPS + 1)]
        return pair_terms(
            own, factors_a, segments, STEPS + 1, width, d_rows, added=[(terms, kept)]
        )

    terms = lax.fori_loop(ROUNDS, jnp.maximum(others, ROUNDS), add_round, terms)
    a_rows = factors_a.shape[0]
    terms = terms[:, :, : factors_b.shape[0]]
    terms = terms.reshape(STEPS + 1, a_rows, pairs, -1).swapaxes(1, 2)
    summed = summed_over_narrow(terms.reshape(STEPS + 1, 1, -1))
    given_one = rotated(jnp.where(feeds_one, summed[STEPS:], 0.0), 1)
    given_two = rotated(jnp.where(feeds_two, summed[STEPS:], 0.0), 2)
    return jnp.concatenate([summed[:1], summed[1:2] + given_one, summed[2:3] + given_two])


def solution(mesh):
    return jax.shard_map(
        local,
        mesh=mesh,
        in_specs=(P(), P("blk", "narrow", None), P("blk", "narrow", None), P()),
        out_specs=P(None, "blk", "narrow"),
        check_vma=False,
    )
```

```python
import functools

import jax
import jax.numpy as jnp
from jax import lax
from jax.experimental import pallas as pl
from jax.experimental.pallas import tpu as pltpu
from jax.sharding import PartitionSpec as P

STEPS = 3
MOST = 8
ROUNDS = 3
GROUP = 16
LANES = 128
ROW = MOST + 1

(
    OWN,
    LIGHT,
    LIGHT_0,
    LIGHT_1,
    NEXT,
    AFTER,
    LEAD,
    PART,
    REST,
    REST_PART,
    MINE,
    MINE_L,
    MINE_H,
    FED_1,
    FED_2,
    FED_1_L,
    FED_1_H,
    FED_2_L,
    FED_2_H,
    MISC,
) = range(20)
FIRST = MISC * ROW + 3
AHEAD = 4
PARTS = 4
VMEM = 60 * 1024 * 1024
SMALL = pl.CostEstimate(flops=1024, bytes_accessed=1024, transcendentals=0)


def send(value, pairs):
    return lax.ppermute(value, "blk", pairs)


def rotated(value, by):
    size = lax.axis_size("blk")
    return send(value, [(i, (i + by) % size) for i in range(size)])


def lists_kernel(position_ref, screen_ref, out_ref):
    tiles, subs = screen_ref.shape
    position = position_ref[0]

    def count_of(tile):
        return sum(jnp.where(screen_ref[tile, s] != 0, 1, 0) for s in range(subs))

    def look(tile, found):
        best, fullest, others = found
        count = count_of(tile)
        larger = count > best
        others = jnp.where(larger, best, jnp.maximum(others, count))
        return jnp.where(larger, count, best), jnp.where(larger, tile, fullest), others

    zero = jnp.int32(0)
    best, fullest, others = lax.fori_loop(0, tiles, look, (zero, zero, zero))

    def fill(row, tile, skip, count):
        for k in range(MOST):
            out_ref[row * ROW + k] = 0
        seen = jnp.int32(0)
        for s in range(subs):
            kept = screen_ref[tile, s] != 0

            @pl.when(kept & (seen >= skip))
            def _():
                out_ref[row * ROW + seen - skip] = s

            seen += jnp.where(kept, 1, 0)
        out_ref[row * ROW + MOST] = seen if count is None else count

    following = lax.rem(position + 1, tiles)
    second = lax.rem(position + 2, tiles)
    is_first = lax.rem(position, 2) == 0
    own_count = count_of(position)
    extra = jnp.maximum(best - ROUNDS, 0)
    light = jnp.minimum(own_count, ROUNDS)
    fill(OWN, position, 0, own_count)
    fill(LIGHT, position, 0, light)
    fill(LIGHT_0, position, 0, jnp.where(is_first, light, 0))
    fill(LIGHT_1, position, 0, jnp.where(is_first, 0, light))
    fill(NEXT, following, 0, None)
    fill(AFTER, second, 0, None)
    fill(MINE, fullest, ROUNDS, jnp.where(position == fullest, extra, 0))
    fill(FED_1, fullest, ROUNDS, jnp.where(following == fullest, extra, 0))
    fill(FED_2, fullest, ROUNDS, jnp.where(second == fullest, extra, 0))
    for lower, upper, deals in (
        (MINE_L, MINE_H, position == fullest),
        (FED_1_L, FED_1_H, following == fullest),
        (FED_2_L, FED_2_H, second == fullest),
    ):
        all_of = jnp.where(deals, extra, 0)
        fill(lower, fullest, ROUNDS, jnp.minimum(all_of, ROUNDS))
        fill(upper, fullest, 2 * ROUNDS, jnp.maximum(all_of - ROUNDS, 0))
    for k in range(ROW):
        for row, part, source in ((LEAD, PART, MINE_L), (REST, REST_PART, MINE_H)):
            other = out_ref[NEXT * ROW + k] if k < ROUNDS else 0
            out_ref[row * ROW + k] = jnp.where(is_first, out_ref[source * ROW + k], other)
            out_ref[part * ROW + k] = jnp.where(is_first, 0, 0 if part == PART else 1)
    out_ref[MISC * ROW] = jnp.where(fullest < 2, 2, 0) + lax.rem(fullest, 2)
    out_ref[MISC * ROW + 1] = fullest
    out_ref[MISC * ROW + 2] = others
    out_ref[FIRST] = jnp.where(is_first, 1, 0)
    for k in range(4, ROW):
        out_ref[MISC * ROW + k] = 0


def kept_lists(position, screen):
    return pl.pallas_call(
        lists_kernel,
        in_specs=[pl.BlockSpec(memory_space=pltpu.SMEM)] * 2,
        out_specs=pl.BlockSpec(memory_space=pltpu.SMEM),
        out_shape=jax.ShapeDtypeStruct(((MISC + 1) * ROW,), jnp.int32),
        name="kept_lists",
    )(position.reshape(1), screen)


class Columns:
    def __init__(self, row, slots, start, extent, part=None, passing=None):
        self.row, self.slots, self.start, self.extent = row, slots, start, extent
        self.part, self.passing = part, passing


class Panel:
    def __init__(self, start, extent):
        self.start, self.extent = start, extent


def take_kernel(kinds, lists_ref, amplitudes, panel, *refs):
    count = len(kinds)
    sems = refs[-1]
    stages, outs = refs[-1 - count : -1], refs[-1 - 2 * count : -1 - count]

    def columns_load(kind, passing, width):
        def load(s, act):
            def own():
                sub = pl.multiple_of(lists_ref[kind.row * ROW + s] * width, width)
                first = kind.start
                if kind.part is not None:
                    further = lists_ref[kind.part * ROW + s] * kind.extent
                    first = pl.multiple_of(first + further, kind.extent)
                act(amplitudes.at[:, pl.ds(first, kind.extent), pl.ds(sub, width)])

            if passing is None:
                own()
            else:
                pl.when(lists_ref[FIRST] != 0)(lambda: act(passing.at[s]))
                pl.when(lists_ref[FIRST] == 0)(own)

        return load

    def panel_load(kind, share):
        def load(n, act):
            act(panel.at[pl.ds(n * share, share), pl.ds(kind.start, kind.extent), :])

        return load

    jobs = []
    given = 0
    for n, kind in enumerate(kinds):
        if isinstance(kind, Columns):
            passing = None
            if kind.passing is not None:
                passing = refs[given]
                given += 1
            load = columns_load(kind, passing, outs[n].shape[-1])
            jobs.append((load, lambda s, n=n: outs[n].at[s], kind.slots))
        else:
            share = stages[n].shape[1]
            load = panel_load(kind, share)
            jobs.append((load, lambda s, n=n, share=share: outs[n].at[pl.ds(s * share, share)], PARTS))

    def loops(act):
        for n, (load, target, pieces) in enumerate(jobs):

            def body(s, carry):
                act(n, s, load, target)
                return carry

            lax.fori_loop(0, pieces, body, 0)

    def start(n, s, load, target):
        stage = stages[n].at[s]
        load(s, lambda source: pltpu.make_async_copy(source, stage, sems.at[0, n, s]).start())

    def pass_on(n, s, load, target):
        stage = stages[n].at[s]
        pltpu.make_async_copy(stage, stage, sems.at[0, n, s]).wait()
        pltpu.make_async_copy(stage, target(s), sems.at[1, n, s]).start()

    def finish(n, s, load, target):
        stage = stages[n].at[s]
        pltpu.make_async_copy(stage, stage, sems.at[1, n, s]).wait()

    for act in (start, pass_on, finish):
        loops(act)


def take(lists, amplitudes, panel, kinds, width, behind=()):
    pairs = amplitudes.shape[0]
    b_rows, _, aux = panel.shape
    shapes, stages = [], []
    for kind in kinds:
        if isinstance(kind, Columns):
            shapes.append((kind.slots, pairs, kind.extent, width))
            stages.append(shapes[-1])
        else:
            shapes.append((b_rows, kind.extent, aux))
            stages.append((PARTS, b_rows // PARTS, kind.extent, aux))
    passed = [kind.passing for kind in kinds if getattr(kind, "passing", None) is not None]
    others = passed + list(behind)
    return pl.pallas_call(
        functools.partial(take_kernel, kinds),
        in_specs=[pl.BlockSpec(memory_space=pltpu.SMEM)]
        + [pl.BlockSpec(memory_space=pltpu.HBM)] * (2 + len(others)),
        out_specs=[pl.BlockSpec(memory_space=pltpu.HBM)] * len(kinds),
        out_shape=[jax.ShapeDtypeStruct(shape, amplitudes.dtype) for shape in shapes],
        scratch_shapes=[pltpu.VMEM(shape, amplitudes.dtype) for shape in stages]
        + [pltpu.SemaphoreType.DMA((2, len(kinds), max(shape[0] for shape in stages)))],
        compiler_params=pltpu.CompilerParams(vmem_limit_bytes=VMEM),
        cost_estimate=SMALL,
        name="take",
    )(lists, amplitudes, panel, *others)


def tie_kernel(*refs):
    pass


def tied(value, *behind):
    return pl.pallas_call(
        tie_kernel,
        in_specs=[pl.BlockSpec(memory_space=pltpu.HBM)] * (1 + len(behind)),
        out_specs=pl.BlockSpec(memory_space=pltpu.HBM),
        out_shape=jax.ShapeDtypeStruct(value.shape, value.dtype),
        input_output_aliases={0: 0},
        cost_estimate=SMALL,
        name="tied",
    )(value, *behind)


class Segment:
    def __init__(self, into, row, slots, amps, panel, extent, amp_at=0, panel_at=0, slot_at=0):
        self.into, self.row, self.slots = into, row, slots
        self.amps, self.panel, self.extent = amps, panel, extent
        self.amp_at, self.panel_at, self.slot_at = amp_at, panel_at, slot_at


def terms_kernel(segments, places, moves, d_rows, lists_ref, *refs):
    added, arrays = refs[: len(moves)], refs[len(moves) : -8]
    out_ref, amp_buf, panel_buf, factor_buf, mixed, total, sems, factor_sems = refs[-8:]
    factors = arrays[0]
    outs = out_ref.shape[0]
    _, most, pairs, _, width = amp_buf.shape
    b_rows = panel_buf.shape[1]
    _, _, a_rows, _, aux = factor_buf.shape

    counts = [lists_ref[seg.row * ROW + MOST] for seg in segments]
    starts, orders = [], []
    begin = order = jnp.int32(0)
    for seg, count in zip(segments, counts):
        starts.append(begin)
        orders.append(order)
        begin = begin + jnp.where(count > 0, seg.extent // d_rows, 0)
        order = order + jnp.where(count > 0, 1, 0)
    items = begin

    def pick(at, values):
        found = values[0]
        for s in range(1, len(segments)):
            found = jnp.where(at == s, values[s], found)
        return found

    def pick_row(o, values):
        found = values[0]
        for n in range(1, len(values)):
            found = jnp.where(o == n, values[n], found)
        return found

    def locate(t):
        at = jnp.int32(0)
        for s in range(len(segments)):
            at = jnp.where((counts[s] > 0) & (t >= starts[s]), s, at)
        return at, t - pick(at, starts), lax.rem(pick(at, orders), AHEAD)

    def fetch(t):
        at, block, turn = locate(t)
        slot = lax.rem(t, AHEAD)
        for s, seg in enumerate(segments):
            amps, panel = arrays[places[s][0]], arrays[places[s][1]]

            @pl.when(at == s)
            def _():
                amp_d = pl.ds(pl.multiple_of(seg.amp_at + block * d_rows, d_rows), d_rows)
                panel_d = pl.ds(pl.multiple_of(seg.panel_at + block * d_rows, d_rows), d_rows)
                pltpu.make_async_copy(
                    panel.at[:, panel_d, :], panel_buf.at[slot], sems.at[slot, most]
                ).start()

                def one(k, carry):
                    sub = pl.multiple_of(lists_ref[seg.row * ROW + k] * width, width)
                    columns = pl.ds(sub, width)
                    if len(amps.shape) == 3:
                        source = amps.at[:, amp_d, columns]
                    else:
                        source = amps.at[seg.slot_at + k, :, amp_d, :]
                    pltpu.make_async_copy(
                        source, amp_buf.at[slot, k], sems.at[slot, k]
                    ).start()

                    @pl.when(block == 0)
                    def _():
                        pltpu.make_async_copy(
                            factors.at[:, columns, :],
                            factor_buf.at[turn, k],
                            factor_sems.at[turn, k],
                        ).start()

                    return carry

                lax.fori_loop(0, counts[s], one, 0)

    def arrive(slot, block, turn, count):
        piece = panel_buf.at[slot]
        pltpu.make_async_copy(piece, piece, sems.at[slot, most]).wait()

        def one(k, carry):
            piece = amp_buf.at[slot, k]
            pltpu.make_async_copy(piece, piece, sems.at[slot, k]).wait()

            @pl.when(block == 0)
            def _():
                piece = factor_buf.at[turn, k]
                pltpu.make_async_copy(piece, piece, factor_sems.at[turn, k]).wait()

            return carry

        lax.fori_loop(0, count, one, 0)

    @pl.when(items > 0)
    def _():
        total[...] = jnp.zeros_like(total)

    def mix(low, top, slot, turn, count):
        columns = [amp_buf[slot, k].reshape(pairs * d_rows, width) for k in range(top)]
        for k in range(low, top):
            columns[k] = jnp.where(k < count, columns[k], jnp.zeros_like(columns[k]))
        lhs = jnp.concatenate(columns, axis=1)
        for a in range(a_rows):
            rows = [factor_buf[turn, k, a] for k in range(top)]
            for k in range(low, top):
                rows[k] = jnp.where(k < count, rows[k], jnp.zeros_like(rows[k]))
            product = jnp.dot(
                lhs, jnp.concatenate(rows, axis=0), preferred_element_type=jnp.float32
            )
            mixed[a] = product.astype(mixed.dtype).reshape(pairs, d_rows, aux)

    tops = set()
    for slots in {seg.slots for seg in segments}:
        tops |= {ROUNDS, slots} if slots == MOST else {slots}
    tops = sorted(top for top in tops if top <= ROUNDS or top == most)

    def step(n, carry):
        @pl.when(n < items)
        def _():
            fetch(n)

        @pl.when(n >= AHEAD - 1)
        def _():
            t = n - (AHEAD - 1)
            at, block, turn = locate(t)
            slot = lax.rem(t, AHEAD)
            count = pick(at, counts)
            into = pick(at, [seg.into for seg in segments])
            arrive(slot, block, turn, count)
            for low, top in zip([0] + tops, tops):

                @pl.when((count > low) & (count <= top))
                def _():
                    mix(low + 1, top, slot, turn, count)

            partial = total[into]
            for g in range(0, d_rows, GROUP):
                lhs = jnp.concatenate(
                    [mixed[a, :, g : g + GROUP, :].reshape(-1, aux) for a in range(a_rows)],
                    axis=0,
                )
                rhs = panel_buf[slot, :, g : g + GROUP, :].reshape(b_rows * GROUP, aux)
                partial += lax.dot_general(
                    lhs, rhs, (((1,), (1,)), ((), ())), preferred_element_type=jnp.float32
                )
            total[into] = partial

        return carry

    lax.fori_loop(0, jnp.where(items > 0, items + AHEAD - 1, 0), step, 0)

    out_ref[...] = jnp.zeros_like(out_ref)
    used = [jnp.int32(0)] * outs
    for seg, count in zip(segments, counts):
        used[seg.into] = used[seg.into] + count

    def finish(o, carry):
        @pl.when(pick_row(o, used) > 0)
        def _():
            _, rows, columns = total.shape
            row_d = lax.broadcasted_iota(jnp.int32, (rows, columns), 0) % GROUP
            column_d = lax.broadcasted_iota(jnp.int32, (rows, columns), 1) % GROUP
            kept = jnp.where(row_d == column_d, total[o], 0.0)
            kept = kept.reshape(rows // GROUP, GROUP, columns).sum(axis=1)
            from_b = lax.broadcasted_iota(jnp.int32, (columns, LANES), 0) // GROUP
            to_b = lax.broadcasted_iota(jnp.int32, (columns, LANES), 1)
            gather = jnp.where(from_b == to_b, 1.0, 0.0)
            out_ref[o] = jnp.dot(
                kept,
                gather,
                precision=lax.Precision.HIGHEST,
                preferred_element_type=jnp.float32,
            )

        return carry

    lax.fori_loop(0, outs, finish, 0)

    for ref, pairs_of in zip(added, moves):
        for source, target in pairs_of:
            out_ref[target] += ref[source]


def pair_terms(lists, factors_a, segments, outs, width, d_rows, behind=(), added=()):
    arrays, places = [factors_a], []
    for seg in segments:
        place = []
        for array in (seg.amps, seg.panel):
            known = [n for n, other in enumerate(arrays) if other is array]
            place.append(known[0] if known else len(arrays))
            if not known:
                arrays.append(array)
        places.append(place)
    arrays += behind
    a_rows, _, aux = factors_a.shape
    pairs = segments[0].amps.shape[-3]
    b_rows = segments[0].panel.shape[0]
    most = max(2, *(seg.slots for seg in segments))
    return pl.pallas_call(
        functools.partial(terms_kernel, segments, places, [moves for _, moves in added], d_rows),
        in_specs=[pl.BlockSpec(memory_space=pltpu.SMEM)]
        + [pl.BlockSpec(memory_space=pltpu.VMEM)] * len(added)
        + [pl.BlockSpec(memory_space=pltpu.HBM)] * len(arrays),
        out_specs=pl.BlockSpec(memory_space=pltpu.VMEM),
        scratch_shapes=[
            pltpu.VMEM((AHEAD, most, pairs, d_rows, width), jnp.bfloat16),
            pltpu.VMEM((AHEAD, b_rows, d_rows, aux), jnp.bfloat16),
            pltpu.VMEM((AHEAD, most, a_rows, width, aux), jnp.bfloat16),
            pltpu.VMEM((a_rows, pairs, d_rows, aux), jnp.bfloat16),
            pltpu.VMEM((outs, a_rows * pairs * GROUP, b_rows * GROUP), jnp.float32),
            pltpu.SemaphoreType.DMA((AHEAD, most + 1)),
            pltpu.SemaphoreType.DMA((AHEAD, most)),
        ],
        out_shape=jax.ShapeDtypeStruct((outs, a_rows * pairs, LANES), jnp.float32),
        compiler_params=pltpu.CompilerParams(vmem_limit_bytes=VMEM),
        cost_estimate=SMALL,
        name="pair_terms",
    )(lists, *(array for array, _ in added), *arrays)


def summed_over_narrow(value):
    size = lax.axis_size("narrow")
    me = lax.axis_index("narrow")
    share = value.shape[2] // size

    def part(owner):
        return lax.dynamic_slice_in_dim(value, owner * share, share, 2)

    parts = [part(me)]
    for k in range(1, size):
        to = [(i, (i + k) % size) for i in range(size)]
        parts.append(lax.ppermute(part((me + k) % size), "narrow", to))
    return sum(parts[1:], parts[0])


def local(factors_a, factors_b, amplitudes, screen):
    pairs, d_extent, virtuals = amplitudes.shape
    width = virtuals // screen.shape[1]
    tiles = lax.axis_size("blk")
    position = lax.axis_index("blk")
    extras = MOST - ROUNDS
    d_rows = min(64, d_extent // 4)

    lists = kept_lists(position, screen)
    fullest = lists[MISC * ROW + 1]
    others = lists[MISC * ROW + 2]
    is_first = position % 2 == 0
    is_full = position == fullest
    feeds_one = (position + 1) % tiles == fullest
    feeds_two = (position + 2) % tiles == fullest

    evens, odds = range(0, tiles, 2), range(1, tiles, 2)
    up = [(i, i + 1) for i in evens]
    down = [(i + 1, i) for i in evens]
    around = [(i, (i + 2) % tiles) for i in range(tiles)]

    def run(wrapped, odd, operands):
        lists, factors_a, factors_b, amplitudes = operands
        terms = functools.partial(pair_terms, lists, factors_a, width=width, d_rows=d_rows)
        copy = functools.partial(take, lists, amplitudes, factors_b, width=width)
        columns_of = functools.partial(Segment, panel=factors_b)
        given_to = functools.partial(Segment, amps=amplitudes, slots=extras)

        def ahead(at):
            return (at >= tiles - 2) == wrapped

        def hops(keep):
            return [(at, to) for at, to in around if keep(at)]

        def backs(keep):
            return [(to, at) for at, to in around if keep(at)]

        half, quarter = d_extent // 2, d_extent // 4
        low = 5 * d_extent // 8 // d_rows * d_rows
        high = d_extent - low
        own = columns_of(0, row=OWN, slots=MOST, amps=amplitudes, extent=d_extent)
        after = functools.partial(Columns, AFTER, ROUNDS)
        near = functools.partial(Columns, NEXT, ROUNDS)
        light = functools.partial(columns_of, slots=ROUNDS)
        mine = functools.partial(columns_of, row=MINE, slots=extras)
        if odd:
            given = max(3 * d_extent // 8 // d_rows, 1) * d_rows
            moved = d_extent - given

            def seconds(at):
                return at in odds and ahead(at)

            (extra,) = copy([Columns(MINE, extras, 0, moved)])
            extra_one = send(extra, up)
            extra_two = send(extra, hops(seconds))
            near_l, direct, panel = copy(
                [near(0, low), after(0, d_extent), Panel(moved, given)], behind=[extra]
            )
            side_l = send(near_l, down)
            got_direct = send(direct, hops(lambda at: at in evens))
            far = send(panel, backs(seconds))

            near_h, near_l, own_near_h, panel = copy(
                [near(low, high), near(0, low), near(low, high), Panel(moved, given)],
                behind=[near_l],
            )
            near_h = tied(near_h, side_l)
            side_h = send(near_h, down)
            (pass_l,) = copy([after(0, low, passing=side_l)], behind=[near_h])
            panel = tied(panel, side_h, extra_one, pass_l)
            beside = send(panel, down)
            near_l = tied(near_l, panel)
            own_l = send(near_l, up)
            pass_l = tied(pass_l, near_l, got_direct, extra_two)
            on_l = send(pass_l, around)
            (pass_h,) = copy([after(low, high, passing=side_h)], behind=[panel])
            pass_h = tied(pass_h, pass_l, far)
            on_h = send(pass_h, around)
            near_h = tied(own_near_h, pass_h)
            own_h = send(near_h, up)

            first = terms(
                [
                    own,
                    light(2, row=LIGHT_0, amps=got_direct, extent=d_extent),
                    mine(1, amps=extra_one, extent=moved),
                    mine(2, amps=extra_two, extent=moved),
                    given_to(3, row=FED_2, panel=far, extent=given, amp_at=moved),
                ],
                4,
                behind=[near_h],
            )
            then = terms(
                [
                    light(0, row=LIGHT_0, amps=on_l, extent=low),
                    light(1, row=LIGHT_1, amps=on_l, extent=low),
                    light(0, row=LIGHT_1, amps=own_l, extent=low),
                ],
                2,
                behind=[first],
            )
            return terms(
                [
                    light(1, row=LIGHT_0, amps=on_h, extent=high, panel_at=low),
                    light(2, row=LIGHT_1, amps=on_h, extent=high, panel_at=low),
                    light(1, row=LIGHT_1, amps=own_h, extent=high, panel_at=low),
                    given_to(3, row=FED_1, panel=beside, extent=given, amp_at=moved),
                ],
                4,
                added=[(first, [(0, 0), (1, 1), (2, 2), (3, 3)]), (then, [(0, 1), (1, 2)])],
            )
        else:
            def firsts(at):
                return at in evens and ahead(at)

            def early(at):
                return at in odds or ahead(at)

            lead = functools.partial(Columns, LEAD, ROUNDS, 0, half)
            rest = functools.partial(Columns, REST, ROUNDS, 0, half)
            lead_l, lead_h, extra = copy(
                [
                    lead(part=PART),
                    rest(part=REST_PART),
                    Columns(MINE, extras, 0, quarter),
                ]
            )
            got_lead_l = send(lead_l, hops(early))
            got_lead_h = send(lead_h, hops(early))
            cross = send(extra, down)
            beside, panel_0 = copy(
                [near(0, d_extent), Panel(half, quarter)], behind=[lead_l]
            )
            side = send(beside, up)
            far_0 = send(panel_0, backs(firsts))
            panel_1, after_l, after_h = copy(
                [Panel(half + quarter, quarter), after(0, low), after(low, high)],
                behind=[panel_0],
            )

            lead_down_l = send(got_lead_l, down)
            here = terms([own], 1, behind=[panel_1])
            panel_1 = tied(panel_1, cross, here)
            far_1 = send(panel_1, backs(firsts))
            (extra,) = copy(
                [Columns(MINE, extras, quarter, quarter, passing=cross)], behind=[panel_1]
            )
            got_lead_l = tied(got_lead_l, extra)
            lead_down_l = send(got_lead_l, down)
            far_0 = tied(far_0, extra, got_lead_l)
            up_0 = send(far_0, up)
            extra = tied(extra, got_lead_h)
            got_extra = send(extra, hops(ahead))
            got_lead_h = tied(got_lead_h, extra)
            lead_down_h = send(got_lead_h, down)
            after_l = tied(after_l, extra, side, lead_down_l)
            got_l = send(after_l, around)
            far_1 = tied(far_1, after_l)
            up_1 = send(far_1, up)
            got_extra = tied(got_extra, far_1)
            extra_down = send(got_extra, down)
            after_h = tied(after_h, got_extra, lead_down_h)
            got_h = send(after_h, around)

            first = terms(
                [
                    light(0, row=LIGHT_1, amps=side, extent=d_extent),
                    light(0, row=LIGHT_0, amps=lead_down_l, extent=half),
                    light(0, row=LIGHT_0, amps=lead_down_h, extent=half, panel_at=half),
                    light(1, row=MINE_L, amps=got_lead_l, extent=half),
                    light(1, row=MINE_H, amps=got_lead_h, extent=half),
                ],
                2,
                behind=[after_h],
            )

            def both(segment, *rows, **more):
                return [
                    segment(row=row, slot_at=n * ROUNDS, **more) for n, row in enumerate(rows)
                ]

            fed = functools.partial(Segment, amps=amplitudes, slots=ROUNDS, extent=quarter)
            extras_of = functools.partial(light, 1, extent=quarter)
            then = terms(
                both(fed, FED_1_L, FED_1_H, into=0, panel=up_0, amp_at=half)
                + both(fed, FED_2_L, FED_2_H, into=0, panel=far_0, amp_at=half)
                + both(fed, FED_2_L, FED_2_H, into=0, panel=far_1, amp_at=half + quarter)
                + both(extras_of, MINE_L, MINE_H, amps=got_extra)
                + both(extras_of, MINE_L, MINE_H, amps=extra_down, panel_at=quarter)
                + [light(2, row=LIGHT, amps=got_l, extent=low)],
                3,
                behind=[first],
            )
            return terms(
                [light(2, row=LIGHT, amps=got_h, extent=high, panel_at=low)]
                + both(fed, FED_1_L, FED_1_H, into=3, panel=up_1, amp_at=half + quarter),
                4,
                added=[
                    (here, [(0, 0)]),
                    (first, [(0, 1), (1, 2)]),
                    (then, [(0, 3), (1, 1), (2, 2)]),
                ],
            )

    branches = [
        functools.partial(run, wrapped, odd) for wrapped in (False, True) for odd in (False, True)
    ]
    operands = (lists, factors_a, factors_b, amplitudes)
    terms = lax.switch(lists[MISC * ROW], branches, operands)
    def add_round(r, terms):

        def only(row, count):
            sub = lax.dynamic_slice_in_dim(lists, row * ROW + r, 1)
            return jnp.concatenate([sub, jnp.zeros(MOST - 1, jnp.int32), count.reshape(1)])

        has = jnp.where((r < lists[OWN * ROW + MOST]) & ~is_full, 1, 0).astype(jnp.int32)
        own = only(OWN, has)
        moved = [
            rotated(
                take(
                    only(row, has), amplitudes, factors_b, [Columns(0, 1, 0, d_extent)], width
                )[0],
                by,
            )
            for row, by in ((NEXT, 1), (AFTER, 2))
        ]
        segments = [
            Segment(1 + n, 0, 1, columns, factors_b, d_extent) for n, columns in enumerate(moved)
        ]
        kept = [(n, n) for n in range(STEPS + 1)]
        return pair_terms(
            own, factors_a, segments, STEPS + 1, width, d_rows, added=[(terms, kept)]
        )

    terms = lax.fori_loop(ROUNDS, jnp.maximum(others, ROUNDS), add_round, terms)
    a_rows = factors_a.shape[0]
    terms = terms[:, :, : factors_b.shape[0]]
    terms = terms.reshape(STEPS + 1, a_rows, pairs, -1).swapaxes(1, 2)
    summed = summed_over_narrow(terms.reshape(STEPS + 1, 1, -1))
    given_one = rotated(jnp.where(feeds_one, summed[STEPS:], 0.0), 1)
    given_two = rotated(jnp.where(feeds_two, summed[STEPS:], 0.0), 2)
    return jnp.concatenate([summed[:1], summed[1:2] + given_one, summed[2:3] + given_two])


def solution(mesh):
    return jax.shard_map(
        local,
        mesh=mesh,
        in_specs=(P(), P("blk", "narrow", None), P("blk", "narrow", None), P()),
        out_specs=P(None, "blk", "narrow"),
        check_vma=False,
    )
```

```python
import functools

import jax
import jax.numpy as jnp
from jax import lax
from jax.experimental import pallas as pl
from jax.experimental.pallas import tpu as pltpu
from jax.sharding import PartitionSpec as P

STEPS = 3
MOST = 8
ROUNDS = 3
GROUP = 16
LANES = 128
ROW = MOST + 1

(
    OWN,
    LIGHT,
    LIGHT_0,
    LIGHT_1,
    NEXT,
    AFTER,
    LEAD,
    PART,
    REST,
    REST_PART,
    MINE,
    MINE_L,
    MINE_H,
    FED_1,
    FED_2,
    FED_1_L,
    FED_1_H,
    FED_2_L,
    FED_2_H,
    MISC,
) = range(20)
FIRST = MISC * ROW + 3
AHEAD = 4
PARTS = 4
VMEM = 60 * 1024 * 1024
SMALL = pl.CostEstimate(flops=1024, bytes_accessed=1024, transcendentals=0)


def send(value, pairs):
    return lax.ppermute(value, "blk", pairs)


def rotated(value, by):
    size = lax.axis_size("blk")
    return send(value, [(i, (i + by) % size) for i in range(size)])


def lists_kernel(position_ref, screen_ref, out_ref):
    tiles, subs = screen_ref.shape
    position = position_ref[0]

    def count_of(tile):
        return sum(jnp.where(screen_ref[tile, s] != 0, 1, 0) for s in range(subs))

    def look(tile, found):
        best, fullest, others = found
        count = count_of(tile)
        larger = count > best
        others = jnp.where(larger, best, jnp.maximum(others, count))
        return jnp.where(larger, count, best), jnp.where(larger, tile, fullest), others

    zero = jnp.int32(0)
    best, fullest, others = lax.fori_loop(0, tiles, look, (zero, zero, zero))

    def fill(row, tile, skip, count):
        for k in range(MOST):
            out_ref[row * ROW + k] = 0
        seen = jnp.int32(0)
        for s in range(subs):
            kept = screen_ref[tile, s] != 0

            @pl.when(kept & (seen >= skip))
            def _():
                out_ref[row * ROW + seen - skip] = s

            seen += jnp.where(kept, 1, 0)
        out_ref[row * ROW + MOST] = seen if count is None else count

    following = lax.rem(position + 1, tiles)
    second = lax.rem(position + 2, tiles)
    is_first = lax.rem(position, 2) == 0
    own_count = count_of(position)
    extra = jnp.maximum(best - ROUNDS, 0)
    light = jnp.minimum(own_count, ROUNDS)
    fill(OWN, position, 0, own_count)
    fill(LIGHT, position, 0, light)
    fill(LIGHT_0, position, 0, jnp.where(is_first, light, 0))
    fill(LIGHT_1, position, 0, jnp.where(is_first, 0, light))
    fill(NEXT, following, 0, None)
    fill(AFTER, second, 0, None)
    fill(MINE, fullest, ROUNDS, jnp.where(position == fullest, extra, 0))
    fill(FED_1, fullest, ROUNDS, jnp.where(following == fullest, extra, 0))
    fill(FED_2, fullest, ROUNDS, jnp.where(second == fullest, extra, 0))
    for lower, upper, deals in (
        (MINE_L, MINE_H, position == fullest),
        (FED_1_L, FED_1_H, following == fullest),
        (FED_2_L, FED_2_H, second == fullest),
    ):
        all_of = jnp.where(deals, extra, 0)
        fill(lower, fullest, ROUNDS, jnp.minimum(all_of, ROUNDS))
        fill(upper, fullest, 2 * ROUNDS, jnp.maximum(all_of - ROUNDS, 0))
    for k in range(ROW):
        for row, part, source in ((LEAD, PART, MINE_L), (REST, REST_PART, MINE_H)):
            other = out_ref[NEXT * ROW + k] if k < ROUNDS else 0
            out_ref[row * ROW + k] = jnp.where(is_first, out_ref[source * ROW + k], other)
            out_ref[part * ROW + k] = jnp.where(is_first, 0, 0 if part == PART else 1)
    out_ref[MISC * ROW] = jnp.where(fullest < 2, 2, 0) + lax.rem(fullest, 2)
    out_ref[MISC * ROW + 1] = fullest
    out_ref[MISC * ROW + 2] = others
    out_ref[FIRST] = jnp.where(is_first, 1, 0)
    for k in range(4, ROW):
        out_ref[MISC * ROW + k] = 0


def kept_lists(position, screen):
    return pl.pallas_call(
        lists_kernel,
        in_specs=[pl.BlockSpec(memory_space=pltpu.SMEM)] * 2,
        out_specs=pl.BlockSpec(memory_space=pltpu.SMEM),
        out_shape=jax.ShapeDtypeStruct(((MISC + 1) * ROW,), jnp.int32),
        name="kept_lists",
    )(position.reshape(1), screen)


class Columns:
    def __init__(self, row, slots, start, extent, part=None, passing=None):
        self.row, self.slots, self.start, self.extent = row, slots, start, extent
        self.part, self.passing = part, passing


class Panel:
    def __init__(self, start, extent):
        self.start, self.extent = start, extent


def take_kernel(kinds, lists_ref, amplitudes, panel, *refs):
    count = len(kinds)
    sems = refs[-1]
    stages, outs = refs[-1 - count : -1], refs[-1 - 2 * count : -1 - count]

    def columns_load(kind, passing, width):
        def load(s, act):
            def own():
                sub = pl.multiple_of(lists_ref[kind.row * ROW + s] * width, width)
                first = kind.start
                if kind.part is not None:
                    further = lists_ref[kind.part * ROW + s] * kind.extent
                    first = pl.multiple_of(first + further, kind.extent)
                act(amplitudes.at[:, pl.ds(first, kind.extent), pl.ds(sub, width)])

            if passing is None:
                own()
            else:
                pl.when(lists_ref[FIRST] != 0)(lambda: act(passing.at[s]))
                pl.when(lists_ref[FIRST] == 0)(own)

        return load

    def panel_load(kind, share):
        def load(n, act):
            act(panel.at[pl.ds(n * share, share), pl.ds(kind.start, kind.extent), :])

        return load

    jobs = []
    given = 0
    for n, kind in enumerate(kinds):
        if isinstance(kind, Columns):
            passing = None
            if kind.passing is not None:
                passing = refs[given]
                given += 1
            load = columns_load(kind, passing, outs[n].shape[-1])
            jobs.append((load, lambda s, n=n: outs[n].at[s], kind.slots))
        else:
            share = stages[n].shape[1]
            load = panel_load(kind, share)
            jobs.append((load, lambda s, n=n, share=share: outs[n].at[pl.ds(s * share, share)], PARTS))

    def loops(act):
        for n, (load, target, pieces) in enumerate(jobs):

            def body(s, carry):
                act(n, s, load, target)
                return carry

            lax.fori_loop(0, pieces, body, 0)

    def start(n, s, load, target):
        stage = stages[n].at[s]
        load(s, lambda source: pltpu.make_async_copy(source, stage, sems.at[0, n, s]).start())

    def pass_on(n, s, load, target):
        stage = stages[n].at[s]
        pltpu.make_async_copy(stage, stage, sems.at[0, n, s]).wait()
        pltpu.make_async_copy(stage, target(s), sems.at[1, n, s]).start()

    def finish(n, s, load, target):
        stage = stages[n].at[s]
        pltpu.make_async_copy(stage, stage, sems.at[1, n, s]).wait()

    for act in (start, pass_on, finish):
        loops(act)


def take(lists, amplitudes, panel, kinds, width, behind=()):
    pairs = amplitudes.shape[0]
    b_rows, _, aux = panel.shape
    shapes, stages = [], []
    for kind in kinds:
        if isinstance(kind, Columns):
            shapes.append((kind.slots, pairs, kind.extent, width))
            stages.append(shapes[-1])
        else:
            shapes.append((b_rows, kind.extent, aux))
            stages.append((PARTS, b_rows // PARTS, kind.extent, aux))
    passed = [kind.passing for kind in kinds if getattr(kind, "passing", None) is not None]
    others = passed + list(behind)
    return pl.pallas_call(
        functools.partial(take_kernel, kinds),
        in_specs=[pl.BlockSpec(memory_space=pltpu.SMEM)]
        + [pl.BlockSpec(memory_space=pltpu.HBM)] * (2 + len(others)),
        out_specs=[pl.BlockSpec(memory_space=pltpu.HBM)] * len(kinds),
        out_shape=[jax.ShapeDtypeStruct(shape, amplitudes.dtype) for shape in shapes],
        scratch_shapes=[pltpu.VMEM(shape, amplitudes.dtype) for shape in stages]
        + [pltpu.SemaphoreType.DMA((2, len(kinds), max(shape[0] for shape in stages)))],
        compiler_params=pltpu.CompilerParams(vmem_limit_bytes=VMEM),
        cost_estimate=SMALL,
        name="take",
    )(lists, amplitudes, panel, *others)


def tie_kernel(*refs):
    pass


def tied(value, *behind):
    return pl.pallas_call(
        tie_kernel,
        in_specs=[pl.BlockSpec(memory_space=pltpu.HBM)] * (1 + len(behind)),
        out_specs=pl.BlockSpec(memory_space=pltpu.HBM),
        out_shape=jax.ShapeDtypeStruct(value.shape, value.dtype),
        input_output_aliases={0: 0},
        cost_estimate=SMALL,
        name="tied",
    )(value, *behind)


class Segment:
    def __init__(self, into, row, slots, amps, panel, extent, amp_at=0, panel_at=0, slot_at=0):
        self.into, self.row, self.slots = into, row, slots
        self.amps, self.panel, self.extent = amps, panel, extent
        self.amp_at, self.panel_at, self.slot_at = amp_at, panel_at, slot_at


def terms_kernel(segments, places, moves, d_rows, lists_ref, *refs):
    added, arrays = refs[: len(moves)], refs[len(moves) : -8]
    out_ref, amp_buf, panel_buf, factor_buf, mixed, total, sems, factor_sems = refs[-8:]
    factors = arrays[0]
    outs = out_ref.shape[0]
    _, most, pairs, _, width = amp_buf.shape
    b_rows = panel_buf.shape[1]
    _, _, a_rows, _, aux = factor_buf.shape

    counts = [lists_ref[seg.row * ROW + MOST] for seg in segments]
    starts, orders = [], []
    begin = order = jnp.int32(0)
    for seg, count in zip(segments, counts):
        starts.append(begin)
        orders.append(order)
        begin = begin + jnp.where(count > 0, seg.extent // d_rows, 0)
        order = order + jnp.where(count > 0, 1, 0)
    items = begin

    def pick(at, values):
        found = values[0]
        for s in range(1, len(segments)):
            found = jnp.where(at == s, values[s], found)
        return found

    def pick_row(o, values):
        found = values[0]
        for n in range(1, len(values)):
            found = jnp.where(o == n, values[n], found)
        return found

    def locate(t):
        at = jnp.int32(0)
        for s in range(len(segments)):
            at = jnp.where((counts[s] > 0) & (t >= starts[s]), s, at)
        return at, t - pick(at, starts), lax.rem(pick(at, orders), AHEAD)

    def fetch(t):
        at, block, turn = locate(t)
        slot = lax.rem(t, AHEAD)
        for s, seg in enumerate(segments):
            amps, panel = arrays[places[s][0]], arrays[places[s][1]]

            @pl.when(at == s)
            def _():
                amp_d = pl.ds(pl.multiple_of(seg.amp_at + block * d_rows, d_rows), d_rows)
                panel_d = pl.ds(pl.multiple_of(seg.panel_at + block * d_rows, d_rows), d_rows)
                pltpu.make_async_copy(
                    panel.at[:, panel_d, :], panel_buf.at[slot], sems.at[slot, most]
                ).start()

                def one(k, carry):
                    sub = pl.multiple_of(lists_ref[seg.row * ROW + k] * width, width)
                    columns = pl.ds(sub, width)
                    if len(amps.shape) == 3:
                        source = amps.at[:, amp_d, columns]
                    else:
                        source = amps.at[seg.slot_at + k, :, amp_d, :]
                    pltpu.make_async_copy(
                        source, amp_buf.at[slot, k], sems.at[slot, k]
                    ).start()

                    @pl.when(block == 0)
                    def _():
                        pltpu.make_async_copy(
                            factors.at[:, columns, :],
                            factor_buf.at[turn, k],
                            factor_sems.at[turn, k],
                        ).start()

                    return carry

                lax.fori_loop(0, counts[s], one, 0)

    def arrive(slot, block, turn, count):
        piece = panel_buf.at[slot]
        pltpu.make_async_copy(piece, piece, sems.at[slot, most]).wait()

        def one(k, carry):
            piece = amp_buf.at[slot, k]
            pltpu.make_async_copy(piece, piece, sems.at[slot, k]).wait()

            @pl.when(block == 0)
            def _():
                piece = factor_buf.at[turn, k]
                pltpu.make_async_copy(piece, piece, factor_sems.at[turn, k]).wait()

            return carry

        lax.fori_loop(0, count, one, 0)

    @pl.when(items > 0)
    def _():
        total[...] = jnp.zeros_like(total)

    def mix(low, top, slot, turn, count):
        columns = [amp_buf[slot, k].reshape(pairs * d_rows, width) for k in range(top)]
        for k in range(low, top):
            columns[k] = jnp.where(k < count, columns[k], jnp.zeros_like(columns[k]))
        lhs = jnp.concatenate(columns, axis=1)
        for a in range(a_rows):
            rows = [factor_buf[turn, k, a] for k in range(top)]
            for k in range(low, top):
                rows[k] = jnp.where(k < count, rows[k], jnp.zeros_like(rows[k]))
            product = jnp.dot(
                lhs, jnp.concatenate(rows, axis=0), preferred_element_type=jnp.float32
            )
            mixed[a] = product.astype(mixed.dtype).reshape(pairs, d_rows, aux)

    tops = set()
    for slots in {seg.slots for seg in segments}:
        tops |= {ROUNDS, slots} if slots == MOST else {slots}
    tops = sorted(top for top in tops if top <= ROUNDS or top == most)

    def step(n, carry):
        @pl.when(n < items)
        def _():
            fetch(n)

        @pl.when(n >= AHEAD - 1)
        def _():
            t = n - (AHEAD - 1)
            at, block, turn = locate(t)
            slot = lax.rem(t, AHEAD)
            count = pick(at, counts)
            into = pick(at, [seg.into for seg in segments])
            arrive(slot, block, turn, count)
            for low, top in zip([0] + tops, tops):

                @pl.when((count > low) & (count <= top))
                def _():
                    mix(low + 1, top, slot, turn, count)

            partial = total[into]
            for g in range(0, d_rows, GROUP):
                lhs = jnp.concatenate(
                    [mixed[a, :, g : g + GROUP, :].reshape(-1, aux) for a in range(a_rows)],
                    axis=0,
                )
                rhs = panel_buf[slot, :, g : g + GROUP, :].reshape(b_rows * GROUP, aux)
                partial += lax.dot_general(
                    lhs, rhs, (((1,), (1,)), ((), ())), preferred_element_type=jnp.float32
                )
            total[into] = partial

        return carry

    lax.fori_loop(0, jnp.where(items > 0, items + AHEAD - 1, 0), step, 0)

    out_ref[...] = jnp.zeros_like(out_ref)
    used = [jnp.int32(0)] * outs
    for seg, count in zip(segments, counts):
        used[seg.into] = used[seg.into] + count

    def finish(o, carry):
        @pl.when(pick_row(o, used) > 0)
        def _():
            _, rows, columns = total.shape
            row_d = lax.broadcasted_iota(jnp.int32, (rows, columns), 0) % GROUP
            column_d = lax.broadcasted_iota(jnp.int32, (rows, columns), 1) % GROUP
            kept = jnp.where(row_d == column_d, total[o], 0.0)
            kept = kept.reshape(rows // GROUP, GROUP, columns).sum(axis=1)
            from_b = lax.broadcasted_iota(jnp.int32, (columns, LANES), 0) // GROUP
            to_b = lax.broadcasted_iota(jnp.int32, (columns, LANES), 1)
            gather = jnp.where(from_b == to_b, 1.0, 0.0)
            out_ref[o] = jnp.dot(
                kept,
                gather,
                precision=lax.Precision.HIGHEST,
                preferred_element_type=jnp.float32,
            )

        return carry

    lax.fori_loop(0, outs, finish, 0)

    for ref, pairs_of in zip(added, moves):
        for source, target in pairs_of:
            out_ref[target] += ref[source]


def pair_terms(lists, factors_a, segments, outs, width, d_rows, behind=(), added=()):
    arrays, places = [factors_a], []
    for seg in segments:
        place = []
        for array in (seg.amps, seg.panel):
            known = [n for n, other in enumerate(arrays) if other is array]
            place.append(known[0] if known else len(arrays))
            if not known:
                arrays.append(array)
        places.append(place)
    arrays += behind
    a_rows, _, aux = factors_a.shape
    pairs = segments[0].amps.shape[-3]
    b_rows = segments[0].panel.shape[0]
    most = max(2, *(seg.slots for seg in segments))
    return pl.pallas_call(
        functools.partial(terms_kernel, segments, places, [moves for _, moves in added], d_rows),
        in_specs=[pl.BlockSpec(memory_space=pltpu.SMEM)]
        + [pl.BlockSpec(memory_space=pltpu.VMEM)] * len(added)
        + [pl.BlockSpec(memory_space=pltpu.HBM)] * len(arrays),
        out_specs=pl.BlockSpec(memory_space=pltpu.VMEM),
        scratch_shapes=[
            pltpu.VMEM((AHEAD, most, pairs, d_rows, width), jnp.bfloat16),
            pltpu.VMEM((AHEAD, b_rows, d_rows, aux), jnp.bfloat16),
            pltpu.VMEM((AHEAD, most, a_rows, width, aux), jnp.bfloat16),
            pltpu.VMEM((a_rows, pairs, d_rows, aux), jnp.bfloat16),
            pltpu.VMEM((outs, a_rows * pairs * GROUP, b_rows * GROUP), jnp.float32),
            pltpu.SemaphoreType.DMA((AHEAD, most + 1)),
            pltpu.SemaphoreType.DMA((AHEAD, most)),
        ],
        out_shape=jax.ShapeDtypeStruct((outs, a_rows * pairs, LANES), jnp.float32),
        compiler_params=pltpu.CompilerParams(vmem_limit_bytes=VMEM),
        cost_estimate=SMALL,
        name="pair_terms",
    )(lists, *(array for array, _ in added), *arrays)


def summed_over_narrow(value):
    size = lax.axis_size("narrow")
    me = lax.axis_index("narrow")
    share = value.shape[2] // size

    def part(owner):
        return lax.dynamic_slice_in_dim(value, owner * share, share, 2)

    parts = [part(me)]
    for k in range(1, size):
        to = [(i, (i + k) % size) for i in range(size)]
        parts.append(lax.ppermute(part((me + k) % size), "narrow", to))
    return sum(parts[1:], parts[0])


def local(factors_a, factors_b, amplitudes, screen):
    pairs, d_extent, virtuals = amplitudes.shape
    width = virtuals // screen.shape[1]
    tiles = lax.axis_size("blk")
    position = lax.axis_index("blk")
    extras = MOST - ROUNDS
    d_rows = min(64, d_extent // 4)

    lists = kept_lists(position, screen)
    fullest = lists[MISC * ROW + 1]
    others = lists[MISC * ROW + 2]
    is_first = position % 2 == 0
    is_full = position == fullest
    feeds_one = (position + 1) % tiles == fullest
    feeds_two = (position + 2) % tiles == fullest

    evens, odds = range(0, tiles, 2), range(1, tiles, 2)
    up = [(i, i + 1) for i in evens]
    down = [(i + 1, i) for i in evens]
    around = [(i, (i + 2) % tiles) for i in range(tiles)]

    def run(wrapped, odd, operands):
        lists, factors_a, factors_b, amplitudes = operands
        terms = functools.partial(pair_terms, lists, factors_a, width=width, d_rows=d_rows)
        copy = functools.partial(take, lists, amplitudes, factors_b, width=width)
        columns_of = functools.partial(Segment, panel=factors_b)
        given_to = functools.partial(Segment, amps=amplitudes, slots=extras)

        def ahead(at):
            return (at >= tiles - 2) == wrapped

        def hops(keep):
            return [(at, to) for at, to in around if keep(at)]

        def backs(keep):
            return [(to, at) for at, to in around if keep(at)]

        half, quarter = d_extent // 2, d_extent // 4
        low = 5 * d_extent // 8 // d_rows * d_rows
        high = d_extent - low
        own = columns_of(0, row=OWN, slots=MOST, amps=amplitudes, extent=d_extent)
        after = functools.partial(Columns, AFTER, ROUNDS)
        near = functools.partial(Columns, NEXT, ROUNDS)
        light = functools.partial(columns_of, slots=ROUNDS)
        mine = functools.partial(columns_of, row=MINE, slots=extras)
        if odd:
            given = max(3 * d_extent // 8 // d_rows, 1) * d_rows
            moved = d_extent - given

            def seconds(at):
                return at in odds and ahead(at)

            extra, near_l = copy([Columns(MINE, extras, 0, moved), near(0, low)])
            extra_one = send(extra, up)
            extra_two = send(extra, hops(seconds))
            side_l = send(near_l, down)
            direct, panel = copy(
                [after(0, d_extent), Panel(moved, given)], behind=[extra]
            )
            got_direct = send(direct, hops(lambda at: at in evens))
            far = send(panel, backs(seconds))

            near_h, near_l, own_near_h, panel = copy(
                [near(low, high), near(0, low), near(low, high), Panel(moved, given)],
                behind=[direct],
            )
            near_h = tied(near_h, side_l)
            side_h = send(near_h, down)
            (pass_l,) = copy([after(0, low, passing=side_l)], behind=[near_h])
            panel = tied(panel, side_h, extra_one, pass_l)
            beside = send(panel, down)
            near_l = tied(near_l, panel)
            own_l = send(near_l, up)
            pass_l = tied(pass_l, near_l, got_direct, extra_two)
            on_l = send(pass_l, around)
            (pass_h,) = copy([after(low, high, passing=side_h)], behind=[panel])
            pass_h = tied(pass_h, pass_l, far)
            on_h = send(pass_h, around)
            near_h = tied(own_near_h, pass_h)
            own_h = send(near_h, up)

            first = terms(
                [
                    own,
                    light(2, row=LIGHT_0, amps=got_direct, extent=d_extent),
                    mine(1, amps=extra_one, extent=moved),
                    mine(2, amps=extra_two, extent=moved),
                    given_to(3, row=FED_2, panel=far, extent=given, amp_at=moved),
                ],
                4,
                behind=[near_h],
            )
            then = terms(
                [
                    light(0, row=LIGHT_0, amps=on_l, extent=low),
                    light(1, row=LIGHT_1, amps=on_l, extent=low),
                    light(0, row=LIGHT_1, amps=own_l, extent=low),
                ],
                2,
                behind=[first],
            )
            return terms(
                [
                    light(1, row=LIGHT_0, amps=on_h, extent=high, panel_at=low),
                    light(2, row=LIGHT_1, amps=on_h, extent=high, panel_at=low),
                    light(1, row=LIGHT_1, amps=own_h, extent=high, panel_at=low),
                    given_to(3, row=FED_1, panel=beside, extent=given, amp_at=moved),
                ],
                4,
                added=[(first, [(0, 0), (1, 1), (2, 2), (3, 3)]), (then, [(0, 1), (1, 2)])],
            )
        else:
            def firsts(at):
                return at in evens and ahead(at)

            def early(at):
                return at in odds or ahead(at)

            lead = functools.partial(Columns, LEAD, ROUNDS, 0, half)
            rest = functools.partial(Columns, REST, ROUNDS, 0, half)
            lead_l, lead_h, extra = copy(
                [
                    lead(part=PART),
                    rest(part=REST_PART),
                    Columns(MINE, extras, 0, quarter),
                ]
            )
            got_lead_l = send(lead_l, hops(early))
            got_lead_h = send(lead_h, hops(early))
            cross = send(extra, down)
            beside, panel_0 = copy(
                [near(0, d_extent), Panel(half, quarter)], behind=[lead_l]
            )
            side = send(beside, up)
            far_0 = send(panel_0, backs(firsts))
            panel_1, after_l, after_h = copy(
                [Panel(half + quarter, quarter), after(0, low), after(low, high)],
                behind=[panel_0],
            )

            lead_down_l = send(got_lead_l, down)
            here = terms([own], 1, behind=[panel_1])
            panel_1 = tied(panel_1, cross, here)
            far_1 = send(panel_1, backs(firsts))
            (extra,) = copy(
                [Columns(MINE, extras, quarter, quarter, passing=cross)], behind=[panel_1]
            )
            got_lead_l = tied(got_lead_l, extra)
            lead_down_l = send(got_lead_l, down)
            far_0 = tied(far_0, extra, got_lead_l)
            up_0 = send(far_0, up)
            extra = tied(extra, got_lead_h)
            got_extra = send(extra, hops(ahead))
            got_lead_h = tied(got_lead_h, extra)
            lead_down_h = send(got_lead_h, down)
            after_l = tied(after_l, extra, side, lead_down_l)
            got_l = send(after_l, around)
            far_1 = tied(far_1, after_l)
            up_1 = send(far_1, up)
            got_extra = tied(got_extra, far_1)
            extra_down = send(got_extra, down)
            after_h = tied(after_h, got_extra, lead_down_h)
            got_h = send(after_h, around)

            first = terms(
                [
                    light(0, row=LIGHT_1, amps=side, extent=d_extent),
                    light(0, row=LIGHT_0, amps=lead_down_l, extent=half),
                    light(0, row=LIGHT_0, amps=lead_down_h, extent=half, panel_at=half),
                    light(1, row=MINE_L, amps=got_lead_l, extent=half),
                    light(1, row=MINE_H, amps=got_lead_h, extent=half),
                ],
                2,
                behind=[after_h],
            )

            def both(segment, *rows, **more):
                return [
                    segment(row=row, slot_at=n * ROUNDS, **more) for n, row in enumerate(rows)
                ]

            fed = functools.partial(Segment, amps=amplitudes, slots=ROUNDS, extent=quarter)
            extras_of = functools.partial(light, 1, extent=quarter)
            then = terms(
                both(fed, FED_1_L, FED_1_H, into=0, panel=up_0, amp_at=half)
                + both(fed, FED_2_L, FED_2_H, into=0, panel=far_0, amp_at=half)
                + both(fed, FED_2_L, FED_2_H, into=0, panel=far_1, amp_at=half + quarter)
                + both(extras_of, MINE_L, MINE_H, amps=got_extra)
                + both(extras_of, MINE_L, MINE_H, amps=extra_down, panel_at=quarter)
                + [light(2, row=LIGHT, amps=got_l, extent=low)],
                3,
                behind=[first],
            )
            return terms(
                [light(2, row=LIGHT, amps=got_h, extent=high, panel_at=low)]
                + both(fed, FED_1_L, FED_1_H, into=3, panel=up_1, amp_at=half + quarter),
                4,
                added=[
                    (here, [(0, 0)]),
                    (first, [(0, 1), (1, 2)]),
                    (then, [(0, 3), (1, 1), (2, 2)]),
                ],
            )

    branches = [
        functools.partial(run, wrapped, odd) for wrapped in (False, True) for odd in (False, True)
    ]
    operands = (lists, factors_a, factors_b, amplitudes)
    terms = lax.switch(lists[MISC * ROW], branches, operands)
    def add_round(r, terms):

        def only(row, count):
            sub = lax.dynamic_slice_in_dim(lists, row * ROW + r, 1)
            return jnp.concatenate([sub, jnp.zeros(MOST - 1, jnp.int32), count.reshape(1)])

        has = jnp.where((r < lists[OWN * ROW + MOST]) & ~is_full, 1, 0).astype(jnp.int32)
        own = only(OWN, has)
        moved = [
            rotated(
                take(
                    only(row, has), amplitudes, factors_b, [Columns(0, 1, 0, d_extent)], width
                )[0],
                by,
            )
            for row, by in ((NEXT, 1), (AFTER, 2))
        ]
        segments = [
            Segment(1 + n, 0, 1, columns, factors_b, d_extent) for n, columns in enumerate(moved)
        ]
        kept = [(n, n) for n in range(STEPS + 1)]
        return pair_terms(
            own, factors_a, segments, STEPS + 1, width, d_rows, added=[(terms, kept)]
        )

    terms = lax.fori_loop(ROUNDS, jnp.maximum(others, ROUNDS), add_round, terms)
    a_rows = factors_a.shape[0]
    terms = terms[:, :, : factors_b.shape[0]]
    terms = terms.reshape(STEPS + 1, a_rows, pairs, -1).swapaxes(1, 2)
    summed = summed_over_narrow(terms.reshape(STEPS + 1, 1, -1))
    given_one = rotated(jnp.where(feeds_one, summed[STEPS:], 0.0), 1)
    given_two = rotated(jnp.where(feeds_two, summed[STEPS:], 0.0), 2)
    return jnp.concatenate([summed[:1], summed[1:2] + given_one, summed[2:3] + given_two])


def solution(mesh):
    return jax.shard_map(
        local,
        mesh=mesh,
        in_specs=(P(), P("blk", "narrow", None), P("blk", "narrow", None), P()),
        out_specs=P(None, "blk", "narrow"),
        check_vma=False,
    )
```
